32 devices in a mesh: section: 2 (over core), dp: 16 (over z, y, x).
Axes of the slice: x: 2, y: 2, z: 4, core: 2. Of those that a mesh axis runs over, the one named last changes fastest.
Arguments:
- hidden_in: bfloat16 [2, 16, 128, 768], P(None, 'dp'), may hold values from -6 to 6
- out_grad: bfloat16 [2, 16, 128, 768], P(None, 'dp'), may hold values from -6 to 6
- lengths: int32 [2, 16], P(None, 'dp'), may hold values from 32 to 128, as said below
- gain_mixer: bfloat16 [2, 768], P('section', 'dp'), may hold values from 0.5 to 1.5
- w_input: bfloat16 [2, 768, 2304], P('section', 'dp'), may hold values from -0.21875 to 0.21875
- w_taps: bfloat16 [2, 3, 768], P('section', None, 'dp'), may hold values from -0.3125 to 0.3125
- filters: bfloat16 [2, 128, 768], P('section', None, 'dp'), may hold values from -0.5 to 0.5
- w_output: bfloat16 [2, 768, 768], P('section', 'dp'), may hold values from -0.21875 to 0.21875
- gain_mlp: bfloat16 [2, 768], P('section', 'dp'), may hold values from 0.5 to 1.5
- w_gate_up: bfloat16 [2, 768, 6144], P('section', 'dp'), may hold values from -0.21875 to 0.21875
- w_down: bfloat16 [2, 3072, 768], P('section', None, 'dp'), may hold values from -0.109375 to 0.109375
Outputs:
- layer_out: bfloat16 [2, 2, 16, 128, 768], P('section', None, 'dp')
- input_grad: bfloat16 [2, 2, 16, 128, 768], P('section', None, 'dp')
- grad_gain_mixer: float32 [2, 768], P('section', 'dp')
- grad_w_input: float32 [2, 768, 2304], P('section', 'dp')
- grad_w_taps: float32 [2, 3, 768], P('section', None, 'dp')
- grad_filters: float32 [2, 128, 768], P('section', None, 'dp')
- grad_w_output: float32 [2, 768, 768], P('section', 'dp')
- grad_gain_mlp: float32 [2, 768], P('section', 'dp')
- gate_up_weight_gradient: float32 [2, 768, 6144], P('section', 'dp')
- grad_w_down: float32 [2, 3072, 768], P('section', None, 'dp')
The draws below stay inside these ranges and needn't reach their ends.
Inputs may be any that keep to these rules, and one draw needn't show every extreme that they name: `lengths`: each entry is 32, 64 or 128; some entry equals 128.
All inputs are finite; a program needn't handle non-finite values.
Results may differ from the reference program's by a relative error of at most 0.02.
Values may be sent and summed in bfloat16 or wider, within the bound.
A program may use at most 192 MiB of HBM per device.

```python
import jax
import jax.numpy as jnp
from jax import lax

D = 768
FF = 3072
SEQ = 128
M = 2
BATCH = 16


def draw_lengths(key, part):
    key = jax.random.fold_in(key, 7)
    level_key, pick_key = jax.random.split(key)
    levels = jax.random.randint(level_key, (M, BATCH), 0, 3)
    chosen = jax.random.randint(pick_key, (), 0, M * BATCH)
    flat_index = jnp.arange(M * BATCH).reshape(M, BATCH)
    levels = jnp.where(flat_index == chosen, 2, levels)
    quarter = SEQ // 4
    return jnp.where(levels == 0, quarter, jnp.where(levels == 1, 2 * quarter, SEQ)).astype(jnp.int32)


def block_scale(stream_key, shape, shards, least, high):
    factor_of = 1.0
    for axis_at, shards_of in shards:
        steps = jax.random.uniform(jax.random.fold_in(jax.random.fold_in(stream_key, 6), axis_at), (shards_of,), jnp.float32, least / len(shards), high / len(shards))
        factor_of = factor_of * jnp.repeat(jnp.exp(steps), shape[axis_at] // shards_of).reshape((-1,) + (1,) * (len(shape) - 1 - axis_at))
    return factor_of


def bell_draw(own_key, dims, spread, limit, cuts=(), kind=jnp.bfloat16):
    array = spread * jax.random.normal(own_key, dims, jnp.float32)
    if cuts:
        array = array * block_scale(own_key, dims, cuts, -0.22, 0.18)
    return jnp.clip(array, -limit, limit).astype(kind)


def setup_inputs(seed: int = 0) -> dict:
    key_of = jax.random.split(jax.random.key(seed), 12)
    return {
        "hidden_in": bell_draw(key_of[0], (M, BATCH, SEQ, D), 1.0, 6.0, ((1, 16),)),
        "out_grad": bell_draw(key_of[1], (M, BATCH, SEQ, D), 1.0, 6.0, ((1, 16),)),
        "lengths": draw_lengths(jax.random.fold_in(key_of[11], 71), 0),
        "gain_mixer": jnp.clip(1.0 + 0.1 * jax.random.normal(key_of[3], (2, D), jnp.float32), 0.5, 1.5).astype(jnp.bfloat16),
        "w_input": bell_draw(key_of[4], (2, D, 3 * D), D ** -0.5, 0.21875, ((0, 2), (1, 16))),
        "w_taps": bell_draw(key_of[5], (2, 3, D), (3 * SEQ) ** -0.5, 0.3125, ((0, 2), (2, 16))),
        "filters": bell_draw(key_of[6], (2, SEQ, D), SEQ ** -0.5, 0.5, ((0, 2), (2, 16))),
        "w_output": bell_draw(key_of[7], (2, D, D), D ** -0.5, 0.21875, ((0, 2), (1, 16))),
        "gain_mlp": jnp.clip(1.0 + 0.1 * jax.random.normal(key_of[8], (2, D), jnp.float32), 0.5, 1.5).astype(jnp.bfloat16),
        "w_gate_up": bell_draw(key_of[9], (2, D, 2 * FF), D ** -0.5, 0.21875, ((0, 2), (1, 16))),
        "w_down": bell_draw(key_of[10], (2, FF, D), FF ** -0.5, 0.109375, ((0, 2), (2, 16))),
    }


epsilon = 1e-05

@jax.custom_vjp
def low(v):
    return lax.optimization_barrier(v.astype(jnp.bfloat16)).astype(jnp.float32)

@jax.custom_vjp
def low_back(v):
    return v

def low_keep(v):
    return (low(v), None)

def low_pass(kept, grad):
    return (grad,)

def back_keep(v):
    return (v, None)

def back_low(kept, grad):
    return (low(grad),)
low.defvjp(low_keep, low_pass)
low_back.defvjp(back_keep, back_low)

def exact_dot(left_side, right_side):
    return jnp.dot(left_side, right_side, precision=lax.Precision.HIGHEST, preferred_element_type=jnp.float32)

def norm_rows(input_rows, gain_row):
    centered = input_rows - lax.optimization_barrier(jnp.mean(input_rows, axis=1, keepdims=True))
    variance = lax.optimization_barrier(jnp.mean(centered * centered, axis=1, keepdims=True))
    return centered * lax.rsqrt(variance + epsilon) * gain_row

def delayed(input_rows, places):
    return jnp.pad(input_rows, ((places, 0), (0, 0)))[:input_rows.shape[0]]

def causal_conv(kernel, values_part):
    length = values_part.shape[0]
    product = jnp.fft.rfft(kernel, n=2 * length, axis=0) * jnp.fft.rfft(values_part, n=2 * length, axis=0)
    return jnp.fft.irfft(product, n=2 * length, axis=0)[:length]

def block_layer(input_rows, length_now, parameters):
    gain_one, w_inner, tap_weights, filt_static, w_outer, gain_two, w_expand, w_reduce = parameters
    hidden_size_model = w_outer.shape[0]
    hidden_width = w_reduce.shape[0]
    active_rows = (lax.iota(jnp.int32, input_rows.shape[0]) < length_now).astype(input_rows.dtype)[:, None]
    entered = low(norm_rows(input_rows, gain_one))
    projected = low_back(exact_dot(entered, w_inner))
    queries = projected[:, :hidden_size_model]
    keys_part = projected[:, hidden_size_model:2 * hidden_size_model] * active_rows
    values_part = projected[:, 2 * hidden_size_model:] * active_rows
    dynamic = tap_weights[0] * keys_part + tap_weights[1] * delayed(keys_part, 1) + tap_weights[2] * delayed(keys_part, 2)
    kernel = filt_static + dynamic
    gated_rows = low(queries * causal_conv(kernel, values_part))
    after_mixer = input_rows + low_back(exact_dot(gated_rows, w_outer))
    entered_two = low(norm_rows(after_mixer, gain_two))
    expanded = low_back(exact_dot(entered_two, w_expand))
    activated = low(jax.nn.silu(expanded[:, :hidden_width]) * expanded[:, hidden_width:])
    return after_mixer + low_back(exact_dot(activated, w_reduce))

def reference(hidden_in, out_grad, lengths, gain_mixer, w_input, w_taps, filters, w_output, gain_mlp, w_gate_up, w_down):
    stacked = (gain_mixer, w_input, w_taps, filters, w_output, gain_mlp, w_gate_up, w_down)
    parameters = tuple((member.astype(jnp.float32) for member in stacked))
    total_seqs = M * BATCH
    inputs_flat = hidden_in.reshape(total_seqs, SEQ, D).astype(jnp.float32)
    grads_flat = out_grad.reshape(total_seqs, SEQ, D).astype(jnp.float32)
    lengths_flat = lengths.reshape(total_seqs).astype(jnp.int32)

    def one_sequence(carry, item):
        seq_in, seq_grad, seq_length = item

        def forward(all_params, start, offset):
            first_params = tuple((member[0] for member in all_params))
            second_params = tuple((member[1] for member in all_params))
            middle = low_back(low(block_layer(start, seq_length, first_params)) + offset)
            final = block_layer(middle, seq_length, second_params)
            return (middle, final)
        outputs, pullback = jax.vjp(forward, parameters, seq_in, jnp.zeros_like(seq_in))
        middle, final = outputs
        grad_params, grad_start, grad_middle = pullback((jnp.zeros_like(middle), seq_grad))
        carry = jax.tree.map(jnp.add, carry, grad_params)
        return (carry, (middle, final, grad_start, grad_middle))
    initial = jax.tree.map(jnp.zeros_like, parameters)
    totals, collected = lax.scan(one_sequence, initial, (inputs_flat, grads_flat, lengths_flat))
    middles, finals, grad_starts, grad_middles = collected
    layer_out = jnp.stack([middles, finals]).reshape(2, M, BATCH, SEQ, D).astype(jnp.bfloat16)
    input_grad = jnp.stack([grad_starts, grad_middles]).reshape(2, M, BATCH, SEQ, D).astype(jnp.bfloat16)
    return (layer_out, input_grad, totals[0], totals[1], totals[2], totals[3], totals[4], totals[5], totals[6], totals[7])
```

```python
import functools
import math

import jax
import jax.numpy as jnp
from jax import lax
from jax.experimental import pallas as pl
from jax.experimental.pallas import tpu as pltpu
from jax.sharding import PartitionSpec as P

MESH = pl.DeviceIdType.MESH

epsilon = 1e-05
PIECES = ((0, (128,)), (1, (1152,)), (2, (384,)), (3, (1024, 1024, 1024)), (4, (768, 768)))


def passed_along(value, axis, steps):
    count = lax.axis_size(axis)
    first, last = (max(0, -steps), min(count, count - steps))
    return lax.ppermute(value, axis, [(source, source + steps) for source in range(first, last)])


def split_dot(left_side, right_side):
    return jnp.dot(
        left_side, right_side, precision=lax.Precision.HIGH, preferred_element_type=jnp.float32
    )


def split_rows(left_side, right_side):
    return lax.dot_general(
        left_side,
        right_side,
        (((0,), (0,)), ((), ())),
        precision=lax.Precision.HIGH,
        preferred_element_type=jnp.float32,
    )


def dot_rows(left_side, right_side):
    return lax.dot_general(
        left_side, right_side, (((0,), (0,)), ((), ())), preferred_element_type=jnp.float32
    )


def dot_back(left_side, right_side):
    return lax.dot_general(
        left_side, right_side, (((1,), (1,)), ((), ())), preferred_element_type=jnp.float32
    )


def tables(length):
    period = 2 * length
    freq_index = lax.broadcasted_iota(jnp.int32, (length + 1, length), 0)
    time_index = lax.broadcasted_iota(jnp.int32, (length + 1, length), 1)
    angles = (freq_index * time_index % period).astype(jnp.float32) * (2.0 * math.pi / period)
    edge_rows = (freq_index[:, :1] == 0) | (freq_index[:, :1] == length)
    inverse_weight = jnp.where(edge_rows, 1.0, 2.0) / period
    dft_stack = jnp.concatenate([jnp.cos(angles), -jnp.sin(angles)], axis=0)
    return (dft_stack, inverse_weight)


def spectrum(dft_tables, signal):
    dft_stack, inverse_weight = dft_tables
    stacked_out = split_dot(dft_stack, signal)
    middle_row = stacked_out.shape[0] // 2
    return (stacked_out[:middle_row], stacked_out[middle_row:])


def inverse(dft_tables, real_part, imag_part):
    dft_stack, inverse_weight = dft_tables
    return split_rows(
        dft_stack, jnp.concatenate([inverse_weight * real_part, inverse_weight * imag_part], axis=0)
    )


def normalize(input_rows):
    centered = input_rows - jnp.mean(input_rows, axis=1, keepdims=True)
    inv_scale = lax.rsqrt(jnp.mean(centered * centered, axis=1, keepdims=True) + epsilon)
    return (centered * inv_scale, inv_scale)


def norm_back(grad_normed, normed, inv_scale):
    return inv_scale * (
        grad_normed
        - jnp.mean(grad_normed, axis=1, keepdims=True)
        - normed * jnp.mean(grad_normed * normed, axis=1, keepdims=True)
    )


def delayed(input_rows, places):
    return jnp.pad(input_rows, ((places, 0), (0, 0)))[: input_rows.shape[0]]


def advanced(input_rows, places):
    return jnp.pad(input_rows, ((0, places), (0, 0)))[places:]


def layer_forward(input_rows, active_rows, weights, dft_tables):
    gain_one, w_inner, w_tap_rows, filt_static, w_outer, gain_two, w_expand, w_reduce = weights
    hidden_size_model = w_outer.shape[0]
    hidden_width = w_reduce.shape[0]
    tap_weights = w_tap_rows.astype(jnp.float32)
    normed_one, scale_one = normalize(input_rows)
    entered = (normed_one * gain_one.astype(jnp.float32)).astype(jnp.bfloat16)
    projected = jnp.dot(entered, w_inner, preferred_element_type=jnp.float32)
    queries = projected[:, :hidden_size_model]
    keys_part = projected[:, hidden_size_model : 2 * hidden_size_model] * active_rows
    values_part = projected[:, 2 * hidden_size_model :] * active_rows
    dynamic = (
        tap_weights[0] * keys_part
        + tap_weights[1] * delayed(keys_part, 1)
        + tap_weights[2] * delayed(keys_part, 2)
    )
    kernel = filt_static.astype(jnp.float32) + dynamic
    joint_re, joint_im = spectrum(dft_tables, jnp.concatenate([values_part, kernel], axis=1))
    value_re = joint_re[:, :hidden_size_model]
    kernel_re = joint_re[:, hidden_size_model:]
    value_im = joint_im[:, :hidden_size_model]
    kernel_im = joint_im[:, hidden_size_model:]
    convolved = inverse(
        dft_tables,
        kernel_re * value_re - kernel_im * value_im,
        kernel_re * value_im + kernel_im * value_re,
    )
    gated_rows = (queries * convolved).astype(jnp.bfloat16)
    after_mixer = input_rows + jnp.dot(gated_rows, w_outer, preferred_element_type=jnp.float32)
    normed_two, scale_two = normalize(after_mixer)
    entered_two = (normed_two * gain_two.astype(jnp.float32)).astype(jnp.bfloat16)
    expanded = jnp.dot(entered_two, w_expand, preferred_element_type=jnp.float32)
    gate_part = expanded[:, :hidden_width]
    up_part = expanded[:, hidden_width:]
    activated = (jax.nn.silu(gate_part) * up_part).astype(jnp.bfloat16)
    result = after_mixer + jnp.dot(activated, w_reduce, preferred_element_type=jnp.float32)
    stash = (
        normed_one,
        scale_one,
        entered,
        queries,
        keys_part,
        (value_re, value_im, kernel_re, kernel_im),
        convolved,
        gated_rows,
        normed_two,
        scale_two,
        entered_two,
        gate_part,
        up_part,
        activated,
    )
    return (result, stash)


def mlp_backward(received_gradient, weights, stash):
    gain_one, w_inner, w_tap_rows, filt_static, w_outer, gain_two, w_expand, w_reduce = weights
    (
        normed_one,
        scale_one,
        entered,
        queries,
        keys_part,
        spectra,
        convolved,
        gated_rows,
        normed_two,
        scale_two,
        entered_two,
        gate_part,
        up_part,
        activated,
    ) = stash
    grad_low = received_gradient.astype(jnp.bfloat16)
    grad_reduce_w = dot_rows(activated, grad_low)
    grad_act = dot_back(grad_low, w_reduce)
    sigmoid_gate = jax.nn.sigmoid(gate_part)
    grad_gate = grad_act * up_part * (sigmoid_gate * (1.0 + gate_part * (1.0 - sigmoid_gate)))
    grad_up = grad_act * (gate_part * sigmoid_gate)
    grad_expand = jnp.concatenate([grad_gate, grad_up], axis=1).astype(jnp.bfloat16)
    grad_expand_w = dot_rows(entered_two, grad_expand)
    grad_entered_two = dot_back(grad_expand, w_expand)
    grad_gain_two = jnp.sum(grad_entered_two * normed_two, axis=0)
    grad_after = received_gradient + norm_back(
        grad_entered_two * gain_two.astype(jnp.float32), normed_two, scale_two
    )
    return (grad_after, (grad_gain_two, grad_expand_w, grad_reduce_w))


def mixer_backward(grad_after, active_rows, weights, dft_tables, stash):
    gain_one, w_inner, w_tap_rows, filt_static, w_outer, gain_two, w_expand, w_reduce = weights
    (
        normed_one,
        scale_one,
        entered,
        queries,
        keys_part,
        spectra,
        convolved,
        gated_rows,
        normed_two,
        scale_two,
        entered_two,
        gate_part,
        up_part,
        activated,
    ) = stash
    value_re, value_im, kernel_re, kernel_im = spectra
    hidden_size_model = w_outer.shape[0]
    tap_weights = w_tap_rows.astype(jnp.float32)
    grad_mix_low = grad_after.astype(jnp.bfloat16)
    grad_outer_w = dot_rows(gated_rows, grad_mix_low)
    grad_gated = dot_back(grad_mix_low, w_outer)
    grad_queries = grad_gated * convolved
    grad_conv = grad_gated * queries
    grad_re, grad_im = spectrum(dft_tables, grad_conv)
    paired_re = jnp.concatenate(
        [kernel_re * grad_re + kernel_im * grad_im, value_re * grad_re + value_im * grad_im], axis=1
    )
    paired_im = jnp.concatenate(
        [kernel_re * grad_im - kernel_im * grad_re, value_re * grad_im - value_im * grad_re], axis=1
    )
    paired = inverse(dft_tables, paired_re, paired_im)
    grad_values = paired[:, :hidden_size_model] * active_rows
    grad_kernel = paired[:, hidden_size_model:]
    grad_taps = jnp.stack(
        [
            jnp.sum(grad_kernel * keys_part, axis=0),
            jnp.sum(grad_kernel * delayed(keys_part, 1), axis=0),
            jnp.sum(grad_kernel * delayed(keys_part, 2), axis=0),
        ]
    )
    grad_keys = (
        tap_weights[0] * grad_kernel
        + tap_weights[1] * advanced(grad_kernel, 1)
        + tap_weights[2] * advanced(grad_kernel, 2)
    ) * active_rows
    grad_projected = jnp.concatenate([grad_queries, grad_keys, grad_values], axis=1).astype(
        jnp.bfloat16
    )
    inner_weight_gradient = dot_rows(entered, grad_projected)
    grad_entered = dot_back(grad_projected, w_inner)
    grad_gain_one = jnp.sum(grad_entered * normed_one, axis=0)
    grad_inputs = grad_after + norm_back(
        grad_entered * gain_one.astype(jnp.float32), normed_one, scale_one
    )
    return (
        grad_inputs,
        (grad_gain_one, inner_weight_gradient, grad_taps, grad_kernel, grad_outer_w),
    )


def add_terms(received, flipped):
    return tuple(
        (
            jnp.sum(member, axis=0).T if flip else jnp.sum(member, axis=0)
            for member, flip in zip(received, flipped)
        )
    )


def on_device(
    hidden_in,
    out_grad,
    lengths,
    gain_mixer,
    w_input,
    w_taps,
    filters,
    w_output,
    gain_mlp,
    w_gate_up,
    w_down,
):
    first_section = lax.axis_index("section") == 0
    micro_count = hidden_in.shape[0]
    seq_slots = hidden_in.shape[2]
    hidden_size_model = hidden_in.shape[3]
    dft_tables = tables(seq_slots)
    positions = lax.broadcasted_iota(jnp.int32, (seq_slots, 1), 0)
    weights = (
        lax.all_gather(gain_mixer[0], "dp", axis=0, tiled=True),
        lax.all_gather(w_input[0], "dp", axis=0, tiled=True),
        lax.all_gather(w_taps[0], "dp", axis=1, tiled=True),
        lax.all_gather(filters[0], "dp", axis=1, tiled=True),
        lax.all_gather(w_output[0], "dp", axis=0, tiled=True),
        lax.all_gather(gain_mlp[0], "dp", axis=0, tiled=True),
        lax.all_gather(w_gate_up[0], "dp", axis=0, tiled=True),
        lax.all_gather(w_down[0], "dp", axis=1, tiled=True),
    )
    arriving = jnp.zeros((seq_slots, hidden_size_model), jnp.bfloat16)
    outgoing_list = []
    saved_activations = []
    for forward_step in range(micro_count + 1):
        own_index = min(forward_step, micro_count - 1)
        prior_index = max(forward_step - 1, 0)
        input_rows = jnp.where(first_section, hidden_in[own_index, 0], arriving).astype(jnp.float32)
        length_now = jnp.where(first_section, lengths[own_index, 0], lengths[prior_index, 0])
        active_rows = (positions < length_now).astype(jnp.float32)
        result, stash = layer_forward(input_rows, active_rows, weights, dft_tables)
        outgoing = result.astype(jnp.bfloat16)
        outgoing_list.append(outgoing)
        if forward_step < micro_count:
            arriving = passed_along(outgoing, "section", 1)
        saved_activations.append((input_rows, active_rows))
    coming = jnp.zeros((seq_slots, hidden_size_model), jnp.bfloat16)
    mlp_totals = None
    mixer_totals = None
    grads_out = []
    for backward_step in range(micro_count + 1):
        saved_slot_index = micro_count - backward_step
        last_index = max(micro_count - 1 - backward_step, 0)
        live_factor = 1.0 if backward_step < micro_count else 0.0
        received_gradient = jnp.where(
            first_section,
            coming.astype(jnp.float32),
            out_grad[last_index, 0].astype(jnp.float32) * live_factor,
        )
        input_rows, active_rows = saved_activations[saved_slot_index]
        result, stash = layer_forward(input_rows, active_rows, weights, dft_tables)
        grad_after, mlp_grads = mlp_backward(received_gradient, weights, stash)
        mlp_totals = (
            mlp_grads if mlp_totals is None else jax.tree.map(jnp.add, mlp_totals, mlp_grads)
        )
        grad_inputs, mixer_grads = mixer_backward(
            grad_after, active_rows, weights, dft_tables, stash
        )
        mixer_totals = (
            mixer_grads
            if mixer_totals is None
            else jax.tree.map(jnp.add, mixer_totals, mixer_grads)
        )
        outgoing = grad_inputs.astype(jnp.bfloat16)
        grads_out.append(outgoing)
        if backward_step < micro_count:
            coming = passed_along(outgoing, "section", -1)
    first_outputs = jnp.stack(outgoing_list[:micro_count])
    second_outputs = jnp.stack(outgoing_list[1:])
    layer_out = jnp.where(first_section, first_outputs, second_outputs)[None, :, None]
    first_grads = jnp.stack(
        [grads_out[micro_count - batch_index] for batch_index in range(micro_count)]
    )
    second_grads = jnp.stack(
        [grads_out[micro_count - 1 - batch_index] for batch_index in range(micro_count)]
    )
    input_grad = jnp.where(first_section, first_grads, second_grads)[None, :, None]
    all_parts = (
        lax.all_to_all(
            mixer_totals[0][None].astype(jnp.bfloat16),
            "dp",
            split_axis=1,
            concat_axis=0,
            tiled=True,
        ).astype(jnp.float32),
        lax.all_to_all(
            mixer_totals[1][None].astype(jnp.bfloat16),
            "dp",
            split_axis=1,
            concat_axis=0,
            tiled=True,
        ).astype(jnp.float32),
        lax.all_to_all(
            mixer_totals[2].T[None].astype(jnp.bfloat16),
            "dp",
            split_axis=1,
            concat_axis=0,
            tiled=True,
        ).astype(jnp.float32),
        lax.all_to_all(
            mixer_totals[3].T[None].astype(jnp.bfloat16),
            "dp",
            split_axis=1,
            concat_axis=0,
            tiled=True,
        ).astype(jnp.float32),
        lax.all_to_all(
            mixer_totals[4][None].astype(jnp.bfloat16),
            "dp",
            split_axis=1,
            concat_axis=0,
            tiled=True,
        ).astype(jnp.float32),
        lax.all_to_all(
            mlp_totals[0][None].astype(jnp.bfloat16), "dp", split_axis=1, concat_axis=0, tiled=True
        ).astype(jnp.float32),
        lax.all_to_all(
            mlp_totals[1][None].astype(jnp.bfloat16), "dp", split_axis=1, concat_axis=0, tiled=True
        ).astype(jnp.float32),
        lax.all_to_all(
            mlp_totals[2].T[None].astype(jnp.bfloat16),
            "dp",
            split_axis=1,
            concat_axis=0,
            tiled=True,
        ).astype(jnp.float32),
    )
    summed = add_terms(all_parts, (False, False, True, True, False, False, False, True))
    return (
        layer_out,
        input_grad,
        summed[0][None],
        summed[1][None],
        summed[2][None],
        summed[3][None],
        summed[4][None],
        summed[5][None],
        summed[6][None],
        summed[7][None],
    )


class Place:
    def __init__(self):
        self.core = lax.axis_index("section")
        self.index = lax.axis_index("dp")
        self.z = self.index // 4
        self.y = self.index // 2 % 2
        self.x = self.index % 2
        self.layer = 1 - (self.z + 1) // 2 % 2
        self.partner_z = self.z + 1 - 2 * (self.z % 2)

    def chip(self, z=None, y=None, x=None):
        z, y, x = (a if a is not None else b for a, b in ((z, self.z), (y, self.y), (x, self.x)))
        return z * 4 + y * 2 + x

    def x_side(self):
        return (self.core, self.chip(x=1 - self.x))

    def y_side(self):
        return (self.core, self.chip(y=1 - self.y))

    def sibling(self):
        return (1 - self.core, self.index)

    def greet(self):
        barrier = pltpu.get_barrier_semaphore()
        others = [self.x_side(), self.y_side(), self.sibling()]
        for step in (1, 2, 3):
            chip = self.chip(z=(self.z + step) % 4)
            others += [(0, chip), (1, chip)]
        for other in others:
            pl.semaphore_signal(barrier, inc=1, device_id=other, device_id_type=MESH)
        pl.semaphore_wait(barrier, len(others))


def planes_of(layer):
    return (1 - layer, 2 + layer)


def remote(source, target, send, receive, device):
    return pltpu.make_async_remote_copy(
        src_ref=source,
        dst_ref=target,
        send_sem=send,
        recv_sem=receive,
        device_id=device,
        device_id_type=MESH,
    )


def chunks_of(pieces):
    table = []
    for array, parts in pieces:
        start = 0
        for width in parts:
            table.append((array, start, width))
            start += width
    return table


def gather_kernel(table, halves, *refs):
    count = len(halves)
    shards, (hidden, out_grad, live), rest = refs[:count], refs[count : count + 3], refs[count + 3 :]
    gathered, (feed, feed_live), rest = rest[:count], rest[count : count + 2], rest[count + 2 :]
    z_send, z_recv, one_send, one_recv, two_send, two_recv, side_send, side_recv, feed_sems = rest
    here = Place()
    here.greet()
    last = len(table)

    def columns(chunk, half):
        array, start, width = table[chunk]
        return pl.ds(pl.multiple_of(half * halves[array] + start, 128), width)

    def block(chunk, z, y, x):
        return gathered[table[chunk][0]].at[z, y, x, :, columns(chunk, here.core)]

    def z_copy(chunk, plane, half, number):
        array = table[chunk][0]
        cut = columns(chunk, half)
        source = shards[array].at[:, cut]
        target = gathered[array].at[here.z, here.y, here.x, :, cut]
        away = remote(
            source,
            target,
            z_send.at[chunk, number, half],
            z_recv.at[chunk, here.z],
            (half, here.chip(z=plane)),
        )
        near = pltpu.make_async_copy(source, target, z_recv.at[chunk, here.z])
        return away, near

    def z_all(chunk, act):
        for number, plane in enumerate(planes_of(here.core)):
            for half in (0, 1):
                away, near = z_copy(chunk, plane, half, number)
                own = (plane == here.z) & (here.core == half)
                act(own, away, near)

    def z_start(chunk):
        def act(own, away, near):
            pl.when(own)(near.start)
            pl.when(jnp.logical_not(own))(away.start)

        z_all(chunk, act)

    def z_sent(chunk):
        z_all(chunk, lambda own, away, near: pl.when(jnp.logical_not(own))(away.wait_send))

    def arrived(target, receive):
        pltpu.make_async_copy(target, target, receive).wait()

    def first(chunk, z):
        own = block(chunk, z, here.y, here.x)
        side = here.x_side() if z < 2 else here.y_side()
        return remote(own, own, one_send.at[chunk, z], one_recv.at[chunk, z], side)

    def second(chunk, z):
        array = table[chunk][0]
        cut = columns(chunk, here.core)
        if z < 2:
            pair = gathered[array].at[z, here.y, :, :, cut]
            side = here.y_side()
        else:
            pair = gathered[array].at[z, :, here.x, :, cut]
            side = here.x_side()
        return remote(pair, pair, two_send.at[chunk, z], two_recv.at[chunk, z], side)

    def across(chunk):
        whole = gathered[table[chunk][0]].at[:, :, :, :, columns(chunk, here.core)]
        return remote(whole, whole, side_send.at[chunk], side_recv.at[chunk], here.sibling())

    own_feed = here.core == here.layer
    partner = (here.core, here.chip(z=here.partner_z))

    def feed_copies(mine, other):
        keep = pltpu.make_async_copy(mine, feed, feed_sems.at[0])
        give = remote(other, feed, feed_sems.at[1], feed_sems.at[0], partner)
        give_live = remote(live, feed_live, feed_sems.at[3], feed_sems.at[2], partner)
        return keep, give, give_live

    keep_live = pltpu.make_async_copy(live, feed_live, feed_sems.at[2])
    for layer, mine, other in ((0, hidden, out_grad), (1, out_grad, hidden)):

        @pl.when(own_feed & (here.layer == layer))
        def _():
            keep, give, give_live = feed_copies(mine, other)
            keep.start()
            keep_live.start()
            give.start()
            give_live.start()

    window = 2
    for chunk in range(min(window, last)):
        z_start(chunk)
    for step in range(last + 2):
        if step < last:
            for z in range(4):
                arrived(block(step, z, here.y, here.x), z_recv.at[step, z])
                first(step, z).start()
            if step + window < last:
                z_start(step + window)
        if 1 <= step <= last:
            for z in range(4):
                first(step - 1, z).wait_recv()
                second(step - 1, z).start()
        if 2 <= step:
            for z in range(4):
                second(step - 2, z).wait_recv()
            across(step - 2).start()
    arrived(feed, feed_sems.at[0])
    arrived(feed_live, feed_sems.at[2])

    @pl.when(own_feed)
    def _():
        keep, give, give_live = feed_copies(hidden, out_grad)
        give.wait_send()
        give_live.wait_send()

    for chunk in range(last):
        z_sent(chunk)
        for z in range(4):
            first(chunk, z).wait_send()
            second(chunk, z).wait_send()
        across(chunk).wait()


def gather(shards, hidden, out_grad, live, pieces):
    table = chunks_of(pieces)
    halves = [shard.shape[1] // 2 for shard in shards]
    kinds = [jax.ShapeDtypeStruct((4, 2, 2) + shard.shape, shard.dtype) for shard in shards]
    kinds += [jax.ShapeDtypeStruct(hidden.shape, hidden.dtype), jax.ShapeDtypeStruct(live.shape, live.dtype)]
    anywhere = pl.BlockSpec(memory_space=pl.ANY)
    dma, last = pltpu.SemaphoreType.DMA, len(table)
    results = pl.pallas_call(
        functools.partial(gather_kernel, table, halves),
        out_shape=kinds,
        in_specs=[anywhere] * (len(shards) + 3),
        out_specs=[anywhere] * len(kinds),
        scratch_shapes=[
            dma((last, 2, 2)),
            dma((last, 4)),
            dma((last, 4)),
            dma((last, 4)),
            dma((last, 4)),
            dma((last, 4)),
            dma((last,)),
            dma((last,)),
            dma((4,)),
        ],
        compiler_params=pltpu.CompilerParams(collective_id=0, has_side_effects=True),
    )(*shards, hidden, out_grad, live)
    whole = [result.reshape(-1, result.shape[-1]) for result in results[: len(shards)]]
    return whole, results[-2], results[-1]


def scatter_kernel(table, halves, *refs):
    count, last = len(halves), len(table)
    grads, (own_out, own_grad), rest = refs[:count], refs[count : count + 2], refs[count + 2 :]
    sums, (kept_out, kept_grad), rest = rest[:count], rest[count : count + 2], rest[count + 2 :]
    mine, core_in, one_in, two_in, final_in = (rest[k * last : (k + 1) * last] for k in range(5))
    (load, side_send, side_recv, one_send, one_recv, two_send, two_recv, z_send, z_recv, keep) = rest[5 * last :]
    here = Place()
    here.greet()

    def columns(chunk, half):
        array, start, width = table[chunk]
        return pl.ds(pl.multiple_of(half * halves[array] + start, 128), width)

    def fetch(chunk):
        source = grads[table[chunk][0]].at[:, :, :, :, columns(chunk, here.core)]
        return pltpu.make_async_copy(source, mine[chunk], load.at[chunk])

    def across(chunk):
        source = grads[table[chunk][0]].at[:, :, :, :, columns(chunk, 1 - here.core)]
        return remote(source, core_in[chunk], side_send.at[chunk], side_recv.at[chunk], here.sibling())

    def first(chunk, z):
        if z < 2:
            source, side = mine[chunk].at[z, 1 - here.y], here.y_side()
        else:
            source, side = mine[chunk].at[z, :, 1 - here.x], here.x_side()
        return remote(source, one_in[chunk].at[z], one_send.at[chunk, z], one_recv.at[chunk, z], side)

    def second(chunk, z):
        if z < 2:
            source, side = mine[chunk].at[z, here.y, 1 - here.x], here.x_side()
        else:
            source, side = mine[chunk].at[z, 1 - here.y, here.x], here.y_side()
        return remote(source, two_in[chunk].at[z], two_send.at[chunk, z], two_recv.at[chunk, z], side)

    def third(chunk, z):
        source = mine[chunk].at[z, here.y, here.x]
        slot = here.z // 2
        target = final_in[chunk].at[slot, here.core]
        receive = z_recv.at[chunk, slot, here.core]
        away = remote(source, target, z_send.at[chunk, z], receive, (here.layer, here.chip(z=z)))
        near = pltpu.make_async_copy(source, target, receive)
        own = (here.z == z) & (here.core == here.layer)
        return own, away, near

    def add(target, other):
        target[...] = (target[...].astype(jnp.float32) + other[...].astype(jnp.float32)).astype(target.dtype)

    apart = here.core != here.layer
    partner = (1 - here.core, here.chip(z=here.partner_z))
    swaps = [
        remote(own_out, kept_out, keep.at[0], keep.at[1], partner),
        remote(own_grad, kept_grad, keep.at[2], keep.at[3], partner),
    ]
    stays = [
        pltpu.make_async_copy(own_out, kept_out, keep.at[1]),
        pltpu.make_async_copy(own_grad, kept_grad, keep.at[3]),
    ]

    window = 2
    for chunk in range(min(window, last)):
        fetch(chunk).start()
        across(chunk).start()
    for swap, stay in zip(swaps, stays):
        pl.when(apart)(swap.start)
        pl.when(jnp.logical_not(apart))(stay.start)
    for step in range(last + 3):
        if step < last:
            fetch(step).wait()
            across(step).wait_recv()
            if step + window < last:
                fetch(step + window).start()
                across(step + window).start()
            for z in range(4):
                for y in range(2):
                    add(mine[step].at[z, y], core_in[step].at[z, y])
            for z in range(4):
                first(step, z).start()
        if 1 <= step <= last:
            chunk = step - 1
            for z in range(4):
                first(chunk, z).wait_recv()
                for k in range(2):
                    if z < 2:
                        add(mine[chunk].at[z, here.y, k], one_in[chunk].at[z, k])
                    else:
                        add(mine[chunk].at[z, k, here.x], one_in[chunk].at[z, k])
                second(chunk, z).start()
        if 2 <= step <= last + 1:
            chunk = step - 2
            for z in range(4):
                second(chunk, z).wait_recv()
                add(mine[chunk].at[z, here.y, here.x], two_in[chunk].at[z])
                own, away, near = third(chunk, z)
                pl.when(own)(near.start)
                pl.when(jnp.logical_not(own))(away.start)
        if 3 <= step:
            chunk = step - 3
            array = table[chunk][0]
            for half in (0, 1):
                for slot in (0, 1):
                    target = final_in[chunk].at[slot, half]
                    pltpu.make_async_copy(target, target, z_recv.at[chunk, slot, half]).wait()
                sums[array][:, columns(chunk, half)] = final_in[chunk][0, half].astype(jnp.float32) + final_in[
                    chunk
                ][1, half].astype(jnp.float32)
    for swap, stay in zip(swaps, stays):
        pl.when(apart)(swap.wait)
        pl.when(jnp.logical_not(apart))(stay.wait)
    for chunk in range(last):
        across(chunk).wait_send()
        for z in range(4):
            first(chunk, z).wait_send()
            second(chunk, z).wait_send()
            own, away, near = third(chunk, z)
            pl.when(jnp.logical_not(own))(away.wait_send)


def scatter(grads, own_out, own_grad, pieces):
    table = chunks_of(pieces)
    halves = [grad.shape[1] // 2 for grad in grads]
    rows = grads[0].shape[0] // 16
    grads = [grad.reshape(4, 2, 2, rows, grad.shape[1]) for grad in grads]
    kinds = [jax.ShapeDtypeStruct((rows, grad.shape[-1]), jnp.float32) for grad in grads]
    kinds += [jax.ShapeDtypeStruct(own_out.shape, own_out.dtype)] * 2
    anywhere = pl.BlockSpec(memory_space=pl.ANY)
    inside = pl.BlockSpec(memory_space=pltpu.VMEM)
    dma, last = pltpu.SemaphoreType.DMA, len(table)
    room = []
    for lead in ((4, 2, 2), (4, 2, 2), (4, 2), (4,), (2, 2)):
        room += [pltpu.VMEM(lead + (rows, width), jnp.bfloat16) for _, _, width in table]
    return pl.pallas_call(
        functools.partial(scatter_kernel, table, halves),
        out_shape=kinds,
        in_specs=[anywhere] * (len(grads) + 2),
        out_specs=[inside] * len(grads) + [anywhere] * 2,
        scratch_shapes=room
        + [
            dma((last,)),
            dma((last,)),
            dma((last,)),
            dma((last, 4)),
            dma((last, 4)),
            dma((last, 4)),
            dma((last, 4)),
            dma((last, 4)),
            dma((last, 2, 2)),
            dma((4,)),
        ],
        compiler_params=pltpu.CompilerParams(
            collective_id=1, has_side_effects=True, vmem_limit_bytes=56 * 1024 * 1024
        ),
    )(*grads, own_out, own_grad)

def fast_device(
    hidden_in, out_grad, lengths, gain_mixer, w_input, w_taps, filters, w_output, gain_mlp, w_gate_up, w_down
):
    rows = gain_mixer.shape[1]
    micro, _, slots, width = hidden_in.shape
    dft_tables = tables(slots)
    layer = 1 - (lax.axis_index("dp") // 4 + 1) // 2 % 2
    small = jnp.concatenate(
        [filters[0].T, w_taps[0].T, gain_mixer[0][:, None], gain_mlp[0][:, None]], axis=1
    )
    small = jnp.pad(small, ((0, 0), (0, 256 - small.shape[1])))
    shards = (small, w_input[0], w_output[0], w_gate_up[0], w_down[0].T)
    live = jnp.broadcast_to(lengths.astype(jnp.float32).reshape(micro, 1, 1), (micro, 8, 128))
    whole, feed, feed_live = gather(shards, hidden_in[:, 0], out_grad[:, 0], live, PIECES)
    small, w_in, w_out, w_gu, w_dt = whole
    weights = (small[:, 131], w_in, small[:, 128:131].T, small[:, :128].T, w_out, small[:, 132], w_gu, w_dt.T)
    positions = lax.broadcasted_iota(jnp.int32, (slots, 1), 0).astype(jnp.float32)
    active = [(positions < feed_live[m, 0, 0]).astype(jnp.float32) for m in range(micro)]

    forward_pairs = [(4 + k, k) for k in range(4)] + [(8 + k, 12 + k) for k in range(4)]
    back_pairs = [(b, a) for a, b in forward_pairs]

    def run(inputs):
        pairs = [layer_forward(inputs[m].astype(jnp.float32), active[m], weights, dft_tables) for m in range(micro)]
        return jnp.stack([p[0] for p in pairs]).astype(jnp.bfloat16), [p[1] for p in pairs]

    def back(cotangent, stashes):
        outs, totals = [], None
        for m in range(micro):
            grad_after, mlp_grads = mlp_backward(cotangent[m].astype(jnp.float32), weights, stashes[m])
            grad_in, mixer_grads = mixer_backward(grad_after, active[m], weights, dft_tables, stashes[m])
            outs.append(grad_in.astype(jnp.bfloat16))
            both = (mlp_grads, mixer_grads)
            totals = both if totals is None else jax.tree.map(jnp.add, totals, both)
        return jnp.stack(outs), totals

    first_out, _ = run(feed)
    arrived = lax.ppermute(first_out, "dp", forward_pairs)
    result, stashes = run(jnp.where(layer == 0, feed, arrived))
    early, _ = back(feed, stashes)
    arrived = lax.ppermute(early, "dp", back_pairs)
    grad, (mlp, mixer) = back(jnp.where(layer == 1, feed, arrived), stashes)
    grad_gain_two, grad_gu, grad_dn = mlp
    grad_gain_one, grad_in, grad_taps, grad_filters, grad_outer = mixer
    small_grad = jnp.concatenate(
        [grad_filters.T, grad_taps.T, grad_gain_one[:, None], grad_gain_two[:, None]], axis=1
    )
    small_grad = jnp.pad(small_grad, ((0, 0), (0, 256 - small_grad.shape[1])))
    terms = [t.astype(jnp.bfloat16) for t in (small_grad, grad_in, grad_outer, grad_gu, grad_dn.T)]
    s_small, s_in, s_out, s_gu, s_dt, layer_out, input_grad = scatter(terms, result, grad, PIECES)
    return (
        layer_out[None, :, None],
        input_grad[None, :, None],
        s_small[None, :, 131],
        s_in[None],
        s_small[:, 128:131].T[None],
        s_small[:, :128].T[None],
        s_out[None],
        s_small[None, :, 132],
        s_gu[None],
        s_dt.T[None],
    )


def solution(mesh):
    placed = (
        P(None, "dp", None, None),
        P(None, "dp", None, None),
        P(None, "dp"),
        P("section", "dp"),
        P("section", "dp", None),
        P("section", None, "dp"),
        P("section", None, "dp"),
        P("section", "dp", None),
        P("section", "dp"),
        P("section", "dp", None),
        P("section", None, "dp"),
    )
    return jax.shard_map(
        fast_device if mesh.shape["dp"] == 16 and mesh.shape["section"] == 2 else on_device,
        mesh=mesh,
        in_specs=placed,
        out_specs=(
            P("section", None, "dp", None, None),
            P("section", None, "dp", None, None),
            P("section", "dp"),
            P("section", "dp", None),
            P("section", None, "dp"),
            P("section", None, "dp"),
            P("section", "dp", None),
            P("section", "dp"),
            P("section", "dp", None),
            P("section", None, "dp"),
        ),
        check_vma=False,
    )
```

```python
import functools
import math

import jax
import jax.numpy as jnp
from jax import lax
from jax.experimental import pallas as pl
from jax.experimental.pallas import tpu as pltpu
from jax.sharding import PartitionSpec as P

MESH = pl.DeviceIdType.MESH

epsilon = 1e-05
PIECES = ((0, (128,)), (1, (1152,)), (2, (384,)), (3, (1024, 1024, 1024)), (4, (768, 768)))
TERM_PIECES = ((4, (768, 768)), (3, (1024, 1024, 1024)), (2, (384,)), (1, (384, 384, 384)), (0, (128,)))


def passed_along(value, axis, steps):
    count = lax.axis_size(axis)
    first, last = (max(0, -steps), min(count, count - steps))
    return lax.ppermute(value, axis, [(source, source + steps) for source in range(first, last)])


def split_dot(left_side, right_side):
    return jnp.dot(
        left_side, right_side, precision=lax.Precision.HIGH, preferred_element_type=jnp.float32
    )


def split_rows(left_side, right_side):
    return lax.dot_general(
        left_side,
        right_side,
        (((0,), (0,)), ((), ())),
        precision=lax.Precision.HIGH,
        preferred_element_type=jnp.float32,
    )


def dot_rows(left_side, right_side):
    return lax.dot_general(
        left_side, right_side, (((0,), (0,)), ((), ())), preferred_element_type=jnp.float32
    )


def dot_back(left_side, right_side):
    return lax.dot_general(
        left_side, right_side, (((1,), (1,)), ((), ())), preferred_element_type=jnp.float32
    )


def tables(length):
    period = 2 * length
    freq_index = lax.broadcasted_iota(jnp.int32, (length + 1, length), 0)
    time_index = lax.broadcasted_iota(jnp.int32, (length + 1, length), 1)
    angles = (freq_index * time_index % period).astype(jnp.float32) * (2.0 * math.pi / period)
    edge_rows = (freq_index[:, :1] == 0) | (freq_index[:, :1] == length)
    inverse_weight = jnp.where(edge_rows, 1.0, 2.0) / period
    dft_stack = jnp.concatenate([jnp.cos(angles), -jnp.sin(angles)], axis=0)
    return (dft_stack, inverse_weight)


def spectrum(dft_tables, signal):
    dft_stack, inverse_weight = dft_tables
    stacked_out = split_dot(dft_stack, signal)
    middle_row = stacked_out.shape[0] // 2
    return (stacked_out[:middle_row], stacked_out[middle_row:])


def inverse(dft_tables, real_part, imag_part):
    dft_stack, inverse_weight = dft_tables
    return split_rows(
        dft_stack, jnp.concatenate([inverse_weight * real_part, inverse_weight * imag_part], axis=0)
    )


def normalize(input_rows):
    centered = input_rows - jnp.mean(input_rows, axis=1, keepdims=True)
    inv_scale = lax.rsqrt(jnp.mean(centered * centered, axis=1, keepdims=True) + epsilon)
    return (centered * inv_scale, inv_scale)


def norm_back(grad_normed, normed, inv_scale):
    return inv_scale * (
        grad_normed
        - jnp.mean(grad_normed, axis=1, keepdims=True)
        - normed * jnp.mean(grad_normed * normed, axis=1, keepdims=True)
    )


def delayed(input_rows, places):
    return jnp.pad(input_rows, ((places, 0), (0, 0)))[: input_rows.shape[0]]


def advanced(input_rows, places):
    return jnp.pad(input_rows, ((0, places), (0, 0)))[places:]


def layer_forward(input_rows, active_rows, weights, dft_tables):
    gain_one, w_inner, w_tap_rows, filt_static, w_outer, gain_two, w_expand, w_reduce = weights
    hidden_size_model = w_outer.shape[0]
    hidden_width = w_reduce.shape[0]
    tap_weights = w_tap_rows.astype(jnp.float32)
    normed_one, scale_one = normalize(input_rows)
    entered = (normed_one * gain_one.astype(jnp.float32)).astype(jnp.bfloat16)
    projected = jnp.dot(entered, w_inner, preferred_element_type=jnp.float32)
    queries = projected[:, :hidden_size_model]
    keys_part = projected[:, hidden_size_model : 2 * hidden_size_model] * active_rows
    values_part = projected[:, 2 * hidden_size_model :] * active_rows
    dynamic = (
        tap_weights[0] * keys_part
        + tap_weights[1] * delayed(keys_part, 1)
        + tap_weights[2] * delayed(keys_part, 2)
    )
    kernel = filt_static.astype(jnp.float32) + dynamic
    joint_re, joint_im = spectrum(dft_tables, jnp.concatenate([values_part, kernel], axis=1))
    value_re = joint_re[:, :hidden_size_model]
    kernel_re = joint_re[:, hidden_size_model:]
    value_im = joint_im[:, :hidden_size_model]
    kernel_im = joint_im[:, hidden_size_model:]
    convolved = inverse(
        dft_tables,
        kernel_re * value_re - kernel_im * value_im,
        kernel_re * value_im + kernel_im * value_re,
    )
    gated_rows = (queries * convolved).astype(jnp.bfloat16)
    after_mixer = input_rows + jnp.dot(gated_rows, w_outer, preferred_element_type=jnp.float32)
    normed_two, scale_two = normalize(after_mixer)
    entered_two = (normed_two * gain_two.astype(jnp.float32)).astype(jnp.bfloat16)
    expanded = jnp.dot(entered_two, w_expand, preferred_element_type=jnp.float32)
    gate_part = expanded[:, :hidden_width]
    up_part = expanded[:, hidden_width:]
    activated = (jax.nn.silu(gate_part) * up_part).astype(jnp.bfloat16)
    result = after_mixer + jnp.dot(activated, w_reduce, preferred_element_type=jnp.float32)
    stash = (
        normed_one,
        scale_one,
        entered,
        queries,
        keys_part,
        (value_re, value_im, kernel_re, kernel_im),
        convolved,
        gated_rows,
        normed_two,
        scale_two,
        entered_two,
        gate_part,
        up_part,
        activated,
    )
    return (result, stash)


def mlp_backward(received_gradient, weights, stash):
    gain_one, w_inner, w_tap_rows, filt_static, w_outer, gain_two, w_expand, w_reduce = weights
    (
        normed_one,
        scale_one,
        entered,
        queries,
        keys_part,
        spectra,
        convolved,
        gated_rows,
        normed_two,
        scale_two,
        entered_two,
        gate_part,
        up_part,
        activated,
    ) = stash
    grad_low = received_gradient.astype(jnp.bfloat16)
    grad_reduce_w = dot_rows(activated, grad_low)
    grad_act = dot_back(grad_low, w_reduce)
    sigmoid_gate = jax.nn.sigmoid(gate_part)
    grad_gate = grad_act * up_part * (sigmoid_gate * (1.0 + gate_part * (1.0 - sigmoid_gate)))
    grad_up = grad_act * (gate_part * sigmoid_gate)
    grad_expand = jnp.concatenate([grad_gate, grad_up], axis=1).astype(jnp.bfloat16)
    grad_expand_w = dot_rows(entered_two, grad_expand)
    grad_entered_two = dot_back(grad_expand, w_expand)
    grad_gain_two = jnp.sum(grad_entered_two * normed_two, axis=0)
    grad_after = received_gradient + norm_back(
        grad_entered_two * gain_two.astype(jnp.float32), normed_two, scale_two
    )
    return (grad_after, (grad_gain_two, grad_expand_w, grad_reduce_w))


def mixer_backward(grad_after, active_rows, weights, dft_tables, stash):
    gain_one, w_inner, w_tap_rows, filt_static, w_outer, gain_two, w_expand, w_reduce = weights
    (
        normed_one,
        scale_one,
        entered,
        queries,
        keys_part,
        spectra,
        convolved,
        gated_rows,
        normed_two,
        scale_two,
        entered_two,
        gate_part,
        up_part,
        activated,
    ) = stash
    value_re, value_im, kernel_re, kernel_im = spectra
    hidden_size_model = w_outer.shape[0]
    tap_weights = w_tap_rows.astype(jnp.float32)
    grad_mix_low = grad_after.astype(jnp.bfloat16)
    grad_outer_w = dot_rows(gated_rows, grad_mix_low)
    grad_gated = dot_back(grad_mix_low, w_outer)
    grad_queries = grad_gated * convolved
    grad_conv = grad_gated * queries
    grad_re, grad_im = spectrum(dft_tables, grad_conv)
    paired_re = jnp.concatenate(
        [kernel_re * grad_re + kernel_im * grad_im, value_re * grad_re + value_im * grad_im], axis=1
    )
    paired_im = jnp.concatenate(
        [kernel_re * grad_im - kernel_im * grad_re, value_re * grad_im - value_im * grad_re], axis=1
    )
    paired = inverse(dft_tables, paired_re, paired_im)
    grad_values = paired[:, :hidden_size_model] * active_rows
    grad_kernel = paired[:, hidden_size_model:]
    grad_taps = jnp.stack(
        [
            jnp.sum(grad_kernel * keys_part, axis=0),
            jnp.sum(grad_kernel * delayed(keys_part, 1), axis=0),
            jnp.sum(grad_kernel * delayed(keys_part, 2), axis=0),
        ]
    )
    grad_keys = (
        tap_weights[0] * grad_kernel
        + tap_weights[1] * advanced(grad_kernel, 1)
        + tap_weights[2] * advanced(grad_kernel, 2)
    ) * active_rows
    grad_projected = jnp.concatenate([grad_queries, grad_keys, grad_values], axis=1).astype(
        jnp.bfloat16
    )
    inner_weight_gradient = dot_rows(entered, grad_projected)
    grad_entered = dot_back(grad_projected, w_inner)
    grad_gain_one = jnp.sum(grad_entered * normed_one, axis=0)
    grad_inputs = grad_after + norm_back(
        grad_entered * gain_one.astype(jnp.float32), normed_one, scale_one
    )
    return (
        grad_inputs,
        (grad_gain_one, inner_weight_gradient, grad_taps, grad_kernel, grad_outer_w),
    )


def add_terms(received, flipped):
    return tuple(
        (
            jnp.sum(member, axis=0).T if flip else jnp.sum(member, axis=0)
            for member, flip in zip(received, flipped)
        )
    )


def on_device(
    hidden_in,
    out_grad,
    lengths,
    gain_mixer,
    w_input,
    w_taps,
    filters,
    w_output,
    gain_mlp,
    w_gate_up,
    w_down,
):
    first_section = lax.axis_index("section") == 0
    micro_count = hidden_in.shape[0]
    seq_slots = hidden_in.shape[2]
    hidden_size_model = hidden_in.shape[3]
    dft_tables = tables(seq_slots)
    positions = lax.broadcasted_iota(jnp.int32, (seq_slots, 1), 0)
    weights = (
        lax.all_gather(gain_mixer[0], "dp", axis=0, tiled=True),
        lax.all_gather(w_input[0], "dp", axis=0, tiled=True),
        lax.all_gather(w_taps[0], "dp", axis=1, tiled=True),
        lax.all_gather(filters[0], "dp", axis=1, tiled=True),
        lax.all_gather(w_output[0], "dp", axis=0, tiled=True),
        lax.all_gather(gain_mlp[0], "dp", axis=0, tiled=True),
        lax.all_gather(w_gate_up[0], "dp", axis=0, tiled=True),
        lax.all_gather(w_down[0], "dp", axis=1, tiled=True),
    )
    arriving = jnp.zeros((seq_slots, hidden_size_model), jnp.bfloat16)
    outgoing_list = []
    saved_activations = []
    for forward_step in range(micro_count + 1):
        own_index = min(forward_step, micro_count - 1)
        prior_index = max(forward_step - 1, 0)
        input_rows = jnp.where(first_section, hidden_in[own_index, 0], arriving).astype(jnp.float32)
        length_now = jnp.where(first_section, lengths[own_index, 0], lengths[prior_index, 0])
        active_rows = (positions < length_now).astype(jnp.float32)
        result, stash = layer_forward(input_rows, active_rows, weights, dft_tables)
        outgoing = result.astype(jnp.bfloat16)
        outgoing_list.append(outgoing)
        if forward_step < micro_count:
            arriving = passed_along(outgoing, "section", 1)
        saved_activations.append((input_rows, active_rows))
    coming = jnp.zeros((seq_slots, hidden_size_model), jnp.bfloat16)
    mlp_totals = None
    mixer_totals = None
    grads_out = []
    for backward_step in range(micro_count + 1):
        saved_slot_index = micro_count - backward_step
        last_index = max(micro_count - 1 - backward_step, 0)
        live_factor = 1.0 if backward_step < micro_count else 0.0
        received_gradient = jnp.where(
            first_section,
            coming.astype(jnp.float32),
            out_grad[last_index, 0].astype(jnp.float32) * live_factor,
        )
        input_rows, active_rows = saved_activations[saved_slot_index]
        result, stash = layer_forward(input_rows, active_rows, weights, dft_tables)
        grad_after, mlp_grads = mlp_backward(received_gradient, weights, stash)
        mlp_totals = (
            mlp_grads if mlp_totals is None else jax.tree.map(jnp.add, mlp_totals, mlp_grads)
        )
        grad_inputs, mixer_grads = mixer_backward(
            grad_after, active_rows, weights, dft_tables, stash
        )
        mixer_totals = (
            mixer_grads
            if mixer_totals is None
            else jax.tree.map(jnp.add, mixer_totals, mixer_grads)
        )
        outgoing = grad_inputs.astype(jnp.bfloat16)
        grads_out.append(outgoing)
        if backward_step < micro_count:
            coming = passed_along(outgoing, "section", -1)
    first_outputs = jnp.stack(outgoing_list[:micro_count])
    second_outputs = jnp.stack(outgoing_list[1:])
    layer_out = jnp.where(first_section, first_outputs, second_outputs)[None, :, None]
    first_grads = jnp.stack(
        [grads_out[micro_count - batch_index] for batch_index in range(micro_count)]
    )
    second_grads = jnp.stack(
        [grads_out[micro_count - 1 - batch_index] for batch_index in range(micro_count)]
    )
    input_grad = jnp.where(first_section, first_grads, second_grads)[None, :, None]
    all_parts = (
        lax.all_to_all(
            mixer_totals[0][None].astype(jnp.bfloat16),
            "dp",
            split_axis=1,
            concat_axis=0,
            tiled=True,
        ).astype(jnp.float32),
        lax.all_to_all(
            mixer_totals[1][None].astype(jnp.bfloat16),
            "dp",
            split_axis=1,
            concat_axis=0,
            tiled=True,
        ).astype(jnp.float32),
        lax.all_to_all(
            mixer_totals[2].T[None].astype(jnp.bfloat16),
            "dp",
            split_axis=1,
            concat_axis=0,
            tiled=True,
        ).astype(jnp.float32),
        lax.all_to_all(
            mixer_totals[3].T[None].astype(jnp.bfloat16),
            "dp",
            split_axis=1,
            concat_axis=0,
            tiled=True,
        ).astype(jnp.float32),
        lax.all_to_all(
            mixer_totals[4][None].astype(jnp.bfloat16),
            "dp",
            split_axis=1,
            concat_axis=0,
            tiled=True,
        ).astype(jnp.float32),
        lax.all_to_all(
            mlp_totals[0][None].astype(jnp.bfloat16), "dp", split_axis=1, concat_axis=0, tiled=True
        ).astype(jnp.float32),
        lax.all_to_all(
            mlp_totals[1][None].astype(jnp.bfloat16), "dp", split_axis=1, concat_axis=0, tiled=True
        ).astype(jnp.float32),
        lax.all_to_all(
            mlp_totals[2].T[None].astype(jnp.bfloat16),
            "dp",
            split_axis=1,
            concat_axis=0,
            tiled=True,
        ).astype(jnp.float32),
    )
    summed = add_terms(all_parts, (False, False, True, True, False, False, False, True))
    return (
        layer_out,
        input_grad,
        summed[0][None],
        summed[1][None],
        summed[2][None],
        summed[3][None],
        summed[4][None],
        summed[5][None],
        summed[6][None],
        summed[7][None],
    )


class Place:
    def __init__(self):
        self.core = lax.axis_index("section")
        self.index = lax.axis_index("dp")
        self.z = self.index // 4
        self.y = self.index // 2 % 2
        self.x = self.index % 2
        self.layer = 1 - (self.z + 1) // 2 % 2
        self.partner_z = self.z + 1 - 2 * (self.z % 2)

    def chip(self, z=None, y=None, x=None):
        z, y, x = (a if a is not None else b for a, b in ((z, self.z), (y, self.y), (x, self.x)))
        return z * 4 + y * 2 + x

    def x_side(self):
        return (self.core, self.chip(x=1 - self.x))

    def y_side(self):
        return (self.core, self.chip(y=1 - self.y))

    def sibling(self):
        return (1 - self.core, self.index)

    def greet(self):
        barrier = pltpu.get_barrier_semaphore()
        others = [self.x_side(), self.y_side(), self.sibling()]
        for step in (1, 2, 3):
            chip = self.chip(z=(self.z + step) % 4)
            others += [(0, chip), (1, chip)]
        for other in others:
            pl.semaphore_signal(barrier, inc=1, device_id=other, device_id_type=MESH)
        pl.semaphore_wait(barrier, len(others))


def planes_of(layer):
    return (1 - layer, 2 + layer)


def remote(source, target, send, receive, device):
    return pltpu.make_async_remote_copy(
        src_ref=source,
        dst_ref=target,
        send_sem=send,
        recv_sem=receive,
        device_id=device,
        device_id_type=MESH,
    )


def chunks_of(pieces):
    table = []
    for array, parts in pieces:
        start = 0
        for width in parts:
            table.append((array, start, width))
            start += width
    return table


def gather_kernel(table, halves, *refs):
    count = len(halves)
    shards, (hidden, out_grad, live), rest = refs[:count], refs[count : count + 3], refs[count + 3 :]
    gathered, (feed, feed_live), rest = rest[:count], rest[count : count + 2], rest[count + 2 :]
    z_send, z_recv, one_send, one_recv, two_send, two_recv, side_send, side_recv, feed_sems = rest
    here = Place()
    here.greet()
    last = len(table)

    def columns(chunk, half):
        array, start, width = table[chunk]
        return pl.ds(pl.multiple_of(half * halves[array] + start, 128), width)

    def block(chunk, z, y, x):
        return gathered[table[chunk][0]].at[z, y, x, :, columns(chunk, here.core)]

    def z_copy(chunk, plane, half, number):
        array = table[chunk][0]
        cut = columns(chunk, half)
        source = shards[array].at[:, cut]
        target = gathered[array].at[here.z, here.y, here.x, :, cut]
        away = remote(
            source,
            target,
            z_send.at[chunk, number, half],
            z_recv.at[chunk, here.z],
            (half, here.chip(z=plane)),
        )
        near = pltpu.make_async_copy(source, target, z_recv.at[chunk, here.z])
        return away, near

    def z_all(chunk, act):
        for number, plane in enumerate(planes_of(here.core)):
            for half in (0, 1):
                away, near = z_copy(chunk, plane, half, number)
                own = (plane == here.z) & (here.core == half)
                act(own, away, near)

    def z_start(chunk):
        def act(own, away, near):
            pl.when(own)(near.start)
            pl.when(jnp.logical_not(own))(away.start)

        z_all(chunk, act)

    def z_sent(chunk):
        z_all(chunk, lambda own, away, near: pl.when(jnp.logical_not(own))(away.wait_send))

    def arrived(target, receive):
        pltpu.make_async_copy(target, target, receive).wait()

    def first(chunk, z):
        own = block(chunk, z, here.y, here.x)
        side = here.x_side() if z < 2 else here.y_side()
        return remote(own, own, one_send.at[chunk, z], one_recv.at[chunk, z], side)

    def second(chunk, z):
        array = table[chunk][0]
        cut = columns(chunk, here.core)
        if z < 2:
            pair = gathered[array].at[z, here.y, :, :, cut]
            side = here.y_side()
        else:
            pair = gathered[array].at[z, :, here.x, :, cut]
            side = here.x_side()
        return remote(pair, pair, two_send.at[chunk, z], two_recv.at[chunk, z], side)

    def across(chunk):
        whole = gathered[table[chunk][0]].at[:, :, :, :, columns(chunk, here.core)]
        return remote(whole, whole, side_send.at[chunk], side_recv.at[chunk], here.sibling())

    own_feed = here.core == here.layer
    partner = (here.core, here.chip(z=here.partner_z))

    def feed_copies(mine, other):
        keep = pltpu.make_async_copy(mine, feed, feed_sems.at[0])
        give = remote(other, feed, feed_sems.at[1], feed_sems.at[0], partner)
        give_live = remote(live, feed_live, feed_sems.at[3], feed_sems.at[2], partner)
        return keep, give, give_live

    keep_live = pltpu.make_async_copy(live, feed_live, feed_sems.at[2])
    for layer, mine, other in ((0, hidden, out_grad), (1, out_grad, hidden)):

        @pl.when(own_feed & (here.layer == layer))
        def _():
            keep, give, give_live = feed_copies(mine, other)
            keep.start()
            keep_live.start()
            give.start()
            give_live.start()

    window = 2
    for chunk in range(min(window, last)):
        z_start(chunk)
    for step in range(last + 2):
        if step < last:
            for z in range(4):
                arrived(block(step, z, here.y, here.x), z_recv.at[step, z])
                first(step, z).start()
            if step + window < last:
                z_start(step + window)
        if 1 <= step <= last:
            for z in range(4):
                first(step - 1, z).wait_recv()
                second(step - 1, z).start()
        if 2 <= step:
            for z in range(4):
                second(step - 2, z).wait_recv()
            across(step - 2).start()
    arrived(feed, feed_sems.at[0])
    arrived(feed_live, feed_sems.at[2])

    @pl.when(own_feed)
    def _():
        keep, give, give_live = feed_copies(hidden, out_grad)
        give.wait_send()
        give_live.wait_send()

    for chunk in range(last):
        z_sent(chunk)
        for z in range(4):
            first(chunk, z).wait_send()
            second(chunk, z).wait_send()
        across(chunk).wait()


def gather(shards, hidden, out_grad, live, pieces):
    table = chunks_of(pieces)
    halves = [shard.shape[1] // 2 for shard in shards]
    kinds = [jax.ShapeDtypeStruct((4, 2, 2) + shard.shape, shard.dtype) for shard in shards]
    kinds += [jax.ShapeDtypeStruct(hidden.shape, hidden.dtype), jax.ShapeDtypeStruct(live.shape, live.dtype)]
    anywhere = pl.BlockSpec(memory_space=pl.ANY)
    dma, last = pltpu.SemaphoreType.DMA, len(table)
    results = pl.pallas_call(
        functools.partial(gather_kernel, table, halves),
        out_shape=kinds,
        in_specs=[anywhere] * (len(shards) + 3),
        out_specs=[anywhere] * len(kinds),
        scratch_shapes=[
            dma((last, 2, 2)),
            dma((last, 4)),
            dma((last, 4)),
            dma((last, 4)),
            dma((last, 4)),
            dma((last, 4)),
            dma((last,)),
            dma((last,)),
            dma((4,)),
        ],
        compiler_params=pltpu.CompilerParams(collective_id=0, has_side_effects=True),
    )(*shards, hidden, out_grad, live)
    whole = [result.reshape(-1, result.shape[-1]) for result in results[: len(shards)]]
    return whole, results[-2], results[-1]


def left_dot(left_side, right_side):
    return lax.dot_general(
        left_side, right_side, (((1,), (0,)), ((), ())), preferred_element_type=jnp.float32
    )


def halves_of(table):
    high = table.astype(jnp.bfloat16)
    rest = (table - high.astype(jnp.float32)).astype(jnp.bfloat16)
    return jnp.concatenate([high, rest, high], axis=1)


def parts(signal):
    high = signal.astype(jnp.bfloat16)
    rest = (signal - high.astype(jnp.float32)).astype(jnp.bfloat16)
    return jnp.concatenate([high, high, rest], axis=0)


def packed_tables(length):
    period = 2 * length
    freq = lax.broadcasted_iota(jnp.int32, (length, length), 0)
    time = lax.broadcasted_iota(jnp.int32, (length, length), 1)
    angles = (freq * time % period).astype(jnp.float32) * (2.0 * math.pi / period)
    edge = (1 - 2 * (time % 2)).astype(jnp.float32)
    cosines = jnp.cos(angles)
    sines = jnp.where(freq == 0, edge, -jnp.sin(angles))
    table = jnp.concatenate([cosines, sines], axis=0)
    row = lax.broadcasted_iota(jnp.int32, (period, 1), 0) % length
    weight = jnp.where(row == 0, 1.0, 2.0) / period
    return halves_of(table), halves_of((table * weight).T)


def work_kernel(table, widths, *refs):
    refs = list(refs)

    def take(number):
        taken = refs[:number]
        del refs[:number]
        return taken

    stored = take(5)
    fed, live, dft, idft = take(4)
    sums = take(5)
    kept_out, kept_grad = take(2)
    weight = take(5)
    (feed, arrive, x_in, e_in, out_low, grad_low) = take(6)
    (filt, rows8, norm_one, norm_two, scale_one, scale_two) = take(6)
    (left, queries, keys, values, convolved, value_spec, kernel_spec) = take(7)
    (total, after, expanded, active, projected, after_low, small_terms) = take(7)
    lefts = take(4)
    other_small, other_projected, other_after, other_expanded, other_active = take(5)
    last = len(table)
    mine = take(last)
    final_in = take(last)
    one_small, two_small = take(2)
    (load, swap_sems, send, recv, one_send, one_recv, two_send, two_recv, z_send, z_recv, ready) = take(11)

    here = Place()
    here.greet()
    tokens, features = x_in.shape
    slots = filt.shape[0]
    micro = tokens // slots
    hidden = active.shape[1]
    f32, low = jnp.float32, jnp.bfloat16

    loads = [pltpu.make_async_copy(fed, feed, load.at[5])]
    loads += [pltpu.make_async_copy(stored[k], weight[k], load.at[k]) for k in range(5)]
    for one in loads:
        one.start()

    def matrix(number, start, width):
        ref = weight[number]
        return ref[:, :, pl.ds(start, width)].reshape(ref.shape[0] * ref.shape[1], width)

    def in_rows(block, body):
        lax.fori_loop(0, tokens // block, lambda i, c: (body(pl.ds(pl.multiple_of(i * block, block), block)), c)[1], 0)

    def normed(rows, rows_in, normal, scale, gain):
        centered = rows_in - jnp.mean(rows_in, axis=1, keepdims=True)
        inv = lax.rsqrt(jnp.mean(centered * centered, axis=1, keepdims=True) + epsilon)
        n = centered * inv
        normal[rows] = n
        scale[rows] = jnp.broadcast_to(inv, (n.shape[0], 128))
        left[rows] = (n * gain).astype(low)

    row_at = lax.broadcasted_iota(jnp.int32, (slots, 256), 0)
    first_row = row_at == 0

    def later(rows, places):
        return jnp.where(row_at >= places, pltpu.roll(rows, places, 0), 0.0)

    def sooner(rows, places):
        return jnp.where(row_at < slots - places, pltpu.roll(rows, slots - places, 0), 0.0)

    def mixer_blocks(body):
        cuts = features // 256

        def step(i, carry):
            m, cut = i // cuts, i % cuts
            rows = pl.ds(pl.multiple_of(m * slots, slots), slots)
            columns = pl.ds(pl.multiple_of(cut * 256, 256), 256)
            live_rows = (row_at.astype(f32) < live[m, 0:1, columns]).astype(f32)
            body(m, rows, columns, live_rows, cut)
            return carry

        lax.fori_loop(0, micro * cuts, step, 0)

    def other_half(number):
        return pl.ds(pl.multiple_of((1 - here.core) * (widths[number] // 2), 128), widths[number] // 2)

    def to_sibling(number, source, target):
        return remote(source, target, send.at[number], recv.at[number], here.sibling())

    def left_copy(k):
        return to_sibling(k, lefts[k].at[0], lefts[k].at[1])

    def right_copy(k):
        source, target = (
            (projected, other_projected),
            (after_low, other_after),
            (expanded, other_expanded),
            (active, other_active),
        )[k]
        return to_sibling(4 + k, source.at[:, other_half(1 + k)], target)

    def small_copy():
        return to_sibling(8, small_terms.at[1 - here.core], other_small)

    partner = (here.core, here.chip(z=here.partner_z))
    give_out = remote(out_low, arrive, swap_sems.at[0], swap_sems.at[1], partner)
    give_grad = remote(grad_low, arrive, swap_sems.at[0], swap_sems.at[1], partner)

    loads[1].wait()
    filt[...] = matrix(0, 0, 128).astype(f32).T
    rows8[...] = matrix(0, 128, 128).astype(f32).T[:8]
    loads[0].wait()

    @pl.when(here.layer == 0)
    def _():
        x_in[...] = feed[...]

    @pl.when(here.layer == 1)
    def _():
        give_out.wait_recv()
        x_in[...] = arrive[...]
        e_in[...] = feed[...]

    in_rows(64, lambda rows: normed(rows, x_in[rows].astype(f32), norm_one, scale_one, rows8[3:4]))
    lefts[0][0] = left[...].T
    left_copy(0).start()
    loads[2].wait()
    for k, target in enumerate((queries, keys, values)):
        target[...] = left_dot(left[...], matrix(1, k * features, features))

    def mix(m, rows, columns, live_rows, cut):
        taps = [rows8[j : j + 1, columns] for j in range(3)]
        k = keys[rows, columns] * live_rows
        keys[rows, columns] = k
        v = values[rows, columns] * live_rows
        kernel = filt[:, columns] + taps[0] * k + taps[1] * later(k, 1) + taps[2] * later(k, 2)
        spec = left_dot(dft[...], parts(jnp.concatenate([v, kernel], axis=1)))
        value_spec[m, :, columns] = spec[:, :256]
        kernel_spec[m, :, columns] = spec[:, 256:]
        v_re, v_im = spec[:slots, :256], spec[slots:, :256]
        k_re, k_im = spec[:slots, 256:], spec[slots:, 256:]
        both = k_im * v_im
        re = k_re * v_re - jnp.where(first_row, 0.0, both)
        im = jnp.where(first_row, both, k_re * v_im + k_im * v_re)
        out = left_dot(idft[...], parts(jnp.concatenate([re, im], axis=0)))
        convolved[rows, columns] = out
        left[rows, columns] = (queries[rows, columns] * out).astype(low)

    mixer_blocks(mix)
    lefts[1][0] = left[...].T
    left_copy(1).start()
    loads[3].wait()
    total[...] = x_in[...].astype(f32) + left_dot(left[...], matrix(2, 0, features))
    in_rows(64, lambda rows: normed(rows, total[rows], norm_two, scale_two, rows8[4:5]))
    lefts[2][0] = left[...].T
    left_copy(2).start()
    loads[4].wait()
    loads[5].wait()
    tile = 512

    def tiles(body):
        lax.fori_loop(0, hidden // tile, lambda i, c: (body(pl.multiple_of(i * tile, tile)), c)[1], 0)

    def feed_forward(start):
        gate = left_dot(left[...], matrix(3, start, tile))
        up = left_dot(left[...], matrix(3, hidden + start, tile))
        act = (gate * jax.nn.sigmoid(gate) * up).astype(low)
        expanded[:, pl.ds(start, tile)] = gate.astype(low)
        expanded[:, pl.ds(hidden + start, tile)] = up.astype(low)
        active[:, pl.ds(start, tile)] = act
        total[...] += dot_back(act, matrix(4, start, tile))

    tiles(feed_forward)
    right_copy(3).start()
    out_low[...] = total[...].astype(low)

    @pl.when(here.layer == 0)
    def _():
        give_out.start()
        give_grad.wait_recv()
        e_in[...] = arrive[...]

    lefts[3][0] = e_in[...].T
    left_copy(3).start()
    total[...] = jnp.zeros_like(total)

    def feed_forward_back(start):
        grad_act = left_dot(e_in[...], matrix(4, start, tile))
        gate = expanded[:, pl.ds(start, tile)].astype(f32)
        up = expanded[:, pl.ds(hidden + start, tile)].astype(f32)
        sig = jax.nn.sigmoid(gate)
        grad_gate = (grad_act * up * (sig * (1.0 + gate * (1.0 - sig)))).astype(low)
        grad_up = (grad_act * (gate * sig)).astype(low)
        expanded[:, pl.ds(start, tile)] = grad_gate
        expanded[:, pl.ds(hidden + start, tile)] = grad_up
        total[...] += dot_back(grad_gate, matrix(3, start, tile)) + dot_back(grad_up, matrix(3, hidden + start, tile))

    tiles(feed_forward_back)
    right_copy(2).start()
    for side in (here.x_side(), here.y_side()):
        pl.semaphore_signal(ready, inc=1, device_id=side, device_id_type=MESH)

    offsets, place = [], 0
    for array, _, width in table:
        offsets.append(place)
        place += width if array else 0

    def one_in(chunk, z):
        width = table[chunk][2]
        if table[chunk][0] == 0:
            return one_small.at[z]
        return weight[3].at[pl.ds(2 * z, 2), :, pl.ds(offsets[chunk], width)]

    def two_in(chunk, z):
        width = table[chunk][2]
        if table[chunk][0] == 0:
            return two_small.at[z]
        return weight[3].at[8 + z, :, pl.ds(offsets[chunk], width)]

    def first(chunk, z):
        if z < 2:
            source, side = mine[chunk].at[z, 1 - here.y], here.y_side()
        else:
            source, side = mine[chunk].at[z, :, 1 - here.x], here.x_side()
        return remote(source, one_in(chunk, z), one_send.at[chunk, z], one_recv.at[chunk, z], side)

    def second(chunk, z):
        if z < 2:
            source, side = mine[chunk].at[z, here.y, 1 - here.x], here.x_side()
        else:
            source, side = mine[chunk].at[z, 1 - here.y, here.x], here.y_side()
        return remote(source, two_in(chunk, z), two_send.at[chunk, z], two_recv.at[chunk, z], side)

    def third(chunk, z):
        source = mine[chunk].at[z, here.y, here.x]
        slot = here.z // 2
        target = final_in[chunk].at[slot, here.core]
        receive = z_recv.at[chunk, slot, here.core]
        own = (here.z == z) & (here.core == here.layer)

        def away():
            return remote(source, target, z_send.at[chunk, z], receive, (here.layer, here.chip(z=z)))

        def near():
            return pltpu.make_async_copy(source, target, receive)

        return own, away, near

    def add(target, other):
        target[...] = (target[...].astype(f32) + other[...].astype(f32)).astype(target.dtype)

    def place_block(chunk, block):
        rows = block.shape[0] // 16
        for z in range(4):
            for k in range(4):
                at = (z * 4 + k) * rows
                mine[chunk][z, k // 2, k % 2] = block[at : at + rows]

    def terms(chunk):
        array, start, width = table[chunk]
        if array == 0:
            block = (small_terms[here.core] + other_small[...]).T
        else:
            source, other = (
                (projected, other_projected),
                (after_low, other_after),
                (expanded, other_expanded),
                (active, other_active),
            )[array - 1]
            own_at = pl.multiple_of(here.core * (widths[array] // 2) + start, 128)
            block = left_dot(lefts[array - 1][0], source[:, pl.ds(own_at, width)])
            block += left_dot(lefts[array - 1][1], other[:, pl.ds(start, width)])
        place_block(chunk, block.astype(low))
        for z in range(4):
            first(chunk, z).start()

    def feed_forward_terms():
        pl.semaphore_wait(ready, 2)
        left_copy(3).wait_recv()
        right_copy(3).wait_recv()
        for chunk in range(last):
            if table[chunk][0] == 4:
                terms(chunk)
        left_copy(2).wait_recv()
        right_copy(2).wait_recv()
        for chunk in range(last):
            if table[chunk][0] == 3:
                terms(chunk)

    pl.when(here.layer == 0)(feed_forward_terms)

    def norm_grad(rows, grad, normal, scale, gain, at):
        n = normal[rows]
        small_terms[1, at : at + 1] += jnp.sum(grad * n, axis=0, keepdims=True)
        q = grad * gain
        back = q - jnp.mean(q, axis=1, keepdims=True) - n * jnp.mean(q * n, axis=1, keepdims=True)
        return scale[rows][:, :1] * back

    small_terms[...] = jnp.zeros_like(small_terms)

    def after_back(rows):
        grad = e_in[rows].astype(f32) + norm_grad(rows, total[rows], norm_two, scale_two, rows8[4:5], 4)
        after[rows] = grad
        after_low[rows] = grad.astype(low)

    in_rows(64, after_back)
    right_copy(1).start()
    total[...] = dot_back(after_low[...], matrix(2, 0, features))

    def mix_back(m, rows, columns, live_rows, cut):
        taps = [rows8[j : j + 1, columns] for j in range(3)]
        grad = total[rows, columns]
        projected[rows, columns] = (grad * convolved[rows, columns]).astype(low)
        spec = left_dot(dft[...], parts(grad * queries[rows, columns]))
        g_re, g_im = spec[:slots], spec[slots:]
        pairs = []
        for other in (kernel_spec, value_spec):
            o_re, o_im = other[m, :slots, columns], other[m, slots:, columns]
            both = o_im * g_im
            re = o_re * g_re + jnp.where(first_row, 0.0, both)
            im = jnp.where(first_row, both, o_re * g_im - o_im * g_re)
            pairs.append(jnp.concatenate([re, im], axis=0))
        paired = left_dot(idft[...], parts(jnp.concatenate(pairs, axis=1)))
        projected[rows, pl.ds(pl.multiple_of(2 * features + cut * 256, 256), 256)] = (
            paired[:, :256] * live_rows
        ).astype(low)
        grad_kernel = paired[:, 256:]
        small_terms[0, :, columns] += grad_kernel
        k = keys[rows, columns]
        for j in range(3):
            moved = later(k, j) if j else k
            small_terms[1, j : j + 1, columns] += jnp.sum(grad_kernel * moved, axis=0, keepdims=True)
        grad_keys = taps[0] * grad_kernel + taps[1] * sooner(grad_kernel, 1) + taps[2] * sooner(grad_kernel, 2)
        projected[rows, pl.ds(pl.multiple_of(features + cut * 256, 256), 256)] = (grad_keys * live_rows).astype(low)

    mixer_blocks(mix_back)
    right_copy(0).start()
    total[...] = dot_back(projected[...], matrix(1, 0, 3 * features))

    def input_back(rows):
        grad = after[rows] + norm_grad(rows, total[rows], norm_one, scale_one, rows8[3:4], 3)
        grad_low[rows] = grad.astype(low)

    in_rows(64, input_back)
    small_copy().start()

    @pl.when(here.layer == 1)
    def _():
        give_grad.start()
        feed_forward_terms()

    left_copy(1).wait_recv()
    right_copy(1).wait_recv()
    for chunk in range(last):
        if table[chunk][0] == 2:
            terms(chunk)
    left_copy(0).wait_recv()
    right_copy(0).wait_recv()
    for chunk in range(last):
        if table[chunk][0] == 1:
            terms(chunk)
    small_copy().wait_recv()
    for chunk in range(last):
        if table[chunk][0] == 0:
            terms(chunk)

    apart = here.core != here.layer
    across = (1 - here.core, here.chip(z=here.partner_z))
    swaps = [
        remote(out_low, kept_out, swap_sems.at[2], swap_sems.at[3], across),
        remote(grad_low, kept_grad, swap_sems.at[4], swap_sems.at[5], across),
    ]
    stays = [
        pltpu.make_async_copy(out_low, kept_out, swap_sems.at[3]),
        pltpu.make_async_copy(grad_low, kept_grad, swap_sems.at[5]),
    ]
    for swap, stay in zip(swaps, stays):
        pl.when(apart)(swap.start)
        pl.when(jnp.logical_not(apart))(stay.start)

    for step in range(last + 1):
        if step < last:
            for z in range(4):
                first(step, z).wait_recv()
                for k in range(2):
                    if z < 2:
                        add(mine[step].at[z, here.y, k], one_in(step, z).at[k])
                    else:
                        add(mine[step].at[z, k, here.x], one_in(step, z).at[k])
                second(step, z).start()
        if 1 <= step:
            chunk = step - 1
            for z in range(4):
                second(chunk, z).wait_recv()
                add(mine[chunk].at[z, here.y, here.x], two_in(chunk, z))
                own, away, near = third(chunk, z)
                pl.when(own)(lambda: near().start())
                pl.when(jnp.logical_not(own))(lambda: away().start())
    for chunk in range(last):
        array, start, width = table[chunk]
        for half in (0, 1):
            for slot in (0, 1):
                target = final_in[chunk].at[slot, half]
                pltpu.make_async_copy(target, target, z_recv.at[chunk, slot, half]).wait()
            cut = pl.ds(half * (widths[array] // 2) + start, width)
            sums[array][:, cut] = final_in[chunk][0, half].astype(f32) + final_in[chunk][1, half].astype(f32)

    for k in range(4):
        left_copy(k).wait_send()
        right_copy(k).wait_send()
    small_copy().wait_send()
    give_out.wait_send()
    for swap, stay in zip(swaps, stays):
        pl.when(apart)(swap.wait)
        pl.when(jnp.logical_not(apart))(stay.wait)
    for chunk in range(last):
        for z in range(4):
            first(chunk, z).wait_send()
            second(chunk, z).wait_send()
            own, away, near = third(chunk, z)
            pl.when(jnp.logical_not(own))(lambda: away().wait_send())


def work(whole, feed, live, pieces):
    table = chunks_of(pieces)
    widths = [array.shape[1] for array in whole]
    features = whole[0].shape[0]
    rows = features // 16
    micro, slots, _ = feed.shape
    tokens, hidden = micro * slots, widths[4]
    stored = [array.reshape(16, rows, array.shape[1]) for array in whole]
    dft, idft = packed_tables(slots)
    live = jnp.tile(live, (1, 1, features // live.shape[-1]))
    low, f32 = jnp.bfloat16, jnp.float32
    kinds = [jax.ShapeDtypeStruct((rows, width), f32) for width in widths]
    kinds += [jax.ShapeDtypeStruct((tokens, features), low)] * 2
    anywhere = pl.BlockSpec(memory_space=pl.ANY)
    inside = pl.BlockSpec(memory_space=pltpu.VMEM)
    dma, last, vmem = pltpu.SemaphoreType.DMA, len(table), pltpu.VMEM
    act, act_low = (tokens, features), vmem((tokens, features), low)
    room = [vmem(array.shape, low) for array in stored]
    room += [act_low] * 6
    room += [vmem((slots, features), f32), vmem((8, features), f32), vmem(act, f32), vmem(act, f32)]
    room += [vmem((tokens, 128), f32)] * 2
    room += [act_low] + [vmem(act, f32)] * 4 + [vmem((micro, 2 * slots, features), f32)] * 2
    room += [vmem(act, f32)] * 2 + [vmem((tokens, 2 * hidden), low), vmem((tokens, hidden), low)]
    room += [vmem((tokens, 3 * features), low), act_low, vmem((2, slots, features), f32)]
    room += [vmem((2, features, tokens), low)] * 4
    room += [vmem((slots, features), f32)] + [vmem((tokens, width // 2), low) for width in widths[1:]]
    for lead in ((4, 2, 2), (2, 2)):
        room += [vmem(lead + (rows, width), low) for _, _, width in table]
    room += [vmem((4, 2, rows, 128), low), vmem((4, rows, 128), low)]
    room += [dma((6,)), dma((6,)), dma((9,)), dma((9,))]
    room += [dma((last, 4))] * 5 + [dma((last, 2, 2)), pltpu.SemaphoreType.REGULAR]
    results = pl.pallas_call(
        functools.partial(work_kernel, table, widths),
        out_shape=kinds,
        in_specs=[anywhere] * 6 + [inside] * 3,
        out_specs=[inside] * 5 + [anywhere] * 2,
        scratch_shapes=room,
        compiler_params=pltpu.CompilerParams(
            collective_id=1, has_side_effects=True, vmem_limit_bytes=62 * 1024 * 1024
        ),
    )(*stored, feed.reshape(tokens, features), live, dft, idft)
    return results[:5], results[5].reshape(feed.shape), results[6].reshape(feed.shape)

def fast_device(
    hidden_in, out_grad, lengths, gain_mixer, w_input, w_taps, filters, w_output, gain_mlp, w_gate_up, w_down
):
    micro = hidden_in.shape[0]
    small = jnp.concatenate(
        [filters[0].T, w_taps[0].T, gain_mixer[0][:, None], gain_mlp[0][:, None]], axis=1
    )
    small = jnp.pad(small, ((0, 0), (0, 256 - small.shape[1])))
    shards = (small, w_input[0], w_output[0], w_gate_up[0], w_down[0].T)
    live = jnp.broadcast_to(lengths.astype(jnp.float32).reshape(micro, 1, 1), (micro, 8, 128))
    whole, feed, feed_live = gather(shards, hidden_in[:, 0], out_grad[:, 0], live, PIECES)
    (s_small, s_in, s_out, s_gu, s_dt), layer_out, input_grad = work(whole, feed, feed_live, TERM_PIECES)
    return (
        layer_out[None, :, None],
        input_grad[None, :, None],
        s_small[None, :, 131],
        s_in[None],
        s_small[:, 128:131].T[None],
        s_small[:, :128].T[None],
        s_out[None],
        s_small[None, :, 132],
        s_gu[None],
        s_dt.T[None],
    )


def solution(mesh):
    placed = (
        P(None, "dp", None, None),
        P(None, "dp", None, None),
        P(None, "dp"),
        P("section", "dp"),
        P("section", "dp", None),
        P("section", None, "dp"),
        P("section", None, "dp"),
        P("section", "dp", None),
        P("section", "dp"),
        P("section", "dp", None),
        P("section", None, "dp"),
    )
    return jax.shard_map(
        fast_device if mesh.shape["dp"] == 16 and mesh.shape["section"] == 2 else on_device,
        mesh=mesh,
        in_specs=placed,
        out_specs=(
            P("section", None, "dp", None, None),
            P("section", None, "dp", None, None),
            P("section", "dp"),
            P("section", "dp", None),
            P("section", None, "dp"),
            P("section", None, "dp"),
            P("section", "dp", None),
            P("section", "dp"),
            P("section", "dp", None),
            P("section", None, "dp"),
        ),
        check_vma=False,
    )
```

```python
import functools
import math

import jax
import jax.numpy as jnp
import ml_dtypes
import numpy as np
from jax import lax
from jax.experimental import pallas as pl
from jax.experimental.pallas import tpu as pltpu
from jax.sharding import PartitionSpec as P

MESH = pl.DeviceIdType.MESH

epsilon = 1e-05
GET_PIECES = (
    (0, 128, False),
    (1, 384, False),
    (1, 384, False),
    (1, 384, False),
    (2, 384, False),
    (3, 1024, False),
    (3, 1024, False),
    (3, 1024, False),
    (4, 512, False),
    (4, 512, False),
    (4, 512, False),
)
PUT_PIECES = (
    (4, 768, False),
    (4, 768, False),
    (3, 1024, False),
    (3, 1024, False),
    (3, 1024, False),
    (2, 384, False),
    (1, 384, False),
    (1, 384, False),
    (1, 384, False),
    (0, 128, False),
)


def passed_along(value, axis, steps):
    count = lax.axis_size(axis)
    first, last = (max(0, -steps), min(count, count - steps))
    return lax.ppermute(value, axis, [(source, source + steps) for source in range(first, last)])


def split_dot(left_side, right_side):
    return jnp.dot(
        left_side, right_side, precision=lax.Precision.HIGH, preferred_element_type=jnp.float32
    )


def split_rows(left_side, right_side):
    return lax.dot_general(
        left_side,
        right_side,
        (((0,), (0,)), ((), ())),
        precision=lax.Precision.HIGH,
        preferred_element_type=jnp.float32,
    )


def dot_rows(left_side, right_side):
    return lax.dot_general(
        left_side, right_side, (((0,), (0,)), ((), ())), preferred_element_type=jnp.float32
    )


def dot_back(left_side, right_side):
    return lax.dot_general(
        left_side, right_side, (((1,), (1,)), ((), ())), preferred_element_type=jnp.float32
    )


def tables(length):
    period = 2 * length
    freq_index = lax.broadcasted_iota(jnp.int32, (length + 1, length), 0)
    time_index = lax.broadcasted_iota(jnp.int32, (length + 1, length), 1)
    angles = (freq_index * time_index % period).astype(jnp.float32) * (2.0 * math.pi / period)
    edge_rows = (freq_index[:, :1] == 0) | (freq_index[:, :1] == length)
    inverse_weight = jnp.where(edge_rows, 1.0, 2.0) / period
    dft_stack = jnp.concatenate([jnp.cos(angles), -jnp.sin(angles)], axis=0)
    return (dft_stack, inverse_weight)


def spectrum(dft_tables, signal):
    dft_stack, inverse_weight = dft_tables
    stacked_out = split_dot(dft_stack, signal)
    middle_row = stacked_out.shape[0] // 2
    return (stacked_out[:middle_row], stacked_out[middle_row:])


def inverse(dft_tables, real_part, imag_part):
    dft_stack, inverse_weight = dft_tables
    return split_rows(
        dft_stack, jnp.concatenate([inverse_weight * real_part, inverse_weight * imag_part], axis=0)
    )


def normalize(input_rows):
    centered = input_rows - jnp.mean(input_rows, axis=1, keepdims=True)
    inv_scale = lax.rsqrt(jnp.mean(centered * centered, axis=1, keepdims=True) + epsilon)
    return (centered * inv_scale, inv_scale)


def norm_back(grad_normed, normed, inv_scale):
    return inv_scale * (
        grad_normed
        - jnp.mean(grad_normed, axis=1, keepdims=True)
        - normed * jnp.mean(grad_normed * normed, axis=1, keepdims=True)
    )


def delayed(input_rows, places):
    return jnp.pad(input_rows, ((places, 0), (0, 0)))[: input_rows.shape[0]]


def advanced(input_rows, places):
    return jnp.pad(input_rows, ((0, places), (0, 0)))[places:]


def layer_forward(input_rows, active_rows, weights, dft_tables):
    gain_one, w_inner, w_tap_rows, filt_static, w_outer, gain_two, w_expand, w_reduce = weights
    hidden_size_model = w_outer.shape[0]
    hidden_width = w_reduce.shape[0]
    tap_weights = w_tap_rows.astype(jnp.float32)
    normed_one, scale_one = normalize(input_rows)
    entered = (normed_one * gain_one.astype(jnp.float32)).astype(jnp.bfloat16)
    projected = jnp.dot(entered, w_inner, preferred_element_type=jnp.float32)
    queries = projected[:, :hidden_size_model]
    keys_part = projected[:, hidden_size_model : 2 * hidden_size_model] * active_rows
    values_part = projected[:, 2 * hidden_size_model :] * active_rows
    dynamic = (
        tap_weights[0] * keys_part
        + tap_weights[1] * delayed(keys_part, 1)
        + tap_weights[2] * delayed(keys_part, 2)
    )
    kernel = filt_static.astype(jnp.float32) + dynamic
    joint_re, joint_im = spectrum(dft_tables, jnp.concatenate([values_part, kernel], axis=1))
    value_re = joint_re[:, :hidden_size_model]
    kernel_re = joint_re[:, hidden_size_model:]
    value_im = joint_im[:, :hidden_size_model]
    kernel_im = joint_im[:, hidden_size_model:]
    convolved = inverse(
        dft_tables,
        kernel_re * value_re - kernel_im * value_im,
        kernel_re * value_im + kernel_im * value_re,
    )
    gated_rows = (queries * convolved).astype(jnp.bfloat16)
    after_mixer = input_rows + jnp.dot(gated_rows, w_outer, preferred_element_type=jnp.float32)
    normed_two, scale_two = normalize(after_mixer)
    entered_two = (normed_two * gain_two.astype(jnp.float32)).astype(jnp.bfloat16)
    expanded = jnp.dot(entered_two, w_expand, preferred_element_type=jnp.float32)
    gate_part = expanded[:, :hidden_width]
    up_part = expanded[:, hidden_width:]
    activated = (jax.nn.silu(gate_part) * up_part).astype(jnp.bfloat16)
    result = after_mixer + jnp.dot(activated, w_reduce, preferred_element_type=jnp.float32)
    stash = (
        normed_one,
        scale_one,
        entered,
        queries,
        keys_part,
        (value_re, value_im, kernel_re, kernel_im),
        convolved,
        gated_rows,
        normed_two,
        scale_two,
        entered_two,
        gate_part,
        up_part,
        activated,
    )
    return (result, stash)


def mlp_backward(received_gradient, weights, stash):
    gain_one, w_inner, w_tap_rows, filt_static, w_outer, gain_two, w_expand, w_reduce = weights
    (
        normed_one,
        scale_one,
        entered,
        queries,
        keys_part,
        spectra,
        convolved,
        gated_rows,
        normed_two,
        scale_two,
        entered_two,
        gate_part,
        up_part,
        activated,
    ) = stash
    grad_low = received_gradient.astype(jnp.bfloat16)
    grad_reduce_w = dot_rows(activated, grad_low)
    grad_act = dot_back(grad_low, w_reduce)
    sigmoid_gate = jax.nn.sigmoid(gate_part)
    grad_gate = grad_act * up_part * (sigmoid_gate * (1.0 + gate_part * (1.0 - sigmoid_gate)))
    grad_up = grad_act * (gate_part * sigmoid_gate)
    grad_expand = jnp.concatenate([grad_gate, grad_up], axis=1).astype(jnp.bfloat16)
    grad_expand_w = dot_rows(entered_two, grad_expand)
    grad_entered_two = dot_back(grad_expand, w_expand)
    grad_gain_two = jnp.sum(grad_entered_two * normed_two, axis=0)
    grad_after = received_gradient + norm_back(
        grad_entered_two * gain_two.astype(jnp.float32), normed_two, scale_two
    )
    return (grad_after, (grad_gain_two, grad_expand_w, grad_reduce_w))


def mixer_backward(grad_after, active_rows, weights, dft_tables, stash):
    gain_one, w_inner, w_tap_rows, filt_static, w_outer, gain_two, w_expand, w_reduce = weights
    (
        normed_one,
        scale_one,
        entered,
        queries,
        keys_part,
        spectra,
        convolved,
        gated_rows,
        normed_two,
        scale_two,
        entered_two,
        gate_part,
        up_part,
        activated,
    ) = stash
    value_re, value_im, kernel_re, kernel_im = spectra
    hidden_size_model = w_outer.shape[0]
    tap_weights = w_tap_rows.astype(jnp.float32)
    grad_mix_low = grad_after.astype(jnp.bfloat16)
    grad_outer_w = dot_rows(gated_rows, grad_mix_low)
    grad_gated = dot_back(grad_mix_low, w_outer)
    grad_queries = grad_gated * convolved
    grad_conv = grad_gated * queries
    grad_re, grad_im = spectrum(dft_tables, grad_conv)
    paired_re = jnp.concatenate(
        [kernel_re * grad_re + kernel_im * grad_im, value_re * grad_re + value_im * grad_im], axis=1
    )
    paired_im = jnp.concatenate(
        [kernel_re * grad_im - kernel_im * grad_re, value_re * grad_im - value_im * grad_re], axis=1
    )
    paired = inverse(dft_tables, paired_re, paired_im)
    grad_values = paired[:, :hidden_size_model] * active_rows
    grad_kernel = paired[:, hidden_size_model:]
    grad_taps = jnp.stack(
        [
            jnp.sum(grad_kernel * keys_part, axis=0),
            jnp.sum(grad_kernel * delayed(keys_part, 1), axis=0),
            jnp.sum(grad_kernel * delayed(keys_part, 2), axis=0),
        ]
    )
    grad_keys = (
        tap_weights[0] * grad_kernel
        + tap_weights[1] * advanced(grad_kernel, 1)
        + tap_weights[2] * advanced(grad_kernel, 2)
    ) * active_rows
    grad_projected = jnp.concatenate([grad_queries, grad_keys, grad_values], axis=1).astype(
        jnp.bfloat16
    )
    inner_weight_gradient = dot_rows(entered, grad_projected)
    grad_entered = dot_back(grad_projected, w_inner)
    grad_gain_one = jnp.sum(grad_entered * normed_one, axis=0)
    grad_inputs = grad_after + norm_back(
        grad_entered * gain_one.astype(jnp.float32), normed_one, scale_one
    )
    return (
        grad_inputs,
        (grad_gain_one, inner_weight_gradient, grad_taps, grad_kernel, grad_outer_w),
    )


def add_terms(received, flipped):
    return tuple(
        (
            jnp.sum(member, axis=0).T if flip else jnp.sum(member, axis=0)
            for member, flip in zip(received, flipped)
        )
    )


def on_device(
    hidden_in,
    out_grad,
    lengths,
    gain_mixer,
    w_input,
    w_taps,
    filters,
    w_output,
    gain_mlp,
    w_gate_up,
    w_down,
):
    first_section = lax.axis_index("section") == 0
    micro_count = hidden_in.shape[0]
    seq_slots = hidden_in.shape[2]
    hidden_size_model = hidden_in.shape[3]
    dft_tables = tables(seq_slots)
    positions = lax.broadcasted_iota(jnp.int32, (seq_slots, 1), 0)
    weights = (
        lax.all_gather(gain_mixer[0], "dp", axis=0, tiled=True),
        lax.all_gather(w_input[0], "dp", axis=0, tiled=True),
        lax.all_gather(w_taps[0], "dp", axis=1, tiled=True),
        lax.all_gather(filters[0], "dp", axis=1, tiled=True),
        lax.all_gather(w_output[0], "dp", axis=0, tiled=True),
        lax.all_gather(gain_mlp[0], "dp", axis=0, tiled=True),
        lax.all_gather(w_gate_up[0], "dp", axis=0, tiled=True),
        lax.all_gather(w_down[0], "dp", axis=1, tiled=True),
    )
    arriving = jnp.zeros((seq_slots, hidden_size_model), jnp.bfloat16)
    outgoing_list = []
    saved_activations = []
    for forward_step in range(micro_count + 1):
        own_index = min(forward_step, micro_count - 1)
        prior_index = max(forward_step - 1, 0)
        input_rows = jnp.where(first_section, hidden_in[own_index, 0], arriving).astype(jnp.float32)
        length_now = jnp.where(first_section, lengths[own_index, 0], lengths[prior_index, 0])
        active_rows = (positions < length_now).astype(jnp.float32)
        result, stash = layer_forward(input_rows, active_rows, weights, dft_tables)
        outgoing = result.astype(jnp.bfloat16)
        outgoing_list.append(outgoing)
        if forward_step < micro_count:
            arriving = passed_along(outgoing, "section", 1)
        saved_activations.append((input_rows, active_rows))
    coming = jnp.zeros((seq_slots, hidden_size_model), jnp.bfloat16)
    mlp_totals = None
    mixer_totals = None
    grads_out = []
    for backward_step in range(micro_count + 1):
        saved_slot_index = micro_count - backward_step
        last_index = max(micro_count - 1 - backward_step, 0)
        live_factor = 1.0 if backward_step < micro_count else 0.0
        received_gradient = jnp.where(
            first_section,
            coming.astype(jnp.float32),
            out_grad[last_index, 0].astype(jnp.float32) * live_factor,
        )
        input_rows, active_rows = saved_activations[saved_slot_index]
        result, stash = layer_forward(input_rows, active_rows, weights, dft_tables)
        grad_after, mlp_grads = mlp_backward(received_gradient, weights, stash)
        mlp_totals = (
            mlp_grads if mlp_totals is None else jax.tree.map(jnp.add, mlp_totals, mlp_grads)
        )
        grad_inputs, mixer_grads = mixer_backward(
            grad_after, active_rows, weights, dft_tables, stash
        )
        mixer_totals = (
            mixer_grads
            if mixer_totals is None
            else jax.tree.map(jnp.add, mixer_totals, mixer_grads)
        )
        outgoing = grad_inputs.astype(jnp.bfloat16)
        grads_out.append(outgoing)
        if backward_step < micro_count:
            coming = passed_along(outgoing, "section", -1)
    first_outputs = jnp.stack(outgoing_list[:micro_count])
    second_outputs = jnp.stack(outgoing_list[1:])
    layer_out = jnp.where(first_section, first_outputs, second_outputs)[None, :, None]
    first_grads = jnp.stack(
        [grads_out[micro_count - batch_index] for batch_index in range(micro_count)]
    )
    second_grads = jnp.stack(
        [grads_out[micro_count - 1 - batch_index] for batch_index in range(micro_count)]
    )
    input_grad = jnp.where(first_section, first_grads, second_grads)[None, :, None]
    all_parts = (
        lax.all_to_all(
            mixer_totals[0][None].astype(jnp.bfloat16),
            "dp",
            split_axis=1,
            concat_axis=0,
            tiled=True,
        ).astype(jnp.float32),
        lax.all_to_all(
            mixer_totals[1][None].astype(jnp.bfloat16),
            "dp",
            split_axis=1,
            concat_axis=0,
            tiled=True,
        ).astype(jnp.float32),
        lax.all_to_all(
            mixer_totals[2].T[None].astype(jnp.bfloat16),
            "dp",
            split_axis=1,
            concat_axis=0,
            tiled=True,
        ).astype(jnp.float32),
        lax.all_to_all(
            mixer_totals[3].T[None].astype(jnp.bfloat16),
            "dp",
            split_axis=1,
            concat_axis=0,
            tiled=True,
        ).astype(jnp.float32),
        lax.all_to_all(
            mixer_totals[4][None].astype(jnp.bfloat16),
            "dp",
            split_axis=1,
            concat_axis=0,
            tiled=True,
        ).astype(jnp.float32),
        lax.all_to_all(
            mlp_totals[0][None].astype(jnp.bfloat16), "dp", split_axis=1, concat_axis=0, tiled=True
        ).astype(jnp.float32),
        lax.all_to_all(
            mlp_totals[1][None].astype(jnp.bfloat16), "dp", split_axis=1, concat_axis=0, tiled=True
        ).astype(jnp.float32),
        lax.all_to_all(
            mlp_totals[2].T[None].astype(jnp.bfloat16),
            "dp",
            split_axis=1,
            concat_axis=0,
            tiled=True,
        ).astype(jnp.float32),
    )
    summed = add_terms(all_parts, (False, False, True, True, False, False, False, True))
    return (
        layer_out,
        input_grad,
        summed[0][None],
        summed[1][None],
        summed[2][None],
        summed[3][None],
        summed[4][None],
        summed[5][None],
        summed[6][None],
        summed[7][None],
    )


class Place:
    def __init__(self):
        self.core = lax.axis_index("section")
        self.index = lax.axis_index("dp")
        self.z = self.index // 4
        self.y = self.index // 2 % 2
        self.x = self.index % 2
        self.layer = 1 - (self.z + 1) // 2 % 2
        self.home = self.z // 2
        self.first_layer = self.layer == 0
        self.second_layer = self.layer == 1
        self.partner = self.chip(z=self.z + 1 - 2 * (self.z % 2))

    def chip(self, z=None, y=None, x=None):
        z, y, x = (a if a is not None else b for a, b in ((z, self.z), (y, self.y), (x, self.x)))
        return z * 4 + y * 2 + x

    def x_side(self):
        return (self.core, self.chip(x=1 - self.x))

    def y_side(self):
        return (self.core, self.chip(y=1 - self.y))

    def sibling(self):
        return (1 - self.core, self.index)

    def middle(self):
        return (self.core, self.chip(z=3 - self.z))

    def greet(self):
        barrier = pltpu.get_barrier_semaphore()
        others = [self.x_side(), self.y_side(), self.sibling()]
        for step in (1, 2, 3):
            chip = self.chip(z=(self.z + step) % 4)
            others += [(0, chip), (1, chip)]
        for other in others:
            pl.semaphore_signal(barrier, inc=1, device_id=other, device_id_type=MESH)
        pl.semaphore_wait(barrier, len(others))


def remote(source, target, send, receive, device):
    return pltpu.make_async_remote_copy(
        src_ref=source,
        dst_ref=target,
        send_sem=send,
        recv_sem=receive,
        device_id=device,
        device_id_type=MESH,
    )


def chunks_of(pieces):
    table, places = [], {}
    for array, width, shared in pieces:
        start = places.get(array, 0)
        table.append((array, start, width, shared))
        places[array] = start + width
    return table


def left_dot(left_side, right_side):
    return lax.dot_general(
        left_side, right_side, (((1,), (0,)), ((), ())), preferred_element_type=jnp.float32
    )


def parts(signal):
    high = signal.astype(jnp.bfloat16)
    rest = (signal - high.astype(jnp.float32)).astype(jnp.bfloat16)
    return jnp.concatenate([high, high, rest], axis=0)


def halves_of(table):
    high = table.astype(ml_dtypes.bfloat16)
    rest = (table - high.astype(np.float64)).astype(ml_dtypes.bfloat16)
    return np.concatenate([high, rest, high], axis=1)


def packed_tables(length):
    period = 2 * length
    freq, time = np.arange(length)[:, None], np.arange(length)[None, :]
    angles = (freq * time % period) * (2.0 * math.pi / period)
    sines = np.where(freq == 0, 1.0 - 2.0 * (time % 2), -np.sin(angles))
    table = np.concatenate([np.cos(angles), sines], axis=0)
    weight = np.where(np.arange(period)[:, None] % length == 0, 1.0, 2.0) / period
    return halves_of(table), halves_of((table * weight).T)


def layer_kernel(get_table, put_table, widths, *refs):
    refs = list(refs)

    def take(number):
        taken = refs[:number]
        del refs[:number]
        return taken

    filters_in, taps_in, gain_one_in, gain_two_in, lengths_in, dft, idft = take(7)
    shards, (hidden_in, grad_in) = [None] + take(4), take(2)
    landed, (kept_out, kept_grad) = take(5), take(2)
    own_small, rows_in, live_own, live = take(4)
    weight = take(5)
    feed, arrive, x_in, e_in, out_low, grad_low = take(6)
    filt, rows8, norm_one, norm_two, scale_one, scale_two = take(6)
    left, queries, keys, values, convolved, value_spec, kernel_spec = take(7)
    total, after, expanded, active, projected, after_low, small_terms = take(7)
    lefts = take(4)
    other_small, other_projected, other_after, other_expanded, other_active = take(5)
    mine = take(len(put_table))
    one_small, two_small = take(2)
    get_z_send, get_z_recv, get_one_send, get_one_recv, get_two_send, get_two_recv = take(6)
    get_mid_send, get_mid_recv, get_side_send, get_side_recv, feed_sems = take(5)
    swap_sems, send, recv = take(3)
    one_send, one_recv, two_send, two_recv, z_send, z_recv, mid_send, mid_recv, ready = take(9)

    here = Place()
    tokens, features = x_in.shape
    slots = filt.shape[0]
    micro = tokens // slots
    hidden = active.shape[1]
    f32, low = jnp.float32, jnp.bfloat16
    shards[0] = own_small

    rows_in[...] = jnp.zeros_like(rows_in)
    own = taps_in.shape[1]
    rows_in[0:3, 0:own] = taps_in[...].astype(f32)
    rows_in[3:4, 0:own] = gain_one_in[...].astype(f32)
    rows_in[4:5, 0:own] = gain_two_in[...].astype(f32)
    own_small[:, :128] = filters_in[...]
    own_small[:, 128:] = rows_in[...].T[:own].astype(low)
    for m in range(micro):
        live_own[m] = jnp.full(live_own.shape[1:], lengths_in[m, 0], jnp.int32).astype(f32)
    here.greet()

    own_feed = here.core == here.layer
    partner = (here.core, here.partner)
    for layer, kept, given in ((0, hidden_in, grad_in), (1, grad_in, hidden_in)):

        @pl.when(own_feed & (here.layer == layer))
        def _():
            pltpu.make_async_copy(kept, feed, feed_sems.at[0]).start()
            pltpu.make_async_copy(live_own, live, feed_sems.at[2]).start()
            remote(given, feed, feed_sems.at[1], feed_sems.at[0], partner).start()
            remote(live_own, live, feed_sems.at[3], feed_sems.at[2], partner).start()

    def arrived(target, receive):
        pltpu.make_async_copy(target, target, receive).wait()

    def fed():
        arrived(feed, feed_sems.at[0])
        arrived(live, feed_sems.at[2])

    def columns(table, chunk, half):
        array, start, width, _ = table[chunk]
        return pl.ds(pl.multiple_of(half * (widths[array] // 2) + start, 128), width)

    def at_home(z):
        return z // 2 == here.home

    def when(condition, action):
        if condition is True:
            action()
        else:
            pl.when(condition)(action)

    def z_all(chunk, visit):
        array, _, _, shared = get_table[chunk]
        for number, plane in enumerate((1 - here.core, 2 + here.core)):
            wanted = (here.core == 1) | (here.home == number) if shared else here.z >= 0
            for half in (0, 1):
                own = (plane == here.z) & (here.core == half)
                cut = columns(get_table, chunk, half)
                source, target = shards[array].at[:, cut], weight[array].at[here.z, here.y, here.x, :, cut]
                sems = get_z_send.at[chunk, number, half], get_z_recv.at[chunk, here.z]
                visit(wanted, own, source, target, sems, (half, here.chip(z=plane)))

    def z_start(chunk):
        def visit(wanted, own, source, target, sems, device):
            @pl.when(wanted & own)
            def _():
                pltpu.make_async_copy(source, target, sems[1]).start()

            @pl.when(wanted & jnp.logical_not(own))
            def _():
                remote(source, target, *sems, device).start()

        z_all(chunk, visit)

    def z_sent(chunk):
        def visit(wanted, own, source, target, sems, device):
            @pl.when(wanted & jnp.logical_not(own))
            def _():
                remote(source, target, *sems, device).wait_send()

        z_all(chunk, visit)

    def far(step):
        return (here.z + step) % 4

    def handled(table, chunk, z):
        return here.second_layer | at_home(z) if table[chunk][3] else True

    def get_first(chunk, step):
        block = weight[get_table[chunk][0]].at[far(step), here.y, here.x, :, columns(get_table, chunk, here.core)]
        side = here.y_side() if step % 2 else here.x_side()
        return remote(block, block, get_one_send.at[chunk, step], get_one_recv.at[chunk, step], side)

    def get_second(chunk, step):
        ref, cut = weight[get_table[chunk][0]], columns(get_table, chunk, here.core)
        if step % 2:
            pair, side = ref.at[far(step), :, here.x, :, cut], here.x_side()
        else:
            pair, side = ref.at[far(step), here.y, :, :, cut], here.y_side()
        return remote(pair, pair, get_two_send.at[chunk, step], get_two_recv.at[chunk, step], side)

    def get_middle(chunk, z):
        block = weight[get_table[chunk][0]].at[z, :, :, :, columns(get_table, chunk, here.core)]
        return remote(block, block, get_mid_send.at[chunk, z % 2], get_mid_recv.at[chunk, z % 2], here.middle())

    def get_across(chunk):
        whole = weight[get_table[chunk][0]].at[:, :, :, :, columns(get_table, chunk, here.core)]
        return remote(whole, whole, get_side_send.at[chunk], get_side_recv.at[chunk], here.sibling())

    def one_step(chunk, step):
        def action():
            z = far(step)
            block = weight[get_table[chunk][0]].at[z, here.y, here.x, :, columns(get_table, chunk, here.core)]
            arrived(block, get_z_recv.at[chunk, z])
            get_first(chunk, step).start()

        when(handled(get_table, chunk, far(step)), action)

    def two_steps(chunk, step):
        def action():
            get_first(chunk, step).wait_recv()
            get_second(chunk, step).start()

        when(handled(get_table, chunk, far(step)), action)

    def three_steps(chunk, step):
        def action():
            get_second(chunk, step).wait_recv()
            if get_table[chunk][3]:

                @pl.when(here.first_layer)
                def _():
                    get_middle(chunk, far(step)).start()

        when(handled(get_table, chunk, far(step)), action)

    def pass_on(chunk):
        if get_table[chunk][3]:

            @pl.when(here.first_layer)
            def _():
                for k in range(2):
                    get_middle(chunk, 2 * (1 - here.home) + k).wait_recv()

        get_across(chunk).start()

    def gather(on_chunk):
        last = len(get_table)
        window = 2
        for chunk in range(min(window, last)):
            z_start(chunk)
        one_step(0, 0)
        for now in range(last + 4):
            if now + 1 < last:
                one_step(now + 1, 0)
            if now < last:
                for step in (1, 3, 2):
                    one_step(now, step)
            if now + window < last:
                z_start(now + window)
            if 0 <= now - 1 < last:
                for step in range(4):
                    two_steps(now - 1, step)
            if 0 <= now - 2 < last:
                for step in range(4):
                    three_steps(now - 2, step)
                if not get_table[now - 2][3]:
                    pass_on(now - 2)
            if 0 <= now - 3 < last and get_table[now - 3][3]:
                pass_on(now - 3)
            for chunk in (now - 3, now - 4):
                if 0 <= chunk < last and get_table[chunk][3] == (chunk == now - 4):
                    get_across(chunk).wait_recv()
                    on_chunk(chunk)

    def gathered():
        for chunk in range(len(get_table)):
            z_sent(chunk)
            for step in range(4):

                def action():
                    get_first(chunk, step).wait_send()
                    get_second(chunk, step).wait_send()

                when(handled(get_table, chunk, far(step)), action)
            if get_table[chunk][3]:

                @pl.when(here.first_layer)
                def _():
                    for k in range(2):
                        get_middle(chunk, 2 * here.home + k).wait_send()

            get_across(chunk).wait_send()

    def matrix(number, start, width):
        ref = weight[number]
        return ref[:, :, :, :, pl.ds(start, width)].reshape(features, width)

    def in_rows(block, body):
        lax.fori_loop(0, tokens // block, lambda i, c: (body(pl.ds(pl.multiple_of(i * block, block), block)), c)[1], 0)

    def normed(rows, rows_in, normal, scale, gain):
        centered = rows_in - jnp.mean(rows_in, axis=1, keepdims=True)
        inv = lax.rsqrt(jnp.mean(centered * centered, axis=1, keepdims=True) + epsilon)
        n = centered * inv
        normal[rows] = n
        scale[rows] = jnp.broadcast_to(inv, (n.shape[0], 128))
        left[rows] = (n * gain).astype(low)

    row_at = lax.broadcasted_iota(jnp.int32, (slots, 256), 0)
    first_row = row_at == 0

    def later(rows, places):
        return jnp.where(row_at >= places, pltpu.roll(rows, places, 0), 0.0)

    def sooner(rows, places):
        return jnp.where(row_at < slots - places, pltpu.roll(rows, slots - places, 0), 0.0)

    cuts = features // 256

    def mixer_blocks(body, start=0, stop=None):
        def step(i, carry):
            m, cut = i // cuts, i % cuts
            rows = pl.ds(pl.multiple_of(m * slots, slots), slots)
            taken = pl.ds(pl.multiple_of(cut * 256, 256), 256)
            body(m, rows, taken, cut)
            return carry

        lax.fori_loop(start, micro * cuts if stop is None else stop, step, 0)

    def live_rows(m):
        return (row_at.astype(f32) < jnp.concatenate([live[m, 0:1, :]] * 2, axis=1)).astype(f32)

    def to_sibling(number, source, target):
        return remote(source, target, send.at[number], recv.at[number], here.sibling())

    def left_copy(k):
        return to_sibling(k, lefts[k].at[0], lefts[k].at[1])

    def right_sides(k):
        return (
            (projected, other_projected),
            (after_low, other_after),
            (expanded, other_expanded),
            (active, other_active),
        )[k]

    def right_copy(k):
        source, target = right_sides(k)
        half = widths[1 + k] // 2
        cut = pl.ds(pl.multiple_of((1 - here.core) * half, 128), half)
        return to_sibling(4 + k, source.at[:, cut], target)

    def small_copy():
        return to_sibling(8, small_terms.at[1 - here.core], other_small)

    give_out = remote(out_low, arrive, swap_sems.at[0], swap_sems.at[1], partner)
    give_grad = remote(grad_low, arrive, swap_sems.at[0], swap_sems.at[1], partner)

    def enter():
        filt[...] = matrix(0, 0, 128).astype(f32).T
        rows8[...] = matrix(0, 128, 128).astype(f32).T[:8]
        in_rows(64, lambda rows: normed(rows, x_in[rows].astype(f32), norm_one, scale_one, rows8[3:4]))
        lefts[0][0] = left[...].T
        left_copy(0).start()

    def mix(m, rows, taken, cut):
        taps = [rows8[j : j + 1, taken] for j in range(3)]
        alive = live_rows(m)
        k = keys[rows, taken] * alive
        keys[rows, taken] = k
        v = values[rows, taken] * alive
        kernel = filt[:, taken] + taps[0] * k + taps[1] * later(k, 1) + taps[2] * later(k, 2)
        spec = left_dot(dft[...], parts(jnp.concatenate([v, kernel], axis=1)))
        value_spec[m, :, taken] = spec[:, :256]
        kernel_spec[m, :, taken] = spec[:, 256:]
        v_re, v_im = spec[:slots, :256], spec[slots:, :256]
        k_re, k_im = spec[:slots, 256:], spec[slots:, 256:]
        both = k_im * v_im
        re = k_re * v_re - jnp.where(first_row, 0.0, both)
        im = jnp.where(first_row, both, k_re * v_im + k_im * v_re)
        out = left_dot(idft[...], parts(jnp.concatenate([re, im], axis=0)))
        convolved[rows, taken] = out
        left[rows, taken] = (queries[rows, taken] * out).astype(low)

    def mixer():
        for k, target in enumerate((queries, keys, values)):
            target[...] = left_dot(left[...], matrix(1, k * features, features))
        mixer_blocks(mix)
        lefts[1][0] = left[...].T
        left_copy(1).start()

    def mixer_out():
        total[...] = x_in[...].astype(f32) + left_dot(left[...], matrix(2, 0, features))
        in_rows(64, lambda rows: normed(rows, total[rows], norm_two, scale_two, rows8[4:5]))
        lefts[2][0] = left[...].T
        left_copy(2).start()

    tile = 512

    def tiles(start, width, body):
        lax.fori_loop(0, width // tile, lambda i, c: (body(pl.multiple_of(start + i * tile, 128)), c)[1], 0)

    def expand(start):
        gate = left_dot(left[...], matrix(3, start, tile))
        up = left_dot(left[...], matrix(3, pl.multiple_of(hidden + start, 128), tile))
        expanded[:, pl.ds(start, tile)] = gate.astype(low)
        expanded[:, pl.ds(pl.multiple_of(hidden + start, 128), tile)] = up.astype(low)
        active[:, pl.ds(start, tile)] = (gate * jax.nn.sigmoid(gate) * up).astype(low)

    def reduce_on(start, width):
        total[...] += dot_back(active[:, pl.ds(start, width)], matrix(4, start, width))

    def layer_done():
        right_copy(3).start()
        out_low[...] = total[...].astype(low)

    ends = {array: max(k for k, entry in enumerate(get_table) if entry[0] == array) for array in range(5)}

    def as_it_comes(chunk):
        array, start, width, _ = get_table[chunk]

        @pl.when(here.first_layer)
        def _():
            if array == 0:
                x_in[...] = feed[...]
                enter()
            if array == 1 and ends[1] == chunk:
                mixer()
            if array == 2 and ends[2] == chunk:
                mixer_out()
            if array == 3:
                tiles(start, width, expand)
            if array == 4:
                for half in (0, 1):
                    reduce_on(half * (hidden // 2) + start, width)

    def on_chunk(chunk):
        if chunk == ends[0]:
            fed()
        as_it_comes(chunk)

    gather(on_chunk)

    @pl.when(here.first_layer)
    def _():
        layer_done()
        give_out.start()
        gathered()
        give_grad.wait_recv()
        e_in[...] = arrive[...]

    @pl.when(here.second_layer)
    def _():
        gathered()
        give_out.wait_recv()
        x_in[...] = arrive[...]
        e_in[...] = feed[...]
        enter()
        mixer()
        mixer_out()

        def both(start):
            expand(start)
            reduce_on(start, tile)

        tiles(0, hidden, both)
        layer_done()

    lefts[3][0] = e_in[...].T
    left_copy(3).start()
    total[...] = jnp.zeros_like(total)

    def expand_back(start):
        again = pl.multiple_of(hidden + start, 128)
        grad_act = left_dot(e_in[...], matrix(4, start, tile))
        gate = expanded[:, pl.ds(start, tile)].astype(f32)
        up = expanded[:, pl.ds(again, tile)].astype(f32)
        sig = jax.nn.sigmoid(gate)
        grad_gate = (grad_act * up * (sig * (1.0 + gate * (1.0 - sig)))).astype(low)
        grad_up = (grad_act * (gate * sig)).astype(low)
        expanded[:, pl.ds(start, tile)] = grad_gate
        expanded[:, pl.ds(again, tile)] = grad_up
        total[...] += dot_back(grad_gate, matrix(3, start, tile)) + dot_back(grad_up, matrix(3, again, tile))

    tiles(0, hidden, expand_back)
    right_copy(2).start()
    for side in (here.x_side(), here.y_side()):
        pl.semaphore_signal(ready, inc=1, device_id=side, device_id_type=MESH)

    @pl.when(here.first_layer)
    def _():
        pl.semaphore_signal(ready, inc=1, device_id=here.middle(), device_id_type=MESH)

    def norm_grad(rows, grad, normal, scale, gain, at):
        n = normal[rows]
        small_terms[1, at : at + 1] += jnp.sum(grad * n, axis=0, keepdims=True)
        q = grad * gain
        back = q - jnp.mean(q, axis=1, keepdims=True) - n * jnp.mean(q * n, axis=1, keepdims=True)
        return scale[rows][:, :1] * back

    def after_back():
        small_terms[...] = jnp.zeros_like(small_terms)

        def body(rows):
            grad = e_in[rows].astype(f32) + norm_grad(rows, total[rows], norm_two, scale_two, rows8[4:5], 4)
            after[rows] = grad
            after_low[rows] = grad.astype(low)

        in_rows(64, body)
        right_copy(1).start()

    def gated_back():
        total[...] = dot_back(after_low[...], matrix(2, 0, features))

    def mix_back(m, rows, taken, cut):
        taps = [rows8[j : j + 1, taken] for j in range(3)]
        alive = live_rows(m)
        grad = total[rows, taken]
        projected[rows, taken] = (grad * convolved[rows, taken]).astype(low)
        spec = left_dot(dft[...], parts(grad * queries[rows, taken]))
        g_re, g_im = spec[:slots], spec[slots:]
        pairs = []
        for other in (kernel_spec, value_spec):
            o_re, o_im = other[m, :slots, taken], other[m, slots:, taken]
            both = o_im * g_im
            re = o_re * g_re + jnp.where(first_row, 0.0, both)
            im = jnp.where(first_row, both, o_re * g_im - o_im * g_re)
            pairs.append(jnp.concatenate([re, im], axis=0))
        paired = left_dot(idft[...], parts(jnp.concatenate(pairs, axis=1)))
        at_values = pl.ds(pl.multiple_of(2 * features + cut * 256, 256), 256)
        projected[rows, at_values] = (paired[:, :256] * alive).astype(low)
        grad_kernel = paired[:, 256:]
        small_terms[0, :, taken] += grad_kernel
        k = keys[rows, taken]
        for j in range(3):
            moved = later(k, j) if j else k
            small_terms[1, j : j + 1, taken] += jnp.sum(grad_kernel * moved, axis=0, keepdims=True)
        grad_keys = taps[0] * grad_kernel + taps[1] * sooner(grad_kernel, 1) + taps[2] * sooner(grad_kernel, 2)
        at_keys = pl.ds(pl.multiple_of(features + cut * 256, 256), 256)
        projected[rows, at_keys] = (grad_keys * alive).astype(low)

    def mixed_back(start, stop):
        mixer_blocks(mix_back, start, stop)
        if stop == micro * cuts:
            right_copy(0).start()

    def input_back():
        total[...] = dot_back(projected[...], matrix(1, 0, 3 * features))

        def body(rows):
            grad = after[rows] + norm_grad(rows, total[rows], norm_one, scale_one, rows8[3:4], 3)
            grad_low[rows] = grad.astype(low)

        in_rows(64, body)
        small_copy().start()

    half_way = micro * cuts // 2
    pieces = [
        after_back,
        gated_back,
        functools.partial(mixed_back, 0, half_way),
        functools.partial(mixed_back, half_way, micro * cuts),
        input_back,
    ]

    @pl.when(here.second_layer)
    def _():
        for piece in pieces:
            piece()
        give_grad.start()

    offsets, place = [], 0
    for array, _, width, _ in put_table:
        offsets.append(place)
        place += width if array else 0

    def room(chunk):
        return pl.ds(offsets[chunk], put_table[chunk][2])

    def one_in(chunk, z):
        if put_table[chunk][0] == 0:
            return one_small.at[z]
        return weight[3].at[z, 0, :, :, room(chunk)]

    def two_in(chunk, z):
        if put_table[chunk][0] == 0:
            return two_small.at[z]
        return weight[3].at[z, 1, 0, :, room(chunk)]

    def mid_in(chunk, z, k):
        return weight[3].at[z, 1, 1, k, :, room(chunk)]

    def put_first(chunk, step):
        z = far(step)
        if step % 2:
            source, side = mine[chunk].at[z, :, 1 - here.x], here.x_side()
        else:
            source, side = mine[chunk].at[z, 1 - here.y], here.y_side()
        return remote(source, one_in(chunk, step), one_send.at[chunk, step], one_recv.at[chunk, step], side)

    def put_second(chunk, step):
        z = far(step)
        if step % 2:
            source, side = mine[chunk].at[z, 1 - here.y, here.x], here.y_side()
        else:
            source, side = mine[chunk].at[z, here.y, 1 - here.x], here.x_side()
        return remote(source, two_in(chunk, step), two_send.at[chunk, step], two_recv.at[chunk, step], side)

    def put_third(chunk, step, act):
        z = far(step)
        source = mine[chunk].at[z, here.y, here.x]
        target = landed[put_table[chunk][0]].at[here.home, :, columns(put_table, chunk, here.core)]
        receive = z_recv.at[chunk, here.home, here.core]
        own = (here.z == z) & (here.core == here.layer)
        if act == "start":

            @pl.when(own)
            def _():
                pltpu.make_async_copy(source, target, receive).start()

        @pl.when(jnp.logical_not(own))
        def _():
            away = remote(source, target, z_send.at[chunk, step], receive, (here.layer, here.chip(z=z)))
            getattr(away, act)()

    def add(target, other):
        target[...] = (target[...].astype(f32) + other[...].astype(f32)).astype(target.dtype)

    waits = [False] * 5

    def terms(chunk):
        array, start, width, shared = put_table[chunk]
        if array == 0:
            small_copy().wait_recv()
            block = (small_terms[here.core] + other_small[...]).T
        else:
            if not waits[array]:
                waits[array] = True
                left_copy(array - 1).wait_recv()
                right_copy(array - 1).wait_recv()
            source, other = right_sides(array - 1)
            own_at = pl.multiple_of(here.core * (widths[array] // 2) + start, 128)
            block = left_dot(lefts[array - 1][0], source[:, pl.ds(own_at, width)])
            block += left_dot(lefts[array - 1][1], other[:, pl.ds(start, width)])
        block = block.astype(low)
        rows = features // 16
        for z in range(4):
            for k in range(4):
                at = (z * 4 + k) * rows
                mine[chunk][z, k // 2, k % 2] = block[at : at + rows]
        for step in range(4):
            put_first(chunk, step).start()

    def sum_one(chunk):
        for step in range(4):
            z = far(step)
            put_first(chunk, step).wait_recv()
            for k in range(2):
                if step % 2:
                    add(mine[chunk].at[z, k, here.x], one_in(chunk, step).at[k])
                else:
                    add(mine[chunk].at[z, here.y, k], one_in(chunk, step).at[k])
            put_second(chunk, step).start()

    def sum_two(chunk):
        for step in range(4):
            put_second(chunk, step).wait_recv()
            add(mine[chunk].at[far(step), here.y, here.x], two_in(chunk, step))
            put_third(chunk, step, "start")

    pl.when(here.first_layer)(lambda: pl.semaphore_wait(ready, 3))
    pl.when(here.second_layer)(lambda: pl.semaphore_wait(ready, 2))

    apart = here.core != here.layer
    over = (1 - here.core, here.partner)

    def swap(source, target, number, act):
        sems = swap_sems.at[number], swap_sems.at[number + 1]

        @pl.when(apart)
        def _():
            getattr(remote(source, target, *sems, over), act)()

        @pl.when(jnp.logical_not(apart))
        def _():
            getattr(pltpu.make_async_copy(source, target, sems[1]), act)()

    last = len(put_table)
    needs = {array: min(k for k, entry in enumerate(put_table) if entry[0] == array) for array in range(5)}
    due = [max(0, needs[1] - 5 + k) for k in range(4)] + [needs[0] - 2]
    terms(0)
    swap(out_low, kept_out, 2, "start")
    for now in range(last + 1):
        for piece, at in zip(pieces, due):
            if at == now:
                pl.when(here.first_layer)(piece)
        if now + 1 < last:
            terms(now + 1)
        if now < last:
            sum_one(now)
        if 1 <= now:
            sum_two(now - 1)
        if now == needs[0]:
            swap(grad_low, kept_grad, 4, "start")

    for chunk in range(last):
        for half in (0, 1):
            for slot in (0, 1):
                target = landed[put_table[chunk][0]].at[slot, :, columns(put_table, chunk, half)]
                arrived(target, z_recv.at[chunk, slot, half])
        for step in range(4):
            put_first(chunk, step).wait_send()
            put_second(chunk, step).wait_send()
            put_third(chunk, step, "wait_send")

    @pl.when(own_feed)
    def _():
        remote(hidden_in, feed, feed_sems.at[1], feed_sems.at[0], partner).wait_send()
        remote(live_own, live, feed_sems.at[3], feed_sems.at[2], partner).wait_send()

    for k in range(4):
        left_copy(k).wait_send()
        right_copy(k).wait_send()
    small_copy().wait_send()
    give_out.wait_send()
    swap(out_low, kept_out, 2, "wait")
    swap(grad_low, kept_grad, 4, "wait")


def finish_kernel(*refs):
    landed, (out, grad) = refs[:5], refs[5:7]
    s_filters, s_taps, s_one, s_two = refs[7:11]
    sums, (to_out, to_grad), sems = refs[11:15], refs[15:17], refs[17]
    copies = [pltpu.make_async_copy(out, to_out, sems.at[0]), pltpu.make_async_copy(grad, to_grad, sems.at[1])]
    for copy in copies:
        copy.start()
    small = landed[0][0].astype(jnp.float32) + landed[0][1].astype(jnp.float32)
    s_filters[...] = small[:, :128]
    own = small.shape[0]
    rows = jnp.pad(small[:, 128:], ((0, 128 - own), (0, 0))).T
    s_taps[...] = rows[0:3, :own]
    s_one[...] = rows[3:4, :own]
    s_two[...] = rows[4:5, :own]
    for number, result in enumerate(sums):
        result[...] = landed[1 + number][0].astype(jnp.float32) + landed[1 + number][1].astype(jnp.float32)
    for copy in copies:
        copy.wait()


def fast_device(
    hidden_in, out_grad, lengths, gain_mixer, w_input, w_taps, filters, w_output, gain_mlp, w_gate_up, w_down
):
    micro, _, slots, features = hidden_in.shape
    tokens, rows = micro * slots, gain_mixer.shape[1]
    shards = (w_input[0], w_output[0], w_gate_up[0], w_down[0].T)
    widths = [256] + [shard.shape[1] for shard in shards]
    hidden = widths[4]
    get_table, put_table = chunks_of(GET_PIECES), chunks_of(PUT_PIECES)
    dft, idft = (jnp.asarray(table) for table in packed_tables(slots))
    low, f32 = jnp.bfloat16, jnp.float32
    anywhere = pl.BlockSpec(memory_space=pl.ANY)
    inside = pl.BlockSpec(memory_space=pltpu.VMEM)
    dma, vmem = pltpu.SemaphoreType.DMA, pltpu.VMEM
    act, act_low = (tokens, features), vmem((tokens, features), low)
    kinds = [jax.ShapeDtypeStruct((2, rows, width), low) for width in widths]
    kinds += [jax.ShapeDtypeStruct((tokens, features), low)] * 2
    room = [vmem((rows, 256), low), vmem((128, 128), f32)] + [vmem((micro, 8, 128), f32)] * 2
    room += [vmem((4, 2, 2, rows, width), low) for width in widths]
    room += [act_low] * 6
    room += [vmem((slots, features), f32), vmem((8, features), f32), vmem(act, f32), vmem(act, f32)]
    room += [vmem((tokens, 128), f32)] * 2
    room += [act_low] + [vmem(act, f32)] * 4 + [vmem((micro, 2 * slots, features), f32)] * 2
    room += [vmem(act, f32)] * 2 + [vmem((tokens, 2 * hidden), low), vmem((tokens, hidden), low)]
    room += [vmem((tokens, 3 * features), low), act_low, vmem((2, slots, features), f32)]
    room += [vmem((2, features, tokens), low)] * 4
    room += [vmem((slots, features), f32)] + [vmem((tokens, width // 2), low) for width in widths[1:]]
    room += [vmem((4, 2, 2, rows, entry[2]), low) for entry in put_table]
    room += [vmem((4, 2, rows, 128), low), vmem((4, rows, 128), low)]
    got, put = len(get_table), len(put_table)
    room += [dma((got, 2, 2))] + [dma((got, 4))] * 5 + [dma((got, 2))] * 2 + [dma((got,))] * 2 + [dma((4,))]
    room += [dma((6,)), dma((9,)), dma((9,))]
    room += [dma((put, 4))] * 5 + [dma((put, 2, 2))] + [dma((put,))] * 2 + [pltpu.SemaphoreType.REGULAR]
    results = pl.pallas_call(
        functools.partial(layer_kernel, get_table, put_table, widths),
        out_shape=kinds,
        in_specs=[inside] * 4 + [pl.BlockSpec(memory_space=pltpu.SMEM)] + [inside] * 2 + [anywhere] * 6,
        out_specs=[anywhere] * 7,
        scratch_shapes=room,
        compiler_params=pltpu.CompilerParams(
            collective_id=0, has_side_effects=True, vmem_limit_bytes=62 * 1024 * 1024
        ),
    )(
        filters[0].T,
        w_taps[0],
        gain_mixer,
        gain_mlp,
        lengths,
        dft,
        idft,
        *shards,
        hidden_in.reshape(tokens, features),
        out_grad.reshape(tokens, features),
    )
    kinds = [(rows, 128), (3, rows), (1, rows), (1, rows)] + [(rows, width) for width in widths[1:]]
    kinds = [jax.ShapeDtypeStruct(kind, f32) for kind in kinds] + kinds_of(results[5:])
    s_filters, s_taps, s_one, s_two, s_in, s_out, s_gu, s_dt, layer_out, input_grad = pl.pallas_call(
        finish_kernel,
        out_shape=kinds,
        in_specs=[inside] * 5 + [anywhere] * 2,
        out_specs=[inside] * 8 + [anywhere] * 2,
        scratch_shapes=[dma((2,))],
        compiler_params=pltpu.CompilerParams(vmem_limit_bytes=32 * 1024 * 1024),
    )(*results)
    shape = (1, micro, 1, slots, features)
    return (
        layer_out.reshape(shape),
        input_grad.reshape(shape),
        s_one,
        s_in[None],
        s_taps[None],
        s_filters.T[None],
        s_out[None],
        s_two,
        s_gu[None],
        s_dt.T[None],
    )


def kinds_of(arrays):
    return [jax.ShapeDtypeStruct(array.shape, array.dtype) for array in arrays]


def solution(mesh):
    placed = (
        P(None, "dp", None, None),
        P(None, "dp", None, None),
        P(None, "dp"),
        P("section", "dp"),
        P("section", "dp", None),
        P("section", None, "dp"),
        P("section", None, "dp"),
        P("section", "dp", None),
        P("section", "dp"),
        P("section", "dp", None),
        P("section", None, "dp"),
    )
    return jax.shard_map(
        fast_device if mesh.shape["dp"] == 16 and mesh.shape["section"] == 2 else on_device,
        mesh=mesh,
        in_specs=placed,
        out_specs=(
            P("section", None, "dp", None, None),
            P("section", None, "dp", None, None),
            P("section", "dp"),
            P("section", "dp", None),
            P("section", None, "dp"),
            P("section", None, "dp"),
            P("section", "dp", None),
            P("section", "dp"),
            P("section", "dp", None),
            P("section", None, "dp"),
        ),
        check_vma=False,
    )
```

```python
import functools
import math

import jax
import jax.numpy as jnp
import ml_dtypes
import numpy as np
from jax import lax
from jax.experimental import pallas as pl
from jax.experimental.pallas import tpu as pltpu
from jax.sharding import PartitionSpec as P

MESH = pl.DeviceIdType.MESH

epsilon = 1e-05
GET_PIECES = (
    (0, 128, False),
    (1, 384, False),
    (1, 384, False),
    (1, 384, False),
    (2, 384, False),
    (3, 1024, False),
    (3, 1024, False),
    (3, 1024, False),
    (4, 512, False),
    (4, 512, False),
    (4, 512, False),
)
PUT_PIECES = (
    (4, 768, False),
    (4, 768, False),
    (3, 1024, False),
    (3, 1024, False),
    (3, 1024, False),
    (2, 384, False),
    (1, 384, False),
    (1, 384, False),
    (1, 384, False),
    (0, 128, False),
)
GET_LAGS = (5, 9, 1, 2, 3)
ROWS_UNROLL = 2
MIX_UNROLL = 3
TILE_UNROLL = 2


def passed_along(value, axis, steps):
    count = lax.axis_size(axis)
    first, last = (max(0, -steps), min(count, count - steps))
    return lax.ppermute(value, axis, [(source, source + steps) for source in range(first, last)])


def split_dot(left_side, right_side):
    return jnp.dot(
        left_side, right_side, precision=lax.Precision.HIGH, preferred_element_type=jnp.float32
    )


def split_rows(left_side, right_side):
    return lax.dot_general(
        left_side,
        right_side,
        (((0,), (0,)), ((), ())),
        precision=lax.Precision.HIGH,
        preferred_element_type=jnp.float32,
    )


def dot_rows(left_side, right_side):
    return lax.dot_general(
        left_side, right_side, (((0,), (0,)), ((), ())), preferred_element_type=jnp.float32
    )


def dot_back(left_side, right_side):
    return lax.dot_general(
        left_side, right_side, (((1,), (1,)), ((), ())), preferred_element_type=jnp.float32
    )


def tables(length):
    period = 2 * length
    freq_index = lax.broadcasted_iota(jnp.int32, (length + 1, length), 0)
    time_index = lax.broadcasted_iota(jnp.int32, (length + 1, length), 1)
    angles = (freq_index * time_index % period).astype(jnp.float32) * (2.0 * math.pi / period)
    edge_rows = (freq_index[:, :1] == 0) | (freq_index[:, :1] == length)
    inverse_weight = jnp.where(edge_rows, 1.0, 2.0) / period
    dft_stack = jnp.concatenate([jnp.cos(angles), -jnp.sin(angles)], axis=0)
    return (dft_stack, inverse_weight)


def spectrum(dft_tables, signal):
    dft_stack, inverse_weight = dft_tables
    stacked_out = split_dot(dft_stack, signal)
    middle_row = stacked_out.shape[0] // 2
    return (stacked_out[:middle_row], stacked_out[middle_row:])


def inverse(dft_tables, real_part, imag_part):
    dft_stack, inverse_weight = dft_tables
    return split_rows(
        dft_stack, jnp.concatenate([inverse_weight * real_part, inverse_weight * imag_part], axis=0)
    )


def normalize(input_rows):
    centered = input_rows - jnp.mean(input_rows, axis=1, keepdims=True)
    inv_scale = lax.rsqrt(jnp.mean(centered * centered, axis=1, keepdims=True) + epsilon)
    return (centered * inv_scale, inv_scale)


def norm_back(grad_normed, normed, inv_scale):
    return inv_scale * (
        grad_normed
        - jnp.mean(grad_normed, axis=1, keepdims=True)
        - normed * jnp.mean(grad_normed * normed, axis=1, keepdims=True)
    )


def delayed(input_rows, places):
    return jnp.pad(input_rows, ((places, 0), (0, 0)))[: input_rows.shape[0]]


def advanced(input_rows, places):
    return jnp.pad(input_rows, ((0, places), (0, 0)))[places:]


def layer_forward(input_rows, active_rows, weights, dft_tables):
    gain_one, w_inner, w_tap_rows, filt_static, w_outer, gain_two, w_expand, w_reduce = weights
    hidden_size_model = w_outer.shape[0]
    hidden_width = w_reduce.shape[0]
    tap_weights = w_tap_rows.astype(jnp.float32)
    normed_one, scale_one = normalize(input_rows)
    entered = (normed_one * gain_one.astype(jnp.float32)).astype(jnp.bfloat16)
    projected = jnp.dot(entered, w_inner, preferred_element_type=jnp.float32)
    queries = projected[:, :hidden_size_model]
    keys_part = projected[:, hidden_size_model : 2 * hidden_size_model] * active_rows
    values_part = projected[:, 2 * hidden_size_model :] * active_rows
    dynamic = (
        tap_weights[0] * keys_part
        + tap_weights[1] * delayed(keys_part, 1)
        + tap_weights[2] * delayed(keys_part, 2)
    )
    kernel = filt_static.astype(jnp.float32) + dynamic
    joint_re, joint_im = spectrum(dft_tables, jnp.concatenate([values_part, kernel], axis=1))
    value_re = joint_re[:, :hidden_size_model]
    kernel_re = joint_re[:, hidden_size_model:]
    value_im = joint_im[:, :hidden_size_model]
    kernel_im = joint_im[:, hidden_size_model:]
    convolved = inverse(
        dft_tables,
        kernel_re * value_re - kernel_im * value_im,
        kernel_re * value_im + kernel_im * value_re,
    )
    gated_rows = (queries * convolved).astype(jnp.bfloat16)
    after_mixer = input_rows + jnp.dot(gated_rows, w_outer, preferred_element_type=jnp.float32)
    normed_two, scale_two = normalize(after_mixer)
    entered_two = (normed_two * gain_two.astype(jnp.float32)).astype(jnp.bfloat16)
    expanded = jnp.dot(entered_two, w_expand, preferred_element_type=jnp.float32)
    gate_part = expanded[:, :hidden_width]
    up_part = expanded[:, hidden_width:]
    activated = (jax.nn.silu(gate_part) * up_part).astype(jnp.bfloat16)
    result = after_mixer + jnp.dot(activated, w_reduce, preferred_element_type=jnp.float32)
    stash = (
        normed_one,
        scale_one,
        entered,
        queries,
        keys_part,
        (value_re, value_im, kernel_re, kernel_im),
        convolved,
        gated_rows,
        normed_two,
        scale_two,
        entered_two,
        gate_part,
        up_part,
        activated,
    )
    return (result, stash)


def mlp_backward(received_gradient, weights, stash):
    gain_one, w_inner, w_tap_rows, filt_static, w_outer, gain_two, w_expand, w_reduce = weights
    (
        normed_one,
        scale_one,
        entered,
        queries,
        keys_part,
        spectra,
        convolved,
        gated_rows,
        normed_two,
        scale_two,
        entered_two,
        gate_part,
        up_part,
        activated,
    ) = stash
    grad_low = received_gradient.astype(jnp.bfloat16)
    grad_reduce_w = dot_rows(activated, grad_low)
    grad_act = dot_back(grad_low, w_reduce)
    sigmoid_gate = jax.nn.sigmoid(gate_part)
    grad_gate = grad_act * up_part * (sigmoid_gate * (1.0 + gate_part * (1.0 - sigmoid_gate)))
    grad_up = grad_act * (gate_part * sigmoid_gate)
    grad_expand = jnp.concatenate([grad_gate, grad_up], axis=1).astype(jnp.bfloat16)
    grad_expand_w = dot_rows(entered_two, grad_expand)
    grad_entered_two = dot_back(grad_expand, w_expand)
    grad_gain_two = jnp.sum(grad_entered_two * normed_two, axis=0)
    grad_after = received_gradient + norm_back(
        grad_entered_two * gain_two.astype(jnp.float32), normed_two, scale_two
    )
    return (grad_after, (grad_gain_two, grad_expand_w, grad_reduce_w))


def mixer_backward(grad_after, active_rows, weights, dft_tables, stash):
    gain_one, w_inner, w_tap_rows, filt_static, w_outer, gain_two, w_expand, w_reduce = weights
    (
        normed_one,
        scale_one,
        entered,
        queries,
        keys_part,
        spectra,
        convolved,
        gated_rows,
        normed_two,
        scale_two,
        entered_two,
        gate_part,
        up_part,
        activated,
    ) = stash
    value_re, value_im, kernel_re, kernel_im = spectra
    hidden_size_model = w_outer.shape[0]
    tap_weights = w_tap_rows.astype(jnp.float32)
    grad_mix_low = grad_after.astype(jnp.bfloat16)
    grad_outer_w = dot_rows(gated_rows, grad_mix_low)
    grad_gated = dot_back(grad_mix_low, w_outer)
    grad_queries = grad_gated * convolved
    grad_conv = grad_gated * queries
    grad_re, grad_im = spectrum(dft_tables, grad_conv)
    paired_re = jnp.concatenate(
        [kernel_re * grad_re + kernel_im * grad_im, value_re * grad_re + value_im * grad_im], axis=1
    )
    paired_im = jnp.concatenate(
        [kernel_re * grad_im - kernel_im * grad_re, value_re * grad_im - value_im * grad_re], axis=1
    )
    paired = inverse(dft_tables, paired_re, paired_im)
    grad_values = paired[:, :hidden_size_model] * active_rows
    grad_kernel = paired[:, hidden_size_model:]
    grad_taps = jnp.stack(
        [
            jnp.sum(grad_kernel * keys_part, axis=0),
            jnp.sum(grad_kernel * delayed(keys_part, 1), axis=0),
            jnp.sum(grad_kernel * delayed(keys_part, 2), axis=0),
        ]
    )
    grad_keys = (
        tap_weights[0] * grad_kernel
        + tap_weights[1] * advanced(grad_kernel, 1)
        + tap_weights[2] * advanced(grad_kernel, 2)
    ) * active_rows
    grad_projected = jnp.concatenate([grad_queries, grad_keys, grad_values], axis=1).astype(
        jnp.bfloat16
    )
    inner_weight_gradient = dot_rows(entered, grad_projected)
    grad_entered = dot_back(grad_projected, w_inner)
    grad_gain_one = jnp.sum(grad_entered * normed_one, axis=0)
    grad_inputs = grad_after + norm_back(
        grad_entered * gain_one.astype(jnp.float32), normed_one, scale_one
    )
    return (
        grad_inputs,
        (grad_gain_one, inner_weight_gradient, grad_taps, grad_kernel, grad_outer_w),
    )


def add_terms(received, flipped):
    return tuple(
        (
            jnp.sum(member, axis=0).T if flip else jnp.sum(member, axis=0)
            for member, flip in zip(received, flipped)
        )
    )


def on_device(
    hidden_in,
    out_grad,
    lengths,
    gain_mixer,
    w_input,
    w_taps,
    filters,
    w_output,
    gain_mlp,
    w_gate_up,
    w_down,
):
    first_section = lax.axis_index("section") == 0
    micro_count = hidden_in.shape[0]
    seq_slots = hidden_in.shape[2]
    hidden_size_model = hidden_in.shape[3]
    dft_tables = tables(seq_slots)
    positions = lax.broadcasted_iota(jnp.int32, (seq_slots, 1), 0)
    weights = (
        lax.all_gather(gain_mixer[0], "dp", axis=0, tiled=True),
        lax.all_gather(w_input[0], "dp", axis=0, tiled=True),
        lax.all_gather(w_taps[0], "dp", axis=1, tiled=True),
        lax.all_gather(filters[0], "dp", axis=1, tiled=True),
        lax.all_gather(w_output[0], "dp", axis=0, tiled=True),
        lax.all_gather(gain_mlp[0], "dp", axis=0, tiled=True),
        lax.all_gather(w_gate_up[0], "dp", axis=0, tiled=True),
        lax.all_gather(w_down[0], "dp", axis=1, tiled=True),
    )
    arriving = jnp.zeros((seq_slots, hidden_size_model), jnp.bfloat16)
    outgoing_list = []
    saved_activations = []
    for forward_step in range(micro_count + 1):
        own_index = min(forward_step, micro_count - 1)
        prior_index = max(forward_step - 1, 0)
        input_rows = jnp.where(first_section, hidden_in[own_index, 0], arriving).astype(jnp.float32)
        length_now = jnp.where(first_section, lengths[own_index, 0], lengths[prior_index, 0])
        active_rows = (positions < length_now).astype(jnp.float32)
        result, stash = layer_forward(input_rows, active_rows, weights, dft_tables)
        outgoing = result.astype(jnp.bfloat16)
        outgoing_list.append(outgoing)
        if forward_step < micro_count:
            arriving = passed_along(outgoing, "section", 1)
        saved_activations.append((input_rows, active_rows))
    coming = jnp.zeros((seq_slots, hidden_size_model), jnp.bfloat16)
    mlp_totals = None
    mixer_totals = None
    grads_out = []
    for backward_step in range(micro_count + 1):
        saved_slot_index = micro_count - backward_step
        last_index = max(micro_count - 1 - backward_step, 0)
        live_factor = 1.0 if backward_step < micro_count else 0.0
        received_gradient = jnp.where(
            first_section,
            coming.astype(jnp.float32),
            out_grad[last_index, 0].astype(jnp.float32) * live_factor,
        )
        input_rows, active_rows = saved_activations[saved_slot_index]
        result, stash = layer_forward(input_rows, active_rows, weights, dft_tables)
        grad_after, mlp_grads = mlp_backward(received_gradient, weights, stash)
        mlp_totals = (
            mlp_grads if mlp_totals is None else jax.tree.map(jnp.add, mlp_totals, mlp_grads)
        )
        grad_inputs, mixer_grads = mixer_backward(
            grad_after, active_rows, weights, dft_tables, stash
        )
        mixer_totals = (
            mixer_grads
            if mixer_totals is None
            else jax.tree.map(jnp.add, mixer_totals, mixer_grads)
        )
        outgoing = grad_inputs.astype(jnp.bfloat16)
        grads_out.append(outgoing)
        if backward_step < micro_count:
            coming = passed_along(outgoing, "section", -1)
    first_outputs = jnp.stack(outgoing_list[:micro_count])
    second_outputs = jnp.stack(outgoing_list[1:])
    layer_out = jnp.where(first_section, first_outputs, second_outputs)[None, :, None]
    first_grads = jnp.stack(
        [grads_out[micro_count - batch_index] for batch_index in range(micro_count)]
    )
    second_grads = jnp.stack(
        [grads_out[micro_count - 1 - batch_index] for batch_index in range(micro_count)]
    )
    input_grad = jnp.where(first_section, first_grads, second_grads)[None, :, None]
    all_parts = (
        lax.all_to_all(
            mixer_totals[0][None].astype(jnp.bfloat16),
            "dp",
            split_axis=1,
            concat_axis=0,
            tiled=True,
        ).astype(jnp.float32),
        lax.all_to_all(
            mixer_totals[1][None].astype(jnp.bfloat16),
            "dp",
            split_axis=1,
            concat_axis=0,
            tiled=True,
        ).astype(jnp.float32),
        lax.all_to_all(
            mixer_totals[2].T[None].astype(jnp.bfloat16),
            "dp",
            split_axis=1,
            concat_axis=0,
            tiled=True,
        ).astype(jnp.float32),
        lax.all_to_all(
            mixer_totals[3].T[None].astype(jnp.bfloat16),
            "dp",
            split_axis=1,
            concat_axis=0,
            tiled=True,
        ).astype(jnp.float32),
        lax.all_to_all(
            mixer_totals[4][None].astype(jnp.bfloat16),
            "dp",
            split_axis=1,
            concat_axis=0,
            tiled=True,
        ).astype(jnp.float32),
        lax.all_to_all(
            mlp_totals[0][None].astype(jnp.bfloat16), "dp", split_axis=1, concat_axis=0, tiled=True
        ).astype(jnp.float32),
        lax.all_to_all(
            mlp_totals[1][None].astype(jnp.bfloat16), "dp", split_axis=1, concat_axis=0, tiled=True
        ).astype(jnp.float32),
        lax.all_to_all(
            mlp_totals[2].T[None].astype(jnp.bfloat16),
            "dp",
            split_axis=1,
            concat_axis=0,
            tiled=True,
        ).astype(jnp.float32),
    )
    summed = add_terms(all_parts, (False, False, True, True, False, False, False, True))
    return (
        layer_out,
        input_grad,
        summed[0][None],
        summed[1][None],
        summed[2][None],
        summed[3][None],
        summed[4][None],
        summed[5][None],
        summed[6][None],
        summed[7][None],
    )


class Place:
    def __init__(self):
        self.core = lax.axis_index("section")
        self.index = lax.axis_index("dp")
        self.z = self.index // 4
        self.y = self.index // 2 % 2
        self.x = self.index % 2
        self.layer = 1 - (self.z + 1) // 2 % 2
        self.home = self.z // 2
        self.first_layer = self.layer == 0
        self.second_layer = self.layer == 1
        self.partner = self.chip(z=self.z + 1 - 2 * (self.z % 2))

    def chip(self, z=None, y=None, x=None):
        z, y, x = (a if a is not None else b for a, b in ((z, self.z), (y, self.y), (x, self.x)))
        return z * 4 + y * 2 + x

    def x_side(self):
        return (self.core, self.chip(x=1 - self.x))

    def y_side(self):
        return (self.core, self.chip(y=1 - self.y))

    def sibling(self):
        return (1 - self.core, self.index)

    def middle(self):
        return (self.core, self.chip(z=3 - self.z))

    def greet(self):
        barrier = pltpu.get_barrier_semaphore()
        others = [self.x_side(), self.y_side(), self.sibling()]
        for step in (1, 2, 3):
            chip = self.chip(z=(self.z + step) % 4)
            others += [(0, chip), (1, chip)]
        for other in others:
            pl.semaphore_signal(barrier, inc=1, device_id=other, device_id_type=MESH)
        pl.semaphore_wait(barrier, len(others))


def remote(source, target, send, receive, device):
    return pltpu.make_async_remote_copy(
        src_ref=source,
        dst_ref=target,
        send_sem=send,
        recv_sem=receive,
        device_id=device,
        device_id_type=MESH,
    )


def chunks_of(pieces):
    table, places = [], {}
    for array, width, shared in pieces:
        start = places.get(array, 0)
        table.append((array, start, width, shared))
        places[array] = start + width
    return table


def left_dot(left_side, right_side):
    return lax.dot_general(
        left_side, right_side, (((1,), (0,)), ((), ())), preferred_element_type=jnp.float32
    )


def sigmoid(value):
    return 0.5 * jnp.tanh(0.5 * value) + 0.5


def parts(signal):
    high = signal.astype(jnp.bfloat16)
    rest = (signal - high.astype(jnp.float32)).astype(jnp.bfloat16)
    return jnp.concatenate([high, high, rest], axis=0)


def halves_of(table):
    high = table.astype(ml_dtypes.bfloat16)
    rest = (table - high.astype(np.float64)).astype(ml_dtypes.bfloat16)
    return np.concatenate([high, rest, high], axis=1)


def packed_tables(length):
    period = 2 * length
    freq, time = np.arange(length)[:, None], np.arange(length)[None, :]
    angles = (freq * time % period) * (2.0 * math.pi / period)
    sines = np.where(freq == 0, 1.0 - 2.0 * (time % 2), -np.sin(angles))
    table = np.concatenate([np.cos(angles), sines], axis=0)
    weight = np.where(np.arange(period)[:, None] % length == 0, 1.0, 2.0) / period
    return halves_of(table), halves_of((table * weight).T)


def layer_kernel(get_table, put_table, widths, *refs):
    refs = list(refs)

    def take(number):
        taken = refs[:number]
        del refs[:number]
        return taken

    filters_in, taps_in, gain_one_in, gain_two_in, lengths_in, dft, idft = take(7)
    shards, (hidden_in, grad_in) = [None] + take(4), take(2)
    landed, (kept_out, kept_grad) = take(5), take(2)
    own_small, rows_in, live_own, live = take(4)
    weight = take(5)
    feed, arrive, x_in, e_in, out_low, grad_low = take(6)
    filt, rows8, norm_one, norm_two, scale_one, scale_two = take(6)
    entered, gated, again, queries, keys, values, convolved, value_spec, kernel_spec = take(9)
    total, after, expanded, active, projected, after_low, small_terms = take(7)
    lefts = take(4)
    other_small, other_projected, other_after, other_expanded, other_active = take(5)
    mine = take(len(put_table))
    one_small, two_small = take(2)
    get_z_send, get_z_recv, get_one_send, get_one_recv, get_two_send, get_two_recv = take(6)
    get_mid_send, get_mid_recv, get_side_send, get_side_recv, feed_sems = take(5)
    swap_sems, give_send, give_recv, send, recv = take(5)
    one_send, one_recv, two_send, two_recv, z_send, z_recv, mid_send, mid_recv, ready = take(9)

    here = Place()
    tokens, features = x_in.shape
    slots = filt.shape[0]
    micro = tokens // slots
    hidden = active.shape[1]
    f32, low = jnp.float32, jnp.bfloat16
    shards[0] = own_small

    rows_in[...] = jnp.zeros_like(rows_in)
    own = taps_in.shape[1]
    rows_in[0:3, 0:own] = taps_in[...].astype(f32)
    rows_in[3:4, 0:own] = gain_one_in[...].astype(f32)
    rows_in[4:5, 0:own] = gain_two_in[...].astype(f32)
    own_small[:, :128] = filters_in[...]
    own_small[:, 128:] = rows_in[...].T[:own].astype(low)
    for m in range(micro):
        live_own[m] = jnp.full(live_own.shape[1:], lengths_in[0, m], jnp.int32).astype(f32)
    here.greet()

    own_feed = here.core == here.layer
    partner = (here.core, here.partner)
    for layer, kept, given in ((0, hidden_in, grad_in), (1, grad_in, hidden_in)):

        @pl.when(own_feed & (here.layer == layer))
        def _():
            pltpu.make_async_copy(kept, feed, feed_sems.at[0]).start()
            pltpu.make_async_copy(live_own, live, feed_sems.at[2]).start()
            remote(given, feed, feed_sems.at[1], feed_sems.at[0], partner).start()
            remote(live_own, live, feed_sems.at[3], feed_sems.at[2], partner).start()

    def arrived(target, receive):
        pltpu.make_async_copy(target, target, receive).wait()

    def fed():
        arrived(feed, feed_sems.at[0])
        arrived(live, feed_sems.at[2])

    def columns(table, chunk, half):
        array, start, width, _ = table[chunk]
        return pl.ds(pl.multiple_of(half * (widths[array] // 2) + start, 128), width)

    def at_home(z):
        return z // 2 == here.home

    def when(condition, action):
        if condition is True:
            action()
        else:
            pl.when(condition)(action)

    def z_all(chunk, visit, near):
        array, _, _, shared = get_table[chunk]
        for number, plane in enumerate((1 - here.core, 2 + here.core)):
            wanted = (plane == here.z) if near else (plane != here.z)
            if shared:
                wanted = wanted & ((here.core == 1) | (here.home == number))
            for half in (0, 1):
                cut = columns(get_table, chunk, half)
                source, target = shards[array].at[:, cut], weight[array].at[here.z, here.y, here.x, :, cut]
                sems = get_z_send.at[chunk, number, half], get_z_recv.at[chunk, here.z]
                visit(wanted, here.core == half, source, target, sems, (half, here.chip(z=plane)))

    def z_start(chunk, near):
        def visit(wanted, own, source, target, sems, device):
            if not near:

                @pl.when(wanted)
                def _():
                    remote(source, target, *sems, device).start()

                return

            @pl.when(wanted & own)
            def _():
                pltpu.make_async_copy(source, target, sems[1]).start()

            @pl.when(wanted & jnp.logical_not(own))
            def _():
                remote(source, target, *sems, device).start()

        z_all(chunk, visit, near)

    def z_sent(chunk):
        for near in (False, True):

            def visit(wanted, own, source, target, sems, device):
                @pl.when(wanted & jnp.logical_not(own) if near else wanted)
                def _():
                    remote(source, target, *sems, device).wait_send()

            z_all(chunk, visit, near)

    def far(step):
        return (here.z + step) % 4

    def handled(table, chunk, z):
        return here.second_layer | at_home(z) if table[chunk][3] else True

    def get_first(chunk, step):
        block = weight[get_table[chunk][0]].at[far(step), here.y, here.x, :, columns(get_table, chunk, here.core)]
        side = here.y_side() if (step + chunk) % 2 else here.x_side()
        return remote(block, block, get_one_send.at[chunk, step], get_one_recv.at[chunk, step], side)

    def get_second(chunk, step):
        ref, cut = weight[get_table[chunk][0]], columns(get_table, chunk, here.core)
        if (step + chunk) % 2:
            pair, side = ref.at[far(step), :, here.x, :, cut], here.x_side()
        else:
            pair, side = ref.at[far(step), here.y, :, :, cut], here.y_side()
        return remote(pair, pair, get_two_send.at[chunk, step], get_two_recv.at[chunk, step], side)

    def get_middle(chunk, z):
        block = weight[get_table[chunk][0]].at[z, :, :, :, columns(get_table, chunk, here.core)]
        return remote(block, block, get_mid_send.at[chunk, z % 2], get_mid_recv.at[chunk, z % 2], here.middle())

    def get_across(chunk):
        whole = weight[get_table[chunk][0]].at[:, :, :, :, columns(get_table, chunk, here.core)]
        return remote(whole, whole, get_side_send.at[chunk], get_side_recv.at[chunk], here.sibling())

    def one_step(chunk, step):
        def action():
            z = far(step)
            block = weight[get_table[chunk][0]].at[z, here.y, here.x, :, columns(get_table, chunk, here.core)]
            arrived(block, get_z_recv.at[chunk, z])
            get_first(chunk, step).start()

        when(handled(get_table, chunk, far(step)), action)

    def two_steps(chunk, step):
        def action():
            get_first(chunk, step).wait_recv()
            get_second(chunk, step).start()

        when(handled(get_table, chunk, far(step)), action)

    def three_steps(chunk, step):
        def action():
            get_second(chunk, step).wait_recv()
            if get_table[chunk][3]:

                @pl.when(here.first_layer)
                def _():
                    get_middle(chunk, far(step)).start()

        when(handled(get_table, chunk, far(step)), action)

    def pass_on(chunk):
        if get_table[chunk][3]:

            @pl.when(here.first_layer)
            def _():
                for k in range(2):
                    get_middle(chunk, 2 * (1 - here.home) + k).wait_recv()

        get_across(chunk).start()

    def gather(on_chunk):
        last = len(get_table)
        ahead, own_ahead, two_lag, three_lag, done_lag = GET_LAGS
        for chunk in range(last):
            z_start(chunk, True)

        def z_first():
            for chunk in range(min(ahead, last)):
                z_start(chunk, False)

        pl.when(here.core == 0)(z_first)
        for chunk in range(min(own_ahead, last)):
            one_step(chunk, 0)
        for chunk in range(min(own_ahead, last) - 1):
            two_steps(chunk, 0)
        pl.when(here.core == 1)(z_first)
        for now in range(last + done_lag + 1):
            if now + own_ahead < last:
                one_step(now + own_ahead, 0)
            if 0 <= now + own_ahead - 1 < last:
                two_steps(now + own_ahead - 1, 0)
            if now < last:
                for step in (1, 3, 2):
                    one_step(now, step)
            if now + ahead < last:
                z_start(now + ahead, False)
            if 0 <= now - two_lag < last:
                for step in (1, 3, 2):
                    two_steps(now - two_lag, step)
            if 0 <= now - three_lag < last:
                for step in range(4):
                    three_steps(now - three_lag, step)
                if not get_table[now - three_lag][3]:
                    pass_on(now - three_lag)
            if 0 <= now - three_lag - 1 < last and get_table[now - three_lag - 1][3]:
                pass_on(now - three_lag - 1)
            for chunk in (now - done_lag, now - done_lag - 1):
                if 0 <= chunk < last and get_table[chunk][3] == (chunk == now - done_lag - 1):
                    get_across(chunk).wait_recv()
                    on_chunk(chunk)

    def gathered():
        for chunk in range(len(get_table)):
            z_sent(chunk)
            for step in range(4):

                def action():
                    get_first(chunk, step).wait_send()
                    get_second(chunk, step).wait_send()

                when(handled(get_table, chunk, far(step)), action)
            if get_table[chunk][3]:

                @pl.when(here.first_layer)
                def _():
                    for k in range(2):
                        get_middle(chunk, 2 * here.home + k).wait_send()

            get_across(chunk).wait_send()

    def matrix(number, start, width):
        ref = weight[number]
        return ref[:, :, :, :, pl.ds(start, width)].reshape(features, width)

    def in_rows(body, start=0, count=tokens):
        block = 64

        def step(i, carry):
            body(pl.ds(pl.multiple_of(start + i * block, block), block))
            return carry

        lax.fori_loop(0, count // block, step, 0, unroll=ROWS_UNROLL)

    def sequence(m):
        return pl.ds(pl.multiple_of(m * slots, slots), slots)

    def normed(rows, rows_in, normal, scale, gain, target):
        centered = rows_in - jnp.mean(rows_in, axis=1, keepdims=True)
        inv = lax.rsqrt(jnp.mean(centered * centered, axis=1, keepdims=True) + epsilon)
        n = centered * inv
        normal[rows] = n
        scale[rows] = jnp.broadcast_to(inv, (n.shape[0], 128))
        target[rows] = (n * gain).astype(low)

    row_at = lax.broadcasted_iota(jnp.int32, (slots, 256), 0)
    first_row = row_at == 0

    def later(rows, places):
        return jnp.where(row_at >= places, pltpu.roll(rows, places, 0), 0.0)

    def sooner(rows, places):
        return jnp.where(row_at < slots - places, pltpu.roll(rows, slots - places, 0), 0.0)

    cuts = features // 256

    def mixer_blocks(m, body):
        def step(cut, carry):
            body(m, sequence(m), pl.ds(pl.multiple_of(cut * 256, 256), 256), cut)
            return carry

        lax.fori_loop(0, cuts, step, 0, unroll=MIX_UNROLL)

    def live_rows(m):
        return (row_at.astype(f32) < jnp.concatenate([live[m, 0:1, :]] * 2, axis=1)).astype(f32)

    def to_sibling(number, source, target):
        return remote(source, target, send.at[number], recv.at[number], here.sibling())

    def left_copy(k):
        return to_sibling(k, lefts[k].at[0], lefts[k].at[1])

    def right_sides(k):
        return (
            (projected, other_projected),
            (after_low, other_after),
            (expanded, other_expanded),
            (active, other_active),
        )[k]

    def right_copy(k):
        source, target = right_sides(k)
        half = widths[1 + k] // 2
        cut = pl.ds(pl.multiple_of((1 - here.core) * half, 128), half)
        return to_sibling(4 + k, source.at[:, cut], target)

    def small_copy():
        return to_sibling(8, small_terms.at[1 - here.core], other_small)

    def give(source, m):
        rows = pl.ds(m * slots, slots)
        return remote(source.at[rows], arrive.at[rows], give_send.at[m], give_recv.at[m], partner)

    def received(target, m):
        rows = sequence(m)
        arrived(arrive.at[rows], give_recv.at[m])
        target[rows] = arrive[rows]

    def turned(k):
        lefts[k][0] = (entered, gated, again, e_in)[k][...].T
        left_copy(k).start()

    def small_weights():
        filt[...] = matrix(0, 0, 128).astype(f32).T
        rows8[...] = matrix(0, 128, 128).astype(f32).T[:8]

    def enter(m):
        def body(rows):
            normed(rows, x_in[rows].astype(f32), norm_one, scale_one, rows8[3:4], entered)

        in_rows(body, m * slots, slots)

    def mix(m, rows, taken, cut):
        taps = [rows8[j : j + 1, taken] for j in range(3)]
        alive = live_rows(m)
        k = keys[rows, taken] * alive
        keys[rows, taken] = k
        v = values[rows, taken] * alive
        kernel = filt[:, taken] + taps[0] * k + taps[1] * later(k, 1) + taps[2] * later(k, 2)
        spec = left_dot(dft[...], parts(jnp.concatenate([v, kernel], axis=1)))
        value_spec[m, :, taken] = spec[:, :256]
        kernel_spec[m, :, taken] = spec[:, 256:]
        v_re, v_im = spec[:slots, :256], spec[slots:, :256]
        k_re, k_im = spec[:slots, 256:], spec[slots:, 256:]
        both = k_im * v_im
        re = k_re * v_re - jnp.where(first_row, 0.0, both)
        im = jnp.where(first_row, both, k_re * v_im + k_im * v_re)
        out = left_dot(idft[...], parts(jnp.concatenate([re, im], axis=0)))
        convolved[rows, taken] = out
        gated[rows, taken] = (queries[rows, taken] * out).astype(low)

    def mixer(m):
        rows = sequence(m)
        for k, target in enumerate((queries, keys, values)):
            target[rows] = left_dot(entered[rows], matrix(1, k * features, features))
        mixer_blocks(m, mix)

    def mixer_out(m):
        rows = sequence(m)
        total[rows] = x_in[rows].astype(f32) + left_dot(gated[rows], matrix(2, 0, features))

        def body(rows):
            normed(rows, total[rows], norm_two, scale_two, rows8[4:5], again)

        in_rows(body, m * slots, slots)

    def each_sequence(*bodies):
        def step(m, carry):
            for body in bodies:
                body(m)
            return carry

        lax.fori_loop(0, micro, step, 0)

    tile = 512

    def tiles(start, width, body):
        def step(i, carry):
            body(pl.multiple_of(start + i * tile, 128))
            return carry

        lax.fori_loop(0, width // tile, step, 0, unroll=TILE_UNROLL)

    def expand(start):
        gate = left_dot(again[...], matrix(3, start, tile))
        up = left_dot(again[...], matrix(3, pl.multiple_of(hidden + start, 128), tile))
        expanded[:, pl.ds(start, tile)] = gate.astype(low)
        expanded[:, pl.ds(pl.multiple_of(hidden + start, 128), tile)] = up.astype(low)
        active[:, pl.ds(start, tile)] = (gate * sigmoid(gate) * up).astype(low)

    def reduce_on(start, width):
        total[...] += dot_back(active[:, pl.ds(start, width)], matrix(4, start, width))

    def layer_done():
        right_copy(3).start()
        out_low[...] = total[...].astype(low)

    ends = {array: max(k for k, entry in enumerate(get_table) if entry[0] == array) for array in range(5)}

    def as_it_comes(chunk):
        array, start, width, _ = get_table[chunk]

        @pl.when(here.first_layer)
        def _():
            if array == 0:
                x_in[...] = feed[...]
                small_weights()
                each_sequence(enter)
                turned(0)
            if array == 1 and ends[1] == chunk:
                each_sequence(mixer)
                turned(1)
            if array == 2 and ends[2] == chunk:
                each_sequence(mixer_out)
                turned(2)
            if array == 3:
                tiles(start, width, expand)
            if array == 4:
                for half in (0, 1):
                    reduce_on(half * (hidden // 2) + start, width)

    def on_chunk(chunk):
        if chunk == ends[0]:
            fed()
        as_it_comes(chunk)

    gather(on_chunk)

    @pl.when(here.first_layer)
    def _():
        layer_done()
        for m in range(micro):
            give(out_low, m).start()
            give(out_low, m).wait_send()
        gathered()
        for m in range(micro):
            received(e_in, m)
        turned(3)

    @pl.when(here.second_layer)
    def _():
        small_weights()
        e_in[...] = feed[...]
        gathered()
        each_sequence(functools.partial(received, x_in), enter, mixer, mixer_out)

        def both(start):
            expand(start)
            reduce_on(start, tile)

        tiles(0, hidden, both)
        layer_done()

    total[...] = jnp.zeros_like(total)

    def expand_back(start):
        again = pl.multiple_of(hidden + start, 128)
        grad_act = left_dot(e_in[...], matrix(4, start, tile))
        gate = expanded[:, pl.ds(start, tile)].astype(f32)
        up = expanded[:, pl.ds(again, tile)].astype(f32)
        sig = sigmoid(gate)
        grad_gate = (grad_act * up * (sig * (1.0 + gate * (1.0 - sig)))).astype(low)
        grad_up = (grad_act * (gate * sig)).astype(low)
        expanded[:, pl.ds(start, tile)] = grad_gate
        expanded[:, pl.ds(again, tile)] = grad_up
        total[...] += dot_back(grad_gate, matrix(3, start, tile)) + dot_back(grad_up, matrix(3, again, tile))

    tiles(0, hidden, expand_back)
    right_copy(2).start()
    for side in (here.x_side(), here.y_side()):
        pl.semaphore_signal(ready, inc=1, device_id=side, device_id_type=MESH)

    @pl.when(here.first_layer)
    def _():
        pl.semaphore_signal(ready, inc=1, device_id=here.middle(), device_id_type=MESH)

    def norm_grad(rows, grad, normal, scale, gain, at):
        n = normal[rows]
        small_terms[1, at : at + 1] += jnp.sum(grad * n, axis=0, keepdims=True)
        q = grad * gain
        back = q - jnp.mean(q, axis=1, keepdims=True) - n * jnp.mean(q * n, axis=1, keepdims=True)
        return scale[rows][:, :1] * back

    def after_back():
        small_terms[...] = jnp.zeros_like(small_terms)

        def body(rows):
            grad = e_in[rows].astype(f32) + norm_grad(rows, total[rows], norm_two, scale_two, rows8[4:5], 4)
            after[rows] = grad
            after_low[rows] = grad.astype(low)

        in_rows(body)
        right_copy(1).start()

    def gated_back():
        total[...] = dot_back(after_low[...], matrix(2, 0, features))

    def mix_back(m, rows, taken, cut):
        taps = [rows8[j : j + 1, taken] for j in range(3)]
        alive = live_rows(m)
        grad = total[rows, taken]
        projected[rows, taken] = (grad * convolved[rows, taken]).astype(low)
        spec = left_dot(dft[...], parts(grad * queries[rows, taken]))
        g_re, g_im = spec[:slots], spec[slots:]
        pairs = []
        for other in (kernel_spec, value_spec):
            o_re, o_im = other[m, :slots, taken], other[m, slots:, taken]
            both = o_im * g_im
            re = o_re * g_re + jnp.where(first_row, 0.0, both)
            im = jnp.where(first_row, both, o_re * g_im - o_im * g_re)
            pairs.append(jnp.concatenate([re, im], axis=0))
        paired = left_dot(idft[...], parts(jnp.concatenate(pairs, axis=1)))
        at_values = pl.ds(pl.multiple_of(2 * features + cut * 256, 256), 256)
        projected[rows, at_values] = (paired[:, :256] * alive).astype(low)
        grad_kernel = paired[:, 256:]
        small_terms[0, :, taken] += grad_kernel
        k = keys[rows, taken]
        for j in range(3):
            moved = later(k, j) if j else k
            small_terms[1, j : j + 1, taken] += jnp.sum(grad_kernel * moved, axis=0, keepdims=True)
        grad_keys = taps[0] * grad_kernel + taps[1] * sooner(grad_kernel, 1) + taps[2] * sooner(grad_kernel, 2)
        at_keys = pl.ds(pl.multiple_of(features + cut * 256, 256), 256)
        projected[rows, at_keys] = (grad_keys * alive).astype(low)

    def mixed_back(m):
        mixer_blocks(m, mix_back)

    def input_back(m):
        rows = sequence(m)
        total[rows] = dot_back(projected[rows], matrix(1, 0, 3 * features))

        def body(rows):
            grad = after[rows] + norm_grad(rows, total[rows], norm_one, scale_one, rows8[3:4], 3)
            grad_low[rows] = grad.astype(low)

        in_rows(body, m * slots, slots)

    pieces = [after_back, gated_back]
    for m in range(micro):
        pieces += [functools.partial(mixed_back, m), functools.partial(input_back, m)]

    def last_copies():
        right_copy(0).start()
        small_copy().start()

    pieces += [last_copies]

    @pl.when(here.second_layer)
    def _():
        after_back()
        gated_back()
        for m in range(micro):
            mixed_back(m)
            input_back(m)
            if m:
                give(grad_low, m - 1).wait_send()
            give(grad_low, m).start()
        last_copies()
        for k in (3, 2, 1, 0):
            turned(k)

    offsets, place = [], 0
    for array, _, width, _ in put_table:
        offsets.append(place)
        place += width if array else 0

    def room(chunk):
        return pl.ds(offsets[chunk], put_table[chunk][2])

    def one_in(chunk, z):
        if put_table[chunk][0] == 0:
            return one_small.at[z]
        return weight[3].at[z, 0, :, :, room(chunk)]

    def two_in(chunk, z):
        if put_table[chunk][0] == 0:
            return two_small.at[z]
        return weight[3].at[z, 1, 0, :, room(chunk)]

    def mid_in(chunk, z, k):
        return weight[3].at[z, 1, 1, k, :, room(chunk)]

    def put_first(chunk, step):
        z = far(step)
        if step % 2:
            source, side = mine[chunk].at[z, :, 1 - here.x], here.x_side()
        else:
            source, side = mine[chunk].at[z, 1 - here.y], here.y_side()
        return remote(source, one_in(chunk, step), one_send.at[chunk, step], one_recv.at[chunk, step], side)

    def put_second(chunk, step):
        z = far(step)
        if step % 2:
            source, side = mine[chunk].at[z, 1 - here.y, here.x], here.y_side()
        else:
            source, side = mine[chunk].at[z, here.y, 1 - here.x], here.x_side()
        return remote(source, two_in(chunk, step), two_send.at[chunk, step], two_recv.at[chunk, step], side)

    def put_third(chunk, step, act):
        z = far(step)
        source = mine[chunk].at[z, here.y, here.x]
        target = landed[put_table[chunk][0]].at[here.home, :, columns(put_table, chunk, here.core)]
        receive = z_recv.at[chunk, here.home, here.core]
        own = (here.z == z) & (here.core == here.layer)
        if act == "start":

            @pl.when(own)
            def _():
                pltpu.make_async_copy(source, target, receive).start()

        @pl.when(jnp.logical_not(own))
        def _():
            away = remote(source, target, z_send.at[chunk, step], receive, (here.layer, here.chip(z=z)))
            getattr(away, act)()

    def add(target, other):
        target[...] = (target[...].astype(f32) + other[...].astype(f32)).astype(target.dtype)

    waits = [False] * 5

    def terms(chunk):
        array, start, width, shared = put_table[chunk]
        if array == 0:
            small_copy().wait_recv()
            block = (small_terms[here.core] + other_small[...]).T
        else:
            if not waits[array]:
                waits[array] = True
                left_copy(array - 1).wait_recv()
                right_copy(array - 1).wait_recv()
            source, other = right_sides(array - 1)
            own_at = pl.multiple_of(here.core * (widths[array] // 2) + start, 128)
            block = left_dot(lefts[array - 1][0], source[:, pl.ds(own_at, width)])
            block += left_dot(lefts[array - 1][1], other[:, pl.ds(start, width)])
        block = block.astype(low)
        rows = features // 16
        for z in range(4):
            for k in range(4):
                at = (z * 4 + k) * rows
                mine[chunk][z, k // 2, k % 2] = block[at : at + rows]
        for step in range(4):
            put_first(chunk, step).start()

    def sum_one(chunk):
        for step in range(4):
            z = far(step)
            put_first(chunk, step).wait_recv()
            for k in range(2):
                if step % 2:
                    add(mine[chunk].at[z, k, here.x], one_in(chunk, step).at[k])
                else:
                    add(mine[chunk].at[z, here.y, k], one_in(chunk, step).at[k])
            put_second(chunk, step).start()

    def sum_two(chunk):
        for step in range(4):
            put_second(chunk, step).wait_recv()
            add(mine[chunk].at[far(step), here.y, here.x], two_in(chunk, step))
            put_third(chunk, step, "start")

    pl.when(here.first_layer)(lambda: pl.semaphore_wait(ready, 3))
    pl.when(here.second_layer)(lambda: pl.semaphore_wait(ready, 2))

    apart = here.core != here.layer
    over = (1 - here.core, here.partner)

    def swap(source, target, number, act):
        sems = swap_sems.at[number], swap_sems.at[number + 1]

        @pl.when(apart)
        def _():
            getattr(remote(source, target, *sems, over), act)()

        @pl.when(jnp.logical_not(apart))
        def _():
            getattr(pltpu.make_async_copy(source, target, sems[1]), act)()

    last = len(put_table)
    needs = {array: min(k for k, entry in enumerate(put_table) if entry[0] == array) for array in range(5)}
    due = [max(0, needs[1] - len(pieces) + k) for k in range(len(pieces))]
    terms(0)
    swap(out_low, kept_out, 0, "start")
    for now in range(last + 1):
        for piece, at in zip(pieces, due):
            if at == now:
                pl.when(here.first_layer)(piece)
        if now + 1 < last:
            terms(now + 1)
        if now < last:
            sum_one(now)
        if 1 <= now:
            sum_two(now - 1)
        if now == needs[0]:
            swap(grad_low, kept_grad, 2, "start")

    for chunk in range(last):
        for half in (0, 1):
            for slot in (0, 1):
                target = landed[put_table[chunk][0]].at[slot, :, columns(put_table, chunk, half)]
                arrived(target, z_recv.at[chunk, slot, half])
        for step in range(4):
            put_first(chunk, step).wait_send()
            put_second(chunk, step).wait_send()
            put_third(chunk, step, "wait_send")

    @pl.when(own_feed)
    def _():
        remote(hidden_in, feed, feed_sems.at[1], feed_sems.at[0], partner).wait_send()
        remote(live_own, live, feed_sems.at[3], feed_sems.at[2], partner).wait_send()

    for k in range(4):
        left_copy(k).wait_send()
        right_copy(k).wait_send()
    small_copy().wait_send()
    pl.when(here.second_layer)(lambda: give(grad_low, micro - 1).wait_send())
    swap(out_low, kept_out, 0, "wait")
    swap(grad_low, kept_grad, 2, "wait")


def finish_kernel(*refs):
    landed, (out, grad) = refs[:5], refs[5:7]
    s_filters, s_taps, s_one, s_two = refs[7:11]
    sums, (to_out, to_grad) = refs[11:15], refs[15:17]
    to_out[...] = out[...]
    to_grad[...] = grad[...]
    small = landed[0][0].astype(jnp.float32) + landed[0][1].astype(jnp.float32)
    s_filters[...] = small[:, :128]
    own = small.shape[0]
    rows = jnp.pad(small[:, 128:], ((0, 128 - own), (0, 0))).T
    for j in range(3):
        s_taps[j] = rows[j : j + 1, :own]
    s_one[...] = rows[3:4, :own]
    s_two[...] = rows[4:5, :own]
    for number, result in enumerate(sums):
        result[...] = landed[1 + number][0].astype(jnp.float32) + landed[1 + number][1].astype(jnp.float32)


def fast_device(
    hidden_in, out_grad, lengths, gain_mixer, w_input, w_taps, filters, w_output, gain_mlp, w_gate_up, w_down
):
    micro, _, slots, features = hidden_in.shape
    tokens, rows = micro * slots, gain_mixer.shape[1]
    shards = (w_input[0], w_output[0], w_gate_up[0], w_down[0].T)
    widths = [256] + [shard.shape[1] for shard in shards]
    hidden = widths[4]
    get_table, put_table = chunks_of(GET_PIECES), chunks_of(PUT_PIECES)
    dft, idft = (jnp.asarray(table) for table in packed_tables(slots))
    low, f32 = jnp.bfloat16, jnp.float32
    anywhere = pl.BlockSpec(memory_space=pl.ANY)
    inside = pl.BlockSpec(memory_space=pltpu.VMEM)
    dma, vmem = pltpu.SemaphoreType.DMA, pltpu.VMEM
    act, act_low = (tokens, features), vmem((tokens, features), low)
    kinds = [jax.ShapeDtypeStruct((2, rows, width), low) for width in widths]
    kinds += [jax.ShapeDtypeStruct((tokens, features), low)] * 2
    room = [vmem((rows, 256), low), vmem((128, 128), f32)] + [vmem((micro, 8, 128), f32)] * 2
    room += [vmem((4, 2, 2, rows, width), low) for width in widths]
    room += [act_low] * 6
    room += [vmem((slots, features), f32), vmem((8, features), f32), vmem(act, f32), vmem(act, f32)]
    room += [vmem((tokens, 128), f32)] * 2
    room += [act_low] * 3 + [vmem(act, f32)] * 4 + [vmem((micro, 2 * slots, features), f32)] * 2
    room += [vmem(act, f32)] * 2 + [vmem((tokens, 2 * hidden), low), vmem((tokens, hidden), low)]
    room += [vmem((tokens, 3 * features), low), act_low, vmem((2, slots, features), f32)]
    room += [vmem((2, features, tokens), low)] * 4
    room += [vmem((slots, features), f32)] + [vmem((tokens, width // 2), low) for width in widths[1:]]
    room += [vmem((4, 2, 2, rows, entry[2]), low) for entry in put_table]
    room += [vmem((4, 2, rows, 128), low), vmem((4, rows, 128), low)]
    got, put = len(get_table), len(put_table)
    room += [dma((got, 2, 2))] + [dma((got, 4))] * 5 + [dma((got, 2))] * 2 + [dma((got,))] * 2 + [dma((4,))]
    room += [dma((4,)), dma((micro,)), dma((micro,)), dma((9,)), dma((9,))]
    room += [dma((put, 4))] * 5 + [dma((put, 2, 2))] + [dma((put,))] * 2 + [pltpu.SemaphoreType.REGULAR]
    results = pl.pallas_call(
        functools.partial(layer_kernel, get_table, put_table, widths),
        out_shape=kinds,
        in_specs=[inside] * 4 + [pl.BlockSpec(memory_space=pltpu.SMEM)] + [inside] * 2 + [anywhere] * 6,
        out_specs=[anywhere] * 7,
        scratch_shapes=room,
        compiler_params=pltpu.CompilerParams(
            collective_id=0, has_side_effects=True, vmem_limit_bytes=62 * 1024 * 1024
        ),
    )(
        filters[0].T,
        w_taps[0],
        gain_mixer,
        gain_mlp,
        lengths.T,
        dft,
        idft,
        *shards,
        hidden_in.reshape(tokens, features),
        out_grad.reshape(tokens, features),
    )
    kinds = [(rows, 128), (3, 1, rows), (1, rows), (1, rows)] + [(rows, width) for width in widths[1:]]
    kinds = [jax.ShapeDtypeStruct(kind, f32) for kind in kinds] + kinds_of(results[5:])
    s_filters, s_taps, s_one, s_two, s_in, s_out, s_gu, s_dt, layer_out, input_grad = pl.pallas_call(
        finish_kernel,
        out_shape=kinds,
        in_specs=[inside] * 7,
        out_specs=[inside] * 10,
        compiler_params=pltpu.CompilerParams(vmem_limit_bytes=62 * 1024 * 1024),
    )(*results)
    shape = (1, micro, 1, slots, features)
    return (
        layer_out.reshape(shape),
        input_grad.reshape(shape),
        s_one,
        s_in[None],
        s_taps.transpose(1, 0, 2),
        s_filters.T[None],
        s_out[None],
        s_two,
        s_gu[None],
        s_dt.T[None],
    )


def kinds_of(arrays):
    return [jax.ShapeDtypeStruct(array.shape, array.dtype) for array in arrays]


def solution(mesh):
    placed = (
        P(None, "dp", None, None),
        P(None, "dp", None, None),
        P(None, "dp"),
        P("section", "dp"),
        P("section", "dp", None),
        P("section", None, "dp"),
        P("section", None, "dp"),
        P("section", "dp", None),
        P("section", "dp"),
        P("section", "dp", None),
        P("section", None, "dp"),
    )
    return jax.shard_map(
        fast_device if mesh.shape["dp"] == 16 and mesh.shape["section"] == 2 else on_device,
        mesh=mesh,
        in_specs=placed,
        out_specs=(
            P("section", None, "dp", None, None),
            P("section", None, "dp", None, None),
            P("section", "dp"),
            P("section", "dp", None),
            P("section", None, "dp"),
            P("section", None, "dp"),
            P("section", "dp", None),
            P("section", "dp"),
            P("section", "dp", None),
            P("section", None, "dp"),
        ),
        check_vma=False,
    )
```

```python
import functools
import math

import jax
import jax.numpy as jnp
import ml_dtypes
import numpy as np
from jax import lax
from jax.experimental import pallas as pl
from jax.experimental.pallas import tpu as pltpu
from jax.sharding import PartitionSpec as P

MESH = pl.DeviceIdType.MESH

epsilon = 1e-05
GET_PIECES = (
    (0, 128, False),
    (1, 384, False),
    (1, 384, False),
    (1, 384, False),
    (2, 384, False),
    (3, 1024, False),
    (3, 1024, False),
    (3, 1024, False),
    (4, 512, False),
    (4, 512, False),
    (4, 512, False),
)
PUT_PIECES = (
    (4, 768, False),
    (4, 768, False),
    (3, 1024, False),
    (3, 1024, False),
    (1, 384, False),
    (1, 384, False),
    (0, 128, False),
    (1, 384, False),
    (2, 384, False),
    (3, 512, True),
    (3, 512, True),
)
GET_LAGS = (5, 7, 1, 2, 3)
ROWS_UNROLL = 2
MIX_UNROLL = 3
TILE_UNROLL = 2


def passed_along(value, axis, steps):
    count = lax.axis_size(axis)
    first, last = (max(0, -steps), min(count, count - steps))
    return lax.ppermute(value, axis, [(source, source + steps) for source in range(first, last)])


def split_dot(left_side, right_side):
    return jnp.dot(
        left_side, right_side, precision=lax.Precision.HIGH, preferred_element_type=jnp.float32
    )


def split_rows(left_side, right_side):
    return lax.dot_general(
        left_side,
        right_side,
        (((0,), (0,)), ((), ())),
        precision=lax.Precision.HIGH,
        preferred_element_type=jnp.float32,
    )


def dot_rows(left_side, right_side):
    return lax.dot_general(
        left_side, right_side, (((0,), (0,)), ((), ())), preferred_element_type=jnp.float32
    )


def dot_back(left_side, right_side):
    return lax.dot_general(
        left_side, right_side, (((1,), (1,)), ((), ())), preferred_element_type=jnp.float32
    )


def tables(length):
    period = 2 * length
    freq_index = lax.broadcasted_iota(jnp.int32, (length + 1, length), 0)
    time_index = lax.broadcasted_iota(jnp.int32, (length + 1, length), 1)
    angles = (freq_index * time_index % period).astype(jnp.float32) * (2.0 * math.pi / period)
    edge_rows = (freq_index[:, :1] == 0) | (freq_index[:, :1] == length)
    inverse_weight = jnp.where(edge_rows, 1.0, 2.0) / period
    dft_stack = jnp.concatenate([jnp.cos(angles), -jnp.sin(angles)], axis=0)
    return (dft_stack, inverse_weight)


def spectrum(dft_tables, signal):
    dft_stack, inverse_weight = dft_tables
    stacked_out = split_dot(dft_stack, signal)
    middle_row = stacked_out.shape[0] // 2
    return (stacked_out[:middle_row], stacked_out[middle_row:])


def inverse(dft_tables, real_part, imag_part):
    dft_stack, inverse_weight = dft_tables
    return split_rows(
        dft_stack, jnp.concatenate([inverse_weight * real_part, inverse_weight * imag_part], axis=0)
    )


def normalize(input_rows):
    centered = input_rows - jnp.mean(input_rows, axis=1, keepdims=True)
    inv_scale = lax.rsqrt(jnp.mean(centered * centered, axis=1, keepdims=True) + epsilon)
    return (centered * inv_scale, inv_scale)


def norm_back(grad_normed, normed, inv_scale):
    return inv_scale * (
        grad_normed
        - jnp.mean(grad_normed, axis=1, keepdims=True)
        - normed * jnp.mean(grad_normed * normed, axis=1, keepdims=True)
    )


def delayed(input_rows, places):
    return jnp.pad(input_rows, ((places, 0), (0, 0)))[: input_rows.shape[0]]


def advanced(input_rows, places):
    return jnp.pad(input_rows, ((0, places), (0, 0)))[places:]


def layer_forward(input_rows, active_rows, weights, dft_tables):
    gain_one, w_inner, w_tap_rows, filt_static, w_outer, gain_two, w_expand, w_reduce = weights
    hidden_size_model = w_outer.shape[0]
    hidden_width = w_reduce.shape[0]
    tap_weights = w_tap_rows.astype(jnp.float32)
    normed_one, scale_one = normalize(input_rows)
    entered = (normed_one * gain_one.astype(jnp.float32)).astype(jnp.bfloat16)
    projected = jnp.dot(entered, w_inner, preferred_element_type=jnp.float32)
    queries = projected[:, :hidden_size_model]
    keys_part = projected[:, hidden_size_model : 2 * hidden_size_model] * active_rows
    values_part = projected[:, 2 * hidden_size_model :] * active_rows
    dynamic = (
        tap_weights[0] * keys_part
        + tap_weights[1] * delayed(keys_part, 1)
        + tap_weights[2] * delayed(keys_part, 2)
    )
    kernel = filt_static.astype(jnp.float32) + dynamic
    joint_re, joint_im = spectrum(dft_tables, jnp.concatenate([values_part, kernel], axis=1))
    value_re = joint_re[:, :hidden_size_model]
    kernel_re = joint_re[:, hidden_size_model:]
    value_im = joint_im[:, :hidden_size_model]
    kernel_im = joint_im[:, hidden_size_model:]
    convolved = inverse(
        dft_tables,
        kernel_re * value_re - kernel_im * value_im,
        kernel_re * value_im + kernel_im * value_re,
    )
    gated_rows = (queries * convolved).astype(jnp.bfloat16)
    after_mixer = input_rows + jnp.dot(gated_rows, w_outer, preferred_element_type=jnp.float32)
    normed_two, scale_two = normalize(after_mixer)
    entered_two = (normed_two * gain_two.astype(jnp.float32)).astype(jnp.bfloat16)
    expanded = jnp.dot(entered_two, w_expand, preferred_element_type=jnp.float32)
    gate_part = expanded[:, :hidden_width]
    up_part = expanded[:, hidden_width:]
    activated = (jax.nn.silu(gate_part) * up_part).astype(jnp.bfloat16)
    result = after_mixer + jnp.dot(activated, w_reduce, preferred_element_type=jnp.float32)
    stash = (
        normed_one,
        scale_one,
        entered,
        queries,
        keys_part,
        (value_re, value_im, kernel_re, kernel_im),
        convolved,
        gated_rows,
        normed_two,
        scale_two,
        entered_two,
        gate_part,
        up_part,
        activated,
    )
    return (result, stash)


def mlp_backward(received_gradient, weights, stash):
    gain_one, w_inner, w_tap_rows, filt_static, w_outer, gain_two, w_expand, w_reduce = weights
    (
        normed_one,
        scale_one,
        entered,
        queries,
        keys_part,
        spectra,
        convolved,
        gated_rows,
        normed_two,
        scale_two,
        entered_two,
        gate_part,
        up_part,
        activated,
    ) = stash
    grad_low = received_gradient.astype(jnp.bfloat16)
    grad_reduce_w = dot_rows(activated, grad_low)
    grad_act = dot_back(grad_low, w_reduce)
    sigmoid_gate = jax.nn.sigmoid(gate_part)
    grad_gate = grad_act * up_part * (sigmoid_gate * (1.0 + gate_part * (1.0 - sigmoid_gate)))
    grad_up = grad_act * (gate_part * sigmoid_gate)
    grad_expand = jnp.concatenate([grad_gate, grad_up], axis=1).astype(jnp.bfloat16)
    grad_expand_w = dot_rows(entered_two, grad_expand)
    grad_entered_two = dot_back(grad_expand, w_expand)
    grad_gain_two = jnp.sum(grad_entered_two * normed_two, axis=0)
    grad_after = received_gradient + norm_back(
        grad_entered_two * gain_two.astype(jnp.float32), normed_two, scale_two
    )
    return (grad_after, (grad_gain_two, grad_expand_w, grad_reduce_w))


def mixer_backward(grad_after, active_rows, weights, dft_tables, stash):
    gain_one, w_inner, w_tap_rows, filt_static, w_outer, gain_two, w_expand, w_reduce = weights
    (
        normed_one,
        scale_one,
        entered,
        queries,
        keys_part,
        spectra,
        convolved,
        gated_rows,
        normed_two,
        scale_two,
        entered_two,
        gate_part,
        up_part,
        activated,
    ) = stash
    value_re, value_im, kernel_re, kernel_im = spectra
    hidden_size_model = w_outer.shape[0]
    tap_weights = w_tap_rows.astype(jnp.float32)
    grad_mix_low = grad_after.astype(jnp.bfloat16)
    grad_outer_w = dot_rows(gated_rows, grad_mix_low)
    grad_gated = dot_back(grad_mix_low, w_outer)
    grad_queries = grad_gated * convolved
    grad_conv = grad_gated * queries
    grad_re, grad_im = spectrum(dft_tables, grad_conv)
    paired_re = jnp.concatenate(
        [kernel_re * grad_re + kernel_im * grad_im, value_re * grad_re + value_im * grad_im], axis=1
    )
    paired_im = jnp.concatenate(
        [kernel_re * grad_im - kernel_im * grad_re, value_re * grad_im - value_im * grad_re], axis=1
    )
    paired = inverse(dft_tables, paired_re, paired_im)
    grad_values = paired[:, :hidden_size_model] * active_rows
    grad_kernel = paired[:, hidden_size_model:]
    grad_taps = jnp.stack(
        [
            jnp.sum(grad_kernel * keys_part, axis=0),
            jnp.sum(grad_kernel * delayed(keys_part, 1), axis=0),
            jnp.sum(grad_kernel * delayed(keys_part, 2), axis=0),
        ]
    )
    grad_keys = (
        tap_weights[0] * grad_kernel
        + tap_weights[1] * advanced(grad_kernel, 1)
        + tap_weights[2] * advanced(grad_kernel, 2)
    ) * active_rows
    grad_projected = jnp.concatenate([grad_queries, grad_keys, grad_values], axis=1).astype(
        jnp.bfloat16
    )
    inner_weight_gradient = dot_rows(entered, grad_projected)
    grad_entered = dot_back(grad_projected, w_inner)
    grad_gain_one = jnp.sum(grad_entered * normed_one, axis=0)
    grad_inputs = grad_after + norm_back(
        grad_entered * gain_one.astype(jnp.float32), normed_one, scale_one
    )
    return (
        grad_inputs,
        (grad_gain_one, inner_weight_gradient, grad_taps, grad_kernel, grad_outer_w),
    )


def add_terms(received, flipped):
    return tuple(
        (
            jnp.sum(member, axis=0).T if flip else jnp.sum(member, axis=0)
            for member, flip in zip(received, flipped)
        )
    )


def on_device(
    hidden_in,
    out_grad,
    lengths,
    gain_mixer,
    w_input,
    w_taps,
    filters,
    w_output,
    gain_mlp,
    w_gate_up,
    w_down,
):
    first_section = lax.axis_index("section") == 0
    micro_count = hidden_in.shape[0]
    seq_slots = hidden_in.shape[2]
    hidden_size_model = hidden_in.shape[3]
    dft_tables = tables(seq_slots)
    positions = lax.broadcasted_iota(jnp.int32, (seq_slots, 1), 0)
    weights = (
        lax.all_gather(gain_mixer[0], "dp", axis=0, tiled=True),
        lax.all_gather(w_input[0], "dp", axis=0, tiled=True),
        lax.all_gather(w_taps[0], "dp", axis=1, tiled=True),
        lax.all_gather(filters[0], "dp", axis=1, tiled=True),
        lax.all_gather(w_output[0], "dp", axis=0, tiled=True),
        lax.all_gather(gain_mlp[0], "dp", axis=0, tiled=True),
        lax.all_gather(w_gate_up[0], "dp", axis=0, tiled=True),
        lax.all_gather(w_down[0], "dp", axis=1, tiled=True),
    )
    arriving = jnp.zeros((seq_slots, hidden_size_model), jnp.bfloat16)
    outgoing_list = []
    saved_activations = []
    for forward_step in range(micro_count + 1):
        own_index = min(forward_step, micro_count - 1)
        prior_index = max(forward_step - 1, 0)
        input_rows = jnp.where(first_section, hidden_in[own_index, 0], arriving).astype(jnp.float32)
        length_now = jnp.where(first_section, lengths[own_index, 0], lengths[prior_index, 0])
        active_rows = (positions < length_now).astype(jnp.float32)
        result, stash = layer_forward(input_rows, active_rows, weights, dft_tables)
        outgoing = result.astype(jnp.bfloat16)
        outgoing_list.append(outgoing)
        if forward_step < micro_count:
            arriving = passed_along(outgoing, "section", 1)
        saved_activations.append((input_rows, active_rows))
    coming = jnp.zeros((seq_slots, hidden_size_model), jnp.bfloat16)
    mlp_totals = None
    mixer_totals = None
    grads_out = []
    for backward_step in range(micro_count + 1):
        saved_slot_index = micro_count - backward_step
        last_index = max(micro_count - 1 - backward_step, 0)
        live_factor = 1.0 if backward_step < micro_count else 0.0
        received_gradient = jnp.where(
            first_section,
            coming.astype(jnp.float32),
            out_grad[last_index, 0].astype(jnp.float32) * live_factor,
        )
        input_rows, active_rows = saved_activations[saved_slot_index]
        result, stash = layer_forward(input_rows, active_rows, weights, dft_tables)
        grad_after, mlp_grads = mlp_backward(received_gradient, weights, stash)
        mlp_totals = (
            mlp_grads if mlp_totals is None else jax.tree.map(jnp.add, mlp_totals, mlp_grads)
        )
        grad_inputs, mixer_grads = mixer_backward(
            grad_after, active_rows, weights, dft_tables, stash
        )
        mixer_totals = (
            mixer_grads
            if mixer_totals is None
            else jax.tree.map(jnp.add, mixer_totals, mixer_grads)
        )
        outgoing = grad_inputs.astype(jnp.bfloat16)
        grads_out.append(outgoing)
        if backward_step < micro_count:
            coming = passed_along(outgoing, "section", -1)
    first_outputs = jnp.stack(outgoing_list[:micro_count])
    second_outputs = jnp.stack(outgoing_list[1:])
    layer_out = jnp.where(first_section, first_outputs, second_outputs)[None, :, None]
    first_grads = jnp.stack(
        [grads_out[micro_count - batch_index] for batch_index in range(micro_count)]
    )
    second_grads = jnp.stack(
        [grads_out[micro_count - 1 - batch_index] for batch_index in range(micro_count)]
    )
    input_grad = jnp.where(first_section, first_grads, second_grads)[None, :, None]
    all_parts = (
        lax.all_to_all(
            mixer_totals[0][None].astype(jnp.bfloat16),
            "dp",
            split_axis=1,
            concat_axis=0,
            tiled=True,
        ).astype(jnp.float32),
        lax.all_to_all(
            mixer_totals[1][None].astype(jnp.bfloat16),
            "dp",
            split_axis=1,
            concat_axis=0,
            tiled=True,
        ).astype(jnp.float32),
        lax.all_to_all(
            mixer_totals[2].T[None].astype(jnp.bfloat16),
            "dp",
            split_axis=1,
            concat_axis=0,
            tiled=True,
        ).astype(jnp.float32),
        lax.all_to_all(
            mixer_totals[3].T[None].astype(jnp.bfloat16),
            "dp",
            split_axis=1,
            concat_axis=0,
            tiled=True,
        ).astype(jnp.float32),
        lax.all_to_all(
            mixer_totals[4][None].astype(jnp.bfloat16),
            "dp",
            split_axis=1,
            concat_axis=0,
            tiled=True,
        ).astype(jnp.float32),
        lax.all_to_all(
            mlp_totals[0][None].astype(jnp.bfloat16), "dp", split_axis=1, concat_axis=0, tiled=True
        ).astype(jnp.float32),
        lax.all_to_all(
            mlp_totals[1][None].astype(jnp.bfloat16), "dp", split_axis=1, concat_axis=0, tiled=True
        ).astype(jnp.float32),
        lax.all_to_all(
            mlp_totals[2].T[None].astype(jnp.bfloat16),
            "dp",
            split_axis=1,
            concat_axis=0,
            tiled=True,
        ).astype(jnp.float32),
    )
    summed = add_terms(all_parts, (False, False, True, True, False, False, False, True))
    return (
        layer_out,
        input_grad,
        summed[0][None],
        summed[1][None],
        summed[2][None],
        summed[3][None],
        summed[4][None],
        summed[5][None],
        summed[6][None],
        summed[7][None],
    )


class Place:
    def __init__(self):
        self.core = lax.axis_index("section")
        self.index = lax.axis_index("dp")
        self.z = self.index // 4
        self.y = self.index // 2 % 2
        self.x = self.index % 2
        self.layer = 1 - (self.z + 1) // 2 % 2
        self.home = self.z // 2
        self.first_layer = self.layer == 0
        self.second_layer = self.layer == 1
        self.partner = self.chip(z=self.z + 1 - 2 * (self.z % 2))

    def chip(self, z=None, y=None, x=None):
        z, y, x = (a if a is not None else b for a, b in ((z, self.z), (y, self.y), (x, self.x)))
        return z * 4 + y * 2 + x

    def x_side(self):
        return (self.core, self.chip(x=1 - self.x))

    def y_side(self):
        return (self.core, self.chip(y=1 - self.y))

    def sibling(self):
        return (1 - self.core, self.index)

    def middle(self):
        return (self.core, self.chip(z=3 - self.z))

    def greet(self):
        barrier = pltpu.get_barrier_semaphore()
        others = [self.x_side(), self.y_side(), self.sibling()]
        for step in (1, 2, 3):
            chip = self.chip(z=(self.z + step) % 4)
            others += [(0, chip), (1, chip)]
        for other in others:
            pl.semaphore_signal(barrier, inc=1, device_id=other, device_id_type=MESH)
        pl.semaphore_wait(barrier, len(others))


def remote(source, target, send, receive, device):
    return pltpu.make_async_remote_copy(
        src_ref=source,
        dst_ref=target,
        send_sem=send,
        recv_sem=receive,
        device_id=device,
        device_id_type=MESH,
    )


def chunks_of(pieces):
    table, places = [], {}
    for array, width, shared in pieces:
        start = places.get(array, 0)
        table.append((array, start, width, shared))
        places[array] = start + width
    return table


def left_dot(left_side, right_side):
    return lax.dot_general(
        left_side, right_side, (((1,), (0,)), ((), ())), preferred_element_type=jnp.float32
    )


def sigmoid(value):
    return 0.5 * jnp.tanh(0.5 * value) + 0.5


def parts(signal):
    high = signal.astype(jnp.bfloat16)
    rest = (signal - high.astype(jnp.float32)).astype(jnp.bfloat16)
    return jnp.concatenate([high, high, rest], axis=0)


def halves_of(table):
    high = table.astype(ml_dtypes.bfloat16)
    rest = (table - high.astype(np.float64)).astype(ml_dtypes.bfloat16)
    return np.concatenate([high, rest, high], axis=1)


def packed_tables(length):
    period = 2 * length
    freq, time = np.arange(length)[:, None], np.arange(length)[None, :]
    angles = (freq * time % period) * (2.0 * math.pi / period)
    sines = np.where(freq == 0, 1.0 - 2.0 * (time % 2), -np.sin(angles))
    table = np.concatenate([np.cos(angles), sines], axis=0)
    weight = np.where(np.arange(period)[:, None] % length == 0, 1.0, 2.0) / period
    return halves_of(table), halves_of((table * weight).T)


def layer_kernel(get_table, put_table, widths, *refs):
    refs = list(refs)

    def take(number):
        taken = refs[:number]
        del refs[:number]
        return taken

    filters_in, taps_in, gain_one_in, gain_two_in, lengths_in, dft, idft = take(7)
    shards, (hidden_in, grad_in) = [None] + take(4), take(2)
    landed, (kept_out, kept_grad) = take(5), take(2)
    own_small, rows_in, live_own, live = take(4)
    weight = take(5)
    feed, arrive, x_in, e_in, out_low, grad_low = take(6)
    filt, rows8, norm_one, norm_two, scale_one, scale_two = take(6)
    entered, gated, again, queries, keys, values, convolved, value_spec, kernel_spec = take(9)
    total, after, expanded, active, projected, after_low, small_terms = take(7)
    lefts = take(4)
    other_small, other_projected, other_after, other_expanded, other_active = take(5)
    mine = take(len(put_table))
    one_small, two_small, one_down, two_down = take(4)
    get_z_send, get_z_recv, get_one_send, get_one_recv, get_two_send, get_two_recv = take(6)
    get_mid_send, get_mid_recv, get_side_send, get_side_recv, feed_sems = take(5)
    swap_sems, give_send, give_recv, send, recv = take(5)
    one_send, one_recv, two_send, two_recv, z_send, z_recv, mid_send, mid_recv, ready, ready_mid = take(10)

    here = Place()
    tokens, features = x_in.shape
    slots = filt.shape[0]
    micro = tokens // slots
    hidden = active.shape[1]
    f32, low = jnp.float32, jnp.bfloat16
    shards[0] = own_small

    here.greet()

    for m in range(micro):
        live_own[m] = jnp.full(live_own.shape[1:], lengths_in[0, m], jnp.int32).astype(f32)

    own_feed = here.core == here.layer
    partner = (here.core, here.partner)
    for layer, kept, given in ((0, hidden_in, grad_in), (1, grad_in, hidden_in)):

        @pl.when(own_feed & (here.layer == layer))
        def _():
            pltpu.make_async_copy(kept, feed, feed_sems.at[0]).start()
            pltpu.make_async_copy(live_own, live, feed_sems.at[2]).start()
            remote(given, feed, feed_sems.at[1], feed_sems.at[0], partner).start()
            remote(live_own, live, feed_sems.at[3], feed_sems.at[2], partner).start()

    def arrived(target, receive):
        pltpu.make_async_copy(target, target, receive).wait()

    def fed():
        arrived(feed, feed_sems.at[0])
        arrived(live, feed_sems.at[2])

    def small_shard():
        rows_in[...] = jnp.zeros_like(rows_in)
        own = taps_in.shape[1]
        rows_in[0:3, 0:own] = taps_in[...].astype(f32)
        rows_in[3:4, 0:own] = gain_one_in[...].astype(f32)
        rows_in[4:5, 0:own] = gain_two_in[...].astype(f32)
        own_small[:, :128] = filters_in[...]
        own_small[:, 128:] = rows_in[...].T[:own].astype(low)

    def columns(table, chunk, half):
        array, start, width, _ = table[chunk]
        return pl.ds(pl.multiple_of(half * (widths[array] // 2) + start, 128), width)

    def at_home(z):
        return z // 2 == here.home

    def when(condition, action):
        if condition is True:
            action()
        else:
            pl.when(condition)(action)

    def z_all(chunk, visit, near):
        array, _, _, shared = get_table[chunk]
        for number, plane in enumerate((1 - here.core, 2 + here.core)):
            wanted = (plane == here.z) if near else (plane != here.z)
            if shared:
                wanted = wanted & ((here.core == 1) | (here.home == number))
            for half in (0, 1):
                cut = columns(get_table, chunk, half)
                source, target = shards[array].at[:, cut], weight[array].at[here.z, here.y, here.x, :, cut]
                sems = get_z_send.at[chunk, number, half], get_z_recv.at[chunk, here.z]
                visit(wanted, here.core == half, source, target, sems, (half, here.chip(z=plane)))

    def z_start(chunk, near):
        def visit(wanted, own, source, target, sems, device):
            if not near:

                @pl.when(wanted)
                def _():
                    remote(source, target, *sems, device).start()

                return

            @pl.when(wanted & own)
            def _():
                pltpu.make_async_copy(source, target, sems[1]).start()

            @pl.when(wanted & jnp.logical_not(own))
            def _():
                remote(source, target, *sems, device).start()

        z_all(chunk, visit, near)

    def z_sent(chunk):
        for near in (False, True):

            def visit(wanted, own, source, target, sems, device):
                @pl.when(wanted & jnp.logical_not(own) if near else wanted)
                def _():
                    remote(source, target, *sems, device).wait_send()

            z_all(chunk, visit, near)

    def far(step):
        return (here.z + step) % 4

    def handled(table, chunk, z):
        return here.second_layer | at_home(z) if table[chunk][3] else True

    def get_first(chunk, step):
        block = weight[get_table[chunk][0]].at[far(step), here.y, here.x, :, columns(get_table, chunk, here.core)]
        side = here.y_side() if (step + chunk) % 2 else here.x_side()
        return remote(block, block, get_one_send.at[chunk, step], get_one_recv.at[chunk, step], side)

    def get_second(chunk, step):
        ref, cut = weight[get_table[chunk][0]], columns(get_table, chunk, here.core)
        if (step + chunk) % 2:
            pair, side = ref.at[far(step), :, here.x, :, cut], here.x_side()
        else:
            pair, side = ref.at[far(step), here.y, :, :, cut], here.y_side()
        return remote(pair, pair, get_two_send.at[chunk, step], get_two_recv.at[chunk, step], side)

    def get_middle(chunk, z):
        block = weight[get_table[chunk][0]].at[z, :, :, :, columns(get_table, chunk, here.core)]
        return remote(block, block, get_mid_send.at[chunk, z % 2], get_mid_recv.at[chunk, z % 2], here.middle())

    def get_across(chunk):
        whole = weight[get_table[chunk][0]].at[:, :, :, :, columns(get_table, chunk, here.core)]
        return remote(whole, whole, get_side_send.at[chunk], get_side_recv.at[chunk], here.sibling())

    def one_step(chunk, step):
        def action():
            z = far(step)
            block = weight[get_table[chunk][0]].at[z, here.y, here.x, :, columns(get_table, chunk, here.core)]
            arrived(block, get_z_recv.at[chunk, z])
            get_first(chunk, step).start()

        when(handled(get_table, chunk, far(step)), action)

    def two_steps(chunk, step):
        def action():
            get_first(chunk, step).wait_recv()
            get_second(chunk, step).start()

        when(handled(get_table, chunk, far(step)), action)

    def three_steps(chunk, step):
        def action():
            get_second(chunk, step).wait_recv()
            if get_table[chunk][3]:

                @pl.when(here.first_layer)
                def _():
                    get_middle(chunk, far(step)).start()

        when(handled(get_table, chunk, far(step)), action)

    def pass_on(chunk):
        if get_table[chunk][3]:

            @pl.when(here.first_layer)
            def _():
                for k in range(2):
                    get_middle(chunk, 2 * (1 - here.home) + k).wait_recv()

        get_across(chunk).start()

    def gather(on_chunk):
        last = len(get_table)
        ahead, own_ahead, two_lag, three_lag, done_lag = GET_LAGS
        for chunk in range(1, last):
            z_start(chunk, True)
        small_shard()
        z_start(0, True)

        def z_first():
            for chunk in range(min(ahead, last)):
                z_start(chunk, False)

        pl.when(here.core == 0)(z_first)
        for chunk in range(min(own_ahead, last)):
            one_step(chunk, 0)
        for chunk in range(min(own_ahead, last) - 1):
            two_steps(chunk, 0)
        pl.when(here.core == 1)(z_first)
        for now in range(last + done_lag + 1):
            if now + own_ahead < last:
                one_step(now + own_ahead, 0)
            if 0 <= now + own_ahead - 1 < last:
                two_steps(now + own_ahead - 1, 0)
            if now < last:
                for step in (1, 3, 2):
                    one_step(now, step)
            if now + ahead < last:
                z_start(now + ahead, False)
            if 0 <= now - two_lag < last:
                for step in (1, 3, 2):
                    two_steps(now - two_lag, step)
            if 0 <= now - three_lag < last:
                for step in range(4):
                    three_steps(now - three_lag, step)
                if not get_table[now - three_lag][3]:
                    pass_on(now - three_lag)
            if 0 <= now - three_lag - 1 < last and get_table[now - three_lag - 1][3]:
                pass_on(now - three_lag - 1)
            for chunk in (now - done_lag, now - done_lag - 1):
                if 0 <= chunk < last and get_table[chunk][3] == (chunk == now - done_lag - 1):
                    get_across(chunk).wait_recv()
                    on_chunk(chunk)

    def gathered():
        for chunk in range(len(get_table)):
            z_sent(chunk)
            for step in range(4):

                def action():
                    get_first(chunk, step).wait_send()
                    get_second(chunk, step).wait_send()

                when(handled(get_table, chunk, far(step)), action)
            if get_table[chunk][3]:

                @pl.when(here.first_layer)
                def _():
                    for k in range(2):
                        get_middle(chunk, 2 * here.home + k).wait_send()

            get_across(chunk).wait_send()

    def matrix(number, start, width):
        ref = weight[number]
        return ref[:, :, :, :, pl.ds(start, width)].reshape(features, width)

    def in_rows(body, start=0, count=tokens):
        block = 64

        def step(i, carry):
            body(pl.ds(pl.multiple_of(start + i * block, block), block))
            return carry

        lax.fori_loop(0, count // block, step, 0, unroll=ROWS_UNROLL)

    def sequence(m):
        return pl.ds(pl.multiple_of(m * slots, slots), slots)

    def normed(rows, rows_in, normal, scale, gain, target):
        centered = rows_in - jnp.mean(rows_in, axis=1, keepdims=True)
        inv = lax.rsqrt(jnp.mean(centered * centered, axis=1, keepdims=True) + epsilon)
        n = centered * inv
        normal[rows] = n
        scale[rows] = jnp.broadcast_to(inv, (n.shape[0], 128))
        target[rows] = (n * gain).astype(low)

    row_at = lax.broadcasted_iota(jnp.int32, (slots, 256), 0)
    first_row = row_at == 0

    def later(rows, places):
        return jnp.where(row_at >= places, pltpu.roll(rows, places, 0), 0.0)

    def sooner(rows, places):
        return jnp.where(row_at < slots - places, pltpu.roll(rows, slots - places, 0), 0.0)

    cuts = features // 256

    def mixer_blocks(m, body):
        def step(cut, carry):
            body(m, sequence(m), pl.ds(pl.multiple_of(cut * 256, 256), 256), cut)
            return carry

        lax.fori_loop(0, cuts, step, 0, unroll=MIX_UNROLL)

    def live_rows(m):
        return (row_at.astype(f32) < jnp.concatenate([live[m, 0:1, :]] * 2, axis=1)).astype(f32)

    def to_sibling(number, source, target):
        return remote(source, target, send.at[number], recv.at[number], here.sibling())

    def left_copy(k):
        return to_sibling(k, lefts[k].at[0], lefts[k].at[1])

    def right_sides(k):
        return (
            (projected, other_projected),
            (after_low, other_after),
            (expanded, other_expanded),
            (active, other_active),
        )[k]

    def right_copy(k):
        source, target = right_sides(k)
        half = widths[1 + k] // 2
        cut = pl.ds(pl.multiple_of((1 - here.core) * half, 128), half)
        return to_sibling(4 + k, source.at[:, cut], target)

    def small_copy():
        return to_sibling(8, small_terms.at[1 - here.core], other_small)

    def give(source, m):
        rows = pl.ds(m * slots, slots)
        return remote(source.at[rows], arrive.at[rows], give_send.at[m], give_recv.at[m], partner)

    def received(target, m):
        rows = sequence(m)
        arrived(arrive.at[rows], give_recv.at[m])
        target[rows] = arrive[rows]

    def turned(k):
        lefts[k][0] = (entered, gated, again, e_in)[k][...].T
        left_copy(k).start()

    def small_weights():
        filt[...] = matrix(0, 0, 128).astype(f32).T
        rows8[...] = matrix(0, 128, 128).astype(f32).T[:8]

    def enter(m):
        def body(rows):
            normed(rows, x_in[rows].astype(f32), norm_one, scale_one, rows8[3:4], entered)

        in_rows(body, m * slots, slots)

    def mix(m, rows, taken, cut):
        taps = [rows8[j : j + 1, taken] for j in range(3)]
        alive = live_rows(m)
        k = keys[rows, taken] * alive
        keys[rows, taken] = k
        v = values[rows, taken] * alive
        kernel = filt[:, taken] + taps[0] * k + taps[1] * later(k, 1) + taps[2] * later(k, 2)
        spec = left_dot(dft[...], parts(jnp.concatenate([v, kernel], axis=1)))
        value_spec[m, :, taken] = spec[:, :256]
        kernel_spec[m, :, taken] = spec[:, 256:]
        v_re, v_im = spec[:slots, :256], spec[slots:, :256]
        k_re, k_im = spec[:slots, 256:], spec[slots:, 256:]
        both = k_im * v_im
        re = k_re * v_re - jnp.where(first_row, 0.0, both)
        im = jnp.where(first_row, both, k_re * v_im + k_im * v_re)
        out = left_dot(idft[...], parts(jnp.concatenate([re, im], axis=0)))
        convolved[rows, taken] = out
        gated[rows, taken] = (queries[rows, taken] * out).astype(low)

    def mixer(m):
        rows = sequence(m)
        for k, target in enumerate((queries, keys, values)):
            target[rows] = left_dot(entered[rows], matrix(1, k * features, features))
        mixer_blocks(m, mix)

    def mixer_out(m):
        rows = sequence(m)
        total[rows] = x_in[rows].astype(f32) + left_dot(gated[rows], matrix(2, 0, features))

        def body(rows):
            normed(rows, total[rows], norm_two, scale_two, rows8[4:5], again)

        in_rows(body, m * slots, slots)

    def each_sequence(*bodies):
        def step(m, carry):
            for body in bodies:
                body(m)
            return carry

        lax.fori_loop(0, micro, step, 0)

    tile = 512

    def tiles(start, width, body):
        def step(i, carry):
            body(pl.multiple_of(start + i * tile, 128))
            return carry

        lax.fori_loop(0, width // tile, step, 0, unroll=TILE_UNROLL)

    def expand(start):
        gate = left_dot(again[...], matrix(3, start, tile))
        up = left_dot(again[...], matrix(3, pl.multiple_of(hidden + start, 128), tile))
        expanded[:, pl.ds(start, tile)] = gate.astype(low)
        expanded[:, pl.ds(pl.multiple_of(hidden + start, 128), tile)] = up.astype(low)
        active[:, pl.ds(start, tile)] = (gate * sigmoid(gate) * up).astype(low)

    def reduce_on(start, width):
        total[...] += dot_back(active[:, pl.ds(start, width)], matrix(4, start, width))

    def layer_done():
        right_copy(3).start()
        out_low[...] = total[...].astype(low)

    ends = {array: max(k for k, entry in enumerate(get_table) if entry[0] == array) for array in range(5)}

    def as_it_comes(chunk):
        array, start, width, _ = get_table[chunk]

        @pl.when(here.first_layer)
        def _():
            if array == 0:
                x_in[...] = feed[...]
                small_weights()
                each_sequence(enter)
                turned(0)
            if array == 1 and ends[1] == chunk:
                each_sequence(mixer)
                turned(1)
            if array == 2 and ends[2] == chunk:
                each_sequence(mixer_out)
                turned(2)
            if array == 3:
                tiles(start, width, expand)
            if array == 4:
                for half in (0, 1):
                    reduce_on(half * (hidden // 2) + start, width)

    def on_chunk(chunk):
        if chunk == ends[0]:
            fed()
        as_it_comes(chunk)

    gather(on_chunk)

    @pl.when(here.first_layer)
    def _():
        layer_done()
        for m in range(micro):
            give(out_low, m).start()
            give(out_low, m).wait_send()
        gathered()
        for m in range(micro):
            received(e_in, m)
        turned(3)

    @pl.when(here.second_layer)
    def _():
        small_weights()
        e_in[...] = feed[...]
        turned(3)
        gathered()
        each_sequence(functools.partial(received, x_in), enter, mixer, mixer_out)

        def both(start):
            expand(start)
            reduce_on(start, tile)

        tiles(0, hidden, both)
        layer_done()

    offsets, place = [], 0
    for array, _, width, _ in put_table:
        offsets.append(place)
        place += width if array in (1, 2, 3) else 0

    def one_in(chunk, z):
        array, start, width, _ = put_table[chunk]
        if array == 0:
            return one_small.at[z]
        if array == 4:
            return one_down.at[z, :, :, pl.ds(start, width)]
        return weight[3].at[z, 0, :, :, pl.ds(offsets[chunk], width)]

    def two_in(chunk, z):
        array, start, width, _ = put_table[chunk]
        if array == 0:
            return two_small.at[z]
        if array == 4:
            return two_down.at[z, :, pl.ds(start, width)]
        return weight[3].at[z, 1, 0, :, pl.ds(offsets[chunk], width)]

    def put_first(chunk, step):
        z = far(step)
        if step % 2:
            source, side = mine[chunk].at[z, :, 1 - here.x], here.x_side()
        else:
            source, side = mine[chunk].at[z, 1 - here.y], here.y_side()
        return remote(source, one_in(chunk, step), one_send.at[chunk, step], one_recv.at[chunk, step], side)

    def put_second(chunk, step):
        z = far(step)
        if step % 2:
            source, side = mine[chunk].at[z, 1 - here.y, here.x], here.y_side()
        else:
            source, side = mine[chunk].at[z, here.y, 1 - here.x], here.x_side()
        return remote(source, two_in(chunk, step), two_send.at[chunk, step], two_recv.at[chunk, step], side)

    def put_third(chunk, step, act):
        z = far(step)
        source = mine[chunk].at[z, here.y, here.x]
        target = landed[put_table[chunk][0]].at[here.home, :, columns(put_table, chunk, here.core)]
        receive = z_recv.at[chunk, here.home, here.core]
        own = (here.z == z) & (here.core == here.layer)
        if act == "start":

            @pl.when(own)
            def _():
                pltpu.make_async_copy(source, target, receive).start()

        @pl.when(jnp.logical_not(own))
        def _():
            away = remote(source, target, z_send.at[chunk, step], receive, (here.layer, here.chip(z=z)))
            getattr(away, act)()

    def add(target, other):
        target[...] = (target[...].astype(f32) + other[...].astype(f32)).astype(target.dtype)

    def both_sides(array):
        if array:
            left_copy(array - 1).wait_recv()
            right_copy(array - 1).wait_recv()
        else:
            small_copy().wait_recv()

    def terms(chunk):
        array, start, width, shared = put_table[chunk]
        if array == 0:
            block = (small_terms[here.core] + other_small[...]).T
        else:
            source, other = right_sides(array - 1)
            own_at = pl.multiple_of(here.core * (widths[array] // 2) + start, 128)
            block = left_dot(lefts[array - 1][0], source[:, pl.ds(own_at, width)])
            block += left_dot(lefts[array - 1][1], other[:, pl.ds(start, width)])
        block = block.astype(low)
        rows = features // 16
        for z in range(4):
            for k in range(4):
                at = (z * 4 + k) * rows
                mine[chunk][z, k // 2, k % 2] = block[at : at + rows]
        if not shared:
            for step in range(4):
                put_first(chunk, step).start()
            return

        @pl.when(here.second_layer)
        def _():
            for step in range(4):
                put_first(chunk, step).start()

        @pl.when(here.first_layer)
        def _():
            if not any(entry[3] for entry in put_table[:chunk]):
                pl.semaphore_wait(ready_mid, 1)
            put_middle(chunk).start()

    def put_middle(chunk):
        source = mine[chunk].at[pl.ds(2 * (1 - here.home), 2)]
        return remote(source, mid_in(chunk), mid_send.at[chunk], mid_recv.at[chunk], here.middle())

    def mid_in(chunk):
        _, start, width, _ = put_table[chunk]
        return weight[4].at[pl.ds(0, 2), :, :, :, pl.ds(start, width)]

    def sum_middle(chunk):
        put_middle(chunk).wait_recv()
        for z in range(2):
            for k in range(4):
                add(mine[chunk].at[2 * here.home + z, k // 2, k % 2], mid_in(chunk).at[z, k // 2, k % 2])
        for step in range(4):
            when(at_home(far(step)), lambda: put_first(chunk, step).start())

    def sum_one(chunk):
        for step in range(4):

            def action():
                z = far(step)
                put_first(chunk, step).wait_recv()
                for k in range(2):
                    if step % 2:
                        add(mine[chunk].at[z, k, here.x], one_in(chunk, step).at[k])
                    else:
                        add(mine[chunk].at[z, here.y, k], one_in(chunk, step).at[k])
                put_second(chunk, step).start()

            when(handled(put_table, chunk, far(step)), action)

    def sum_two(chunk):
        for step in range(4):

            def action():
                put_second(chunk, step).wait_recv()
                add(mine[chunk].at[far(step), here.y, here.x], two_in(chunk, step))
                put_third(chunk, step, "start")

            when(handled(put_table, chunk, far(step)), action)

    last = len(put_table)
    needs = {array: min(k for k, entry in enumerate(put_table) if entry[0] == array) for array in range(5)}
    down = [chunk for chunk in range(last) if put_table[chunk][0] == 4]

    total[...] = jnp.zeros_like(total)

    @pl.when(here.first_layer)
    def _():
        both_sides(4)
        for chunk in down:
            terms(chunk)

    def expand_back(start):
        again = pl.multiple_of(hidden + start, 128)
        grad_act = left_dot(e_in[...], matrix(4, start, tile))
        gate = expanded[:, pl.ds(start, tile)].astype(f32)
        up = expanded[:, pl.ds(again, tile)].astype(f32)
        sig = sigmoid(gate)
        grad_gate = (grad_act * up * (sig * (1.0 + gate * (1.0 - sig)))).astype(low)
        grad_up = (grad_act * (gate * sig)).astype(low)
        expanded[:, pl.ds(start, tile)] = grad_gate
        expanded[:, pl.ds(again, tile)] = grad_up
        total[...] += dot_back(grad_gate, matrix(3, start, tile)) + dot_back(grad_up, matrix(3, again, tile))

    tiles(0, hidden, expand_back)
    right_copy(2).start()
    for side in (here.x_side(), here.y_side()):
        pl.semaphore_signal(ready, inc=1, device_id=side, device_id_type=MESH)
    if any(entry[3] for entry in put_table):

        @pl.when(here.first_layer)
        def _():
            pl.semaphore_signal(ready_mid, inc=1, device_id=here.middle(), device_id_type=MESH)


    def norm_grad(rows, grad, normal, scale, gain, at):
        n = normal[rows]
        small_terms[1, at : at + 1] += jnp.sum(grad * n, axis=0, keepdims=True)
        q = grad * gain
        back = q - jnp.mean(q, axis=1, keepdims=True) - n * jnp.mean(q * n, axis=1, keepdims=True)
        return scale[rows][:, :1] * back

    def after_back():
        small_terms[...] = jnp.zeros_like(small_terms)

        def body(rows):
            grad = e_in[rows].astype(f32) + norm_grad(rows, total[rows], norm_two, scale_two, rows8[4:5], 4)
            after[rows] = grad
            after_low[rows] = grad.astype(low)

        in_rows(body)
        right_copy(1).start()

    def gated_back():
        total[...] = dot_back(after_low[...], matrix(2, 0, features))

    def mix_back(m, rows, taken, cut):
        taps = [rows8[j : j + 1, taken] for j in range(3)]
        alive = live_rows(m)
        grad = total[rows, taken]
        projected[rows, taken] = (grad * convolved[rows, taken]).astype(low)
        spec = left_dot(dft[...], parts(grad * queries[rows, taken]))
        g_re, g_im = spec[:slots], spec[slots:]
        pairs = []
        for other in (kernel_spec, value_spec):
            o_re, o_im = other[m, :slots, taken], other[m, slots:, taken]
            both = o_im * g_im
            re = o_re * g_re + jnp.where(first_row, 0.0, both)
            im = jnp.where(first_row, both, o_re * g_im - o_im * g_re)
            pairs.append(jnp.concatenate([re, im], axis=0))
        paired = left_dot(idft[...], parts(jnp.concatenate(pairs, axis=1)))
        at_values = pl.ds(pl.multiple_of(2 * features + cut * 256, 256), 256)
        projected[rows, at_values] = (paired[:, :256] * alive).astype(low)
        grad_kernel = paired[:, 256:]
        small_terms[0, :, taken] += grad_kernel
        k = keys[rows, taken]
        for j in range(3):
            moved = later(k, j) if j else k
            small_terms[1, j : j + 1, taken] += jnp.sum(grad_kernel * moved, axis=0, keepdims=True)
        grad_keys = taps[0] * grad_kernel + taps[1] * sooner(grad_kernel, 1) + taps[2] * sooner(grad_kernel, 2)
        at_keys = pl.ds(pl.multiple_of(features + cut * 256, 256), 256)
        projected[rows, at_keys] = (grad_keys * alive).astype(low)

    def mixed_back(m):
        mixer_blocks(m, mix_back)

    def input_back(m):
        rows = sequence(m)
        total[rows] = dot_back(projected[rows], matrix(1, 0, 3 * features))

        def body(rows):
            grad = after[rows] + norm_grad(rows, total[rows], norm_one, scale_one, rows8[3:4], 3)
            grad_low[rows] = grad.astype(low)

        in_rows(body, m * slots, slots)

    pieces = [after_back, gated_back]
    for m in range(micro):
        pieces += [functools.partial(mixed_back, m), functools.partial(input_back, m)]

    def last_copies():
        right_copy(0).start()
        small_copy().start()

    pieces += [last_copies]

    @pl.when(here.second_layer)
    def _():
        after_back()
        gated_back()
        for m in range(micro):
            mixed_back(m)
            input_back(m)
            if m == micro - 1:
                both_sides(4)
                terms(down[0])
            if m:
                give(grad_low, m - 1).wait_send()
            give(grad_low, m).start()
        last_copies()
        turned(2)
        for chunk in down[1:]:
            terms(chunk)
        turned(1)
        turned(0)

    pl.semaphore_wait(ready, 2)

    apart = here.core != here.layer
    over = (1 - here.core, here.partner)

    def swap(source, target, number, act):
        sems = swap_sems.at[number], swap_sems.at[number + 1]

        @pl.when(apart)
        def _():
            getattr(remote(source, target, *sems, over), act)()

        @pl.when(jnp.logical_not(apart))
        def _():
            getattr(pltpu.make_async_copy(source, target, sems[1]), act)()

    due = [max(0, needs[1] - len(pieces) + k) for k in range(len(pieces))]
    shared = [chunk for chunk in range(last) if put_table[chunk][3]]
    met = [4]

    swap(out_low, kept_out, 0, "start")
    for now in range(last + 1):
        for piece, at in zip(pieces, due):
            if at == now:
                pl.when(here.first_layer)(piece)
        early = shared if now == 1 else []
        for chunk in early + [now + 1]:
            if chunk < last and chunk not in down and (chunk not in shared or chunk in early):
                if put_table[chunk][0] not in met:
                    met.append(put_table[chunk][0])
                    both_sides(put_table[chunk][0])
                terms(chunk)
        for chunk in shared:
            if now == chunk - 2:
                pl.when(here.first_layer)(functools.partial(sum_middle, chunk))
        if now < last:
            sum_one(now)
        if 1 <= now:
            sum_two(now - 1)
        if now == needs[0]:
            swap(grad_low, kept_grad, 2, "start")

    for chunk in range(last):
        for half in (0, 1):
            for slot in (0, 1):
                target = landed[put_table[chunk][0]].at[slot, :, columns(put_table, chunk, half)]
                wanted = (here.core == 1) | (here.home == slot) if put_table[chunk][3] else True
                when(wanted, functools.partial(arrived, target, z_recv.at[chunk, slot, half]))
        for step in range(4):

            def action():
                put_first(chunk, step).wait_send()
                put_second(chunk, step).wait_send()
                put_third(chunk, step, "wait_send")

            when(handled(put_table, chunk, far(step)), action)
        if put_table[chunk][3]:
            pl.when(here.first_layer)(lambda: put_middle(chunk).wait_send())

    @pl.when(own_feed)
    def _():
        remote(hidden_in, feed, feed_sems.at[1], feed_sems.at[0], partner).wait_send()
        remote(live_own, live, feed_sems.at[3], feed_sems.at[2], partner).wait_send()

    for k in range(4):
        left_copy(k).wait_send()
        right_copy(k).wait_send()
    small_copy().wait_send()
    pl.when(here.second_layer)(lambda: give(grad_low, micro - 1).wait_send())
    swap(out_low, kept_out, 0, "wait")
    swap(grad_low, kept_grad, 2, "wait")


def finish_kernel(put_table, *refs):
    here = Place()
    f32 = jnp.float32
    landed, (out, grad) = refs[:5], refs[5:7]
    s_filters, s_taps, s_one, s_two = refs[7:11]
    sums, (to_out, to_grad) = refs[11:15], refs[15:17]
    to_out[...] = out[...]
    to_grad[...] = grad[...]
    small = landed[0][0].astype(jnp.float32) + landed[0][1].astype(jnp.float32)
    s_filters[...] = small[:, :128]
    own = small.shape[0]
    rows = jnp.pad(small[:, 128:], ((0, 128 - own), (0, 0))).T
    for j in range(3):
        s_taps[j] = rows[j : j + 1, :own]
    s_one[...] = rows[3:4, :own]
    s_two[...] = rows[4:5, :own]
    for array, start, width, shared in put_table:
        for half in range(2 if array else 0):
            cut = pl.ds(half * (landed[array].shape[2] // 2) + start, width)
            if shared:
                near = landed[array][here.home, :, cut].astype(f32)
                other = landed[array][1 - here.home, :, cut].astype(f32)
                sums[array - 1][:, cut] = near + jnp.where(here.core == 0, 0.0, other)
            else:
                sums[array - 1][:, cut] = landed[array][0, :, cut].astype(f32) + landed[array][1, :, cut].astype(f32)


def fast_device(
    hidden_in, out_grad, lengths, gain_mixer, w_input, w_taps, filters, w_output, gain_mlp, w_gate_up, w_down
):
    micro, _, slots, features = hidden_in.shape
    tokens, rows = micro * slots, gain_mixer.shape[1]
    shards = (w_input[0], w_output[0], w_gate_up[0], w_down[0].T)
    widths = [256] + [shard.shape[1] for shard in shards]
    hidden = widths[4]
    get_table, put_table = chunks_of(GET_PIECES), chunks_of(PUT_PIECES)
    dft, idft = (jnp.asarray(table) for table in packed_tables(slots))
    low, f32 = jnp.bfloat16, jnp.float32
    anywhere = pl.BlockSpec(memory_space=pl.ANY)
    inside = pl.BlockSpec(memory_space=pltpu.VMEM)
    dma, vmem = pltpu.SemaphoreType.DMA, pltpu.VMEM
    act, act_low = (tokens, features), vmem((tokens, features), low)
    kinds = [jax.ShapeDtypeStruct((2, rows, width), low) for width in widths]
    kinds += [jax.ShapeDtypeStruct((tokens, features), low)] * 2
    room = [vmem((rows, 256), low), vmem((128, 128), f32)] + [vmem((micro, 8, 128), f32)] * 2
    room += [vmem((4, 2, 2, rows, width), low) for width in widths]
    room += [act_low] * 6
    room += [vmem((slots, features), f32), vmem((8, features), f32), vmem(act, f32), vmem(act, f32)]
    room += [vmem((tokens, 128), f32)] * 2
    room += [act_low] * 3 + [vmem(act, f32)] * 4 + [vmem((micro, 2 * slots, features), f32)] * 2
    room += [vmem(act, f32)] * 2 + [vmem((tokens, 2 * hidden), low), vmem((tokens, hidden), low)]
    room += [vmem((tokens, 3 * features), low), act_low, vmem((2, slots, features), f32)]
    room += [vmem((2, features, tokens), low)] * 4
    room += [vmem((slots, features), f32)] + [vmem((tokens, width // 2), low) for width in widths[1:]]
    room += [vmem((4, 2, 2, rows, entry[2]), low) for entry in put_table]
    for width in (128, hidden // 2):
        room += [vmem((4, 2, rows, width), low), vmem((4, rows, width), low)]
    got, put = len(get_table), len(put_table)
    room += [dma((got, 2, 2))] + [dma((got, 4))] * 5 + [dma((got, 2))] * 2 + [dma((got,))] * 2 + [dma((4,))]
    room += [dma((4,)), dma((micro,)), dma((micro,)), dma((9,)), dma((9,))]
    room += [dma((put, 4))] * 5 + [dma((put, 2, 2))] + [dma((put,))] * 2 + [pltpu.SemaphoreType.REGULAR] * 2
    results = pl.pallas_call(
        functools.partial(layer_kernel, get_table, put_table, widths),
        out_shape=kinds,
        in_specs=[inside] * 4 + [pl.BlockSpec(memory_space=pltpu.SMEM)] + [inside] * 2 + [anywhere] * 6,
        out_specs=[anywhere] * 7,
        scratch_shapes=room,
        compiler_params=pltpu.CompilerParams(
            collective_id=0, has_side_effects=True, vmem_limit_bytes=62 * 1024 * 1024
        ),
    )(
        filters[0].T,
        w_taps[0],
        gain_mixer,
        gain_mlp,
        lengths.T,
        dft,
        idft,
        *shards,
        hidden_in.reshape(tokens, features),
        out_grad.reshape(tokens, features),
    )
    kinds = [(rows, 128), (3, 1, rows), (1, rows), (1, rows)] + [(rows, width) for width in widths[1:]]
    kinds = [jax.ShapeDtypeStruct(kind, f32) for kind in kinds] + kinds_of(results[5:])
    s_filters, s_taps, s_one, s_two, s_in, s_out, s_gu, s_dt, layer_out, input_grad = pl.pallas_call(
        functools.partial(finish_kernel, put_table),
        out_shape=kinds,
        in_specs=[inside] * 7,
        out_specs=[inside] * 10,
        compiler_params=pltpu.CompilerParams(vmem_limit_bytes=62 * 1024 * 1024),
    )(*results)
    shape = (1, micro, 1, slots, features)
    return (
        layer_out.reshape(shape),
        input_grad.reshape(shape),
        s_one,
        s_in[None],
        s_taps.transpose(1, 0, 2),
        s_filters.T[None],
        s_out[None],
        s_two,
        s_gu[None],
        s_dt.T[None],
    )


def kinds_of(arrays):
    return [jax.ShapeDtypeStruct(array.shape, array.dtype) for array in arrays]


def solution(mesh):
    placed = (
        P(None, "dp", None, None),
        P(None, "dp", None, None),
        P(None, "dp"),
        P("section", "dp"),
        P("section", "dp", None),
        P("section", None, "dp"),
        P("section", None, "dp"),
        P("section", "dp", None),
        P("section", "dp"),
        P("section", "dp", None),
        P("section", None, "dp"),
    )
    return jax.shard_map(
        fast_device if mesh.shape["dp"] == 16 and mesh.shape["section"] == 2 else on_device,
        mesh=mesh,
        in_specs=placed,
        out_specs=(
            P("section", None, "dp", None, None),
            P("section", None, "dp", None, None),
            P("section", "dp"),
            P("section", "dp", None),
            P("section", None, "dp"),
            P("section", None, "dp"),
            P("section", "dp", None),
            P("section", "dp"),
            P("section", "dp", None),
            P("section", None, "dp"),
        ),
        check_vma=False,
    )
```

```python
import functools
import math

import jax
import jax.numpy as jnp
import ml_dtypes
import numpy as np
from jax import lax
from jax.experimental import pallas as pl
from jax.experimental.pallas import tpu as pltpu
from jax.sharding import PartitionSpec as P

MESH = pl.DeviceIdType.MESH

epsilon = 1e-05
GET_PIECES = (
    (0, 128, False),
    (1, 384, False),
    (1, 384, False),
    (1, 384, False),
    (2, 384, False),
    (3, 1024, False),
    (3, 1024, False),
    (3, 1024, False),
    (4, 512, False),
    (4, 512, False),
    (4, 512, False),
)
PUT_PIECES = (
    (4, 768, False),
    (4, 768, False),
    (3, 1024, False),
    (3, 1024, False),
    (1, 384, False),
    (1, 384, False),
    (0, 128, False),
    (1, 384, False),
    (2, 384, False),
    (3, 512, True),
    (3, 512, True),
)
GET_LAGS = (5, 7, 1, 2, 3)
ROWS_UNROLL = 2
MIX_UNROLL = 3
TILE_UNROLL = 2


def passed_along(value, axis, steps):
    count = lax.axis_size(axis)
    first, last = (max(0, -steps), min(count, count - steps))
    return lax.ppermute(value, axis, [(source, source + steps) for source in range(first, last)])


def split_dot(left_side, right_side):
    return jnp.dot(
        left_side, right_side, precision=lax.Precision.HIGH, preferred_element_type=jnp.float32
    )


def split_rows(left_side, right_side):
    return lax.dot_general(
        left_side,
        right_side,
        (((0,), (0,)), ((), ())),
        precision=lax.Precision.HIGH,
        preferred_element_type=jnp.float32,
    )


def dot_rows(left_side, right_side):
    return lax.dot_general(
        left_side, right_side, (((0,), (0,)), ((), ())), preferred_element_type=jnp.float32
    )


def dot_back(left_side, right_side):
    return lax.dot_general(
        left_side, right_side, (((1,), (1,)), ((), ())), preferred_element_type=jnp.float32
    )


def tables(length):
    period = 2 * length
    freq_index = lax.broadcasted_iota(jnp.int32, (length + 1, length), 0)
    time_index = lax.broadcasted_iota(jnp.int32, (length + 1, length), 1)
    angles = (freq_index * time_index % period).astype(jnp.float32) * (2.0 * math.pi / period)
    edge_rows = (freq_index[:, :1] == 0) | (freq_index[:, :1] == length)
    inverse_weight = jnp.where(edge_rows, 1.0, 2.0) / period
    dft_stack = jnp.concatenate([jnp.cos(angles), -jnp.sin(angles)], axis=0)
    return (dft_stack, inverse_weight)


def spectrum(dft_tables, signal):
    dft_stack, inverse_weight = dft_tables
    stacked_out = split_dot(dft_stack, signal)
    middle_row = stacked_out.shape[0] // 2
    return (stacked_out[:middle_row], stacked_out[middle_row:])


def inverse(dft_tables, real_part, imag_part):
    dft_stack, inverse_weight = dft_tables
    return split_rows(
        dft_stack, jnp.concatenate([inverse_weight * real_part, inverse_weight * imag_part], axis=0)
    )


def normalize(input_rows):
    centered = input_rows - jnp.mean(input_rows, axis=1, keepdims=True)
    inv_scale = lax.rsqrt(jnp.mean(centered * centered, axis=1, keepdims=True) + epsilon)
    return (centered * inv_scale, inv_scale)


def norm_back(grad_normed, normed, inv_scale):
    return inv_scale * (
        grad_normed
        - jnp.mean(grad_normed, axis=1, keepdims=True)
        - normed * jnp.mean(grad_normed * normed, axis=1, keepdims=True)
    )


def delayed(input_rows, places):
    return jnp.pad(input_rows, ((places, 0), (0, 0)))[: input_rows.shape[0]]


def advanced(input_rows, places):
    return jnp.pad(input_rows, ((0, places), (0, 0)))[places:]


def layer_forward(input_rows, active_rows, weights, dft_tables):
    gain_one, w_inner, w_tap_rows, filt_static, w_outer, gain_two, w_expand, w_reduce = weights
    hidden_size_model = w_outer.shape[0]
    hidden_width = w_reduce.shape[0]
    tap_weights = w_tap_rows.astype(jnp.float32)
    normed_one, scale_one = normalize(input_rows)
    entered = (normed_one * gain_one.astype(jnp.float32)).astype(jnp.bfloat16)
    projected = jnp.dot(entered, w_inner, preferred_element_type=jnp.float32)
    queries = projected[:, :hidden_size_model]
    keys_part = projected[:, hidden_size_model : 2 * hidden_size_model] * active_rows
    values_part = projected[:, 2 * hidden_size_model :] * active_rows
    dynamic = (
        tap_weights[0] * keys_part
        + tap_weights[1] * delayed(keys_part, 1)
        + tap_weights[2] * delayed(keys_part, 2)
    )
    kernel = filt_static.astype(jnp.float32) + dynamic
    joint_re, joint_im = spectrum(dft_tables, jnp.concatenate([values_part, kernel], axis=1))
    value_re = joint_re[:, :hidden_size_model]
    kernel_re = joint_re[:, hidden_size_model:]
    value_im = joint_im[:, :hidden_size_model]
    kernel_im = joint_im[:, hidden_size_model:]
    convolved = inverse(
        dft_tables,
        kernel_re * value_re - kernel_im * value_im,
        kernel_re * value_im + kernel_im * value_re,
    )
    gated_rows = (queries * convolved).astype(jnp.bfloat16)
    after_mixer = input_rows + jnp.dot(gated_rows, w_outer, preferred_element_type=jnp.float32)
    normed_two, scale_two = normalize(after_mixer)
    entered_two = (normed_two * gain_two.astype(jnp.float32)).astype(jnp.bfloat16)
    expanded = jnp.dot(entered_two, w_expand, preferred_element_type=jnp.float32)
    gate_part = expanded[:, :hidden_width]
    up_part = expanded[:, hidden_width:]
    activated = (jax.nn.silu(gate_part) * up_part).astype(jnp.bfloat16)
    result = after_mixer + jnp.dot(activated, w_reduce, preferred_element_type=jnp.float32)
    stash = (
        normed_one,
        scale_one,
        entered,
        queries,
        keys_part,
        (value_re, value_im, kernel_re, kernel_im),
        convolved,
        gated_rows,
        normed_two,
        scale_two,
        entered_two,
        gate_part,
        up_part,
        activated,
    )
    return (result, stash)


def mlp_backward(received_gradient, weights, stash):
    gain_one, w_inner, w_tap_rows, filt_static, w_outer, gain_two, w_expand, w_reduce = weights
    (
        normed_one,
        scale_one,
        entered,
        queries,
        keys_part,
        spectra,
        convolved,
        gated_rows,
        normed_two,
        scale_two,
        entered_two,
        gate_part,
        up_part,
        activated,
    ) = stash
    grad_low = received_gradient.astype(jnp.bfloat16)
    grad_reduce_w = dot_rows(activated, grad_low)
    grad_act = dot_back(grad_low, w_reduce)
    sigmoid_gate = jax.nn.sigmoid(gate_part)
    grad_gate = grad_act * up_part * (sigmoid_gate * (1.0 + gate_part * (1.0 - sigmoid_gate)))
    grad_up = grad_act * (gate_part * sigmoid_gate)
    grad_expand = jnp.concatenate([grad_gate, grad_up], axis=1).astype(jnp.bfloat16)
    grad_expand_w = dot_rows(entered_two, grad_expand)
    grad_entered_two = dot_back(grad_expand, w_expand)
    grad_gain_two = jnp.sum(grad_entered_two * normed_two, axis=0)
    grad_after = received_gradient + norm_back(
        grad_entered_two * gain_two.astype(jnp.float32), normed_two, scale_two
    )
    return (grad_after, (grad_gain_two, grad_expand_w, grad_reduce_w))


def mixer_backward(grad_after, active_rows, weights, dft_tables, stash):
    gain_one, w_inner, w_tap_rows, filt_static, w_outer, gain_two, w_expand, w_reduce = weights
    (
        normed_one,
        scale_one,
        entered,
        queries,
        keys_part,
        spectra,
        convolved,
        gated_rows,
        normed_two,
        scale_two,
        entered_two,
        gate_part,
        up_part,
        activated,
    ) = stash
    value_re, value_im, kernel_re, kernel_im = spectra
    hidden_size_model = w_outer.shape[0]
    tap_weights = w_tap_rows.astype(jnp.float32)
    grad_mix_low = grad_after.astype(jnp.bfloat16)
    grad_outer_w = dot_rows(gated_rows, grad_mix_low)
    grad_gated = dot_back(grad_mix_low, w_outer)
    grad_queries = grad_gated * convolved
    grad_conv = grad_gated * queries
    grad_re, grad_im = spectrum(dft_tables, grad_conv)
    paired_re = jnp.concatenate(
        [kernel_re * grad_re + kernel_im * grad_im, value_re * grad_re + value_im * grad_im], axis=1
    )
    paired_im = jnp.concatenate(
        [kernel_re * grad_im - kernel_im * grad_re, value_re * grad_im - value_im * grad_re], axis=1
    )
    paired = inverse(dft_tables, paired_re, paired_im)
    grad_values = paired[:, :hidden_size_model] * active_rows
    grad_kernel = paired[:, hidden_size_model:]
    grad_taps = jnp.stack(
        [
            jnp.sum(grad_kernel * keys_part, axis=0),
            jnp.sum(grad_kernel * delayed(keys_part, 1), axis=0),
            jnp.sum(grad_kernel * delayed(keys_part, 2), axis=0),
        ]
    )
    grad_keys = (
        tap_weights[0] * grad_kernel
        + tap_weights[1] * advanced(grad_kernel, 1)
        + tap_weights[2] * advanced(grad_kernel, 2)
    ) * active_rows
    grad_projected = jnp.concatenate([grad_queries, grad_keys, grad_values], axis=1).astype(
        jnp.bfloat16
    )
    inner_weight_gradient = dot_rows(entered, grad_projected)
    grad_entered = dot_back(grad_projected, w_inner)
    grad_gain_one = jnp.sum(grad_entered * normed_one, axis=0)
    grad_inputs = grad_after + norm_back(
        grad_entered * gain_one.astype(jnp.float32), normed_one, scale_one
    )
    return (
        grad_inputs,
        (grad_gain_one, inner_weight_gradient, grad_taps, grad_kernel, grad_outer_w),
    )


def add_terms(received, flipped):
    return tuple(
        (
            jnp.sum(member, axis=0).T if flip else jnp.sum(member, axis=0)
            for member, flip in zip(received, flipped)
        )
    )


def on_device(
    hidden_in,
    out_grad,
    lengths,
    gain_mixer,
    w_input,
    w_taps,
    filters,
    w_output,
    gain_mlp,
    w_gate_up,
    w_down,
):
    first_section = lax.axis_index("section") == 0
    micro_count = hidden_in.shape[0]
    seq_slots = hidden_in.shape[2]
    hidden_size_model = hidden_in.shape[3]
    dft_tables = tables(seq_slots)
    positions = lax.broadcasted_iota(jnp.int32, (seq_slots, 1), 0)
    weights = (
        lax.all_gather(gain_mixer[0], "dp", axis=0, tiled=True),
        lax.all_gather(w_input[0], "dp", axis=0, tiled=True),
        lax.all_gather(w_taps[0], "dp", axis=1, tiled=True),
        lax.all_gather(filters[0], "dp", axis=1, tiled=True),
        lax.all_gather(w_output[0], "dp", axis=0, tiled=True),
        lax.all_gather(gain_mlp[0], "dp", axis=0, tiled=True),
        lax.all_gather(w_gate_up[0], "dp", axis=0, tiled=True),
        lax.all_gather(w_down[0], "dp", axis=1, tiled=True),
    )
    arriving = jnp.zeros((seq_slots, hidden_size_model), jnp.bfloat16)
    outgoing_list = []
    saved_activations = []
    for forward_step in range(micro_count + 1):
        own_index = min(forward_step, micro_count - 1)
        prior_index = max(forward_step - 1, 0)
        input_rows = jnp.where(first_section, hidden_in[own_index, 0], arriving).astype(jnp.float32)
        length_now = jnp.where(first_section, lengths[own_index, 0], lengths[prior_index, 0])
        active_rows = (positions < length_now).astype(jnp.float32)
        result, stash = layer_forward(input_rows, active_rows, weights, dft_tables)
        outgoing = result.astype(jnp.bfloat16)
        outgoing_list.append(outgoing)
        if forward_step < micro_count:
            arriving = passed_along(outgoing, "section", 1)
        saved_activations.append((input_rows, active_rows))
    coming = jnp.zeros((seq_slots, hidden_size_model), jnp.bfloat16)
    mlp_totals = None
    mixer_totals = None
    grads_out = []
    for backward_step in range(micro_count + 1):
        saved_slot_index = micro_count - backward_step
        last_index = max(micro_count - 1 - backward_step, 0)
        live_factor = 1.0 if backward_step < micro_count else 0.0
        received_gradient = jnp.where(
            first_section,
            coming.astype(jnp.float32),
            out_grad[last_index, 0].astype(jnp.float32) * live_factor,
        )
        input_rows, active_rows = saved_activations[saved_slot_index]
        result, stash = layer_forward(input_rows, active_rows, weights, dft_tables)
        grad_after, mlp_grads = mlp_backward(received_gradient, weights, stash)
        mlp_totals = (
            mlp_grads if mlp_totals is None else jax.tree.map(jnp.add, mlp_totals, mlp_grads)
        )
        grad_inputs, mixer_grads = mixer_backward(
            grad_after, active_rows, weights, dft_tables, stash
        )
        mixer_totals = (
            mixer_grads
            if mixer_totals is None
            else jax.tree.map(jnp.add, mixer_totals, mixer_grads)
        )
        outgoing = grad_inputs.astype(jnp.bfloat16)
        grads_out.append(outgoing)
        if backward_step < micro_count:
            coming = passed_along(outgoing, "section", -1)
    first_outputs = jnp.stack(outgoing_list[:micro_count])
    second_outputs = jnp.stack(outgoing_list[1:])
    layer_out = jnp.where(first_section, first_outputs, second_outputs)[None, :, None]
    first_grads = jnp.stack(
        [grads_out[micro_count - batch_index] for batch_index in range(micro_count)]
    )
    second_grads = jnp.stack(
        [grads_out[micro_count - 1 - batch_index] for batch_index in range(micro_count)]
    )
    input_grad = jnp.where(first_section, first_grads, second_grads)[None, :, None]
    all_parts = (
        lax.all_to_all(
            mixer_totals[0][None].astype(jnp.bfloat16),
            "dp",
            split_axis=1,
            concat_axis=0,
            tiled=True,
        ).astype(jnp.float32),
        lax.all_to_all(
            mixer_totals[1][None].astype(jnp.bfloat16),
            "dp",
            split_axis=1,
            concat_axis=0,
            tiled=True,
        ).astype(jnp.float32),
        lax.all_to_all(
            mixer_totals[2].T[None].astype(jnp.bfloat16),
            "dp",
            split_axis=1,
            concat_axis=0,
            tiled=True,
        ).astype(jnp.float32),
        lax.all_to_all(
            mixer_totals[3].T[None].astype(jnp.bfloat16),
            "dp",
            split_axis=1,
            concat_axis=0,
            tiled=True,
        ).astype(jnp.float32),
        lax.all_to_all(
            mixer_totals[4][None].astype(jnp.bfloat16),
            "dp",
            split_axis=1,
            concat_axis=0,
            tiled=True,
        ).astype(jnp.float32),
        lax.all_to_all(
            mlp_totals[0][None].astype(jnp.bfloat16), "dp", split_axis=1, concat_axis=0, tiled=True
        ).astype(jnp.float32),
        lax.all_to_all(
            mlp_totals[1][None].astype(jnp.bfloat16), "dp", split_axis=1, concat_axis=0, tiled=True
        ).astype(jnp.float32),
        lax.all_to_all(
            mlp_totals[2].T[None].astype(jnp.bfloat16),
            "dp",
            split_axis=1,
            concat_axis=0,
            tiled=True,
        ).astype(jnp.float32),
    )
    summed = add_terms(all_parts, (False, False, True, True, False, False, False, True))
    return (
        layer_out,
        input_grad,
        summed[0][None],
        summed[1][None],
        summed[2][None],
        summed[3][None],
        summed[4][None],
        summed[5][None],
        summed[6][None],
        summed[7][None],
    )


class Place:
    def __init__(self):
        self.core = lax.axis_index("section")
        self.index = lax.axis_index("dp")
        self.z = self.index // 4
        self.y = self.index // 2 % 2
        self.x = self.index % 2
        self.layer = 1 - (self.z + 1) // 2 % 2
        self.home = self.z // 2
        self.first_layer = self.layer == 0
        self.second_layer = self.layer == 1
        self.partner = self.chip(z=self.z + 1 - 2 * (self.z % 2))

    def chip(self, z=None, y=None, x=None):
        z, y, x = (a if a is not None else b for a, b in ((z, self.z), (y, self.y), (x, self.x)))
        return z * 4 + y * 2 + x

    def x_side(self):
        return (self.core, self.chip(x=1 - self.x))

    def y_side(self):
        return (self.core, self.chip(y=1 - self.y))

    def sibling(self):
        return (1 - self.core, self.index)

    def middle(self):
        return (self.core, self.chip(z=3 - self.z))

    def greet(self):
        barrier = pltpu.get_barrier_semaphore()
        others = [self.x_side(), self.y_side(), self.sibling()]
        for step in (1, 2, 3):
            chip = self.chip(z=(self.z + step) % 4)
            others += [(0, chip), (1, chip)]
        for other in others:
            pl.semaphore_signal(barrier, inc=1, device_id=other, device_id_type=MESH)
        pl.semaphore_wait(barrier, len(others))


def remote(source, target, send, receive, device):
    return pltpu.make_async_remote_copy(
        src_ref=source,
        dst_ref=target,
        send_sem=send,
        recv_sem=receive,
        device_id=device,
        device_id_type=MESH,
    )


def chunks_of(pieces):
    table, places = [], {}
    for array, width, shared in pieces:
        start = places.get(array, 0)
        table.append((array, start, width, shared))
        places[array] = start + width
    return table


def left_dot(left_side, right_side):
    return lax.dot_general(
        left_side, right_side, (((1,), (0,)), ((), ())), preferred_element_type=jnp.float32
    )


def sigmoid(value):
    return 0.5 * jnp.tanh(0.5 * value) + 0.5


def parts(signal):
    high = signal.astype(jnp.bfloat16)
    rest = (signal - high.astype(jnp.float32)).astype(jnp.bfloat16)
    return jnp.concatenate([high, high, rest], axis=0)


def halves_of(table):
    high = table.astype(ml_dtypes.bfloat16)
    rest = (table - high.astype(np.float64)).astype(ml_dtypes.bfloat16)
    return np.concatenate([high, rest, high], axis=1)


def packed_tables(length):
    period = 2 * length
    freq, time = np.arange(length)[:, None], np.arange(length)[None, :]
    angles = (freq * time % period) * (2.0 * math.pi / period)
    sines = np.where(freq == 0, 1.0 - 2.0 * (time % 2), -np.sin(angles))
    table = np.concatenate([np.cos(angles), sines], axis=0)
    weight = np.where(np.arange(period)[:, None] % length == 0, 1.0, 2.0) / period
    return halves_of(table), halves_of((table * weight).T)


def layer_kernel(get_table, put_table, widths, *refs):
    refs = list(refs)

    def take(number):
        taken = refs[:number]
        del refs[:number]
        return taken

    filters_in, taps_in, gain_one_in, gain_two_in, lengths_in, dft, idft = take(7)
    shards, (hidden_in, grad_in) = [None] + take(4), take(2)
    landed, (kept_out, kept_grad) = take(5), take(2)
    own_small, rows_in, live_own, live, nothing, nothing_sems = take(6)
    weight = take(5)
    feed, arrive, x_in, e_in, out_low, grad_low = take(6)
    filt, rows8, norm_one, norm_two, scale_one, scale_two = take(6)
    entered, gated, again, queries, keys, values, convolved, value_spec, kernel_spec = take(9)
    total, after, expanded, active, projected, after_low, small_terms = take(7)
    lefts = take(4)
    other_small, other_projected, other_after, other_expanded, other_active = take(5)
    mine = take(len(put_table))
    one_small, two_small, one_down, two_down = take(4)
    get_z_send, get_z_recv, get_one_send, get_one_recv, get_two_send, get_two_recv = take(6)
    get_mid_send, get_mid_recv, get_side_send, get_side_recv, feed_sems = take(5)
    swap_sems, give_send, give_recv, send, recv = take(5)
    one_send, one_recv, two_send, two_recv, z_send, z_recv, mid_send, mid_recv, ready, ready_mid = take(10)

    here = Place()
    tokens, features = x_in.shape
    slots = filt.shape[0]
    micro = tokens // slots
    hidden = active.shape[1]
    f32, low = jnp.float32, jnp.bfloat16
    shards[0] = own_small

    here.greet()

    for m in range(micro):
        live_own[m] = jnp.full(live_own.shape[1:], lengths_in[0, m], jnp.int32).astype(f32)

    own_feed = here.core == here.layer
    partner = (here.core, here.partner)
    for layer, kept, given in ((0, hidden_in, grad_in), (1, grad_in, hidden_in)):

        @pl.when(own_feed & (here.layer == layer))
        def _():
            pltpu.make_async_copy(kept, feed, feed_sems.at[0]).start()
            pltpu.make_async_copy(live_own, live, feed_sems.at[2]).start()
            remote(given, feed, feed_sems.at[1], feed_sems.at[0], partner).start()
            remote(live_own, live, feed_sems.at[3], feed_sems.at[2], partner).start()

    def arrived(target, receive):
        pltpu.make_async_copy(target, target, receive).wait()

    def fed():
        arrived(feed, feed_sems.at[0])
        arrived(live, feed_sems.at[2])

    def small_shard():
        rows_in[...] = jnp.zeros_like(rows_in)
        own = taps_in.shape[1]
        rows_in[0:3, 0:own] = taps_in[...].astype(f32)
        rows_in[3:4, 0:own] = gain_one_in[...].astype(f32)
        rows_in[4:5, 0:own] = gain_two_in[...].astype(f32)
        own_small[:, :128] = filters_in[...]
        own_small[:, 128:] = rows_in[...].T[:own].astype(low)

    def columns(table, chunk, half):
        array, start, width, _ = table[chunk]
        return pl.ds(pl.multiple_of(half * (widths[array] // 2) + start, 128), width)

    def at_home(z):
        return z // 2 == here.home

    def when(condition, action):
        if condition is True:
            action()
        else:
            pl.when(condition)(action)

    def z_all(chunk, visit, near):
        array, _, _, shared = get_table[chunk]
        for number, plane in enumerate((1 - here.core, 2 + here.core)):
            wanted = (plane == here.z) if near else (plane != here.z)
            if shared:
                wanted = wanted & ((here.core == 1) | (here.home == number))
            for half in (0, 1):
                cut = columns(get_table, chunk, half)
                source, target = shards[array].at[:, cut], weight[array].at[here.z, here.y, here.x, :, cut]
                sems = get_z_send.at[chunk, number, half], get_z_recv.at[chunk, here.z]
                visit(wanted, here.core == half, source, target, sems, (half, here.chip(z=plane)))

    def z_start(chunk, near):
        def visit(wanted, own, source, target, sems, device):
            if not near:

                @pl.when(wanted)
                def _():
                    remote(source, target, *sems, device).start()

                return

            @pl.when(wanted & own)
            def _():
                pltpu.make_async_copy(source, target, sems[1]).start()

            @pl.when(wanted & jnp.logical_not(own))
            def _():
                remote(source, target, *sems, device).start()

        z_all(chunk, visit, near)

    def z_sent(chunk):
        for near in (False, True):

            def visit(wanted, own, source, target, sems, device):
                @pl.when(wanted & jnp.logical_not(own) if near else wanted)
                def _():
                    remote(source, target, *sems, device).wait_send()

            z_all(chunk, visit, near)

    def far(step):
        return (here.z + step) % 4

    def handled(table, chunk, z):
        return here.second_layer | at_home(z) if table[chunk][3] else True

    def get_first(chunk, step):
        block = weight[get_table[chunk][0]].at[far(step), here.y, here.x, :, columns(get_table, chunk, here.core)]
        side = here.y_side() if (step + chunk) % 2 else here.x_side()
        return remote(block, block, get_one_send.at[chunk, step], get_one_recv.at[chunk, step], side)

    def get_second(chunk, step):
        ref, cut = weight[get_table[chunk][0]], columns(get_table, chunk, here.core)
        if (step + chunk) % 2:
            pair, side = ref.at[far(step), :, here.x, :, cut], here.x_side()
        else:
            pair, side = ref.at[far(step), here.y, :, :, cut], here.y_side()
        return remote(pair, pair, get_two_send.at[chunk, step], get_two_recv.at[chunk, step], side)

    def get_middle(chunk, z):
        block = weight[get_table[chunk][0]].at[z, :, :, :, columns(get_table, chunk, here.core)]
        return remote(block, block, get_mid_send.at[chunk, z % 2], get_mid_recv.at[chunk, z % 2], here.middle())

    def get_across(chunk):
        whole = weight[get_table[chunk][0]].at[:, :, :, :, columns(get_table, chunk, here.core)]
        return remote(whole, whole, get_side_send.at[chunk], get_side_recv.at[chunk], here.sibling())

    def one_step(chunk, step):
        def action():
            z = far(step)
            block = weight[get_table[chunk][0]].at[z, here.y, here.x, :, columns(get_table, chunk, here.core)]
            arrived(block, get_z_recv.at[chunk, z])
            get_first(chunk, step).start()

        when(handled(get_table, chunk, far(step)), action)

    def two_steps(chunk, step):
        def action():
            get_first(chunk, step).wait_recv()
            get_second(chunk, step).start()

        when(handled(get_table, chunk, far(step)), action)

    def three_steps(chunk, step):
        def action():
            get_second(chunk, step).wait_recv()
            if get_table[chunk][3]:

                @pl.when(here.first_layer)
                def _():
                    get_middle(chunk, far(step)).start()

        when(handled(get_table, chunk, far(step)), action)

    def pass_on(chunk):
        if get_table[chunk][3]:

            @pl.when(here.first_layer)
            def _():
                for k in range(2):
                    get_middle(chunk, 2 * (1 - here.home) + k).wait_recv()

        get_across(chunk).start()

    def gather(on_chunk):
        last = len(get_table)
        ahead, own_ahead, two_lag, three_lag, done_lag = GET_LAGS
        for chunk in range(1, last):
            z_start(chunk, True)
        small_shard()
        z_start(0, True)

        def z_first():
            for chunk in range(min(ahead, last)):
                z_start(chunk, False)

        pl.when(here.core == 0)(z_first)
        for chunk in range(min(own_ahead, last)):
            one_step(chunk, 0)
        for chunk in range(min(own_ahead, last) - 1):
            two_steps(chunk, 0)
        pl.when(here.core == 1)(z_first)
        for now in range(last + done_lag + 1):
            if now + own_ahead < last:
                one_step(now + own_ahead, 0)
            if 0 <= now + own_ahead - 1 < last:
                two_steps(now + own_ahead - 1, 0)
            if now < last:
                for step in (1, 3, 2):
                    one_step(now, step)
            if now + ahead < last:
                z_start(now + ahead, False)
            if 0 <= now - two_lag < last:
                for step in (1, 3, 2):
                    two_steps(now - two_lag, step)
            if 0 <= now - three_lag < last:
                for step in range(4):
                    three_steps(now - three_lag, step)
                if not get_table[now - three_lag][3]:
                    pass_on(now - three_lag)
            if 0 <= now - three_lag - 1 < last and get_table[now - three_lag - 1][3]:
                pass_on(now - three_lag - 1)
            for chunk in (now - done_lag, now - done_lag - 1):
                if 0 <= chunk < last and get_table[chunk][3] == (chunk == now - done_lag - 1):
                    get_across(chunk).wait_recv()
                    on_chunk(chunk)

    def gathered():
        for chunk in range(len(get_table)):
            z_sent(chunk)
            for step in range(4):

                def action():
                    get_first(chunk, step).wait_send()
                    get_second(chunk, step).wait_send()

                when(handled(get_table, chunk, far(step)), action)
            if get_table[chunk][3]:

                @pl.when(here.first_layer)
                def _():
                    for k in range(2):
                        get_middle(chunk, 2 * here.home + k).wait_send()

            get_across(chunk).wait_send()

    def matrix(number, start, width):
        ref = weight[number]
        return ref[:, :, :, :, pl.ds(start, width)].reshape(features, width)

    def in_rows(body, start=0, count=tokens):
        block = 64

        def step(i, carry):
            body(pl.ds(pl.multiple_of(start + i * block, block), block))
            return carry

        lax.fori_loop(0, count // block, step, 0, unroll=ROWS_UNROLL)

    def sequence(m):
        return pl.ds(pl.multiple_of(m * slots, slots), slots)

    def normed(rows, rows_in, normal, scale, gain, target):
        centered = rows_in - jnp.mean(rows_in, axis=1, keepdims=True)
        inv = lax.rsqrt(jnp.mean(centered * centered, axis=1, keepdims=True) + epsilon)
        n = centered * inv
        normal[rows] = n
        scale[rows] = jnp.broadcast_to(inv, (n.shape[0], 128))
        target[rows] = (n * gain).astype(low)

    row_at = lax.broadcasted_iota(jnp.int32, (slots, 256), 0)
    first_row = row_at == 0

    def later(rows, places):
        return jnp.where(row_at >= places, pltpu.roll(rows, places, 0), 0.0)

    def sooner(rows, places):
        return jnp.where(row_at < slots - places, pltpu.roll(rows, slots - places, 0), 0.0)

    cuts = features // 256

    def mixer_blocks(m, body):
        def step(cut, carry):
            body(m, sequence(m), pl.ds(pl.multiple_of(cut * 256, 256), 256), cut)
            return carry

        lax.fori_loop(0, cuts, step, 0, unroll=MIX_UNROLL)

    def live_rows(m):
        return (row_at.astype(f32) < jnp.concatenate([live[m, 0:1, :]] * 2, axis=1)).astype(f32)

    def to_sibling(number, source, target):
        return remote(source, target, send.at[number], recv.at[number], here.sibling())

    def left_copy(k):
        return to_sibling(k, lefts[k].at[0], lefts[k].at[1])

    def right_sides(k):
        return (
            (projected, other_projected),
            (after_low, other_after),
            (expanded, other_expanded),
            (active, other_active),
        )[k]

    def right_copy(k):
        source, target = right_sides(k)
        half = widths[1 + k] // 2
        cut = pl.ds(pl.multiple_of((1 - here.core) * half, 128), half)
        return to_sibling(4 + k, source.at[:, cut], target)

    def small_copy():
        return to_sibling(8, small_terms.at[1 - here.core], other_small)

    def give(source, m):
        rows = pl.ds(m * slots, slots)
        return remote(source.at[rows], arrive.at[rows], give_send.at[m], give_recv.at[m], partner)

    def received(target, m):
        rows = sequence(m)
        arrived(arrive.at[rows], give_recv.at[m])
        target[rows] = arrive[rows]

    def turned(k):
        lefts[k][0] = (entered, gated, again, e_in)[k][...].T
        left_copy(k).start()

    def small_weights():
        filt[...] = matrix(0, 0, 128).astype(f32).T
        rows8[...] = matrix(0, 128, 128).astype(f32).T[:8]

    def enter(m):
        def body(rows):
            normed(rows, x_in[rows].astype(f32), norm_one, scale_one, rows8[3:4], entered)

        in_rows(body, m * slots, slots)

    def mix(m, rows, taken, cut):
        taps = [rows8[j : j + 1, taken] for j in range(3)]
        alive = live_rows(m)
        k = keys[rows, taken] * alive
        keys[rows, taken] = k
        v = values[rows, taken] * alive
        kernel = filt[:, taken] + taps[0] * k + taps[1] * later(k, 1) + taps[2] * later(k, 2)
        spec = left_dot(dft[...], parts(jnp.concatenate([v, kernel], axis=1)))
        value_spec[m, :, taken] = spec[:, :256]
        kernel_spec[m, :, taken] = spec[:, 256:]
        v_re, v_im = spec[:slots, :256], spec[slots:, :256]
        k_re, k_im = spec[:slots, 256:], spec[slots:, 256:]
        both = k_im * v_im
        re = k_re * v_re - jnp.where(first_row, 0.0, both)
        im = jnp.where(first_row, both, k_re * v_im + k_im * v_re)
        out = left_dot(idft[...], parts(jnp.concatenate([re, im], axis=0)))
        convolved[rows, taken] = out
        gated[rows, taken] = (queries[rows, taken] * out).astype(low)

    def mixer(m):
        rows = sequence(m)
        for k, target in enumerate((queries, keys, values)):
            target[rows] = left_dot(entered[rows], matrix(1, k * features, features))
        mixer_blocks(m, mix)

    def mixer_out(m):
        rows = sequence(m)
        total[rows] = x_in[rows].astype(f32) + left_dot(gated[rows], matrix(2, 0, features))

        def body(rows):
            normed(rows, total[rows], norm_two, scale_two, rows8[4:5], again)

        in_rows(body, m * slots, slots)

    def each_sequence(*bodies):
        def step(m, carry):
            for body in bodies:
                body(m)
            return carry

        lax.fori_loop(0, micro, step, 0)

    tile = 512

    def tiles(start, width, body):
        def step(i, carry):
            body(pl.multiple_of(start + i * tile, 128))
            return carry

        lax.fori_loop(0, width // tile, step, 0, unroll=TILE_UNROLL)

    def expand(start):
        gate = left_dot(again[...], matrix(3, start, tile))
        up = left_dot(again[...], matrix(3, pl.multiple_of(hidden + start, 128), tile))
        expanded[:, pl.ds(start, tile)] = gate.astype(low)
        expanded[:, pl.ds(pl.multiple_of(hidden + start, 128), tile)] = up.astype(low)
        active[:, pl.ds(start, tile)] = (gate * sigmoid(gate) * up).astype(low)

    def reduce_on(start, width):
        total[...] += dot_back(active[:, pl.ds(start, width)], matrix(4, start, width))

    def layer_done():
        right_copy(3).start()
        out_low[...] = total[...].astype(low)

    ends = {array: max(k for k, entry in enumerate(get_table) if entry[0] == array) for array in range(5)}

    def as_it_comes(chunk):
        array, start, width, _ = get_table[chunk]

        @pl.when(here.first_layer)
        def _():
            if array == 0:
                x_in[...] = feed[...]
                small_weights()
                each_sequence(enter)
                turned(0)
            if array == 1 and ends[1] == chunk:
                each_sequence(mixer)
                turned(1)
            if array == 2 and ends[2] == chunk:
                each_sequence(mixer_out)
                turned(2)
            if array == 3:
                tiles(start, width, expand)
            if array == 4:
                for half in (0, 1):
                    reduce_on(half * (hidden // 2) + start, width)

    def on_chunk(chunk):
        if chunk == ends[0]:
            fed()
        as_it_comes(chunk)

    gather(on_chunk)

    @pl.when(here.first_layer)
    def _():
        layer_done()
        for m in range(micro):
            give(out_low, m).start()
            give(out_low, m).wait_send()
        gathered()
        for m in range(micro):
            received(e_in, m)
        turned(3)

    @pl.when(here.second_layer)
    def _():
        small_weights()
        e_in[...] = feed[...]
        turned(3)
        gathered()
        each_sequence(functools.partial(received, x_in), enter, mixer, mixer_out)

        tiles(0, hidden, expand)
        reduce_on(0, hidden)
        layer_done()

    offsets, place = [], 0
    for array, _, width, _ in put_table:
        offsets.append(place)
        place += width if array in (1, 2, 3) else 0

    def one_in(chunk, z):
        array, start, width, _ = put_table[chunk]
        if array == 0:
            return one_small.at[z]
        if array == 4:
            return one_down.at[z, :, :, pl.ds(start, width)]
        return weight[3].at[z, 0, :, :, pl.ds(offsets[chunk], width)]

    def two_in(chunk, z):
        array, start, width, _ = put_table[chunk]
        if array == 0:
            return two_small.at[z]
        if array == 4:
            return two_down.at[z, :, pl.ds(start, width)]
        return weight[3].at[z, 1, 0, :, pl.ds(offsets[chunk], width)]

    def put_first(chunk, step):
        z = far(step)
        if step % 2:
            source, side = mine[chunk].at[z, :, 1 - here.x], here.x_side()
        else:
            source, side = mine[chunk].at[z, 1 - here.y], here.y_side()
        return remote(source, one_in(chunk, step), one_send.at[chunk, step], one_recv.at[chunk, step], side)

    def put_second(chunk, step):
        z = far(step)
        if step % 2:
            source, side = mine[chunk].at[z, 1 - here.y, here.x], here.y_side()
        else:
            source, side = mine[chunk].at[z, here.y, 1 - here.x], here.x_side()
        return remote(source, two_in(chunk, step), two_send.at[chunk, step], two_recv.at[chunk, step], side)

    def put_third(chunk, step, act):
        z = far(step)
        source = mine[chunk].at[z, here.y, here.x]
        target = landed[put_table[chunk][0]].at[here.home, :, columns(put_table, chunk, here.core)]
        receive = z_recv.at[chunk, here.home, here.core]
        own = (here.z == z) & (here.core == here.layer)
        if act == "start":

            @pl.when(own)
            def _():
                pltpu.make_async_copy(source, target, receive).start()

        @pl.when(jnp.logical_not(own))
        def _():
            away = remote(source, target, z_send.at[chunk, step], receive, (here.layer, here.chip(z=z)))
            getattr(away, act)()

    def add(target, other):
        target[...] = (target[...].astype(f32) + other[...].astype(f32)).astype(target.dtype)

    def both_sides(array):
        if array:
            left_copy(array - 1).wait_recv()
            right_copy(array - 1).wait_recv()
        else:
            small_copy().wait_recv()

    def terms(chunk, wait=False):
        array, start, width, shared = put_table[chunk]
        if array == 0:
            if wait:
                both_sides(array)
            block = (small_terms[here.core] + other_small[...]).T
        else:
            source, other = right_sides(array - 1)
            own_at = pl.multiple_of(here.core * (widths[array] // 2) + start, 128)
            block = left_dot(lefts[array - 1][0], source[:, pl.ds(own_at, width)])
            if wait:
                both_sides(array)
            block += left_dot(lefts[array - 1][1], other[:, pl.ds(start, width)])
        block = block.astype(low)
        rows = features // 16
        for z in range(4):
            for k in range(4):
                at = (z * 4 + k) * rows
                mine[chunk][z, k // 2, k % 2] = block[at : at + rows]
        if not shared:
            for step in range(4):
                put_first(chunk, step).start()
            return

        @pl.when(here.second_layer)
        def _():
            for step in range(4):
                put_first(chunk, step).start()

        @pl.when(here.first_layer)
        def _():
            if not any(entry[3] for entry in put_table[:chunk]):
                pl.semaphore_wait(ready_mid, 1)
            put_middle(chunk).start()

    def put_middle(chunk):
        source = mine[chunk].at[pl.ds(2 * (1 - here.home), 2)]
        return remote(source, mid_in(chunk), mid_send.at[chunk], mid_recv.at[chunk], here.middle())

    def mid_in(chunk):
        _, start, width, _ = put_table[chunk]
        return weight[4].at[pl.ds(0, 2), :, :, :, pl.ds(start, width)]

    def sum_middle(chunk):
        put_middle(chunk).wait_recv()
        for z in range(2):
            for k in range(4):
                add(mine[chunk].at[2 * here.home + z, k // 2, k % 2], mid_in(chunk).at[z, k // 2, k % 2])
        for step in range(4):
            when(at_home(far(step)), lambda: put_first(chunk, step).start())

    def sum_one(chunk):
        for step in range(4):

            def action():
                z = far(step)
                put_first(chunk, step).wait_recv()
                for k in range(2):
                    if step % 2:
                        add(mine[chunk].at[z, k, here.x], one_in(chunk, step).at[k])
                    else:
                        add(mine[chunk].at[z, here.y, k], one_in(chunk, step).at[k])
                put_second(chunk, step).start()

            when(handled(put_table, chunk, far(step)), action)

    def sum_two(chunk):
        for step in range(4):

            def action():
                put_second(chunk, step).wait_recv()
                add(mine[chunk].at[far(step), here.y, here.x], two_in(chunk, step))
                put_third(chunk, step, "start")

            when(handled(put_table, chunk, far(step)), action)

    last = len(put_table)
    needs = {array: min(k for k, entry in enumerate(put_table) if entry[0] == array) for array in range(5)}
    down = [chunk for chunk in range(last) if put_table[chunk][0] == 4]

    @pl.when(here.first_layer)
    def _():
        for chunk in down:
            terms(chunk, wait=chunk == down[0])

    def expand_back(start):
        again = pl.multiple_of(hidden + start, 128)
        grad_act = left_dot(e_in[...], matrix(4, start, tile))
        gate = expanded[:, pl.ds(start, tile)].astype(f32)
        up = expanded[:, pl.ds(again, tile)].astype(f32)
        sig = sigmoid(gate)
        grad_gate = (grad_act * up * (sig * (1.0 + gate * (1.0 - sig)))).astype(low)
        grad_up = (grad_act * (gate * sig)).astype(low)
        expanded[:, pl.ds(start, tile)] = grad_gate
        expanded[:, pl.ds(again, tile)] = grad_up

    tiles(0, hidden, expand_back)
    total[...] = dot_back(expanded[...], matrix(3, 0, 2 * hidden))
    right_copy(2).start()
    for side in (here.x_side(), here.y_side()):
        pl.semaphore_signal(ready, inc=1, device_id=side, device_id_type=MESH)
    if any(entry[3] for entry in put_table):

        @pl.when(here.first_layer)
        def _():
            pl.semaphore_signal(ready_mid, inc=1, device_id=here.middle(), device_id_type=MESH)


    def norm_grad(rows, grad, normal, scale, gain, at):
        n = normal[rows]
        small_terms[1, at : at + 1] += jnp.sum(grad * n, axis=0, keepdims=True)
        q = grad * gain
        back = q - jnp.mean(q, axis=1, keepdims=True) - n * jnp.mean(q * n, axis=1, keepdims=True)
        return scale[rows][:, :1] * back

    def after_back():
        small_terms[...] = jnp.zeros_like(small_terms)

        def body(rows):
            grad = e_in[rows].astype(f32) + norm_grad(rows, total[rows], norm_two, scale_two, rows8[4:5], 4)
            after[rows] = grad
            after_low[rows] = grad.astype(low)

        in_rows(body)
        right_copy(1).start()

    def gated_back():
        total[...] = dot_back(after_low[...], matrix(2, 0, features))

    def mix_back(m, rows, taken, cut):
        taps = [rows8[j : j + 1, taken] for j in range(3)]
        alive = live_rows(m)
        grad = total[rows, taken]
        projected[rows, taken] = (grad * convolved[rows, taken]).astype(low)
        spec = left_dot(dft[...], parts(grad * queries[rows, taken]))
        g_re, g_im = spec[:slots], spec[slots:]
        pairs = []
        for other in (kernel_spec, value_spec):
            o_re, o_im = other[m, :slots, taken], other[m, slots:, taken]
            both = o_im * g_im
            re = o_re * g_re + jnp.where(first_row, 0.0, both)
            im = jnp.where(first_row, both, o_re * g_im - o_im * g_re)
            pairs.append(jnp.concatenate([re, im], axis=0))
        paired = left_dot(idft[...], parts(jnp.concatenate(pairs, axis=1)))
        at_values = pl.ds(pl.multiple_of(2 * features + cut * 256, 256), 256)
        projected[rows, at_values] = (paired[:, :256] * alive).astype(low)
        grad_kernel = paired[:, 256:]
        small_terms[0, :, taken] += grad_kernel
        k = keys[rows, taken]
        for j in range(3):
            moved = later(k, j) if j else k
            small_terms[1, j : j + 1, taken] += jnp.sum(grad_kernel * moved, axis=0, keepdims=True)
        grad_keys = taps[0] * grad_kernel + taps[1] * sooner(grad_kernel, 1) + taps[2] * sooner(grad_kernel, 2)
        at_keys = pl.ds(pl.multiple_of(features + cut * 256, 256), 256)
        projected[rows, at_keys] = (grad_keys * alive).astype(low)

    def mixed_back(m):
        mixer_blocks(m, mix_back)

    def input_back(m):
        rows = sequence(m)
        total[rows] = dot_back(projected[rows], matrix(1, 0, 3 * features))

        def body(rows):
            grad = after[rows] + norm_grad(rows, total[rows], norm_one, scale_one, rows8[3:4], 3)
            grad_low[rows] = grad.astype(low)

        in_rows(body, m * slots, slots)

    pieces = [after_back, gated_back]
    for m in range(micro):
        pieces += [functools.partial(mixed_back, m), functools.partial(input_back, m)]

    def last_copies():
        right_copy(0).start()
        small_copy().start()

    pieces += [last_copies]

    @pl.when(here.second_layer)
    def _():
        after_back()
        gated_back()
        for m in range(micro):
            mixed_back(m)
            input_back(m)
            if m == micro - 1:
                terms(down[0], wait=True)
            if m:
                give(grad_low, m - 1).wait_send()
            give(grad_low, m).start()
        last_copies()
        turned(2)
        for chunk in down[1:]:
            terms(chunk)
        turned(1)
        turned(0)

    pl.semaphore_wait(ready, 2)

    def one_sum(act):
        @pl.when(here.core == 0)
        def _():
            for chunk, (array, _, width, shared) in enumerate(put_table):
                for half in range(2 if shared else 0):
                    target = landed[array].at[1 - here.home, :, columns(put_table, chunk, half)]
                    copy = pltpu.make_async_copy(nothing.at[:, pl.ds(0, width)], target, nothing_sems.at[chunk, half])
                    getattr(copy, act)()

    nothing[...] = jnp.zeros_like(nothing)
    one_sum("start")

    apart = here.core != here.layer
    over = (1 - here.core, here.partner)

    def swap(source, target, number, act):
        sems = swap_sems.at[number], swap_sems.at[number + 1]

        @pl.when(apart)
        def _():
            getattr(remote(source, target, *sems, over), act)()

        @pl.when(jnp.logical_not(apart))
        def _():
            getattr(pltpu.make_async_copy(source, target, sems[1]), act)()

    due = [max(0, needs[1] - len(pieces) + k) for k in range(len(pieces))]
    shared = [chunk for chunk in range(last) if put_table[chunk][3]]
    met = [4]

    swap(out_low, kept_out, 0, "start")
    for now in range(last + 1):
        for piece, at in zip(pieces, due):
            if at == now:
                pl.when(here.first_layer)(piece)
        early = shared if now == 1 else []
        for chunk in early + [now + 1]:
            if chunk < last and chunk not in down and (chunk not in shared or chunk in early):
                terms(chunk, wait=put_table[chunk][0] not in met)
                met.append(put_table[chunk][0])
        for chunk in shared:
            if now == chunk - 2:
                pl.when(here.first_layer)(functools.partial(sum_middle, chunk))
        if now < last:
            sum_one(now)
        if 1 <= now:
            sum_two(now - 1)
        if now == needs[0]:
            swap(grad_low, kept_grad, 2, "start")

    one_sum("wait")
    for chunk in range(last):
        for half in (0, 1):
            for slot in (0, 1):
                target = landed[put_table[chunk][0]].at[slot, :, columns(put_table, chunk, half)]
                wanted = (here.core == 1) | (here.home == slot) if put_table[chunk][3] else True
                when(wanted, functools.partial(arrived, target, z_recv.at[chunk, slot, half]))
        for step in range(4):

            def action():
                put_first(chunk, step).wait_send()
                put_second(chunk, step).wait_send()
                put_third(chunk, step, "wait_send")

            when(handled(put_table, chunk, far(step)), action)
        if put_table[chunk][3]:
            pl.when(here.first_layer)(lambda: put_middle(chunk).wait_send())

    @pl.when(own_feed)
    def _():
        remote(hidden_in, feed, feed_sems.at[1], feed_sems.at[0], partner).wait_send()
        remote(live_own, live, feed_sems.at[3], feed_sems.at[2], partner).wait_send()

    for k in range(4):
        left_copy(k).wait_send()
        right_copy(k).wait_send()
    small_copy().wait_send()
    pl.when(here.second_layer)(lambda: give(grad_low, micro - 1).wait_send())
    swap(out_low, kept_out, 0, "wait")
    swap(grad_low, kept_grad, 2, "wait")


def finish_kernel(*refs):
    landed, (out, grad) = refs[:5], refs[5:7]
    s_filters, s_taps, s_one, s_two = refs[7:11]
    sums, (to_out, to_grad) = refs[11:15], refs[15:17]
    to_out[...] = out[...]
    to_grad[...] = grad[...]
    small = landed[0][0].astype(jnp.float32) + landed[0][1].astype(jnp.float32)
    s_filters[...] = small[:, :128]
    own = small.shape[0]
    rows = jnp.pad(small[:, 128:], ((0, 128 - own), (0, 0))).T
    for j in range(3):
        s_taps[j] = rows[j : j + 1, :own]
    s_one[...] = rows[3:4, :own]
    s_two[...] = rows[4:5, :own]
    for number, result in enumerate(sums):
        result[...] = landed[1 + number][0].astype(jnp.float32) + landed[1 + number][1].astype(jnp.float32)


def fast_device(
    hidden_in, out_grad, lengths, gain_mixer, w_input, w_taps, filters, w_output, gain_mlp, w_gate_up, w_down
):
    micro, _, slots, features = hidden_in.shape
    tokens, rows = micro * slots, gain_mixer.shape[1]
    shards = (w_input[0], w_output[0], w_gate_up[0], w_down[0].T)
    widths = [256] + [shard.shape[1] for shard in shards]
    hidden = widths[4]
    get_table, put_table = chunks_of(GET_PIECES), chunks_of(PUT_PIECES)
    dft, idft = (jnp.asarray(table) for table in packed_tables(slots))
    low, f32 = jnp.bfloat16, jnp.float32
    anywhere = pl.BlockSpec(memory_space=pl.ANY)
    inside = pl.BlockSpec(memory_space=pltpu.VMEM)
    dma, vmem = pltpu.SemaphoreType.DMA, pltpu.VMEM
    act, act_low = (tokens, features), vmem((tokens, features), low)
    kinds = [jax.ShapeDtypeStruct((2, rows, width), low) for width in widths]
    kinds += [jax.ShapeDtypeStruct((tokens, features), low)] * 2
    room = [vmem((rows, 256), low), vmem((128, 128), f32)] + [vmem((micro, 8, 128), f32)] * 2
    room += [vmem((rows, max(entry[2] for entry in put_table)), low), dma((len(put_table), 2))]
    room += [vmem((4, 2, 2, rows, width), low) for width in widths]
    room += [act_low] * 6
    room += [vmem((slots, features), f32), vmem((8, features), f32), vmem(act, f32), vmem(act, f32)]
    room += [vmem((tokens, 128), f32)] * 2
    room += [act_low] * 3 + [vmem(act, f32)] * 4 + [vmem((micro, 2 * slots, features), f32)] * 2
    room += [vmem(act, f32)] * 2 + [vmem((tokens, 2 * hidden), low), vmem((tokens, hidden), low)]
    room += [vmem((tokens, 3 * features), low), act_low, vmem((2, slots, features), f32)]
    room += [vmem((2, features, tokens), low)] * 4
    room += [vmem((slots, features), f32)] + [vmem((tokens, width // 2), low) for width in widths[1:]]
    room += [vmem((4, 2, 2, rows, entry[2]), low) for entry in put_table]
    for width in (128, hidden // 2):
        room += [vmem((4, 2, rows, width), low), vmem((4, rows, width), low)]
    got, put = len(get_table), len(put_table)
    room += [dma((got, 2, 2))] + [dma((got, 4))] * 5 + [dma((got, 2))] * 2 + [dma((got,))] * 2 + [dma((4,))]
    room += [dma((4,)), dma((micro,)), dma((micro,)), dma((9,)), dma((9,))]
    room += [dma((put, 4))] * 5 + [dma((put, 2, 2))] + [dma((put,))] * 2 + [pltpu.SemaphoreType.REGULAR] * 2
    results = pl.pallas_call(
        functools.partial(layer_kernel, get_table, put_table, widths),
        out_shape=kinds,
        in_specs=[inside] * 4 + [pl.BlockSpec(memory_space=pltpu.SMEM)] + [inside] * 2 + [anywhere] * 6,
        out_specs=[anywhere] * 7,
        scratch_shapes=room,
        compiler_params=pltpu.CompilerParams(
            collective_id=0, has_side_effects=True, vmem_limit_bytes=62 * 1024 * 1024
        ),
    )(
        filters[0].T,
        w_taps[0],
        gain_mixer,
        gain_mlp,
        lengths.T,
        dft,
        idft,
        *shards,
        hidden_in.reshape(tokens, features),
        out_grad.reshape(tokens, features),
    )
    kinds = [(rows, 128), (3, 1, rows), (1, rows), (1, rows)] + [(rows, width) for width in widths[1:]]
    kinds = [jax.ShapeDtypeStruct(kind, f32) for kind in kinds] + kinds_of(results[5:])
    s_filters, s_taps, s_one, s_two, s_in, s_out, s_gu, s_dt, layer_out, input_grad = pl.pallas_call(
        finish_kernel,
        out_shape=kinds,
        in_specs=[inside] * 7,
        out_specs=[inside] * 10,
        compiler_params=pltpu.CompilerParams(vmem_limit_bytes=62 * 1024 * 1024),
    )(*results)
    shape = (1, micro, 1, slots, features)
    return (
        layer_out.reshape(shape),
        input_grad.reshape(shape),
        s_one,
        s_in[None],
        s_taps.transpose(1, 0, 2),
        s_filters.T[None],
        s_out[None],
        s_two,
        s_gu[None],
        s_dt.T[None],
    )


def kinds_of(arrays):
    return [jax.ShapeDtypeStruct(array.shape, array.dtype) for array in arrays]


def solution(mesh):
    placed = (
        P(None, "dp", None, None),
        P(None, "dp", None, None),
        P(None, "dp"),
        P("section", "dp"),
        P("section", "dp", None),
        P("section", None, "dp"),
        P("section", None, "dp"),
        P("section", "dp", None),
        P("section", "dp"),
        P("section", "dp", None),
        P("section", None, "dp"),
    )
    return jax.shard_map(
        fast_device if mesh.shape["dp"] == 16 and mesh.shape["section"] == 2 else on_device,
        mesh=mesh,
        in_specs=placed,
        out_specs=(
            P("section", None, "dp", None, None),
            P("section", None, "dp", None, None),
            P("section", "dp"),
            P("section", "dp", None),
            P("section", None, "dp"),
            P("section", None, "dp"),
            P("section", "dp", None),
            P("section", "dp"),
            P("section", "dp", None),
            P("section", None, "dp"),
        ),
        check_vma=False,
    )
```

```python
import functools
import math

import jax
import jax.numpy as jnp
import ml_dtypes
import numpy as np
from jax import lax
from jax.experimental import pallas as pl
from jax.experimental.pallas import tpu as pltpu
from jax.sharding import PartitionSpec as P

MESH = pl.DeviceIdType.MESH

epsilon = 1e-05
GET_PIECES = (
    (0, 128, False),
    (1, 384, False),
    (1, 384, False),
    (1, 384, False),
    (2, 384, False),
    (3, 1024, False),
    (3, 1024, False),
    (3, 1024, False),
    (4, 512, False),
    (4, 512, False),
    (4, 512, False),
)
PUT_PIECES = (
    (4, 768, False),
    (4, 768, False),
    (3, 1024, False),
    (3, 1024, False),
    (1, 384, False),
    (1, 384, False),
    (0, 128, False),
    (1, 384, False),
    (2, 384, False),
    (3, 512, True),
    (3, 512, True),
)
GET_LAGS = (5, 7, 1, 2, 3)
ROWS_UNROLL = 2
MIX_UNROLL = 3
TILE_UNROLL = 2


def passed_along(value, axis, steps):
    count = lax.axis_size(axis)
    first, last = (max(0, -steps), min(count, count - steps))
    return lax.ppermute(value, axis, [(source, source + steps) for source in range(first, last)])


def split_dot(left_side, right_side):
    return jnp.dot(
        left_side, right_side, precision=lax.Precision.HIGH, preferred_element_type=jnp.float32
    )


def split_rows(left_side, right_side):
    return lax.dot_general(
        left_side,
        right_side,
        (((0,), (0,)), ((), ())),
        precision=lax.Precision.HIGH,
        preferred_element_type=jnp.float32,
    )


def dot_rows(left_side, right_side):
    return lax.dot_general(
        left_side, right_side, (((0,), (0,)), ((), ())), preferred_element_type=jnp.float32
    )


def dot_back(left_side, right_side):
    return lax.dot_general(
        left_side, right_side, (((1,), (1,)), ((), ())), preferred_element_type=jnp.float32
    )


def tables(length):
    period = 2 * length
    freq_index = lax.broadcasted_iota(jnp.int32, (length + 1, length), 0)
    time_index = lax.broadcasted_iota(jnp.int32, (length + 1, length), 1)
    angles = (freq_index * time_index % period).astype(jnp.float32) * (2.0 * math.pi / period)
    edge_rows = (freq_index[:, :1] == 0) | (freq_index[:, :1] == length)
    inverse_weight = jnp.where(edge_rows, 1.0, 2.0) / period
    dft_stack = jnp.concatenate([jnp.cos(angles), -jnp.sin(angles)], axis=0)
    return (dft_stack, inverse_weight)


def spectrum(dft_tables, signal):
    dft_stack, inverse_weight = dft_tables
    stacked_out = split_dot(dft_stack, signal)
    middle_row = stacked_out.shape[0] // 2
    return (stacked_out[:middle_row], stacked_out[middle_row:])


def inverse(dft_tables, real_part, imag_part):
    dft_stack, inverse_weight = dft_tables
    return split_rows(
        dft_stack, jnp.concatenate([inverse_weight * real_part, inverse_weight * imag_part], axis=0)
    )


def normalize(input_rows):
    centered = input_rows - jnp.mean(input_rows, axis=1, keepdims=True)
    inv_scale = lax.rsqrt(jnp.mean(centered * centered, axis=1, keepdims=True) + epsilon)
    return (centered * inv_scale, inv_scale)


def norm_back(grad_normed, normed, inv_scale):
    return inv_scale * (
        grad_normed
        - jnp.mean(grad_normed, axis=1, keepdims=True)
        - normed * jnp.mean(grad_normed * normed, axis=1, keepdims=True)
    )


def delayed(input_rows, places):
    return jnp.pad(input_rows, ((places, 0), (0, 0)))[: input_rows.shape[0]]


def advanced(input_rows, places):
    return jnp.pad(input_rows, ((0, places), (0, 0)))[places:]


def layer_forward(input_rows, active_rows, weights, dft_tables):
    gain_one, w_inner, w_tap_rows, filt_static, w_outer, gain_two, w_expand, w_reduce = weights
    hidden_size_model = w_outer.shape[0]
    hidden_width = w_reduce.shape[0]
    tap_weights = w_tap_rows.astype(jnp.float32)
    normed_one, scale_one = normalize(input_rows)
    entered = (normed_one * gain_one.astype(jnp.float32)).astype(jnp.bfloat16)
    projected = jnp.dot(entered, w_inner, preferred_element_type=jnp.float32)
    queries = projected[:, :hidden_size_model]
    keys_part = projected[:, hidden_size_model : 2 * hidden_size_model] * active_rows
    values_part = projected[:, 2 * hidden_size_model :] * active_rows
    dynamic = (
        tap_weights[0] * keys_part
        + tap_weights[1] * delayed(keys_part, 1)
        + tap_weights[2] * delayed(keys_part, 2)
    )
    kernel = filt_static.astype(jnp.float32) + dynamic
    joint_re, joint_im = spectrum(dft_tables, jnp.concatenate([values_part, kernel], axis=1))
    value_re = joint_re[:, :hidden_size_model]
    kernel_re = joint_re[:, hidden_size_model:]
    value_im = joint_im[:, :hidden_size_model]
    kernel_im = joint_im[:, hidden_size_model:]
    convolved = inverse(
        dft_tables,
        kernel_re * value_re - kernel_im * value_im,
        kernel_re * value_im + kernel_im * value_re,
    )
    gated_rows = (queries * convolved).astype(jnp.bfloat16)
    after_mixer = input_rows + jnp.dot(gated_rows, w_outer, preferred_element_type=jnp.float32)
    normed_two, scale_two = normalize(after_mixer)
    entered_two = (normed_two * gain_two.astype(jnp.float32)).astype(jnp.bfloat16)
    expanded = jnp.dot(entered_two, w_expand, preferred_element_type=jnp.float32)
    gate_part = expanded[:, :hidden_width]
    up_part = expanded[:, hidden_width:]
    activated = (jax.nn.silu(gate_part) * up_part).astype(jnp.bfloat16)
    result = after_mixer + jnp.dot(activated, w_reduce, preferred_element_type=jnp.float32)
    stash = (
        normed_one,
        scale_one,
        entered,
        queries,
        keys_part,
        (value_re, value_im, kernel_re, kernel_im),
        convolved,
        gated_rows,
        normed_two,
        scale_two,
        entered_two,
        gate_part,
        up_part,
        activated,
    )
    return (result, stash)


def mlp_backward(received_gradient, weights, stash):
    gain_one, w_inner, w_tap_rows, filt_static, w_outer, gain_two, w_expand, w_reduce = weights
    (
        normed_one,
        scale_one,
        entered,
        queries,
        keys_part,
        spectra,
        convolved,
        gated_rows,
        normed_two,
        scale_two,
        entered_two,
        gate_part,
        up_part,
        activated,
    ) = stash
    grad_low = received_gradient.astype(jnp.bfloat16)
    grad_reduce_w = dot_rows(activated, grad_low)
    grad_act = dot_back(grad_low, w_reduce)
    sigmoid_gate = jax.nn.sigmoid(gate_part)
    grad_gate = grad_act * up_part * (sigmoid_gate * (1.0 + gate_part * (1.0 - sigmoid_gate)))
    grad_up = grad_act * (gate_part * sigmoid_gate)
    grad_expand = jnp.concatenate([grad_gate, grad_up], axis=1).astype(jnp.bfloat16)
    grad_expand_w = dot_rows(entered_two, grad_expand)
    grad_entered_two = dot_back(grad_expand, w_expand)
    grad_gain_two = jnp.sum(grad_entered_two * normed_two, axis=0)
    grad_after = received_gradient + norm_back(
        grad_entered_two * gain_two.astype(jnp.float32), normed_two, scale_two
    )
    return (grad_after, (grad_gain_two, grad_expand_w, grad_reduce_w))


def mixer_backward(grad_after, active_rows, weights, dft_tables, stash):
    gain_one, w_inner, w_tap_rows, filt_static, w_outer, gain_two, w_expand, w_reduce = weights
    (
        normed_one,
        scale_one,
        entered,
        queries,
        keys_part,
        spectra,
        convolved,
        gated_rows,
        normed_two,
        scale_two,
        entered_two,
        gate_part,
        up_part,
        activated,
    ) = stash
    value_re, value_im, kernel_re, kernel_im = spectra
    hidden_size_model = w_outer.shape[0]
    tap_weights = w_tap_rows.astype(jnp.float32)
    grad_mix_low = grad_after.astype(jnp.bfloat16)
    grad_outer_w = dot_rows(gated_rows, grad_mix_low)
    grad_gated = dot_back(grad_mix_low, w_outer)
    grad_queries = grad_gated * convolved
    grad_conv = grad_gated * queries
    grad_re, grad_im = spectrum(dft_tables, grad_conv)
    paired_re = jnp.concatenate(
        [kernel_re * grad_re + kernel_im * grad_im, value_re * grad_re + value_im * grad_im], axis=1
    )
    paired_im = jnp.concatenate(
        [kernel_re * grad_im - kernel_im * grad_re, value_re * grad_im - value_im * grad_re], axis=1
    )
    paired = inverse(dft_tables, paired_re, paired_im)
    grad_values = paired[:, :hidden_size_model] * active_rows
    grad_kernel = paired[:, hidden_size_model:]
    grad_taps = jnp.stack(
        [
            jnp.sum(grad_kernel * keys_part, axis=0),
            jnp.sum(grad_kernel * delayed(keys_part, 1), axis=0),
            jnp.sum(grad_kernel * delayed(keys_part, 2), axis=0),
        ]
    )
    grad_keys = (
        tap_weights[0] * grad_kernel
        + tap_weights[1] * advanced(grad_kernel, 1)
        + tap_weights[2] * advanced(grad_kernel, 2)
    ) * active_rows
    grad_projected = jnp.concatenate([grad_queries, grad_keys, grad_values], axis=1).astype(
        jnp.bfloat16
    )
    inner_weight_gradient = dot_rows(entered, grad_projected)
    grad_entered = dot_back(grad_projected, w_inner)
    grad_gain_one = jnp.sum(grad_entered * normed_one, axis=0)
    grad_inputs = grad_after + norm_back(
        grad_entered * gain_one.astype(jnp.float32), normed_one, scale_one
    )
    return (
        grad_inputs,
        (grad_gain_one, inner_weight_gradient, grad_taps, grad_kernel, grad_outer_w),
    )


def add_terms(received, flipped):
    return tuple(
        (
            jnp.sum(member, axis=0).T if flip else jnp.sum(member, axis=0)
            for member, flip in zip(received, flipped)
        )
    )


def on_device(
    hidden_in,
    out_grad,
    lengths,
    gain_mixer,
    w_input,
    w_taps,
    filters,
    w_output,
    gain_mlp,
    w_gate_up,
    w_down,
):
    first_section = lax.axis_index("section") == 0
    micro_count = hidden_in.shape[0]
    seq_slots = hidden_in.shape[2]
    hidden_size_model = hidden_in.shape[3]
    dft_tables = tables(seq_slots)
    positions = lax.broadcasted_iota(jnp.int32, (seq_slots, 1), 0)
    weights = (
        lax.all_gather(gain_mixer[0], "dp", axis=0, tiled=True),
        lax.all_gather(w_input[0], "dp", axis=0, tiled=True),
        lax.all_gather(w_taps[0], "dp", axis=1, tiled=True),
        lax.all_gather(filters[0], "dp", axis=1, tiled=True),
        lax.all_gather(w_output[0], "dp", axis=0, tiled=True),
        lax.all_gather(gain_mlp[0], "dp", axis=0, tiled=True),
        lax.all_gather(w_gate_up[0], "dp", axis=0, tiled=True),
        lax.all_gather(w_down[0], "dp", axis=1, tiled=True),
    )
    arriving = jnp.zeros((seq_slots, hidden_size_model), jnp.bfloat16)
    outgoing_list = []
    saved_activations = []
    for forward_step in range(micro_count + 1):
        own_index = min(forward_step, micro_count - 1)
        prior_index = max(forward_step - 1, 0)
        input_rows = jnp.where(first_section, hidden_in[own_index, 0], arriving).astype(jnp.float32)
        length_now = jnp.where(first_section, lengths[own_index, 0], lengths[prior_index, 0])
        active_rows = (positions < length_now).astype(jnp.float32)
        result, stash = layer_forward(input_rows, active_rows, weights, dft_tables)
        outgoing = result.astype(jnp.bfloat16)
        outgoing_list.append(outgoing)
        if forward_step < micro_count:
            arriving = passed_along(outgoing, "section", 1)
        saved_activations.append((input_rows, active_rows))
    coming = jnp.zeros((seq_slots, hidden_size_model), jnp.bfloat16)
    mlp_totals = None
    mixer_totals = None
    grads_out = []
    for backward_step in range(micro_count + 1):
        saved_slot_index = micro_count - backward_step
        last_index = max(micro_count - 1 - backward_step, 0)
        live_factor = 1.0 if backward_step < micro_count else 0.0
        received_gradient = jnp.where(
            first_section,
            coming.astype(jnp.float32),
            out_grad[last_index, 0].astype(jnp.float32) * live_factor,
        )
        input_rows, active_rows = saved_activations[saved_slot_index]
        result, stash = layer_forward(input_rows, active_rows, weights, dft_tables)
        grad_after, mlp_grads = mlp_backward(received_gradient, weights, stash)
        mlp_totals = (
            mlp_grads if mlp_totals is None else jax.tree.map(jnp.add, mlp_totals, mlp_grads)
        )
        grad_inputs, mixer_grads = mixer_backward(
            grad_after, active_rows, weights, dft_tables, stash
        )
        mixer_totals = (
            mixer_grads
            if mixer_totals is None
            else jax.tree.map(jnp.add, mixer_totals, mixer_grads)
        )
        outgoing = grad_inputs.astype(jnp.bfloat16)
        grads_out.append(outgoing)
        if backward_step < micro_count:
            coming = passed_along(outgoing, "section", -1)
    first_outputs = jnp.stack(outgoing_list[:micro_count])
    second_outputs = jnp.stack(outgoing_list[1:])
    layer_out = jnp.where(first_section, first_outputs, second_outputs)[None, :, None]
    first_grads = jnp.stack(
        [grads_out[micro_count - batch_index] for batch_index in range(micro_count)]
    )
    second_grads = jnp.stack(
        [grads_out[micro_count - 1 - batch_index] for batch_index in range(micro_count)]
    )
    input_grad = jnp.where(first_section, first_grads, second_grads)[None, :, None]
    all_parts = (
        lax.all_to_all(
            mixer_totals[0][None].astype(jnp.bfloat16),
            "dp",
            split_axis=1,
            concat_axis=0,
            tiled=True,
        ).astype(jnp.float32),
        lax.all_to_all(
            mixer_totals[1][None].astype(jnp.bfloat16),
            "dp",
            split_axis=1,
            concat_axis=0,
            tiled=True,
        ).astype(jnp.float32),
        lax.all_to_all(
            mixer_totals[2].T[None].astype(jnp.bfloat16),
            "dp",
            split_axis=1,
            concat_axis=0,
            tiled=True,
        ).astype(jnp.float32),
        lax.all_to_all(
            mixer_totals[3].T[None].astype(jnp.bfloat16),
            "dp",
            split_axis=1,
            concat_axis=0,
            tiled=True,
        ).astype(jnp.float32),
        lax.all_to_all(
            mixer_totals[4][None].astype(jnp.bfloat16),
            "dp",
            split_axis=1,
            concat_axis=0,
            tiled=True,
        ).astype(jnp.float32),
        lax.all_to_all(
            mlp_totals[0][None].astype(jnp.bfloat16), "dp", split_axis=1, concat_axis=0, tiled=True
        ).astype(jnp.float32),
        lax.all_to_all(
            mlp_totals[1][None].astype(jnp.bfloat16), "dp", split_axis=1, concat_axis=0, tiled=True
        ).astype(jnp.float32),
        lax.all_to_all(
            mlp_totals[2].T[None].astype(jnp.bfloat16),
            "dp",
            split_axis=1,
            concat_axis=0,
            tiled=True,
        ).astype(jnp.float32),
    )
    summed = add_terms(all_parts, (False, False, True, True, False, False, False, True))
    return (
        layer_out,
        input_grad,
        summed[0][None],
        summed[1][None],
        summed[2][None],
        summed[3][None],
        summed[4][None],
        summed[5][None],
        summed[6][None],
        summed[7][None],
    )


class Place:
    def __init__(self):
        self.core = lax.axis_index("section")
        self.index = lax.axis_index("dp")
        self.z = self.index // 4
        self.y = self.index // 2 % 2
        self.x = self.index % 2
        self.layer = 1 - (self.z + 1) // 2 % 2
        self.home = self.z // 2
        self.first_layer = self.layer == 0
        self.second_layer = self.layer == 1
        self.partner = self.chip(z=self.z + 1 - 2 * (self.z % 2))

    def chip(self, z=None, y=None, x=None):
        z, y, x = (a if a is not None else b for a, b in ((z, self.z), (y, self.y), (x, self.x)))
        return z * 4 + y * 2 + x

    def x_side(self):
        return (self.core, self.chip(x=1 - self.x))

    def y_side(self):
        return (self.core, self.chip(y=1 - self.y))

    def sibling(self):
        return (1 - self.core, self.index)

    def middle(self):
        return (self.core, self.chip(z=3 - self.z))

    def greet(self):
        barrier = pltpu.get_barrier_semaphore()
        others = [self.x_side(), self.y_side(), self.sibling()]
        for step in (1, 2, 3):
            chip = self.chip(z=(self.z + step) % 4)
            others += [(0, chip), (1, chip)]
        for other in others:
            pl.semaphore_signal(barrier, inc=1, device_id=other, device_id_type=MESH)
        pl.semaphore_wait(barrier, len(others))


def remote(source, target, send, receive, device):
    return pltpu.make_async_remote_copy(
        src_ref=source,
        dst_ref=target,
        send_sem=send,
        recv_sem=receive,
        device_id=device,
        device_id_type=MESH,
    )


def chunks_of(pieces):
    table, places = [], {}
    for array, width, shared in pieces:
        start = places.get(array, 0)
        table.append((array, start, width, shared))
        places[array] = start + width
    return table


def left_dot(left_side, right_side):
    return lax.dot_general(
        left_side, right_side, (((1,), (0,)), ((), ())), preferred_element_type=jnp.float32
    )


def sigmoid(value):
    return 0.5 * jnp.tanh(0.5 * value) + 0.5


def parts(signal):
    high = signal.astype(jnp.bfloat16)
    rest = (signal - high.astype(jnp.float32)).astype(jnp.bfloat16)
    return jnp.concatenate([high, high, rest], axis=0)


def halves_of(table):
    high = table.astype(ml_dtypes.bfloat16)
    rest = (table - high.astype(np.float64)).astype(ml_dtypes.bfloat16)
    return np.concatenate([high, rest, high], axis=1)


def packed_tables(length):
    period = 2 * length
    freq, time = np.arange(length)[:, None], np.arange(length)[None, :]
    angles = (freq * time % period) * (2.0 * math.pi / period)
    sines = np.where(freq == 0, 1.0 - 2.0 * (time % 2), -np.sin(angles))
    table = np.concatenate([np.cos(angles), sines], axis=0)
    weight = np.where(np.arange(period)[:, None] % length == 0, 1.0, 2.0) / period
    return halves_of(table), halves_of((table * weight).T)


def layer_kernel(get_table, put_table, widths, *refs):
    refs = list(refs)

    def take(number):
        taken = refs[:number]
        del refs[:number]
        return taken

    filters_in, taps_in, gain_one_in, gain_two_in, lengths_in, dft, idft = take(7)
    shards, (hidden_in, grad_in) = [None] + take(4), take(2)
    landed, (kept_out, kept_grad) = take(5), take(2)
    own_small, rows_in, live_own, live, nothing, nothing_sems = take(6)
    weight = take(5)
    feed, arrive, x_in, e_in, out_low, grad_low = take(6)
    filt, rows8, norm_one, norm_two, scale_one, scale_two = take(6)
    entered, gated, again, queries, keys, values, convolved, value_spec, kernel_spec = take(9)
    total, after, expanded, active, projected, after_low, small_terms = take(7)
    lefts = take(4)
    other_small, other_projected, other_after, other_expanded, other_active = take(5)
    mine = take(len(put_table))
    one_small, two_small, one_down, two_down = take(4)
    get_z_send, get_z_recv, get_one_send, get_one_recv, get_two_send, get_two_recv = take(6)
    get_mid_send, get_mid_recv, get_side_send, get_side_recv, feed_sems = take(5)
    swap_sems, give_send, give_recv, send, recv = take(5)
    one_send, one_recv, two_send, two_recv, z_send, z_recv, mid_send, mid_recv, ready, ready_mid = take(10)

    here = Place()
    tokens, features = x_in.shape
    slots = filt.shape[0]
    micro = tokens // slots
    hidden = active.shape[1]
    f32, low = jnp.float32, jnp.bfloat16
    shards[0] = own_small

    here.greet()

    for m in range(micro):
        live_own[m] = jnp.full(live_own.shape[1:], lengths_in[0, m], jnp.int32).astype(f32)

    own_feed = here.core == here.layer
    partner = (here.core, here.partner)
    for layer, kept, given in ((0, hidden_in, grad_in), (1, grad_in, hidden_in)):

        @pl.when(own_feed & (here.layer == layer))
        def _():
            pltpu.make_async_copy(kept, feed, feed_sems.at[0]).start()
            pltpu.make_async_copy(live_own, live, feed_sems.at[2]).start()
            remote(given, feed, feed_sems.at[1], feed_sems.at[0], partner).start()
            remote(live_own, live, feed_sems.at[3], feed_sems.at[2], partner).start()

    def arrived(target, receive):
        pltpu.make_async_copy(target, target, receive).wait()

    def fed():
        arrived(feed, feed_sems.at[0])
        arrived(live, feed_sems.at[2])

    def small_shard():
        rows_in[...] = jnp.zeros_like(rows_in)
        own = taps_in.shape[1]
        rows_in[0:3, 0:own] = taps_in[...].astype(f32)
        rows_in[3:4, 0:own] = gain_one_in[...].astype(f32)
        rows_in[4:5, 0:own] = gain_two_in[...].astype(f32)
        own_small[:, :128] = filters_in[...]
        own_small[:, 128:] = rows_in[...].T[:own].astype(low)

    def columns(table, chunk, half):
        array, start, width, _ = table[chunk]
        return pl.ds(pl.multiple_of(half * (widths[array] // 2) + start, 128), width)

    def at_home(z):
        return z // 2 == here.home

    def when(condition, action):
        if condition is True:
            action()
        else:
            pl.when(condition)(action)

    def z_all(chunk, visit, near):
        array, _, _, shared = get_table[chunk]
        for number, plane in enumerate((1 - here.core, 2 + here.core)):
            wanted = (plane == here.z) if near else (plane != here.z)
            if shared:
                wanted = wanted & ((here.core == 1) | (here.home == number))
            for half in (0, 1):
                cut = columns(get_table, chunk, half)
                source, target = shards[array].at[:, cut], weight[array].at[here.z, here.y, here.x, :, cut]
                sems = get_z_send.at[chunk, number, half], get_z_recv.at[chunk, here.z]
                visit(wanted, here.core == half, source, target, sems, (half, here.chip(z=plane)))

    def z_start(chunk, near):
        def visit(wanted, own, source, target, sems, device):
            if not near:

                @pl.when(wanted)
                def _():
                    remote(source, target, *sems, device).start()

                return

            @pl.when(wanted & own)
            def _():
                pltpu.make_async_copy(source, target, sems[1]).start()

            @pl.when(wanted & jnp.logical_not(own))
            def _():
                remote(source, target, *sems, device).start()

        z_all(chunk, visit, near)

    def z_sent(chunk):
        for near in (False, True):

            def visit(wanted, own, source, target, sems, device):
                @pl.when(wanted & jnp.logical_not(own) if near else wanted)
                def _():
                    remote(source, target, *sems, device).wait_send()

            z_all(chunk, visit, near)

    def far(step):
        return (here.z + step) % 4

    def handled(table, chunk, z):
        return here.second_layer | at_home(z) if table[chunk][3] else True

    def get_first(chunk, step):
        block = weight[get_table[chunk][0]].at[far(step), here.y, here.x, :, columns(get_table, chunk, here.core)]
        side = here.y_side() if (step + chunk) % 2 else here.x_side()
        return remote(block, block, get_one_send.at[chunk, step], get_one_recv.at[chunk, step], side)

    def get_second(chunk, step):
        ref, cut = weight[get_table[chunk][0]], columns(get_table, chunk, here.core)
        if (step + chunk) % 2:
            pair, side = ref.at[far(step), :, here.x, :, cut], here.x_side()
        else:
            pair, side = ref.at[far(step), here.y, :, :, cut], here.y_side()
        return remote(pair, pair, get_two_send.at[chunk, step], get_two_recv.at[chunk, step], side)

    def get_middle(chunk, z):
        block = weight[get_table[chunk][0]].at[z, :, :, :, columns(get_table, chunk, here.core)]
        return remote(block, block, get_mid_send.at[chunk, z % 2], get_mid_recv.at[chunk, z % 2], here.middle())

    def get_across(chunk):
        whole = weight[get_table[chunk][0]].at[:, :, :, :, columns(get_table, chunk, here.core)]
        return remote(whole, whole, get_side_send.at[chunk], get_side_recv.at[chunk], here.sibling())

    def one_step(chunk, step):
        def action():
            z = far(step)
            block = weight[get_table[chunk][0]].at[z, here.y, here.x, :, columns(get_table, chunk, here.core)]
            arrived(block, get_z_recv.at[chunk, z])
            get_first(chunk, step).start()

        when(handled(get_table, chunk, far(step)), action)

    def two_steps(chunk, step):
        def action():
            get_first(chunk, step).wait_recv()
            get_second(chunk, step).start()

        when(handled(get_table, chunk, far(step)), action)

    def three_steps(chunk, step):
        def action():
            get_second(chunk, step).wait_recv()
            if get_table[chunk][3]:

                @pl.when(here.first_layer)
                def _():
                    get_middle(chunk, far(step)).start()

        when(handled(get_table, chunk, far(step)), action)

    def pass_on(chunk):
        if get_table[chunk][3]:

            @pl.when(here.first_layer)
            def _():
                for k in range(2):
                    get_middle(chunk, 2 * (1 - here.home) + k).wait_recv()

        get_across(chunk).start()

    def gather(on_chunk):
        last = len(get_table)
        ahead, own_ahead, two_lag, three_lag, done_lag = GET_LAGS
        for chunk in range(1, last):
            z_start(chunk, True)
        small_shard()
        z_start(0, True)

        def z_first():
            for chunk in range(min(ahead, last)):
                z_start(chunk, False)

        pl.when(here.core == 0)(z_first)
        for chunk in range(min(own_ahead, last)):
            one_step(chunk, 0)
        for chunk in range(min(own_ahead, last) - 1):
            two_steps(chunk, 0)
        pl.when(here.core == 1)(z_first)
        for now in range(last + done_lag + 1):
            if now + own_ahead < last:
                one_step(now + own_ahead, 0)
            if 0 <= now + own_ahead - 1 < last:
                two_steps(now + own_ahead - 1, 0)
            if now < last:
                for step in (1, 3, 2):
                    one_step(now, step)
            if now + ahead < last:
                z_start(now + ahead, False)
            if 0 <= now - two_lag < last:
                for step in (1, 3, 2):
                    two_steps(now - two_lag, step)
            if 0 <= now - three_lag < last:
                for step in range(4):
                    three_steps(now - three_lag, step)
                if not get_table[now - three_lag][3]:
                    pass_on(now - three_lag)
            if 0 <= now - three_lag - 1 < last and get_table[now - three_lag - 1][3]:
                pass_on(now - three_lag - 1)
            for chunk in (now - done_lag, now - done_lag - 1):
                if 0 <= chunk < last and get_table[chunk][3] == (chunk == now - done_lag - 1):
                    get_across(chunk).wait_recv()
                    on_chunk(chunk)

    def gathered():
        for chunk in range(len(get_table)):
            z_sent(chunk)
            for step in range(4):

                def action():
                    get_first(chunk, step).wait_send()
                    get_second(chunk, step).wait_send()

                when(handled(get_table, chunk, far(step)), action)
            if get_table[chunk][3]:

                @pl.when(here.first_layer)
                def _():
                    for k in range(2):
                        get_middle(chunk, 2 * here.home + k).wait_send()

            get_across(chunk).wait_send()

    def matrix(number, start, width):
        ref = weight[number]
        return ref[:, :, :, :, pl.ds(start, width)].reshape(features, width)

    alone = [True]

    def times(unroll):
        return unroll if alone[0] else 1

    def in_background(body):
        def whole():
            alone[0] = False
            body()
            alone[0] = True

        return whole

    def in_rows(body, start=0, count=tokens):
        block = 64

        def step(i, carry):
            body(pl.ds(pl.multiple_of(start + i * block, block), block))
            return carry

        lax.fori_loop(0, count // block, step, 0, unroll=times(ROWS_UNROLL))

    def sequence(m):
        return pl.ds(pl.multiple_of(m * slots, slots), slots)

    def normed(rows, rows_in, normal, scale, gain, target):
        centered = rows_in - jnp.mean(rows_in, axis=1, keepdims=True)
        inv = lax.rsqrt(jnp.mean(centered * centered, axis=1, keepdims=True) + epsilon)
        n = centered * inv
        normal[rows] = n
        scale[rows] = jnp.broadcast_to(inv, (n.shape[0], 128))
        target[rows] = (n * gain).astype(low)

    row_at = lax.broadcasted_iota(jnp.int32, (slots, 256), 0)
    first_row = row_at == 0

    def later(rows, places):
        return jnp.where(row_at >= places, pltpu.roll(rows, places, 0), 0.0)

    def sooner(rows, places):
        return jnp.where(row_at < slots - places, pltpu.roll(rows, slots - places, 0), 0.0)

    cuts = features // 256

    def mixer_blocks(m, body):
        def step(cut, carry):
            body(m, sequence(m), pl.ds(pl.multiple_of(cut * 256, 256), 256), cut)
            return carry

        lax.fori_loop(0, cuts, step, 0, unroll=times(MIX_UNROLL))

    def live_rows(m):
        return (row_at.astype(f32) < jnp.concatenate([live[m, 0:1, :]] * 2, axis=1)).astype(f32)

    def to_sibling(number, source, target):
        return remote(source, target, send.at[number], recv.at[number], here.sibling())

    def left_copy(k):
        return to_sibling(k, lefts[k].at[0], lefts[k].at[1])

    def right_sides(k):
        return (
            (projected, other_projected),
            (after_low, other_after),
            (expanded, other_expanded),
            (active, other_active),
        )[k]

    def right_copy(k):
        source, target = right_sides(k)
        half = widths[1 + k] // 2
        cut = pl.ds(pl.multiple_of((1 - here.core) * half, 128), half)
        return to_sibling(4 + k, source.at[:, cut], target)

    def small_copy():
        return to_sibling(8, small_terms.at[1 - here.core], other_small)

    def give(source, m):
        rows = pl.ds(m * slots, slots)
        return remote(source.at[rows], arrive.at[rows], give_send.at[m], give_recv.at[m], partner)

    def received(target, m):
        rows = sequence(m)
        arrived(arrive.at[rows], give_recv.at[m])
        target[rows] = arrive[rows]

    def turned(k):
        lefts[k][0] = (entered, gated, again, e_in)[k][...].T
        left_copy(k).start()

    def small_weights():
        filt[...] = matrix(0, 0, 128).astype(f32).T
        rows8[...] = matrix(0, 128, 128).astype(f32).T[:8]

    def enter(m):
        def body(rows):
            normed(rows, x_in[rows].astype(f32), norm_one, scale_one, rows8[3:4], entered)

        in_rows(body, m * slots, slots)

    def mix(m, rows, taken, cut):
        taps = [rows8[j : j + 1, taken] for j in range(3)]
        alive = live_rows(m)
        k = keys[rows, taken] * alive
        keys[rows, taken] = k
        v = values[rows, taken] * alive
        kernel = filt[:, taken] + taps[0] * k + taps[1] * later(k, 1) + taps[2] * later(k, 2)
        spec = left_dot(dft[...], parts(jnp.concatenate([v, kernel], axis=1)))
        value_spec[m, :, taken] = spec[:, :256]
        kernel_spec[m, :, taken] = spec[:, 256:]
        v_re, v_im = spec[:slots, :256], spec[slots:, :256]
        k_re, k_im = spec[:slots, 256:], spec[slots:, 256:]
        both = k_im * v_im
        re = k_re * v_re - jnp.where(first_row, 0.0, both)
        im = jnp.where(first_row, both, k_re * v_im + k_im * v_re)
        out = left_dot(idft[...], parts(jnp.concatenate([re, im], axis=0)))
        convolved[rows, taken] = out
        gated[rows, taken] = (queries[rows, taken] * out).astype(low)

    def mixer(m):
        rows = sequence(m)
        for k, target in enumerate((queries, keys, values)):
            target[rows] = left_dot(entered[rows], matrix(1, k * features, features))
        mixer_blocks(m, mix)

    def mixer_out(m):
        rows = sequence(m)
        total[rows] = x_in[rows].astype(f32) + left_dot(gated[rows], matrix(2, 0, features))

        def body(rows):
            normed(rows, total[rows], norm_two, scale_two, rows8[4:5], again)

        in_rows(body, m * slots, slots)

    def each_sequence(*bodies):
        def step(m, carry):
            for body in bodies:
                body(m)
            return carry

        lax.fori_loop(0, micro, step, 0)

    tile = 512

    def tiles(start, width, body):
        def step(i, carry):
            body(pl.multiple_of(start + i * tile, 128))
            return carry

        lax.fori_loop(0, width // tile, step, 0, unroll=times(TILE_UNROLL))

    def expand(start):
        gate = left_dot(again[...], matrix(3, start, tile))
        up = left_dot(again[...], matrix(3, pl.multiple_of(hidden + start, 128), tile))
        expanded[:, pl.ds(start, tile)] = gate.astype(low)
        expanded[:, pl.ds(pl.multiple_of(hidden + start, 128), tile)] = up.astype(low)
        active[:, pl.ds(start, tile)] = (gate * sigmoid(gate) * up).astype(low)

    def reduce_on(start, width):
        total[...] += dot_back(active[:, pl.ds(start, width)], matrix(4, start, width))

    def layer_done():
        right_copy(3).start()
        out_low[...] = total[...].astype(low)

    ends = {array: max(k for k, entry in enumerate(get_table) if entry[0] == array) for array in range(5)}

    def as_it_comes(chunk):
        array, start, width, _ = get_table[chunk]

        @pl.when(here.first_layer)
        @in_background
        def _():
            if array == 0:
                x_in[...] = feed[...]
                small_weights()
                each_sequence(enter)
                turned(0)
            if array == 1 and ends[1] == chunk:
                each_sequence(mixer)
                turned(1)
            if array == 2 and ends[2] == chunk:
                each_sequence(mixer_out)
                turned(2)
            if array == 3:
                tiles(start, width, expand)
            if array == 4:
                for half in (0, 1):
                    reduce_on(half * (hidden // 2) + start, width)

    def on_chunk(chunk):
        if chunk == ends[0]:
            fed()
        as_it_comes(chunk)

    gather(on_chunk)

    @pl.when(here.first_layer)
    def _():
        layer_done()
        for m in range(micro):
            give(out_low, m).start()
            give(out_low, m).wait_send()
        gathered()
        for m in range(micro):
            received(e_in, m)
        turned(3)

    @pl.when(here.second_layer)
    def _():
        small_weights()
        e_in[...] = feed[...]
        turned(3)
        gathered()
        each_sequence(functools.partial(received, x_in), enter, mixer, mixer_out)

        tiles(0, hidden, expand)
        reduce_on(0, hidden)
        layer_done()

    offsets, place = [], 0
    for array, _, width, _ in put_table:
        offsets.append(place)
        place += width if array in (1, 2, 3) else 0

    def one_in(chunk, z):
        array, start, width, _ = put_table[chunk]
        if array == 0:
            return one_small.at[z]
        if array == 4:
            return one_down.at[z, :, :, pl.ds(start, width)]
        return weight[3].at[z, 0, :, :, pl.ds(offsets[chunk], width)]

    def two_in(chunk, z):
        array, start, width, _ = put_table[chunk]
        if array == 0:
            return two_small.at[z]
        if array == 4:
            return two_down.at[z, :, pl.ds(start, width)]
        return weight[3].at[z, 1, 0, :, pl.ds(offsets[chunk], width)]

    def put_first(chunk, step):
        z = far(step)
        if step % 2:
            source, side = mine[chunk].at[z, :, 1 - here.x], here.x_side()
        else:
            source, side = mine[chunk].at[z, 1 - here.y], here.y_side()
        return remote(source, one_in(chunk, step), one_send.at[chunk, step], one_recv.at[chunk, step], side)

    def put_second(chunk, step):
        z = far(step)
        if step % 2:
            source, side = mine[chunk].at[z, 1 - here.y, here.x], here.y_side()
        else:
            source, side = mine[chunk].at[z, here.y, 1 - here.x], here.x_side()
        return remote(source, two_in(chunk, step), two_send.at[chunk, step], two_recv.at[chunk, step], side)

    def put_third(chunk, step, act):
        z = far(step)
        source = mine[chunk].at[z, here.y, here.x]
        target = landed[put_table[chunk][0]].at[here.home, :, columns(put_table, chunk, here.core)]
        receive = z_recv.at[chunk, here.home, here.core]
        own = (here.z == z) & (here.core == here.layer)
        if act == "start":

            @pl.when(own)
            def _():
                pltpu.make_async_copy(source, target, receive).start()

        @pl.when(jnp.logical_not(own))
        def _():
            away = remote(source, target, z_send.at[chunk, step], receive, (here.layer, here.chip(z=z)))
            getattr(away, act)()

    def add(target, other):
        target[...] = (target[...].astype(f32) + other[...].astype(f32)).astype(target.dtype)

    def both_sides(array):
        if array:
            left_copy(array - 1).wait_recv()
            right_copy(array - 1).wait_recv()
        else:
            small_copy().wait_recv()

    def place_block(chunk, cut, block):
        rows = features // 16
        for z in range(4):
            for k in range(4):
                at = (z * 4 + k) * rows
                mine[chunk][z, k // 2, k % 2, :, cut] = block[at : at + rows].astype(low)

    def terms(chunk, wait=False):
        array, start, width, shared = put_table[chunk]
        if wait:
            both_sides(array)
        if array == 0:
            place_block(chunk, pl.ds(0, width), (small_terms[here.core] + other_small[...]).T)
        else:
            source, other = right_sides(array - 1)
            own_start = here.core * (widths[array] // 2) + start
            strip = 256 if width % 256 == 0 else width

            def body(i, carry):
                at = i * strip
                block = left_dot(lefts[array - 1][0], source[:, pl.ds(pl.multiple_of(own_start + at, 128), strip)])
                block += left_dot(lefts[array - 1][1], other[:, pl.ds(pl.multiple_of(start + at, 128), strip)])
                place_block(chunk, pl.ds(pl.multiple_of(at, 128), strip), block)
                return carry

            lax.fori_loop(0, width // strip, body, 0)
        if not shared:
            for step in range(4):
                put_first(chunk, step).start()
            return

        @pl.when(here.second_layer)
        def _():
            for step in range(4):
                put_first(chunk, step).start()

        @pl.when(here.first_layer)
        def _():
            if not any(entry[3] for entry in put_table[:chunk]):
                pl.semaphore_wait(ready_mid, 1)
            put_middle(chunk).start()

    def put_middle(chunk):
        source = mine[chunk].at[pl.ds(2 * (1 - here.home), 2)]
        return remote(source, mid_in(chunk), mid_send.at[chunk], mid_recv.at[chunk], here.middle())

    def mid_in(chunk):
        _, start, width, _ = put_table[chunk]
        return weight[4].at[pl.ds(0, 2), :, :, :, pl.ds(start, width)]

    def sum_middle(chunk):
        put_middle(chunk).wait_recv()
        for z in range(2):
            for k in range(4):
                add(mine[chunk].at[2 * here.home + z, k // 2, k % 2], mid_in(chunk).at[z, k // 2, k % 2])
        for step in range(4):
            when(at_home(far(step)), lambda: put_first(chunk, step).start())

    def sum_one(chunk):
        for step in range(4):

            def action():
                z = far(step)
                put_first(chunk, step).wait_recv()
                for k in range(2):
                    if step % 2:
                        add(mine[chunk].at[z, k, here.x], one_in(chunk, step).at[k])
                    else:
                        add(mine[chunk].at[z, here.y, k], one_in(chunk, step).at[k])
                put_second(chunk, step).start()

            when(handled(put_table, chunk, far(step)), action)

    def sum_two(chunk):
        for step in range(4):

            def action():
                put_second(chunk, step).wait_recv()
                add(mine[chunk].at[far(step), here.y, here.x], two_in(chunk, step))
                put_third(chunk, step, "start")

            when(handled(put_table, chunk, far(step)), action)

    last = len(put_table)
    needs = {array: min(k for k, entry in enumerate(put_table) if entry[0] == array) for array in range(5)}
    down = [chunk for chunk in range(last) if put_table[chunk][0] == 4]

    @pl.when(here.first_layer)
    def _():
        for chunk in down:
            terms(chunk, wait=chunk == down[0])

    def expand_back(start):
        again = pl.multiple_of(hidden + start, 128)
        grad_act = left_dot(e_in[...], matrix(4, start, tile))
        gate = expanded[:, pl.ds(start, tile)].astype(f32)
        up = expanded[:, pl.ds(again, tile)].astype(f32)
        sig = sigmoid(gate)
        grad_gate = (grad_act * up * (sig * (1.0 + gate * (1.0 - sig)))).astype(low)
        grad_up = (grad_act * (gate * sig)).astype(low)
        expanded[:, pl.ds(start, tile)] = grad_gate
        expanded[:, pl.ds(again, tile)] = grad_up

    tiles(0, hidden, expand_back)
    total[...] = dot_back(expanded[...], matrix(3, 0, 2 * hidden))
    right_copy(2).start()
    for side in (here.x_side(), here.y_side()):
        pl.semaphore_signal(ready, inc=1, device_id=side, device_id_type=MESH)
    if any(entry[3] for entry in put_table):

        @pl.when(here.first_layer)
        def _():
            pl.semaphore_signal(ready_mid, inc=1, device_id=here.middle(), device_id_type=MESH)


    def norm_grad(rows, grad, normal, scale, gain, at):
        n = normal[rows]
        small_terms[1, at : at + 1] += jnp.sum(grad * n, axis=0, keepdims=True)
        q = grad * gain
        back = q - jnp.mean(q, axis=1, keepdims=True) - n * jnp.mean(q * n, axis=1, keepdims=True)
        return scale[rows][:, :1] * back

    def after_back():
        small_terms[...] = jnp.zeros_like(small_terms)

        def body(rows):
            grad = e_in[rows].astype(f32) + norm_grad(rows, total[rows], norm_two, scale_two, rows8[4:5], 4)
            after[rows] = grad
            after_low[rows] = grad.astype(low)

        in_rows(body)
        right_copy(1).start()

    def gated_back():
        total[...] = dot_back(after_low[...], matrix(2, 0, features))

    def mix_back(m, rows, taken, cut):
        taps = [rows8[j : j + 1, taken] for j in range(3)]
        alive = live_rows(m)
        grad = total[rows, taken]
        projected[rows, taken] = (grad * convolved[rows, taken]).astype(low)
        spec = left_dot(dft[...], parts(grad * queries[rows, taken]))
        g_re, g_im = spec[:slots], spec[slots:]
        pairs = []
        for other in (kernel_spec, value_spec):
            o_re, o_im = other[m, :slots, taken], other[m, slots:, taken]
            both = o_im * g_im
            re = o_re * g_re + jnp.where(first_row, 0.0, both)
            im = jnp.where(first_row, both, o_re * g_im - o_im * g_re)
            pairs.append(jnp.concatenate([re, im], axis=0))
        paired = left_dot(idft[...], parts(jnp.concatenate(pairs, axis=1)))
        at_values = pl.ds(pl.multiple_of(2 * features + cut * 256, 256), 256)
        projected[rows, at_values] = (paired[:, :256] * alive).astype(low)
        grad_kernel = paired[:, 256:]
        small_terms[0, :, taken] += grad_kernel
        k = keys[rows, taken]
        for j in range(3):
            moved = later(k, j) if j else k
            small_terms[1, j : j + 1, taken] += jnp.sum(grad_kernel * moved, axis=0, keepdims=True)
        grad_keys = taps[0] * grad_kernel + taps[1] * sooner(grad_kernel, 1) + taps[2] * sooner(grad_kernel, 2)
        at_keys = pl.ds(pl.multiple_of(features + cut * 256, 256), 256)
        projected[rows, at_keys] = (grad_keys * alive).astype(low)

    def mixed_back(m):
        mixer_blocks(m, mix_back)

    def input_back(m):
        rows = sequence(m)
        total[rows] = dot_back(projected[rows], matrix(1, 0, 3 * features))

        def body(rows):
            grad = after[rows] + norm_grad(rows, total[rows], norm_one, scale_one, rows8[3:4], 3)
            grad_low[rows] = grad.astype(low)

        in_rows(body, m * slots, slots)

    pieces = [after_back, gated_back]
    for m in range(micro):
        pieces += [functools.partial(mixed_back, m), functools.partial(input_back, m)]

    def last_copies():
        right_copy(0).start()
        small_copy().start()

    pieces += [last_copies]

    @pl.when(here.second_layer)
    def _():
        after_back()
        gated_back()
        for m in range(micro):
            mixed_back(m)
            input_back(m)
            if m == micro - 1:
                terms(down[0], wait=True)
            if m:
                give(grad_low, m - 1).wait_send()
            give(grad_low, m).start()
        last_copies()
        turned(2)
        for chunk in down[1:]:
            terms(chunk)
        turned(1)
        turned(0)

    pl.semaphore_wait(ready, 2)

    def one_sum(act):
        @pl.when(here.core == 0)
        def _():
            for chunk, (array, _, width, shared) in enumerate(put_table):
                for half in range(2 if shared else 0):
                    target = landed[array].at[1 - here.home, :, columns(put_table, chunk, half)]
                    copy = pltpu.make_async_copy(nothing.at[:, pl.ds(0, width)], target, nothing_sems.at[chunk, half])
                    getattr(copy, act)()

    nothing[...] = jnp.zeros_like(nothing)
    one_sum("start")

    apart = here.core != here.layer
    over = (1 - here.core, here.partner)

    def swap(source, target, number, act):
        sems = swap_sems.at[number], swap_sems.at[number + 1]

        @pl.when(apart)
        def _():
            getattr(remote(source, target, *sems, over), act)()

        @pl.when(jnp.logical_not(apart))
        def _():
            getattr(pltpu.make_async_copy(source, target, sems[1]), act)()

    due = [max(0, needs[1] - len(pieces) + k) for k in range(len(pieces))]
    shared = [chunk for chunk in range(last) if put_table[chunk][3]]
    met = [4]

    swap(out_low, kept_out, 0, "start")
    for now in range(last + 1):
        for piece, at in zip(pieces, due):
            if at == now:
                pl.when(here.first_layer)(in_background(piece))
        early = shared if now == 1 else []
        for chunk in early + [now + 1]:
            if chunk < last and chunk not in down and (chunk not in shared or chunk in early):
                terms(chunk, wait=put_table[chunk][0] not in met)
                met.append(put_table[chunk][0])
        for chunk in shared:
            if now == chunk - 2:
                pl.when(here.first_layer)(functools.partial(sum_middle, chunk))
        if now < last:
            sum_one(now)
        if 1 <= now:
            sum_two(now - 1)
        if now == needs[0]:
            swap(grad_low, kept_grad, 2, "start")

    one_sum("wait")
    for chunk in range(last):
        for half in (0, 1):
            for slot in (0, 1):
                target = landed[put_table[chunk][0]].at[slot, :, columns(put_table, chunk, half)]
                wanted = (here.core == 1) | (here.home == slot) if put_table[chunk][3] else True
                when(wanted, functools.partial(arrived, target, z_recv.at[chunk, slot, half]))
        for step in range(4):

            def action():
                put_first(chunk, step).wait_send()
                put_second(chunk, step).wait_send()
                put_third(chunk, step, "wait_send")

            when(handled(put_table, chunk, far(step)), action)
        if put_table[chunk][3]:
            pl.when(here.first_layer)(lambda: put_middle(chunk).wait_send())

    @pl.when(own_feed)
    def _():
        remote(hidden_in, feed, feed_sems.at[1], feed_sems.at[0], partner).wait_send()
        remote(live_own, live, feed_sems.at[3], feed_sems.at[2], partner).wait_send()

    for k in range(4):
        left_copy(k).wait_send()
        right_copy(k).wait_send()
    small_copy().wait_send()
    pl.when(here.second_layer)(lambda: give(grad_low, micro - 1).wait_send())
    swap(out_low, kept_out, 0, "wait")
    swap(grad_low, kept_grad, 2, "wait")


def finish_kernel(*refs):
    landed, (out, grad) = refs[:5], refs[5:7]
    s_filters, s_taps, s_one, s_two = refs[7:11]
    sums, (to_out, to_grad) = refs[11:15], refs[15:17]
    to_out[...] = out[...]
    to_grad[...] = grad[...]
    small = landed[0][0].astype(jnp.float32) + landed[0][1].astype(jnp.float32)
    s_filters[...] = small[:, :128]
    own = small.shape[0]
    rows = jnp.pad(small[:, 128:], ((0, 128 - own), (0, 0))).T
    for j in range(3):
        s_taps[j] = rows[j : j + 1, :own]
    s_one[...] = rows[3:4, :own]
    s_two[...] = rows[4:5, :own]
    for number, result in enumerate(sums):
        result[...] = landed[1 + number][0].astype(jnp.float32) + landed[1 + number][1].astype(jnp.float32)


def fast_device(
    hidden_in, out_grad, lengths, gain_mixer, w_input, w_taps, filters, w_output, gain_mlp, w_gate_up, w_down
):
    micro, _, slots, features = hidden_in.shape
    tokens, rows = micro * slots, gain_mixer.shape[1]
    shards = (w_input[0], w_output[0], w_gate_up[0], w_down[0].T)
    widths = [256] + [shard.shape[1] for shard in shards]
    hidden = widths[4]
    get_table, put_table = chunks_of(GET_PIECES), chunks_of(PUT_PIECES)
    dft, idft = (jnp.asarray(table) for table in packed_tables(slots))
    low, f32 = jnp.bfloat16, jnp.float32
    anywhere = pl.BlockSpec(memory_space=pl.ANY)
    inside = pl.BlockSpec(memory_space=pltpu.VMEM)
    dma, vmem = pltpu.SemaphoreType.DMA, pltpu.VMEM
    act, act_low = (tokens, features), vmem((tokens, features), low)
    kinds = [jax.ShapeDtypeStruct((2, rows, width), low) for width in widths]
    kinds += [jax.ShapeDtypeStruct((tokens, features), low)] * 2
    room = [vmem((rows, 256), low), vmem((128, 128), f32)] + [vmem((micro, 8, 128), f32)] * 2
    room += [vmem((rows, max(entry[2] for entry in put_table)), low), dma((len(put_table), 2))]
    room += [vmem((4, 2, 2, rows, width), low) for width in widths]
    room += [act_low] * 6
    room += [vmem((slots, features), f32), vmem((8, features), f32), vmem(act, f32), vmem(act, f32)]
    room += [vmem((tokens, 128), f32)] * 2
    room += [act_low] * 3 + [vmem(act, f32)] * 4 + [vmem((micro, 2 * slots, features), f32)] * 2
    room += [vmem(act, f32)] * 2 + [vmem((tokens, 2 * hidden), low), vmem((tokens, hidden), low)]
    room += [vmem((tokens, 3 * features), low), act_low, vmem((2, slots, features), f32)]
    room += [vmem((2, features, tokens), low)] * 4
    room += [vmem((slots, features), f32)] + [vmem((tokens, width // 2), low) for width in widths[1:]]
    room += [vmem((4, 2, 2, rows, entry[2]), low) for entry in put_table]
    for width in (128, hidden // 2):
        room += [vmem((4, 2, rows, width), low), vmem((4, rows, width), low)]
    got, put = len(get_table), len(put_table)
    room += [dma((got, 2, 2))] + [dma((got, 4))] * 5 + [dma((got, 2))] * 2 + [dma((got,))] * 2 + [dma((4,))]
    room += [dma((4,)), dma((micro,)), dma((micro,)), dma((9,)), dma((9,))]
    room += [dma((put, 4))] * 5 + [dma((put, 2, 2))] + [dma((put,))] * 2 + [pltpu.SemaphoreType.REGULAR] * 2
    results = pl.pallas_call(
        functools.partial(layer_kernel, get_table, put_table, widths),
        out_shape=kinds,
        in_specs=[inside] * 4 + [pl.BlockSpec(memory_space=pltpu.SMEM)] + [inside] * 2 + [anywhere] * 6,
        out_specs=[anywhere] * 7,
        scratch_shapes=room,
        compiler_params=pltpu.CompilerParams(
            collective_id=0, has_side_effects=True, vmem_limit_bytes=62 * 1024 * 1024
        ),
    )(
        filters[0].T,
        w_taps[0],
        gain_mixer,
        gain_mlp,
        lengths.T,
        dft,
        idft,
        *shards,
        hidden_in.reshape(tokens, features),
        out_grad.reshape(tokens, features),
    )
    kinds = [(rows, 128), (3, 1, rows), (1, rows), (1, rows)] + [(rows, width) for width in widths[1:]]
    kinds = [jax.ShapeDtypeStruct(kind, f32) for kind in kinds] + kinds_of(results[5:])
    s_filters, s_taps, s_one, s_two, s_in, s_out, s_gu, s_dt, layer_out, input_grad = pl.pallas_call(
        finish_kernel,
        out_shape=kinds,
        in_specs=[inside] * 7,
        out_specs=[inside] * 10,
        compiler_params=pltpu.CompilerParams(vmem_limit_bytes=62 * 1024 * 1024),
    )(*results)
    shape = (1, micro, 1, slots, features)
    return (
        layer_out.reshape(shape),
        input_grad.reshape(shape),
        s_one,
        s_in[None],
        s_taps.transpose(1, 0, 2),
        s_filters.T[None],
        s_out[None],
        s_two,
        s_gu[None],
        s_dt.T[None],
    )


def kinds_of(arrays):
    return [jax.ShapeDtypeStruct(array.shape, array.dtype) for array in arrays]


def solution(mesh):
    placed = (
        P(None, "dp", None, None),
        P(None, "dp", None, None),
        P(None, "dp"),
        P("section", "dp"),
        P("section", "dp", None),
        P("section", None, "dp"),
        P("section", None, "dp"),
        P("section", "dp", None),
        P("section", "dp"),
        P("section", "dp", None),
        P("section", None, "dp"),
    )
    return jax.shard_map(
        fast_device if mesh.shape["dp"] == 16 and mesh.shape["section"] == 2 else on_device,
        mesh=mesh,
        in_specs=placed,
        out_specs=(
            P("section", None, "dp", None, None),
            P("section", None, "dp", None, None),
            P("section", "dp"),
            P("section", "dp", None),
            P("section", None, "dp"),
            P("section", None, "dp"),
            P("section", "dp", None),
            P("section", "dp"),
            P("section", "dp", None),
            P("section", None, "dp"),
        ),
        check_vma=False,
    )
```

```python
import functools
import math

import jax
import jax.numpy as jnp
import ml_dtypes
import numpy as np
from jax import lax
from jax.experimental import pallas as pl
from jax.experimental.pallas import tpu as pltpu
from jax.sharding import PartitionSpec as P

MESH = pl.DeviceIdType.MESH

epsilon = 1e-05
GET_PIECES = (
    (0, 128, False),
    (1, 384, False),
    (1, 384, False),
    (1, 384, False),
    (2, 384, False),
    (3, 1024, True),
    (3, 1024, False),
    (3, 1024, False),
    (4, 640, False),
    (4, 640, False),
    (4, 256, False),
)
PUT_PIECES = (
    (4, 768, False),
    (4, 768, False),
    (3, 1024, False),
    (3, 1024, False),
    (1, 384, False),
    (1, 384, False),
    (0, 128, False),
    (1, 384, False),
    (2, 384, False),
    (3, 512, True),
    (3, 512, True),
)
GET_LAGS = (5, 7, 1, 2, 3)
SHARED_LAG = 3
ROWS_UNROLL = 2
MIX_UNROLL = 3
TILE_UNROLL = 2


def passed_along(value, axis, steps):
    count = lax.axis_size(axis)
    first, last = (max(0, -steps), min(count, count - steps))
    return lax.ppermute(value, axis, [(source, source + steps) for source in range(first, last)])


def split_dot(left_side, right_side):
    return jnp.dot(
        left_side, right_side, precision=lax.Precision.HIGH, preferred_element_type=jnp.float32
    )


def split_rows(left_side, right_side):
    return lax.dot_general(
        left_side,
        right_side,
        (((0,), (0,)), ((), ())),
        precision=lax.Precision.HIGH,
        preferred_element_type=jnp.float32,
    )


def dot_rows(left_side, right_side):
    return lax.dot_general(
        left_side, right_side, (((0,), (0,)), ((), ())), preferred_element_type=jnp.float32
    )


def dot_back(left_side, right_side):
    return lax.dot_general(
        left_side, right_side, (((1,), (1,)), ((), ())), preferred_element_type=jnp.float32
    )


def tables(length):
    period = 2 * length
    freq_index = lax.broadcasted_iota(jnp.int32, (length + 1, length), 0)
    time_index = lax.broadcasted_iota(jnp.int32, (length + 1, length), 1)
    angles = (freq_index * time_index % period).astype(jnp.float32) * (2.0 * math.pi / period)
    edge_rows = (freq_index[:, :1] == 0) | (freq_index[:, :1] == length)
    inverse_weight = jnp.where(edge_rows, 1.0, 2.0) / period
    dft_stack = jnp.concatenate([jnp.cos(angles), -jnp.sin(angles)], axis=0)
    return (dft_stack, inverse_weight)


def spectrum(dft_tables, signal):
    dft_stack, inverse_weight = dft_tables
    stacked_out = split_dot(dft_stack, signal)
    middle_row = stacked_out.shape[0] // 2
    return (stacked_out[:middle_row], stacked_out[middle_row:])


def inverse(dft_tables, real_part, imag_part):
    dft_stack, inverse_weight = dft_tables
    return split_rows(
        dft_stack, jnp.concatenate([inverse_weight * real_part, inverse_weight * imag_part], axis=0)
    )


def normalize(input_rows):
    centered = input_rows - jnp.mean(input_rows, axis=1, keepdims=True)
    inv_scale = lax.rsqrt(jnp.mean(centered * centered, axis=1, keepdims=True) + epsilon)
    return (centered * inv_scale, inv_scale)


def norm_back(grad_normed, normed, inv_scale):
    return inv_scale * (
        grad_normed
        - jnp.mean(grad_normed, axis=1, keepdims=True)
        - normed * jnp.mean(grad_normed * normed, axis=1, keepdims=True)
    )


def delayed(input_rows, places):
    return jnp.pad(input_rows, ((places, 0), (0, 0)))[: input_rows.shape[0]]


def advanced(input_rows, places):
    return jnp.pad(input_rows, ((0, places), (0, 0)))[places:]


def layer_forward(input_rows, active_rows, weights, dft_tables):
    gain_one, w_inner, w_tap_rows, filt_static, w_outer, gain_two, w_expand, w_reduce = weights
    hidden_size_model = w_outer.shape[0]
    hidden_width = w_reduce.shape[0]
    tap_weights = w_tap_rows.astype(jnp.float32)
    normed_one, scale_one = normalize(input_rows)
    entered = (normed_one * gain_one.astype(jnp.float32)).astype(jnp.bfloat16)
    projected = jnp.dot(entered, w_inner, preferred_element_type=jnp.float32)
    queries = projected[:, :hidden_size_model]
    keys_part = projected[:, hidden_size_model : 2 * hidden_size_model] * active_rows
    values_part = projected[:, 2 * hidden_size_model :] * active_rows
    dynamic = (
        tap_weights[0] * keys_part
        + tap_weights[1] * delayed(keys_part, 1)
        + tap_weights[2] * delayed(keys_part, 2)
    )
    kernel = filt_static.astype(jnp.float32) + dynamic
    joint_re, joint_im = spectrum(dft_tables, jnp.concatenate([values_part, kernel], axis=1))
    value_re = joint_re[:, :hidden_size_model]
    kernel_re = joint_re[:, hidden_size_model:]
    value_im = joint_im[:, :hidden_size_model]
    kernel_im = joint_im[:, hidden_size_model:]
    convolved = inverse(
        dft_tables,
        kernel_re * value_re - kernel_im * value_im,
        kernel_re * value_im + kernel_im * value_re,
    )
    gated_rows = (queries * convolved).astype(jnp.bfloat16)
    after_mixer = input_rows + jnp.dot(gated_rows, w_outer, preferred_element_type=jnp.float32)
    normed_two, scale_two = normalize(after_mixer)
    entered_two = (normed_two * gain_two.astype(jnp.float32)).astype(jnp.bfloat16)
    expanded = jnp.dot(entered_two, w_expand, preferred_element_type=jnp.float32)
    gate_part = expanded[:, :hidden_width]
    up_part = expanded[:, hidden_width:]
    activated = (jax.nn.silu(gate_part) * up_part).astype(jnp.bfloat16)
    result = after_mixer + jnp.dot(activated, w_reduce, preferred_element_type=jnp.float32)
    stash = (
        normed_one,
        scale_one,
        entered,
        queries,
        keys_part,
        (value_re, value_im, kernel_re, kernel_im),
        convolved,
        gated_rows,
        normed_two,
        scale_two,
        entered_two,
        gate_part,
        up_part,
        activated,
    )
    return (result, stash)


def mlp_backward(received_gradient, weights, stash):
    gain_one, w_inner, w_tap_rows, filt_static, w_outer, gain_two, w_expand, w_reduce = weights
    (
        normed_one,
        scale_one,
        entered,
        queries,
        keys_part,
        spectra,
        convolved,
        gated_rows,
        normed_two,
        scale_two,
        entered_two,
        gate_part,
        up_part,
        activated,
    ) = stash
    grad_low = received_gradient.astype(jnp.bfloat16)
    grad_reduce_w = dot_rows(activated, grad_low)
    grad_act = dot_back(grad_low, w_reduce)
    sigmoid_gate = jax.nn.sigmoid(gate_part)
    grad_gate = grad_act * up_part * (sigmoid_gate * (1.0 + gate_part * (1.0 - sigmoid_gate)))
    grad_up = grad_act * (gate_part * sigmoid_gate)
    grad_expand = jnp.concatenate([grad_gate, grad_up], axis=1).astype(jnp.bfloat16)
    grad_expand_w = dot_rows(entered_two, grad_expand)
    grad_entered_two = dot_back(grad_expand, w_expand)
    grad_gain_two = jnp.sum(grad_entered_two * normed_two, axis=0)
    grad_after = received_gradient + norm_back(
        grad_entered_two * gain_two.astype(jnp.float32), normed_two, scale_two
    )
    return (grad_after, (grad_gain_two, grad_expand_w, grad_reduce_w))


def mixer_backward(grad_after, active_rows, weights, dft_tables, stash):
    gain_one, w_inner, w_tap_rows, filt_static, w_outer, gain_two, w_expand, w_reduce = weights
    (
        normed_one,
        scale_one,
        entered,
        queries,
        keys_part,
        spectra,
        convolved,
        gated_rows,
        normed_two,
        scale_two,
        entered_two,
        gate_part,
        up_part,
        activated,
    ) = stash
    value_re, value_im, kernel_re, kernel_im = spectra
    hidden_size_model = w_outer.shape[0]
    tap_weights = w_tap_rows.astype(jnp.float32)
    grad_mix_low = grad_after.astype(jnp.bfloat16)
    grad_outer_w = dot_rows(gated_rows, grad_mix_low)
    grad_gated = dot_back(grad_mix_low, w_outer)
    grad_queries = grad_gated * convolved
    grad_conv = grad_gated * queries
    grad_re, grad_im = spectrum(dft_tables, grad_conv)
    paired_re = jnp.concatenate(
        [kernel_re * grad_re + kernel_im * grad_im, value_re * grad_re + value_im * grad_im], axis=1
    )
    paired_im = jnp.concatenate(
        [kernel_re * grad_im - kernel_im * grad_re, value_re * grad_im - value_im * grad_re], axis=1
    )
    paired = inverse(dft_tables, paired_re, paired_im)
    grad_values = paired[:, :hidden_size_model] * active_rows
    grad_kernel = paired[:, hidden_size_model:]
    grad_taps = jnp.stack(
        [
            jnp.sum(grad_kernel * keys_part, axis=0),
            jnp.sum(grad_kernel * delayed(keys_part, 1), axis=0),
            jnp.sum(grad_kernel * delayed(keys_part, 2), axis=0),
        ]
    )
    grad_keys = (
        tap_weights[0] * grad_kernel
        + tap_weights[1] * advanced(grad_kernel, 1)
        + tap_weights[2] * advanced(grad_kernel, 2)
    ) * active_rows
    grad_projected = jnp.concatenate([grad_queries, grad_keys, grad_values], axis=1).astype(
        jnp.bfloat16
    )
    inner_weight_gradient = dot_rows(entered, grad_projected)
    grad_entered = dot_back(grad_projected, w_inner)
    grad_gain_one = jnp.sum(grad_entered * normed_one, axis=0)
    grad_inputs = grad_after + norm_back(
        grad_entered * gain_one.astype(jnp.float32), normed_one, scale_one
    )
    return (
        grad_inputs,
        (grad_gain_one, inner_weight_gradient, grad_taps, grad_kernel, grad_outer_w),
    )


def add_terms(received, flipped):
    return tuple(
        (
            jnp.sum(member, axis=0).T if flip else jnp.sum(member, axis=0)
            for member, flip in zip(received, flipped)
        )
    )


def on_device(
    hidden_in,
    out_grad,
    lengths,
    gain_mixer,
    w_input,
    w_taps,
    filters,
    w_output,
    gain_mlp,
    w_gate_up,
    w_down,
):
    first_section = lax.axis_index("section") == 0
    micro_count = hidden_in.shape[0]
    seq_slots = hidden_in.shape[2]
    hidden_size_model = hidden_in.shape[3]
    dft_tables = tables(seq_slots)
    positions = lax.broadcasted_iota(jnp.int32, (seq_slots, 1), 0)
    weights = (
        lax.all_gather(gain_mixer[0], "dp", axis=0, tiled=True),
        lax.all_gather(w_input[0], "dp", axis=0, tiled=True),
        lax.all_gather(w_taps[0], "dp", axis=1, tiled=True),
        lax.all_gather(filters[0], "dp", axis=1, tiled=True),
        lax.all_gather(w_output[0], "dp", axis=0, tiled=True),
        lax.all_gather(gain_mlp[0], "dp", axis=0, tiled=True),
        lax.all_gather(w_gate_up[0], "dp", axis=0, tiled=True),
        lax.all_gather(w_down[0], "dp", axis=1, tiled=True),
    )
    arriving = jnp.zeros((seq_slots, hidden_size_model), jnp.bfloat16)
    outgoing_list = []
    saved_activations = []
    for forward_step in range(micro_count + 1):
        own_index = min(forward_step, micro_count - 1)
        prior_index = max(forward_step - 1, 0)
        input_rows = jnp.where(first_section, hidden_in[own_index, 0], arriving).astype(jnp.float32)
        length_now = jnp.where(first_section, lengths[own_index, 0], lengths[prior_index, 0])
        active_rows = (positions < length_now).astype(jnp.float32)
        result, stash = layer_forward(input_rows, active_rows, weights, dft_tables)
        outgoing = result.astype(jnp.bfloat16)
        outgoing_list.append(outgoing)
        if forward_step < micro_count:
            arriving = passed_along(outgoing, "section", 1)
        saved_activations.append((input_rows, active_rows))
    coming = jnp.zeros((seq_slots, hidden_size_model), jnp.bfloat16)
    mlp_totals = None
    mixer_totals = None
    grads_out = []
    for backward_step in range(micro_count + 1):
        saved_slot_index = micro_count - backward_step
        last_index = max(micro_count - 1 - backward_step, 0)
        live_factor = 1.0 if backward_step < micro_count else 0.0
        received_gradient = jnp.where(
            first_section,
            coming.astype(jnp.float32),
            out_grad[last_index, 0].astype(jnp.float32) * live_factor,
        )
        input_rows, active_rows = saved_activations[saved_slot_index]
        result, stash = layer_forward(input_rows, active_rows, weights, dft_tables)
        grad_after, mlp_grads = mlp_backward(received_gradient, weights, stash)
        mlp_totals = (
            mlp_grads if mlp_totals is None else jax.tree.map(jnp.add, mlp_totals, mlp_grads)
        )
        grad_inputs, mixer_grads = mixer_backward(
            grad_after, active_rows, weights, dft_tables, stash
        )
        mixer_totals = (
            mixer_grads
            if mixer_totals is None
            else jax.tree.map(jnp.add, mixer_totals, mixer_grads)
        )
        outgoing = grad_inputs.astype(jnp.bfloat16)
        grads_out.append(outgoing)
        if backward_step < micro_count:
            coming = passed_along(outgoing, "section", -1)
    first_outputs = jnp.stack(outgoing_list[:micro_count])
    second_outputs = jnp.stack(outgoing_list[1:])
    layer_out = jnp.where(first_section, first_outputs, second_outputs)[None, :, None]
    first_grads = jnp.stack(
        [grads_out[micro_count - batch_index] for batch_index in range(micro_count)]
    )
    second_grads = jnp.stack(
        [grads_out[micro_count - 1 - batch_index] for batch_index in range(micro_count)]
    )
    input_grad = jnp.where(first_section, first_grads, second_grads)[None, :, None]
    all_parts = (
        lax.all_to_all(
            mixer_totals[0][None].astype(jnp.bfloat16),
            "dp",
            split_axis=1,
            concat_axis=0,
            tiled=True,
        ).astype(jnp.float32),
        lax.all_to_all(
            mixer_totals[1][None].astype(jnp.bfloat16),
            "dp",
            split_axis=1,
            concat_axis=0,
            tiled=True,
        ).astype(jnp.float32),
        lax.all_to_all(
            mixer_totals[2].T[None].astype(jnp.bfloat16),
            "dp",
            split_axis=1,
            concat_axis=0,
            tiled=True,
        ).astype(jnp.float32),
        lax.all_to_all(
            mixer_totals[3].T[None].astype(jnp.bfloat16),
            "dp",
            split_axis=1,
            concat_axis=0,
            tiled=True,
        ).astype(jnp.float32),
        lax.all_to_all(
            mixer_totals[4][None].astype(jnp.bfloat16),
            "dp",
            split_axis=1,
            concat_axis=0,
            tiled=True,
        ).astype(jnp.float32),
        lax.all_to_all(
            mlp_totals[0][None].astype(jnp.bfloat16), "dp", split_axis=1, concat_axis=0, tiled=True
        ).astype(jnp.float32),
        lax.all_to_all(
            mlp_totals[1][None].astype(jnp.bfloat16), "dp", split_axis=1, concat_axis=0, tiled=True
        ).astype(jnp.float32),
        lax.all_to_all(
            mlp_totals[2].T[None].astype(jnp.bfloat16),
            "dp",
            split_axis=1,
            concat_axis=0,
            tiled=True,
        ).astype(jnp.float32),
    )
    summed = add_terms(all_parts, (False, False, True, True, False, False, False, True))
    return (
        layer_out,
        input_grad,
        summed[0][None],
        summed[1][None],
        summed[2][None],
        summed[3][None],
        summed[4][None],
        summed[5][None],
        summed[6][None],
        summed[7][None],
    )


class Place:
    def __init__(self):
        self.core = lax.axis_index("section")
        self.index = lax.axis_index("dp")
        self.z = self.index // 4
        self.y = self.index // 2 % 2
        self.x = self.index % 2
        self.layer = 1 - (self.z + 1) // 2 % 2
        self.home = self.z // 2
        self.first_layer = self.layer == 0
        self.second_layer = self.layer == 1
        self.partner = self.chip(z=self.z + 1 - 2 * (self.z % 2))

    def chip(self, z=None, y=None, x=None):
        z, y, x = (a if a is not None else b for a, b in ((z, self.z), (y, self.y), (x, self.x)))
        return z * 4 + y * 2 + x

    def x_side(self):
        return (self.core, self.chip(x=1 - self.x))

    def y_side(self):
        return (self.core, self.chip(y=1 - self.y))

    def sibling(self):
        return (1 - self.core, self.index)

    def middle(self):
        return (self.core, self.chip(z=3 - self.z))

    def greet(self):
        barrier = pltpu.get_barrier_semaphore()
        others = [self.x_side(), self.y_side(), self.sibling()]
        for step in (1, 2, 3):
            chip = self.chip(z=(self.z + step) % 4)
            others += [(0, chip), (1, chip)]
        for other in others:
            pl.semaphore_signal(barrier, inc=1, device_id=other, device_id_type=MESH)
        pl.semaphore_wait(barrier, len(others))


def remote(source, target, send, receive, device):
    return pltpu.make_async_remote_copy(
        src_ref=source,
        dst_ref=target,
        send_sem=send,
        recv_sem=receive,
        device_id=device,
        device_id_type=MESH,
    )


def chunks_of(pieces):
    table, places = [], {}
    for array, width, shared in pieces:
        start = places.get(array, 0)
        table.append((array, start, width, shared))
        places[array] = start + width
    return table


def left_dot(left_side, right_side):
    return lax.dot_general(
        left_side, right_side, (((1,), (0,)), ((), ())), preferred_element_type=jnp.float32
    )


def sigmoid(value):
    return 0.5 * jnp.tanh(0.5 * value) + 0.5


def parts(signal):
    high = signal.astype(jnp.bfloat16)
    rest = (signal - high.astype(jnp.float32)).astype(jnp.bfloat16)
    return jnp.concatenate([high, high, rest], axis=0)


def halves_of(table):
    high = table.astype(ml_dtypes.bfloat16)
    rest = (table - high.astype(np.float64)).astype(ml_dtypes.bfloat16)
    return np.concatenate([high, rest, high], axis=1)


def packed_tables(length):
    period = 2 * length
    freq, time = np.arange(length)[:, None], np.arange(length)[None, :]
    angles = (freq * time % period) * (2.0 * math.pi / period)
    sines = np.where(freq == 0, 1.0 - 2.0 * (time % 2), -np.sin(angles))
    table = np.concatenate([np.cos(angles), sines], axis=0)
    weight = np.where(np.arange(period)[:, None] % length == 0, 1.0, 2.0) / period
    return halves_of(table), halves_of((table * weight).T)


def layer_kernel(get_table, put_table, widths, *refs):
    refs = list(refs)

    def take(number):
        taken = refs[:number]
        del refs[:number]
        return taken

    filters_in, taps_in, gain_one_in, gain_two_in, lengths_in, dft, idft = take(7)
    shards, (hidden_in, grad_in) = [None] + take(4), take(2)
    landed, (kept_out, kept_grad) = take(5), take(2)
    own_small, rows_in, live_own, live, nothing, nothing_sems = take(6)
    weight = take(5)
    feed, arrive, x_in, e_in, out_low, grad_low = take(6)
    filt, rows8, norm_one, norm_two, scale_one, scale_two = take(6)
    entered, gated, again, queries, keys, values, convolved, value_spec, kernel_spec = take(9)
    total, after, expanded, active, projected, after_low, small_terms = take(7)
    lefts = take(4)
    other_small, other_projected, other_after, other_expanded, other_active = take(5)
    mine = take(len(put_table))
    one_small, two_small, one_down, two_down = take(4)
    get_z_send, get_z_recv, get_one_send, get_one_recv, get_two_send, get_two_recv = take(6)
    get_mid_send, get_mid_recv, get_side_send, get_side_recv, feed_sems = take(5)
    swap_sems, give_send, give_recv, send, recv = take(5)
    one_send, one_recv, two_send, two_recv, z_send, z_recv, mid_send, mid_recv, ready, ready_mid = take(10)

    here = Place()
    tokens, features = x_in.shape
    slots = filt.shape[0]
    micro = tokens // slots
    hidden = active.shape[1]
    f32, low = jnp.float32, jnp.bfloat16
    shards[0] = own_small

    here.greet()

    for m in range(micro):
        live_own[m] = jnp.full(live_own.shape[1:], lengths_in[0, m], jnp.int32).astype(f32)

    own_feed = here.core == here.layer
    partner = (here.core, here.partner)
    for layer, kept, given in ((0, hidden_in, grad_in), (1, grad_in, hidden_in)):

        @pl.when(own_feed & (here.layer == layer))
        def _():
            pltpu.make_async_copy(kept, feed, feed_sems.at[0]).start()
            pltpu.make_async_copy(live_own, live, feed_sems.at[2]).start()
            remote(given, feed, feed_sems.at[1], feed_sems.at[0], partner).start()
            remote(live_own, live, feed_sems.at[3], feed_sems.at[2], partner).start()

    def arrived(target, receive):
        pltpu.make_async_copy(target, target, receive).wait()

    def fed():
        arrived(feed, feed_sems.at[0])
        arrived(live, feed_sems.at[2])

    def small_shard():
        rows_in[...] = jnp.zeros_like(rows_in)
        own = taps_in.shape[1]
        rows_in[0:3, 0:own] = taps_in[...].astype(f32)
        rows_in[3:4, 0:own] = gain_one_in[...].astype(f32)
        rows_in[4:5, 0:own] = gain_two_in[...].astype(f32)
        own_small[:, :128] = filters_in[...]
        own_small[:, 128:] = rows_in[...].T[:own].astype(low)

    def columns(table, chunk, half):
        array, start, width, _ = table[chunk]
        return pl.ds(pl.multiple_of(half * (widths[array] // 2) + start, 128), width)

    def at_home(z):
        return z // 2 == here.home

    def when(condition, action):
        if condition is True:
            action()
        else:
            pl.when(condition)(action)

    def z_all(chunk, visit, near):
        array, _, _, shared = get_table[chunk]
        for number, plane in enumerate((1 - here.core, 2 + here.core)):
            wanted = (plane == here.z) if near else (plane != here.z)
            if shared:
                wanted = wanted & ((here.core == 1) | (here.home == number))
            for half in (0, 1):
                cut = columns(get_table, chunk, half)
                source, target = shards[array].at[:, cut], weight[array].at[here.z, here.y, here.x, :, cut]
                sems = get_z_send.at[chunk, number, half], get_z_recv.at[chunk, here.z]
                visit(wanted, here.core == half, source, target, sems, (half, here.chip(z=plane)))

    def z_start(chunk, near):
        def visit(wanted, own, source, target, sems, device):
            if not near:

                @pl.when(wanted)
                def _():
                    remote(source, target, *sems, device).start()

                return

            @pl.when(wanted & own)
            def _():
                pltpu.make_async_copy(source, target, sems[1]).start()

            @pl.when(wanted & jnp.logical_not(own))
            def _():
                remote(source, target, *sems, device).start()

        z_all(chunk, visit, near)

    def z_sent(chunk):
        for near in (False, True):

            def visit(wanted, own, source, target, sems, device):
                @pl.when(wanted & jnp.logical_not(own) if near else wanted)
                def _():
                    remote(source, target, *sems, device).wait_send()

            z_all(chunk, visit, near)

    def far(step):
        return (here.z + step) % 4

    def handled(table, chunk, z):
        return here.second_layer | at_home(z) if table[chunk][3] else True

    def get_first(chunk, step):
        block = weight[get_table[chunk][0]].at[far(step), here.y, here.x, :, columns(get_table, chunk, here.core)]
        side = here.y_side() if (step + chunk) % 2 else here.x_side()
        return remote(block, block, get_one_send.at[chunk, step], get_one_recv.at[chunk, step], side)

    def get_second(chunk, step):
        ref, cut = weight[get_table[chunk][0]], columns(get_table, chunk, here.core)
        if (step + chunk) % 2:
            pair, side = ref.at[far(step), :, here.x, :, cut], here.x_side()
        else:
            pair, side = ref.at[far(step), here.y, :, :, cut], here.y_side()
        return remote(pair, pair, get_two_send.at[chunk, step], get_two_recv.at[chunk, step], side)

    def get_middle(chunk, z):
        block = weight[get_table[chunk][0]].at[z, :, :, :, columns(get_table, chunk, here.core)]
        return remote(block, block, get_mid_send.at[chunk, z % 2], get_mid_recv.at[chunk, z % 2], here.middle())

    def get_across(chunk):
        whole = weight[get_table[chunk][0]].at[:, :, :, :, columns(get_table, chunk, here.core)]
        return remote(whole, whole, get_side_send.at[chunk], get_side_recv.at[chunk], here.sibling())

    def one_step(chunk, step):
        def action():
            z = far(step)
            block = weight[get_table[chunk][0]].at[z, here.y, here.x, :, columns(get_table, chunk, here.core)]
            arrived(block, get_z_recv.at[chunk, z])
            get_first(chunk, step).start()

        when(handled(get_table, chunk, far(step)), action)

    def two_steps(chunk, step):
        def action():
            get_first(chunk, step).wait_recv()
            get_second(chunk, step).start()

        when(handled(get_table, chunk, far(step)), action)

    def three_steps(chunk, step):
        def action():
            get_second(chunk, step).wait_recv()
            if get_table[chunk][3]:

                @pl.when(here.first_layer)
                def _():
                    get_middle(chunk, far(step)).start()

        when(handled(get_table, chunk, far(step)), action)

    def pass_on(chunk):
        if get_table[chunk][3]:

            @pl.when(here.first_layer)
            def _():
                for k in range(2):
                    get_middle(chunk, 2 * (1 - here.home) + k).wait_recv()

        get_across(chunk).start()

    def gather(on_chunk):
        last = len(get_table)
        ahead, own_ahead, two_lag, three_lag, done_lag = GET_LAGS
        for chunk in range(1, last):
            z_start(chunk, True)
        small_shard()
        z_start(0, True)

        def z_first():
            for chunk in range(min(ahead, last)):
                z_start(chunk, False)

        pl.when(here.core == 0)(z_first)
        for chunk in range(min(own_ahead, last)):
            one_step(chunk, 0)
        for chunk in range(min(own_ahead, last) - 1):
            two_steps(chunk, 0)
        pl.when(here.core == 1)(z_first)
        for now in range(last + done_lag):
            if now + own_ahead < last:
                one_step(now + own_ahead, 0)
            if 0 <= now + own_ahead - 1 < last:
                two_steps(now + own_ahead - 1, 0)
            if now < last:
                for step in (1, 3, 2):
                    one_step(now, step)
            if now + ahead < last:
                z_start(now + ahead, False)
            if 0 <= now - two_lag < last:
                for step in (1, 3, 2):
                    two_steps(now - two_lag, step)
            if 0 <= now - three_lag < last:
                for step in range(4):
                    three_steps(now - three_lag, step)
                if not get_table[now - three_lag][3]:
                    pass_on(now - three_lag)
            if 0 <= now - three_lag - SHARED_LAG < last and get_table[now - three_lag - SHARED_LAG][3]:
                pass_on(now - three_lag - SHARED_LAG)
            for chunk in (now - done_lag - SHARED_LAG, now - done_lag):
                if 0 <= chunk < last and get_table[chunk][3] == (chunk != now - done_lag):
                    get_across(chunk).wait_recv()
                    on_chunk(chunk)

    def gathered():
        for chunk in range(len(get_table)):
            z_sent(chunk)
            for step in range(4):

                def action():
                    get_first(chunk, step).wait_send()
                    get_second(chunk, step).wait_send()

                when(handled(get_table, chunk, far(step)), action)
            if get_table[chunk][3]:

                @pl.when(here.first_layer)
                def _():
                    for k in range(2):
                        get_middle(chunk, 2 * here.home + k).wait_send()

            get_across(chunk).wait_send()

    def matrix(number, start, width):
        ref = weight[number]
        return ref[:, :, :, :, pl.ds(start, width)].reshape(features, width)

    alone = [True]

    def times(unroll):
        return unroll if alone[0] else 1

    def in_background(body):
        def whole():
            alone[0] = False
            body()
            alone[0] = True

        return whole

    def in_rows(body, start=0, count=tokens):
        block = 64

        def step(i, carry):
            body(pl.ds(pl.multiple_of(start + i * block, block), block))
            return carry

        lax.fori_loop(0, count // block, step, 0, unroll=times(ROWS_UNROLL))

    def sequence(m):
        return pl.ds(pl.multiple_of(m * slots, slots), slots)

    def normed(rows, rows_in, normal, scale, gain, target):
        centered = rows_in - jnp.mean(rows_in, axis=1, keepdims=True)
        inv = lax.rsqrt(jnp.mean(centered * centered, axis=1, keepdims=True) + epsilon)
        n = centered * inv
        normal[rows] = n
        scale[rows] = jnp.broadcast_to(inv, (n.shape[0], 128))
        target[rows] = (n * gain).astype(low)

    row_at = lax.broadcasted_iota(jnp.int32, (slots, 256), 0)
    first_row = row_at == 0

    def later(rows, places):
        return jnp.where(row_at >= places, pltpu.roll(rows, places, 0), 0.0)

    def sooner(rows, places):
        return jnp.where(row_at < slots - places, pltpu.roll(rows, slots - places, 0), 0.0)

    cuts = features // 256

    def mixer_blocks(m, body):
        def step(cut, carry):
            body(m, sequence(m), pl.ds(pl.multiple_of(cut * 256, 256), 256), cut)
            return carry

        lax.fori_loop(0, cuts, step, 0, unroll=times(MIX_UNROLL))

    def live_rows(m):
        return (row_at.astype(f32) < jnp.concatenate([live[m, 0:1, :]] * 2, axis=1)).astype(f32)

    def to_sibling(number, source, target):
        return remote(source, target, send.at[number], recv.at[number], here.sibling())

    def left_copy(k):
        return to_sibling(k, lefts[k].at[0], lefts[k].at[1])

    def right_sides(k):
        return (
            (projected, other_projected),
            (after_low, other_after),
            (expanded, other_expanded),
            (active, other_active),
        )[k]

    def right_copy(k):
        source, target = right_sides(k)
        half = widths[1 + k] // 2
        cut = pl.ds(pl.multiple_of((1 - here.core) * half, 128), half)
        return to_sibling(4 + k, source.at[:, cut], target)

    def small_copy():
        return to_sibling(8, small_terms.at[1 - here.core], other_small)

    def give(source, m):
        rows = pl.ds(m * slots, slots)
        return remote(source.at[rows], arrive.at[rows], give_send.at[m], give_recv.at[m], partner)

    def received(target, m):
        rows = sequence(m)
        arrived(arrive.at[rows], give_recv.at[m])
        target[rows] = arrive[rows]

    def turned(k):
        lefts[k][0] = (entered, gated, again, e_in)[k][...].T
        left_copy(k).start()

    def small_weights():
        filt[...] = matrix(0, 0, 128).astype(f32).T
        rows8[...] = matrix(0, 128, 128).astype(f32).T[:8]

    def enter(m):
        def body(rows):
            normed(rows, x_in[rows].astype(f32), norm_one, scale_one, rows8[3:4], entered)

        in_rows(body, m * slots, slots)

    def mix(m, rows, taken, cut):
        taps = [rows8[j : j + 1, taken] for j in range(3)]
        alive = live_rows(m)
        k = keys[rows, taken] * alive
        keys[rows, taken] = k
        v = values[rows, taken] * alive
        kernel = filt[:, taken] + taps[0] * k + taps[1] * later(k, 1) + taps[2] * later(k, 2)
        spec = left_dot(dft[...], parts(jnp.concatenate([v, kernel], axis=1)))
        value_spec[m, :, taken] = spec[:, :256]
        kernel_spec[m, :, taken] = spec[:, 256:]
        v_re, v_im = spec[:slots, :256], spec[slots:, :256]
        k_re, k_im = spec[:slots, 256:], spec[slots:, 256:]
        both = k_im * v_im
        re = k_re * v_re - jnp.where(first_row, 0.0, both)
        im = jnp.where(first_row, both, k_re * v_im + k_im * v_re)
        out = left_dot(idft[...], parts(jnp.concatenate([re, im], axis=0)))
        convolved[rows, taken] = out
        gated[rows, taken] = (queries[rows, taken] * out).astype(low)

    def mixer(m):
        rows = sequence(m)
        for k, target in enumerate((queries, keys, values)):
            target[rows] = left_dot(entered[rows], matrix(1, k * features, features))
        mixer_blocks(m, mix)

    def mixer_out(m):
        rows = sequence(m)
        total[rows] = x_in[rows].astype(f32) + left_dot(gated[rows], matrix(2, 0, features))

        def body(rows):
            normed(rows, total[rows], norm_two, scale_two, rows8[4:5], again)

        in_rows(body, m * slots, slots)

    def each_sequence(*bodies):
        def step(m, carry):
            for body in bodies:
                body(m)
            return carry

        lax.fori_loop(0, micro, step, 0)

    tile = 512

    def tiles(start, width, body):
        def step(i, carry):
            body(pl.multiple_of(start + i * tile, 128))
            return carry

        lax.fori_loop(0, width // tile, step, 0, unroll=times(TILE_UNROLL))

    def expand(start):
        gate = left_dot(again[...], matrix(3, start, tile))
        up = left_dot(again[...], matrix(3, pl.multiple_of(hidden + start, 128), tile))
        expanded[:, pl.ds(start, tile)] = gate.astype(low)
        expanded[:, pl.ds(pl.multiple_of(hidden + start, 128), tile)] = up.astype(low)
        active[:, pl.ds(start, tile)] = (gate * sigmoid(gate) * up).astype(low)

    def reduce_on(start, width):
        total[...] += dot_back(active[:, pl.ds(start, width)], matrix(4, start, width))

    def layer_done():
        right_copy(3).start()
        out_low[...] = total[...].astype(low)

    ends = {array: max(k for k, entry in enumerate(get_table) if entry[0] == array) for array in range(5)}

    def as_it_comes(chunk):
        array, start, width, _ = get_table[chunk]

        @pl.when(here.first_layer)
        @in_background
        def _():
            if array == 0:
                x_in[...] = feed[...]
                small_weights()
                each_sequence(enter)
                turned(0)
            if array == 1 and ends[1] == chunk:
                each_sequence(mixer)
                turned(1)
            if array == 2 and ends[2] == chunk:
                each_sequence(mixer_out)
                turned(2)
            if array == 3:
                tiles(start, width, expand)
            if array == 4:
                for half in (0, 1):
                    reduce_on(half * (hidden // 2) + start, width)

    def on_chunk(chunk):
        if chunk == ends[0]:
            fed()
        as_it_comes(chunk)

    gather(on_chunk)

    @pl.when(here.first_layer)
    def _():
        layer_done()
        for m in range(micro):
            give(out_low, m).start()
            give(out_low, m).wait_send()
        gathered()
        for m in range(micro):
            received(e_in, m)
        turned(3)

    @pl.when(here.second_layer)
    def _():
        small_weights()
        e_in[...] = feed[...]
        turned(3)
        gathered()
        each_sequence(functools.partial(received, x_in), enter, mixer, mixer_out)

        tiles(0, hidden, expand)
        reduce_on(0, hidden)
        layer_done()

    offsets, place = [], 0
    for array, _, width, _ in put_table:
        offsets.append(place)
        place += width if array in (1, 2, 3) else 0

    def one_in(chunk, z):
        array, start, width, _ = put_table[chunk]
        if array == 0:
            return one_small.at[z]
        if array == 4:
            return one_down.at[z, :, :, pl.ds(start, width)]
        return weight[3].at[z, 0, :, :, pl.ds(offsets[chunk], width)]

    def two_in(chunk, z):
        array, start, width, _ = put_table[chunk]
        if array == 0:
            return two_small.at[z]
        if array == 4:
            return two_down.at[z, :, pl.ds(start, width)]
        return weight[3].at[z, 1, 0, :, pl.ds(offsets[chunk], width)]

    def put_first(chunk, step):
        z = far(step)
        if step % 2:
            source, side = mine[chunk].at[z, :, 1 - here.x], here.x_side()
        else:
            source, side = mine[chunk].at[z, 1 - here.y], here.y_side()
        return remote(source, one_in(chunk, step), one_send.at[chunk, step], one_recv.at[chunk, step], side)

    def put_second(chunk, step):
        z = far(step)
        if step % 2:
            source, side = mine[chunk].at[z, 1 - here.y, here.x], here.y_side()
        else:
            source, side = mine[chunk].at[z, here.y, 1 - here.x], here.x_side()
        return remote(source, two_in(chunk, step), two_send.at[chunk, step], two_recv.at[chunk, step], side)

    def put_third(chunk, step, act):
        z = far(step)
        source = mine[chunk].at[z, here.y, here.x]
        target = landed[put_table[chunk][0]].at[here.home, :, columns(put_table, chunk, here.core)]
        receive = z_recv.at[chunk, here.home, here.core]
        own = (here.z == z) & (here.core == here.layer)
        if act == "start":

            @pl.when(own)
            def _():
                pltpu.make_async_copy(source, target, receive).start()

        @pl.when(jnp.logical_not(own))
        def _():
            away = remote(source, target, z_send.at[chunk, step], receive, (here.layer, here.chip(z=z)))
            getattr(away, act)()

    def add(target, other):
        target[...] = (target[...].astype(f32) + other[...].astype(f32)).astype(target.dtype)

    def both_sides(array):
        if array:
            left_copy(array - 1).wait_recv()
            right_copy(array - 1).wait_recv()
        else:
            small_copy().wait_recv()

    def place_block(chunk, cut, block):
        rows = features // 16
        for z in range(4):
            for k in range(4):
                at = (z * 4 + k) * rows
                mine[chunk][z, k // 2, k % 2, :, cut] = block[at : at + rows].astype(low)

    def terms(chunk, wait=False):
        array, start, width, shared = put_table[chunk]
        if wait:
            both_sides(array)
        if array == 0:
            place_block(chunk, pl.ds(0, width), (small_terms[here.core] + other_small[...]).T)
        else:
            source, other = right_sides(array - 1)
            own_start = here.core * (widths[array] // 2) + start
            strip = 256 if width % 256 == 0 else width

            def body(i, carry):
                at = i * strip
                block = left_dot(lefts[array - 1][0], source[:, pl.ds(pl.multiple_of(own_start + at, 128), strip)])
                block += left_dot(lefts[array - 1][1], other[:, pl.ds(pl.multiple_of(start + at, 128), strip)])
                place_block(chunk, pl.ds(pl.multiple_of(at, 128), strip), block)
                return carry

            lax.fori_loop(0, width // strip, body, 0)
        if not shared:
            for step in range(4):
                put_first(chunk, step).start()
            return

        @pl.when(here.second_layer)
        def _():
            for step in range(4):
                put_first(chunk, step).start()

        @pl.when(here.first_layer)
        def _():
            if not any(entry[3] for entry in put_table[:chunk]):
                pl.semaphore_wait(ready_mid, 1)
            put_middle(chunk).start()

    def put_middle(chunk):
        source = mine[chunk].at[pl.ds(2 * (1 - here.home), 2)]
        return remote(source, mid_in(chunk), mid_send.at[chunk], mid_recv.at[chunk], here.middle())

    def mid_in(chunk):
        _, start, width, _ = put_table[chunk]
        return weight[4].at[pl.ds(0, 2), :, :, :, pl.ds(start, width)]

    def sum_middle(chunk):
        put_middle(chunk).wait_recv()
        for z in range(2):
            for k in range(4):
                add(mine[chunk].at[2 * here.home + z, k // 2, k % 2], mid_in(chunk).at[z, k // 2, k % 2])
        for step in range(4):
            when(at_home(far(step)), lambda: put_first(chunk, step).start())

    def sum_one(chunk):
        for step in range(4):

            def action():
                z = far(step)
                put_first(chunk, step).wait_recv()
                for k in range(2):
                    if step % 2:
                        add(mine[chunk].at[z, k, here.x], one_in(chunk, step).at[k])
                    else:
                        add(mine[chunk].at[z, here.y, k], one_in(chunk, step).at[k])
                put_second(chunk, step).start()

            when(handled(put_table, chunk, far(step)), action)

    def sum_two(chunk):
        for step in range(4):

            def action():
                put_second(chunk, step).wait_recv()
                add(mine[chunk].at[far(step), here.y, here.x], two_in(chunk, step))
                put_third(chunk, step, "start")

            when(handled(put_table, chunk, far(step)), action)

    last = len(put_table)
    needs = {array: min(k for k, entry in enumerate(put_table) if entry[0] == array) for array in range(5)}
    down = [chunk for chunk in range(last) if put_table[chunk][0] == 4]

    @pl.when(here.first_layer)
    def _():
        for chunk in down:
            terms(chunk, wait=chunk == down[0])

    def expand_back(start):
        again = pl.multiple_of(hidden + start, 128)
        grad_act = left_dot(e_in[...], matrix(4, start, tile))
        gate = expanded[:, pl.ds(start, tile)].astype(f32)
        up = expanded[:, pl.ds(again, tile)].astype(f32)
        sig = sigmoid(gate)
        grad_gate = (grad_act * up * (sig * (1.0 + gate * (1.0 - sig)))).astype(low)
        grad_up = (grad_act * (gate * sig)).astype(low)
        expanded[:, pl.ds(start, tile)] = grad_gate
        expanded[:, pl.ds(again, tile)] = grad_up

    tiles(0, hidden, expand_back)
    total[...] = dot_back(expanded[...], matrix(3, 0, 2 * hidden))
    right_copy(2).start()
    for side in (here.x_side(), here.y_side()):
        pl.semaphore_signal(ready, inc=1, device_id=side, device_id_type=MESH)
    if any(entry[3] for entry in put_table):

        @pl.when(here.first_layer)
        def _():
            pl.semaphore_signal(ready_mid, inc=1, device_id=here.middle(), device_id_type=MESH)


    def norm_grad(rows, grad, normal, scale, gain, at):
        n = normal[rows]
        small_terms[1, at : at + 1] += jnp.sum(grad * n, axis=0, keepdims=True)
        q = grad * gain
        back = q - jnp.mean(q, axis=1, keepdims=True) - n * jnp.mean(q * n, axis=1, keepdims=True)
        return scale[rows][:, :1] * back

    def after_back():
        small_terms[...] = jnp.zeros_like(small_terms)

        def body(rows):
            grad = e_in[rows].astype(f32) + norm_grad(rows, total[rows], norm_two, scale_two, rows8[4:5], 4)
            after[rows] = grad
            after_low[rows] = grad.astype(low)

        in_rows(body)
        right_copy(1).start()

    def gated_back():
        total[...] = dot_back(after_low[...], matrix(2, 0, features))

    def mix_back(m, rows, taken, cut):
        taps = [rows8[j : j + 1, taken] for j in range(3)]
        alive = live_rows(m)
        grad = total[rows, taken]
        projected[rows, taken] = (grad * convolved[rows, taken]).astype(low)
        spec = left_dot(dft[...], parts(grad * queries[rows, taken]))
        g_re, g_im = spec[:slots], spec[slots:]
        pairs = []
        for other in (kernel_spec, value_spec):
            o_re, o_im = other[m, :slots, taken], other[m, slots:, taken]
            both = o_im * g_im
            re = o_re * g_re + jnp.where(first_row, 0.0, both)
            im = jnp.where(first_row, both, o_re * g_im - o_im * g_re)
            pairs.append(jnp.concatenate([re, im], axis=0))
        paired = left_dot(idft[...], parts(jnp.concatenate(pairs, axis=1)))
        at_values = pl.ds(pl.multiple_of(2 * features + cut * 256, 256), 256)
        projected[rows, at_values] = (paired[:, :256] * alive).astype(low)
        grad_kernel = paired[:, 256:]
        small_terms[0, :, taken] += grad_kernel
        k = keys[rows, taken]
        for j in range(3):
            moved = later(k, j) if j else k
            small_terms[1, j : j + 1, taken] += jnp.sum(grad_kernel * moved, axis=0, keepdims=True)
        grad_keys = taps[0] * grad_kernel + taps[1] * sooner(grad_kernel, 1) + taps[2] * sooner(grad_kernel, 2)
        at_keys = pl.ds(pl.multiple_of(features + cut * 256, 256), 256)
        projected[rows, at_keys] = (grad_keys * alive).astype(low)

    def mixed_back(m):
        mixer_blocks(m, mix_back)

    def input_back(m):
        rows = sequence(m)
        total[rows] = dot_back(projected[rows], matrix(1, 0, 3 * features))

        def body(rows):
            grad = after[rows] + norm_grad(rows, total[rows], norm_one, scale_one, rows8[3:4], 3)
            grad_low[rows] = grad.astype(low)

        in_rows(body, m * slots, slots)

    pieces = [after_back, gated_back]
    for m in range(micro):
        pieces += [functools.partial(mixed_back, m), functools.partial(input_back, m)]

    def last_copies():
        right_copy(0).start()
        small_copy().start()

    pieces += [last_copies]

    @pl.when(here.second_layer)
    def _():
        after_back()
        gated_back()
        for m in range(micro):
            mixed_back(m)
            input_back(m)
            if m == micro - 1:
                terms(down[0], wait=True)
            if m:
                give(grad_low, m - 1).wait_send()
            give(grad_low, m).start()
        last_copies()
        turned(2)
        for chunk in down[1:]:
            terms(chunk)
        turned(1)
        turned(0)

    pl.semaphore_wait(ready, 2)

    def one_sum(act):
        @pl.when(here.core == 0)
        def _():
            for chunk, (array, _, width, shared) in enumerate(put_table):
                for half in range(2 if shared else 0):
                    target = landed[array].at[1 - here.home, :, columns(put_table, chunk, half)]
                    copy = pltpu.make_async_copy(nothing.at[:, pl.ds(0, width)], target, nothing_sems.at[chunk, half])
                    getattr(copy, act)()

    nothing[...] = jnp.zeros_like(nothing)
    one_sum("start")

    apart = here.core != here.layer
    over = (1 - here.core, here.partner)

    def swap(source, target, number, act):
        sems = swap_sems.at[number], swap_sems.at[number + 1]

        @pl.when(apart)
        def _():
            getattr(remote(source, target, *sems, over), act)()

        @pl.when(jnp.logical_not(apart))
        def _():
            getattr(pltpu.make_async_copy(source, target, sems[1]), act)()

    due = [max(0, needs[1] - len(pieces) + k) for k in range(len(pieces))]
    shared = [chunk for chunk in range(last) if put_table[chunk][3]]
    met = [4]

    swap(out_low, kept_out, 0, "start")
    for now in range(last + 1):
        for piece, at in zip(pieces, due):
            if at == now:
                pl.when(here.first_layer)(in_background(piece))
        early = shared if now == 1 else []
        for chunk in early + [now + 1]:
            if chunk < last and chunk not in down and (chunk not in shared or chunk in early):
                terms(chunk, wait=put_table[chunk][0] not in met)
                met.append(put_table[chunk][0])
        for chunk in shared:
            if now == chunk - 2:
                pl.when(here.first_layer)(functools.partial(sum_middle, chunk))
        if now < last:
            sum_one(now)
        if 1 <= now:
            sum_two(now - 1)
        if now == needs[0]:
            swap(grad_low, kept_grad, 2, "start")

    one_sum("wait")
    for chunk in range(last):
        for half in (0, 1):
            for slot in (0, 1):
                target = landed[put_table[chunk][0]].at[slot, :, columns(put_table, chunk, half)]
                wanted = (here.core == 1) | (here.home == slot) if put_table[chunk][3] else True
                when(wanted, functools.partial(arrived, target, z_recv.at[chunk, slot, half]))
        for step in range(4):

            def action():
                put_first(chunk, step).wait_send()
                put_second(chunk, step).wait_send()
                put_third(chunk, step, "wait_send")

            when(handled(put_table, chunk, far(step)), action)
        if put_table[chunk][3]:
            pl.when(here.first_layer)(lambda: put_middle(chunk).wait_send())

    @pl.when(own_feed)
    def _():
        remote(hidden_in, feed, feed_sems.at[1], feed_sems.at[0], partner).wait_send()
        remote(live_own, live, feed_sems.at[3], feed_sems.at[2], partner).wait_send()

    for k in range(4):
        left_copy(k).wait_send()
        right_copy(k).wait_send()
    small_copy().wait_send()
    pl.when(here.second_layer)(lambda: give(grad_low, micro - 1).wait_send())
    swap(out_low, kept_out, 0, "wait")
    swap(grad_low, kept_grad, 2, "wait")


def finish_kernel(*refs):
    landed, (out, grad) = refs[:5], refs[5:7]
    s_filters, s_taps, s_one, s_two = refs[7:11]
    sums, (to_out, to_grad) = refs[11:15], refs[15:17]
    to_out[...] = out[...]
    to_grad[...] = grad[...]
    small = landed[0][0].astype(jnp.float32) + landed[0][1].astype(jnp.float32)
    s_filters[...] = small[:, :128]
    own = small.shape[0]
    rows = jnp.pad(small[:, 128:], ((0, 128 - own), (0, 0))).T
    for j in range(3):
        s_taps[j] = rows[j : j + 1, :own]
    s_one[...] = rows[3:4, :own]
    s_two[...] = rows[4:5, :own]
    for number, result in enumerate(sums):
        result[...] = landed[1 + number][0].astype(jnp.float32) + landed[1 + number][1].astype(jnp.float32)


def fast_device(
    hidden_in, out_grad, lengths, gain_mixer, w_input, w_taps, filters, w_output, gain_mlp, w_gate_up, w_down
):
    micro, _, slots, features = hidden_in.shape
    tokens, rows = micro * slots, gain_mixer.shape[1]
    shards = (w_input[0], w_output[0], w_gate_up[0], w_down[0].T)
    widths = [256] + [shard.shape[1] for shard in shards]
    hidden = widths[4]
    get_table, put_table = chunks_of(GET_PIECES), chunks_of(PUT_PIECES)
    dft, idft = (jnp.asarray(table) for table in packed_tables(slots))
    low, f32 = jnp.bfloat16, jnp.float32
    anywhere = pl.BlockSpec(memory_space=pl.ANY)
    inside = pl.BlockSpec(memory_space=pltpu.VMEM)
    dma, vmem = pltpu.SemaphoreType.DMA, pltpu.VMEM
    act, act_low = (tokens, features), vmem((tokens, features), low)
    kinds = [jax.ShapeDtypeStruct((2, rows, width), low) for width in widths]
    kinds += [jax.ShapeDtypeStruct((tokens, features), low)] * 2
    room = [vmem((rows, 256), low), vmem((128, 128), f32)] + [vmem((micro, 8, 128), f32)] * 2
    room += [vmem((rows, max(entry[2] for entry in put_table)), low), dma((len(put_table), 2))]
    room += [vmem((4, 2, 2, rows, width), low) for width in widths]
    room += [act_low] * 6
    room += [vmem((slots, features), f32), vmem((8, features), f32), vmem(act, f32), vmem(act, f32)]
    room += [vmem((tokens, 128), f32)] * 2
    room += [act_low] * 3 + [vmem(act, f32)] * 4 + [vmem((micro, 2 * slots, features), f32)] * 2
    room += [vmem(act, f32)] * 2 + [vmem((tokens, 2 * hidden), low), vmem((tokens, hidden), low)]
    room += [vmem((tokens, 3 * features), low), act_low, vmem((2, slots, features), f32)]
    room += [vmem((2, features, tokens), low)] * 4
    room += [vmem((slots, features), f32)] + [vmem((tokens, width // 2), low) for width in widths[1:]]
    room += [vmem((4, 2, 2, rows, entry[2]), low) for entry in put_table]
    for width in (128, hidden // 2):
        room += [vmem((4, 2, rows, width), low), vmem((4, rows, width), low)]
    got, put = len(get_table), len(put_table)
    room += [dma((got, 2, 2))] + [dma((got, 4))] * 5 + [dma((got, 2))] * 2 + [dma((got,))] * 2 + [dma((4,))]
    room += [dma((4,)), dma((micro,)), dma((micro,)), dma((9,)), dma((9,))]
    room += [dma((put, 4))] * 5 + [dma((put, 2, 2))] + [dma((put,))] * 2 + [pltpu.SemaphoreType.REGULAR] * 2
    results = pl.pallas_call(
        functools.partial(layer_kernel, get_table, put_table, widths),
        out_shape=kinds,
        in_specs=[inside] * 4 + [pl.BlockSpec(memory_space=pltpu.SMEM)] + [inside] * 2 + [anywhere] * 6,
        out_specs=[anywhere] * 7,
        scratch_shapes=room,
        compiler_params=pltpu.CompilerParams(
            collective_id=0, has_side_effects=True, vmem_limit_bytes=62 * 1024 * 1024
        ),
    )(
        filters[0].T,
        w_taps[0],
        gain_mixer,
        gain_mlp,
        lengths.T,
        dft,
        idft,
        *shards,
        hidden_in.reshape(tokens, features),
        out_grad.reshape(tokens, features),
    )
    kinds = [(rows, 128), (3, 1, rows), (1, rows), (1, rows)] + [(rows, width) for width in widths[1:]]
    kinds = [jax.ShapeDtypeStruct(kind, f32) for kind in kinds] + kinds_of(results[5:])
    s_filters, s_taps, s_one, s_two, s_in, s_out, s_gu, s_dt, layer_out, input_grad = pl.pallas_call(
        finish_kernel,
        out_shape=kinds,
        in_specs=[inside] * 7,
        out_specs=[inside] * 10,
        compiler_params=pltpu.CompilerParams(vmem_limit_bytes=62 * 1024 * 1024),
    )(*results)
    shape = (1, micro, 1, slots, features)
    return (
        layer_out.reshape(shape),
        input_grad.reshape(shape),
        s_one,
        s_in[None],
        s_taps.transpose(1, 0, 2),
        s_filters.T[None],
        s_out[None],
        s_two,
        s_gu[None],
        s_dt.T[None],
    )


def kinds_of(arrays):
    return [jax.ShapeDtypeStruct(array.shape, array.dtype) for array in arrays]


def solution(mesh):
    placed = (
        P(None, "dp", None, None),
        P(None, "dp", None, None),
        P(None, "dp"),
        P("section", "dp"),
        P("section", "dp", None),
        P("section", None, "dp"),
        P("section", None, "dp"),
        P("section", "dp", None),
        P("section", "dp"),
        P("section", "dp", None),
        P("section", None, "dp"),
    )
    return jax.shard_map(
        fast_device if mesh.shape["dp"] == 16 and mesh.shape["section"] == 2 else on_device,
        mesh=mesh,
        in_specs=placed,
        out_specs=(
            P("section", None, "dp", None, None),
            P("section", None, "dp", None, None),
            P("section", "dp"),
            P("section", "dp", None),
            P("section", None, "dp"),
            P("section", None, "dp"),
            P("section", "dp", None),
            P("section", "dp"),
            P("section", "dp", None),
            P("section", None, "dp"),
        ),
        check_vma=False,
    )
```

```python
import functools
import math

import jax
import jax.numpy as jnp
import ml_dtypes
import numpy as np
from jax import lax
from jax.experimental import pallas as pl
from jax.experimental.pallas import tpu as pltpu
from jax.sharding import PartitionSpec as P

MESH = pl.DeviceIdType.MESH

epsilon = 1e-05
GET_PIECES = (
    (0, 128, False),
    (1, 384, False),
    (1, 384, False),
    (1, 384, False),
    (2, 384, False),
    (3, 1024, True),
    (3, 1024, False),
    (3, 1024, False),
    (4, 640, False),
    (4, 640, False),
    (4, 256, False),
)
PUT_PIECES = (
    (4, 768, False),
    (4, 768, False),
    (3, 1024, False),
    (3, 1024, False),
    (1, 384, False),
    (1, 384, False),
    (0, 128, False),
    (1, 384, False),
    (2, 384, False),
    (3, 512, True),
    (3, 512, True),
)
GET_LAGS = (4, 7, 1, 2, 3)
SHARED_LAG = 3
STEP_WORK = 4.2
ROWS_UNROLL = 2
MIX_UNROLL = 3
TILE_UNROLL = 2


def passed_along(value, axis, steps):
    count = lax.axis_size(axis)
    first, last = (max(0, -steps), min(count, count - steps))
    return lax.ppermute(value, axis, [(source, source + steps) for source in range(first, last)])


def split_dot(left_side, right_side):
    return jnp.dot(
        left_side, right_side, precision=lax.Precision.HIGH, preferred_element_type=jnp.float32
    )


def split_rows(left_side, right_side):
    return lax.dot_general(
        left_side,
        right_side,
        (((0,), (0,)), ((), ())),
        precision=lax.Precision.HIGH,
        preferred_element_type=jnp.float32,
    )


def dot_rows(left_side, right_side):
    return lax.dot_general(
        left_side, right_side, (((0,), (0,)), ((), ())), preferred_element_type=jnp.float32
    )


def dot_back(left_side, right_side):
    return lax.dot_general(
        left_side, right_side, (((1,), (1,)), ((), ())), preferred_element_type=jnp.float32
    )


def tables(length):
    period = 2 * length
    freq_index = lax.broadcasted_iota(jnp.int32, (length + 1, length), 0)
    time_index = lax.broadcasted_iota(jnp.int32, (length + 1, length), 1)
    angles = (freq_index * time_index % period).astype(jnp.float32) * (2.0 * math.pi / period)
    edge_rows = (freq_index[:, :1] == 0) | (freq_index[:, :1] == length)
    inverse_weight = jnp.where(edge_rows, 1.0, 2.0) / period
    dft_stack = jnp.concatenate([jnp.cos(angles), -jnp.sin(angles)], axis=0)
    return (dft_stack, inverse_weight)


def spectrum(dft_tables, signal):
    dft_stack, inverse_weight = dft_tables
    stacked_out = split_dot(dft_stack, signal)
    middle_row = stacked_out.shape[0] // 2
    return (stacked_out[:middle_row], stacked_out[middle_row:])


def inverse(dft_tables, real_part, imag_part):
    dft_stack, inverse_weight = dft_tables
    return split_rows(
        dft_stack, jnp.concatenate([inverse_weight * real_part, inverse_weight * imag_part], axis=0)
    )


def normalize(input_rows):
    centered = input_rows - jnp.mean(input_rows, axis=1, keepdims=True)
    inv_scale = lax.rsqrt(jnp.mean(centered * centered, axis=1, keepdims=True) + epsilon)
    return (centered * inv_scale, inv_scale)


def norm_back(grad_normed, normed, inv_scale):
    return inv_scale * (
        grad_normed
        - jnp.mean(grad_normed, axis=1, keepdims=True)
        - normed * jnp.mean(grad_normed * normed, axis=1, keepdims=True)
    )


def delayed(input_rows, places):
    return jnp.pad(input_rows, ((places, 0), (0, 0)))[: input_rows.shape[0]]


def advanced(input_rows, places):
    return jnp.pad(input_rows, ((0, places), (0, 0)))[places:]


def layer_forward(input_rows, active_rows, weights, dft_tables):
    gain_one, w_inner, w_tap_rows, filt_static, w_outer, gain_two, w_expand, w_reduce = weights
    hidden_size_model = w_outer.shape[0]
    hidden_width = w_reduce.shape[0]
    tap_weights = w_tap_rows.astype(jnp.float32)
    normed_one, scale_one = normalize(input_rows)
    entered = (normed_one * gain_one.astype(jnp.float32)).astype(jnp.bfloat16)
    projected = jnp.dot(entered, w_inner, preferred_element_type=jnp.float32)
    queries = projected[:, :hidden_size_model]
    keys_part = projected[:, hidden_size_model : 2 * hidden_size_model] * active_rows
    values_part = projected[:, 2 * hidden_size_model :] * active_rows
    dynamic = (
        tap_weights[0] * keys_part
        + tap_weights[1] * delayed(keys_part, 1)
        + tap_weights[2] * delayed(keys_part, 2)
    )
    kernel = filt_static.astype(jnp.float32) + dynamic
    joint_re, joint_im = spectrum(dft_tables, jnp.concatenate([values_part, kernel], axis=1))
    value_re = joint_re[:, :hidden_size_model]
    kernel_re = joint_re[:, hidden_size_model:]
    value_im = joint_im[:, :hidden_size_model]
    kernel_im = joint_im[:, hidden_size_model:]
    convolved = inverse(
        dft_tables,
        kernel_re * value_re - kernel_im * value_im,
        kernel_re * value_im + kernel_im * value_re,
    )
    gated_rows = (queries * convolved).astype(jnp.bfloat16)
    after_mixer = input_rows + jnp.dot(gated_rows, w_outer, preferred_element_type=jnp.float32)
    normed_two, scale_two = normalize(after_mixer)
    entered_two = (normed_two * gain_two.astype(jnp.float32)).astype(jnp.bfloat16)
    expanded = jnp.dot(entered_two, w_expand, preferred_element_type=jnp.float32)
    gate_part = expanded[:, :hidden_width]
    up_part = expanded[:, hidden_width:]
    activated = (jax.nn.silu(gate_part) * up_part).astype(jnp.bfloat16)
    result = after_mixer + jnp.dot(activated, w_reduce, preferred_element_type=jnp.float32)
    stash = (
        normed_one,
        scale_one,
        entered,
        queries,
        keys_part,
        (value_re, value_im, kernel_re, kernel_im),
        convolved,
        gated_rows,
        normed_two,
        scale_two,
        entered_two,
        gate_part,
        up_part,
        activated,
    )
    return (result, stash)


def mlp_backward(received_gradient, weights, stash):
    gain_one, w_inner, w_tap_rows, filt_static, w_outer, gain_two, w_expand, w_reduce = weights
    (
        normed_one,
        scale_one,
        entered,
        queries,
        keys_part,
        spectra,
        convolved,
        gated_rows,
        normed_two,
        scale_two,
        entered_two,
        gate_part,
        up_part,
        activated,
    ) = stash
    grad_low = received_gradient.astype(jnp.bfloat16)
    grad_reduce_w = dot_rows(activated, grad_low)
    grad_act = dot_back(grad_low, w_reduce)
    sigmoid_gate = jax.nn.sigmoid(gate_part)
    grad_gate = grad_act * up_part * (sigmoid_gate * (1.0 + gate_part * (1.0 - sigmoid_gate)))
    grad_up = grad_act * (gate_part * sigmoid_gate)
    grad_expand = jnp.concatenate([grad_gate, grad_up], axis=1).astype(jnp.bfloat16)
    grad_expand_w = dot_rows(entered_two, grad_expand)
    grad_entered_two = dot_back(grad_expand, w_expand)
    grad_gain_two = jnp.sum(grad_entered_two * normed_two, axis=0)
    grad_after = received_gradient + norm_back(
        grad_entered_two * gain_two.astype(jnp.float32), normed_two, scale_two
    )
    return (grad_after, (grad_gain_two, grad_expand_w, grad_reduce_w))


def mixer_backward(grad_after, active_rows, weights, dft_tables, stash):
    gain_one, w_inner, w_tap_rows, filt_static, w_outer, gain_two, w_expand, w_reduce = weights
    (
        normed_one,
        scale_one,
        entered,
        queries,
        keys_part,
        spectra,
        convolved,
        gated_rows,
        normed_two,
        scale_two,
        entered_two,
        gate_part,
        up_part,
        activated,
    ) = stash
    value_re, value_im, kernel_re, kernel_im = spectra
    hidden_size_model = w_outer.shape[0]
    tap_weights = w_tap_rows.astype(jnp.float32)
    grad_mix_low = grad_after.astype(jnp.bfloat16)
    grad_outer_w = dot_rows(gated_rows, grad_mix_low)
    grad_gated = dot_back(grad_mix_low, w_outer)
    grad_queries = grad_gated * convolved
    grad_conv = grad_gated * queries
    grad_re, grad_im = spectrum(dft_tables, grad_conv)
    paired_re = jnp.concatenate(
        [kernel_re * grad_re + kernel_im * grad_im, value_re * grad_re + value_im * grad_im], axis=1
    )
    paired_im = jnp.concatenate(
        [kernel_re * grad_im - kernel_im * grad_re, value_re * grad_im - value_im * grad_re], axis=1
    )
    paired = inverse(dft_tables, paired_re, paired_im)
    grad_values = paired[:, :hidden_size_model] * active_rows
    grad_kernel = paired[:, hidden_size_model:]
    grad_taps = jnp.stack(
        [
            jnp.sum(grad_kernel * keys_part, axis=0),
            jnp.sum(grad_kernel * delayed(keys_part, 1), axis=0),
            jnp.sum(grad_kernel * delayed(keys_part, 2), axis=0),
        ]
    )
    grad_keys = (
        tap_weights[0] * grad_kernel
        + tap_weights[1] * advanced(grad_kernel, 1)
        + tap_weights[2] * advanced(grad_kernel, 2)
    ) * active_rows
    grad_projected = jnp.concatenate([grad_queries, grad_keys, grad_values], axis=1).astype(
        jnp.bfloat16
    )
    inner_weight_gradient = dot_rows(entered, grad_projected)
    grad_entered = dot_back(grad_projected, w_inner)
    grad_gain_one = jnp.sum(grad_entered * normed_one, axis=0)
    grad_inputs = grad_after + norm_back(
        grad_entered * gain_one.astype(jnp.float32), normed_one, scale_one
    )
    return (
        grad_inputs,
        (grad_gain_one, inner_weight_gradient, grad_taps, grad_kernel, grad_outer_w),
    )


def add_terms(received, flipped):
    return tuple(
        (
            jnp.sum(member, axis=0).T if flip else jnp.sum(member, axis=0)
            for member, flip in zip(received, flipped)
        )
    )


def on_device(
    hidden_in,
    out_grad,
    lengths,
    gain_mixer,
    w_input,
    w_taps,
    filters,
    w_output,
    gain_mlp,
    w_gate_up,
    w_down,
):
    first_section = lax.axis_index("section") == 0
    micro_count = hidden_in.shape[0]
    seq_slots = hidden_in.shape[2]
    hidden_size_model = hidden_in.shape[3]
    dft_tables = tables(seq_slots)
    positions = lax.broadcasted_iota(jnp.int32, (seq_slots, 1), 0)
    weights = (
        lax.all_gather(gain_mixer[0], "dp", axis=0, tiled=True),
        lax.all_gather(w_input[0], "dp", axis=0, tiled=True),
        lax.all_gather(w_taps[0], "dp", axis=1, tiled=True),
        lax.all_gather(filters[0], "dp", axis=1, tiled=True),
        lax.all_gather(w_output[0], "dp", axis=0, tiled=True),
        lax.all_gather(gain_mlp[0], "dp", axis=0, tiled=True),
        lax.all_gather(w_gate_up[0], "dp", axis=0, tiled=True),
        lax.all_gather(w_down[0], "dp", axis=1, tiled=True),
    )
    arriving = jnp.zeros((seq_slots, hidden_size_model), jnp.bfloat16)
    outgoing_list = []
    saved_activations = []
    for forward_step in range(micro_count + 1):
        own_index = min(forward_step, micro_count - 1)
        prior_index = max(forward_step - 1, 0)
        input_rows = jnp.where(first_section, hidden_in[own_index, 0], arriving).astype(jnp.float32)
        length_now = jnp.where(first_section, lengths[own_index, 0], lengths[prior_index, 0])
        active_rows = (positions < length_now).astype(jnp.float32)
        result, stash = layer_forward(input_rows, active_rows, weights, dft_tables)
        outgoing = result.astype(jnp.bfloat16)
        outgoing_list.append(outgoing)
        if forward_step < micro_count:
            arriving = passed_along(outgoing, "section", 1)
        saved_activations.append((input_rows, active_rows))
    coming = jnp.zeros((seq_slots, hidden_size_model), jnp.bfloat16)
    mlp_totals = None
    mixer_totals = None
    grads_out = []
    for backward_step in range(micro_count + 1):
        saved_slot_index = micro_count - backward_step
        last_index = max(micro_count - 1 - backward_step, 0)
        live_factor = 1.0 if backward_step < micro_count else 0.0
        received_gradient = jnp.where(
            first_section,
            coming.astype(jnp.float32),
            out_grad[last_index, 0].astype(jnp.float32) * live_factor,
        )
        input_rows, active_rows = saved_activations[saved_slot_index]
        result, stash = layer_forward(input_rows, active_rows, weights, dft_tables)
        grad_after, mlp_grads = mlp_backward(received_gradient, weights, stash)
        mlp_totals = (
            mlp_grads if mlp_totals is None else jax.tree.map(jnp.add, mlp_totals, mlp_grads)
        )
        grad_inputs, mixer_grads = mixer_backward(
            grad_after, active_rows, weights, dft_tables, stash
        )
        mixer_totals = (
            mixer_grads
            if mixer_totals is None
            else jax.tree.map(jnp.add, mixer_totals, mixer_grads)
        )
        outgoing = grad_inputs.astype(jnp.bfloat16)
        grads_out.append(outgoing)
        if backward_step < micro_count:
            coming = passed_along(outgoing, "section", -1)
    first_outputs = jnp.stack(outgoing_list[:micro_count])
    second_outputs = jnp.stack(outgoing_list[1:])
    layer_out = jnp.where(first_section, first_outputs, second_outputs)[None, :, None]
    first_grads = jnp.stack(
        [grads_out[micro_count - batch_index] for batch_index in range(micro_count)]
    )
    second_grads = jnp.stack(
        [grads_out[micro_count - 1 - batch_index] for batch_index in range(micro_count)]
    )
    input_grad = jnp.where(first_section, first_grads, second_grads)[None, :, None]
    all_parts = (
        lax.all_to_all(
            mixer_totals[0][None].astype(jnp.bfloat16),
            "dp",
            split_axis=1,
            concat_axis=0,
            tiled=True,
        ).astype(jnp.float32),
        lax.all_to_all(
            mixer_totals[1][None].astype(jnp.bfloat16),
            "dp",
            split_axis=1,
            concat_axis=0,
            tiled=True,
        ).astype(jnp.float32),
        lax.all_to_all(
            mixer_totals[2].T[None].astype(jnp.bfloat16),
            "dp",
            split_axis=1,
            concat_axis=0,
            tiled=True,
        ).astype(jnp.float32),
        lax.all_to_all(
            mixer_totals[3].T[None].astype(jnp.bfloat16),
            "dp",
            split_axis=1,
            concat_axis=0,
            tiled=True,
        ).astype(jnp.float32),
        lax.all_to_all(
            mixer_totals[4][None].astype(jnp.bfloat16),
            "dp",
            split_axis=1,
            concat_axis=0,
            tiled=True,
        ).astype(jnp.float32),
        lax.all_to_all(
            mlp_totals[0][None].astype(jnp.bfloat16), "dp", split_axis=1, concat_axis=0, tiled=True
        ).astype(jnp.float32),
        lax.all_to_all(
            mlp_totals[1][None].astype(jnp.bfloat16), "dp", split_axis=1, concat_axis=0, tiled=True
        ).astype(jnp.float32),
        lax.all_to_all(
            mlp_totals[2].T[None].astype(jnp.bfloat16),
            "dp",
            split_axis=1,
            concat_axis=0,
            tiled=True,
        ).astype(jnp.float32),
    )
    summed = add_terms(all_parts, (False, False, True, True, False, False, False, True))
    return (
        layer_out,
        input_grad,
        summed[0][None],
        summed[1][None],
        summed[2][None],
        summed[3][None],
        summed[4][None],
        summed[5][None],
        summed[6][None],
        summed[7][None],
    )


class Place:
    def __init__(self):
        self.core = lax.axis_index("section")
        self.index = lax.axis_index("dp")
        self.z = self.index // 4
        self.y = self.index // 2 % 2
        self.x = self.index % 2
        self.layer = 1 - (self.z + 1) // 2 % 2
        self.home = self.z // 2
        self.first_layer = self.layer == 0
        self.second_layer = self.layer == 1
        self.partner = self.chip(z=self.z + 1 - 2 * (self.z % 2))

    def chip(self, z=None, y=None, x=None):
        z, y, x = (a if a is not None else b for a, b in ((z, self.z), (y, self.y), (x, self.x)))
        return z * 4 + y * 2 + x

    def x_side(self):
        return (self.core, self.chip(x=1 - self.x))

    def y_side(self):
        return (self.core, self.chip(y=1 - self.y))

    def sibling(self):
        return (1 - self.core, self.index)

    def middle(self):
        return (self.core, self.chip(z=3 - self.z))

    def greet(self):
        barrier = pltpu.get_barrier_semaphore()
        others = [self.x_side(), self.y_side(), self.sibling()]
        for step in (1, 2, 3):
            chip = self.chip(z=(self.z + step) % 4)
            others += [(0, chip), (1, chip)]
        for other in others:
            pl.semaphore_signal(barrier, inc=1, device_id=other, device_id_type=MESH)
        pl.semaphore_wait(barrier, len(others))


def remote(source, target, send, receive, device):
    return pltpu.make_async_remote_copy(
        src_ref=source,
        dst_ref=target,
        send_sem=send,
        recv_sem=receive,
        device_id=device,
        device_id_type=MESH,
    )


def chunks_of(pieces):
    table, places = [], {}
    for array, width, shared in pieces:
        start = places.get(array, 0)
        table.append((array, start, width, shared))
        places[array] = start + width
    return table


def left_dot(left_side, right_side):
    return lax.dot_general(
        left_side, right_side, (((1,), (0,)), ((), ())), preferred_element_type=jnp.float32
    )


def sigmoid(value):
    return 0.5 * jnp.tanh(0.5 * value) + 0.5


def parts(signal):
    high = signal.astype(jnp.bfloat16)
    rest = (signal - high.astype(jnp.float32)).astype(jnp.bfloat16)
    return jnp.concatenate([high, high, rest], axis=0)


def halves_of(table):
    high = table.astype(ml_dtypes.bfloat16)
    rest = (table - high.astype(np.float64)).astype(ml_dtypes.bfloat16)
    return np.concatenate([high, rest, high], axis=1)


def packed_tables(length):
    period = 2 * length
    freq, time = np.arange(length)[:, None], np.arange(length)[None, :]
    angles = (freq * time % period) * (2.0 * math.pi / period)
    sines = np.where(freq == 0, 1.0 - 2.0 * (time % 2), -np.sin(angles))
    table = np.concatenate([np.cos(angles), sines], axis=0)
    weight = np.where(np.arange(period)[:, None] % length == 0, 1.0, 2.0) / period
    return halves_of(table), halves_of((table * weight).T)


def layer_kernel(get_table, put_table, widths, *refs):
    refs = list(refs)

    def take(number):
        taken = refs[:number]
        del refs[:number]
        return taken

    filters_in, taps_in, gain_one_in, gain_two_in, lengths_in, dft, idft = take(7)
    shards, (hidden_in, grad_in) = [None] + take(4), take(2)
    landed, (kept_out, kept_grad) = take(5), take(2)
    own_small, rows_in, live_own, live, nothing, nothing_sems = take(6)
    weight = take(5)
    feed, arrive, x_in, e_in, out_low, grad_low = take(6)
    filt, rows8, norm_one, norm_two, scale_one, scale_two = take(6)
    entered, gated, again, queries, keys, values, convolved, value_spec, kernel_spec = take(9)
    total, after, expanded, active, projected, after_low, small_terms = take(7)
    lefts = take(4)
    other_small, other_projected, other_after, other_expanded, other_active = take(5)
    mine = take(len(put_table))
    one_small, two_small, one_down, two_down = take(4)
    get_z_send, get_z_recv, get_one_send, get_one_recv, get_two_send, get_two_recv = take(6)
    get_mid_send, get_mid_recv, get_side_send, get_side_recv, feed_sems = take(5)
    swap_sems, give_send, give_recv, send, recv = take(5)
    one_send, one_recv, two_send, two_recv, z_send, z_recv, mid_send, mid_recv, ready, ready_mid = take(10)

    here = Place()
    tokens, features = x_in.shape
    slots = filt.shape[0]
    micro = tokens // slots
    hidden = active.shape[1]
    f32, low = jnp.float32, jnp.bfloat16
    shards[0] = own_small

    here.greet()

    for m in range(micro):
        live_own[m] = jnp.full(live_own.shape[1:], lengths_in[0, m], jnp.int32).astype(f32)

    own_feed = here.core == here.layer
    partner = (here.core, here.partner)
    for layer, kept, given in ((0, hidden_in, grad_in), (1, grad_in, hidden_in)):

        @pl.when(own_feed & (here.layer == layer))
        def _():
            pltpu.make_async_copy(kept, feed, feed_sems.at[0]).start()
            pltpu.make_async_copy(live_own, live, feed_sems.at[2]).start()
            remote(given, feed, feed_sems.at[1], feed_sems.at[0], partner).start()
            remote(live_own, live, feed_sems.at[3], feed_sems.at[2], partner).start()

    def arrived(target, receive):
        pltpu.make_async_copy(target, target, receive).wait()

    def fed():
        arrived(feed, feed_sems.at[0])
        arrived(live, feed_sems.at[2])

    def small_shard():
        rows_in[...] = jnp.zeros_like(rows_in)
        own = taps_in.shape[1]
        rows_in[0:3, 0:own] = taps_in[...].astype(f32)
        rows_in[3:4, 0:own] = gain_one_in[...].astype(f32)
        rows_in[4:5, 0:own] = gain_two_in[...].astype(f32)
        own_small[:, :128] = filters_in[...]
        own_small[:, 128:] = rows_in[...].T[:own].astype(low)

    def columns(table, chunk, half):
        array, start, width, _ = table[chunk]
        return pl.ds(pl.multiple_of(half * (widths[array] // 2) + start, 128), width)

    def at_home(z):
        return z // 2 == here.home

    def when(condition, action):
        if condition is True:
            action()
        else:
            pl.when(condition)(action)

    def z_all(chunk, visit, near):
        array, _, _, shared = get_table[chunk]
        for number, plane in enumerate((1 - here.core, 2 + here.core)):
            wanted = (plane == here.z) if near else (plane != here.z)
            if shared:
                wanted = wanted & ((here.core == 1) | (here.home == number))
            for half in (0, 1):
                cut = columns(get_table, chunk, half)
                source, target = shards[array].at[:, cut], weight[array].at[here.z, here.y, here.x, :, cut]
                sems = get_z_send.at[chunk, number, half], get_z_recv.at[chunk, here.z]
                visit(wanted, here.core == half, source, target, sems, (half, here.chip(z=plane)))

    def z_start(chunk, near):
        def visit(wanted, own, source, target, sems, device):
            if not near:

                @pl.when(wanted)
                def _():
                    remote(source, target, *sems, device).start()

                return

            @pl.when(wanted & own)
            def _():
                pltpu.make_async_copy(source, target, sems[1]).start()

            @pl.when(wanted & jnp.logical_not(own))
            def _():
                remote(source, target, *sems, device).start()

        z_all(chunk, visit, near)

    def z_sent(chunk):
        for near in (False, True):

            def visit(wanted, own, source, target, sems, device):
                @pl.when(wanted & jnp.logical_not(own) if near else wanted)
                def _():
                    remote(source, target, *sems, device).wait_send()

            z_all(chunk, visit, near)

    def far(step):
        return (here.z + step) % 4

    def handled(table, chunk, z):
        return here.second_layer | at_home(z) if table[chunk][3] else True

    def get_first(chunk, step):
        block = weight[get_table[chunk][0]].at[far(step), here.y, here.x, :, columns(get_table, chunk, here.core)]
        side = here.y_side() if (step + chunk) % 2 else here.x_side()
        return remote(block, block, get_one_send.at[chunk, step], get_one_recv.at[chunk, step], side)

    def get_second(chunk, step):
        ref, cut = weight[get_table[chunk][0]], columns(get_table, chunk, here.core)
        if (step + chunk) % 2:
            pair, side = ref.at[far(step), :, here.x, :, cut], here.x_side()
        else:
            pair, side = ref.at[far(step), here.y, :, :, cut], here.y_side()
        return remote(pair, pair, get_two_send.at[chunk, step], get_two_recv.at[chunk, step], side)

    def get_middle(chunk, z):
        block = weight[get_table[chunk][0]].at[z, :, :, :, columns(get_table, chunk, here.core)]
        return remote(block, block, get_mid_send.at[chunk, z % 2], get_mid_recv.at[chunk, z % 2], here.middle())

    def get_across(chunk):
        whole = weight[get_table[chunk][0]].at[:, :, :, :, columns(get_table, chunk, here.core)]
        return remote(whole, whole, get_side_send.at[chunk], get_side_recv.at[chunk], here.sibling())

    def one_step(chunk, step):
        def action():
            z = far(step)
            block = weight[get_table[chunk][0]].at[z, here.y, here.x, :, columns(get_table, chunk, here.core)]
            arrived(block, get_z_recv.at[chunk, z])
            get_first(chunk, step).start()

        when(handled(get_table, chunk, far(step)), action)

    def two_steps(chunk, step):
        def action():
            get_first(chunk, step).wait_recv()
            get_second(chunk, step).start()

        when(handled(get_table, chunk, far(step)), action)

    def three_steps(chunk, step):
        def action():
            get_second(chunk, step).wait_recv()
            if get_table[chunk][3]:

                @pl.when(here.first_layer)
                def _():
                    get_middle(chunk, far(step)).start()

        when(handled(get_table, chunk, far(step)), action)

    def pass_on(chunk):
        if get_table[chunk][3]:

            @pl.when(here.first_layer)
            def _():
                for k in range(2):
                    get_middle(chunk, 2 * (1 - here.home) + k).wait_recv()

        get_across(chunk).start()

    def gather(on_step):
        last = len(get_table)
        ahead, own_ahead, two_lag, three_lag, done_lag = GET_LAGS
        for chunk in range(1, last):
            z_start(chunk, True)
        small_shard()
        z_start(0, True)

        def z_first():
            for chunk in range(min(ahead, last)):
                z_start(chunk, False)

        pl.when(here.core == 0)(z_first)
        for chunk in range(min(own_ahead, last)):
            one_step(chunk, 0)
        for chunk in range(min(own_ahead, last) - 1):
            two_steps(chunk, 0)
        pl.when(here.core == 1)(z_first)
        for now in range(last + done_lag):
            if now + own_ahead < last:
                one_step(now + own_ahead, 0)
            if 0 <= now + own_ahead - 1 < last:
                two_steps(now + own_ahead - 1, 0)
            if now < last:
                for step in (1, 3, 2):
                    one_step(now, step)
            if now + ahead < last:
                z_start(now + ahead, False)
            if 0 <= now - two_lag < last:
                for step in (1, 3, 2):
                    two_steps(now - two_lag, step)
            if 0 <= now - three_lag < last:
                for step in range(4):
                    three_steps(now - three_lag, step)
                if not get_table[now - three_lag][3]:
                    pass_on(now - three_lag)
            if 0 <= now - three_lag - SHARED_LAG < last and get_table[now - three_lag - SHARED_LAG][3]:
                pass_on(now - three_lag - SHARED_LAG)
            for chunk in (now - done_lag - SHARED_LAG, now - done_lag):
                if 0 <= chunk < last and get_table[chunk][3] == (chunk != now - done_lag):
                    get_across(chunk).wait_recv()
            on_step(now, now == last + done_lag - 1)

    def gathered():
        for chunk in range(len(get_table)):
            z_sent(chunk)
            for step in range(4):

                def action():
                    get_first(chunk, step).wait_send()
                    get_second(chunk, step).wait_send()

                when(handled(get_table, chunk, far(step)), action)
            if get_table[chunk][3]:

                @pl.when(here.first_layer)
                def _():
                    for k in range(2):
                        get_middle(chunk, 2 * here.home + k).wait_send()

            get_across(chunk).wait_send()

    def matrix(number, start, width):
        ref = weight[number]
        return ref[:, :, :, :, pl.ds(start, width)].reshape(features, width)

    alone = [True]

    def times(unroll):
        return unroll if alone[0] else 1

    def in_background(body):
        def whole():
            alone[0] = False
            body()
            alone[0] = True

        return whole

    def in_rows(body, start=0, count=tokens):
        block = 64

        def step(i, carry):
            body(pl.ds(pl.multiple_of(start + i * block, block), block))
            return carry

        lax.fori_loop(0, count // block, step, 0, unroll=times(ROWS_UNROLL))

    def sequence(m):
        return pl.ds(pl.multiple_of(m * slots, slots), slots)

    def normed(rows, rows_in, normal, scale, gain, target):
        centered = rows_in - jnp.mean(rows_in, axis=1, keepdims=True)
        inv = lax.rsqrt(jnp.mean(centered * centered, axis=1, keepdims=True) + epsilon)
        n = centered * inv
        normal[rows] = n
        scale[rows] = jnp.broadcast_to(inv, (n.shape[0], 128))
        target[rows] = (n * gain).astype(low)

    row_at = lax.broadcasted_iota(jnp.int32, (slots, 256), 0)
    first_row = row_at == 0

    def later(rows, places):
        return jnp.where(row_at >= places, pltpu.roll(rows, places, 0), 0.0)

    def sooner(rows, places):
        return jnp.where(row_at < slots - places, pltpu.roll(rows, slots - places, 0), 0.0)

    cuts = features // 256

    def mixer_blocks(m, body):
        def step(cut, carry):
            body(m, sequence(m), pl.ds(pl.multiple_of(cut * 256, 256), 256), cut)
            return carry

        lax.fori_loop(0, cuts, step, 0, unroll=times(MIX_UNROLL))

    def live_rows(m):
        return (row_at.astype(f32) < jnp.concatenate([live[m, 0:1, :]] * 2, axis=1)).astype(f32)

    def to_sibling(number, source, target):
        return remote(source, target, send.at[number], recv.at[number], here.sibling())

    def left_copy(k):
        return to_sibling(k, lefts[k].at[0], lefts[k].at[1])

    def right_sides(k):
        return (
            (projected, other_projected),
            (after_low, other_after),
            (expanded, other_expanded),
            (active, other_active),
        )[k]

    def right_copy(k):
        source, target = right_sides(k)
        half = widths[1 + k] // 2
        cut = pl.ds(pl.multiple_of((1 - here.core) * half, 128), half)
        return to_sibling(4 + k, source.at[:, cut], target)

    def small_copy():
        return to_sibling(8, small_terms.at[1 - here.core], other_small)

    def give(source, m):
        rows = pl.ds(m * slots, slots)
        return remote(source.at[rows], arrive.at[rows], give_send.at[m], give_recv.at[m], partner)

    def received(target, m):
        rows = sequence(m)
        arrived(arrive.at[rows], give_recv.at[m])
        target[rows] = arrive[rows]

    def turned(k):
        lefts[k][0] = (entered, gated, again, e_in)[k][...].T
        left_copy(k).start()

    def small_weights():
        filt[...] = matrix(0, 0, 128).astype(f32).T
        rows8[...] = matrix(0, 128, 128).astype(f32).T[:8]

    def enter(m):
        def body(rows):
            normed(rows, x_in[rows].astype(f32), norm_one, scale_one, rows8[3:4], entered)

        in_rows(body, m * slots, slots)

    def mix(m, rows, taken, cut):
        taps = [rows8[j : j + 1, taken] for j in range(3)]
        alive = live_rows(m)
        k = keys[rows, taken] * alive
        keys[rows, taken] = k
        v = values[rows, taken] * alive
        kernel = filt[:, taken] + taps[0] * k + taps[1] * later(k, 1) + taps[2] * later(k, 2)
        spec = left_dot(dft[...], parts(jnp.concatenate([v, kernel], axis=1)))
        value_spec[m, :, taken] = spec[:, :256]
        kernel_spec[m, :, taken] = spec[:, 256:]
        v_re, v_im = spec[:slots, :256], spec[slots:, :256]
        k_re, k_im = spec[:slots, 256:], spec[slots:, 256:]
        both = k_im * v_im
        re = k_re * v_re - jnp.where(first_row, 0.0, both)
        im = jnp.where(first_row, both, k_re * v_im + k_im * v_re)
        out = left_dot(idft[...], parts(jnp.concatenate([re, im], axis=0)))
        convolved[rows, taken] = out
        gated[rows, taken] = (queries[rows, taken] * out).astype(low)

    def project(m):
        rows = sequence(m)
        for k, target in enumerate((queries, keys, values)):
            target[rows] = left_dot(entered[rows], matrix(1, k * features, features))

    def mixer(m):
        mixer_blocks(m, mix)

    def mixer_out(m):
        rows = sequence(m)
        total[rows] = x_in[rows].astype(f32) + left_dot(gated[rows], matrix(2, 0, features))

        def body(rows):
            normed(rows, total[rows], norm_two, scale_two, rows8[4:5], again)

        in_rows(body, m * slots, slots)

    def each_sequence(*bodies):
        def step(m, carry):
            for body in bodies:
                body(m)
            return carry

        lax.fori_loop(0, micro, step, 0)

    tile = 512

    def tiles(start, width, body):
        def step(i, carry):
            body(pl.multiple_of(start + i * tile, 128))
            return carry

        lax.fori_loop(0, width // tile, step, 0, unroll=times(TILE_UNROLL))

    def expand(start):
        gate = left_dot(again[...], matrix(3, start, tile))
        up = left_dot(again[...], matrix(3, pl.multiple_of(hidden + start, 128), tile))
        expanded[:, pl.ds(start, tile)] = gate.astype(low)
        expanded[:, pl.ds(pl.multiple_of(hidden + start, 128), tile)] = up.astype(low)
        active[:, pl.ds(start, tile)] = (gate * sigmoid(gate) * up).astype(low)

    def reduce_on(start, width):
        total[...] += dot_back(active[:, pl.ds(start, width)], matrix(4, start, width))

    def layer_done():
        right_copy(3).start()
        out_low[...] = total[...].astype(low)

    def ready_at(array):
        return max(k for k, entry in enumerate(get_table) if entry[0] == array) + GET_LAGS[-1]

    def begin():
        x_in[...] = feed[...]
        small_weights()
        each_sequence(enter)
        turned(0)

    def mixed():
        mixer(micro - 1)
        turned(1)

    def mixed_out():
        each_sequence(mixer_out)
        turned(2)

    def reduce_both(start, width):
        for half in (0, 1):
            reduce_on(half * (hidden // 2) + start, width)

    plan = [(ready_at(0), 1.3, begin), (ready_at(1), 1.4, lambda: each_sequence(project))]
    plan += [(0, 2.2, functools.partial(mixer, m)) for m in range(micro - 1)] + [(0, 2.4, mixed)]
    plan += [(ready_at(2), 1.9, mixed_out)]
    ups = [
        (chunk + GET_LAGS[-1] + (SHARED_LAG if shared else 0), 1.7 * width / 1024, functools.partial(tiles, start, width, expand))
        for chunk, (array, start, width, shared) in enumerate(get_table)
        if array == 3
    ]
    plan += sorted(ups, key=lambda piece: piece[0])
    plan += [
        (chunk + GET_LAGS[-1], 1.0 * width / 1024, functools.partial(reduce_both, start, width))
        for chunk, (array, start, width, _) in enumerate(get_table)
        if array == 4
    ]

    def on_step(now, final):
        if now == ready_at(0):
            fed()
        chosen, spent = [], 0.0
        while plan and plan[0][0] <= now and (final or not chosen or spent + plan[0][1] <= STEP_WORK):
            chosen.append(plan[0][2])
            spent += plan.pop(0)[1]

        @pl.when(here.first_layer)
        @in_background
        def _():
            for piece in chosen:
                piece()

    gather(on_step)

    @pl.when(here.first_layer)
    def _():
        layer_done()
        for m in range(micro):
            give(out_low, m).start()
            give(out_low, m).wait_send()
        gathered()
        for m in range(micro):
            received(e_in, m)
        turned(3)

    @pl.when(here.second_layer)
    def _():
        small_weights()
        e_in[...] = feed[...]
        turned(3)
        gathered()
        each_sequence(functools.partial(received, x_in), enter, project, mixer, mixer_out)

        tiles(0, hidden, expand)
        reduce_on(0, hidden)
        layer_done()

    offsets, place = [], 0
    for array, _, width, _ in put_table:
        offsets.append(place)
        place += width if array in (1, 2, 3) else 0

    def one_in(chunk, z):
        array, start, width, _ = put_table[chunk]
        if array == 0:
            return one_small.at[z]
        if array == 4:
            return one_down.at[z, :, :, pl.ds(start, width)]
        return weight[3].at[z, 0, :, :, pl.ds(offsets[chunk], width)]

    def two_in(chunk, z):
        array, start, width, _ = put_table[chunk]
        if array == 0:
            return two_small.at[z]
        if array == 4:
            return two_down.at[z, :, pl.ds(start, width)]
        return weight[3].at[z, 1, 0, :, pl.ds(offsets[chunk], width)]

    def put_first(chunk, step):
        z = far(step)
        if step % 2:
            source, side = mine[chunk].at[z, :, 1 - here.x], here.x_side()
        else:
            source, side = mine[chunk].at[z, 1 - here.y], here.y_side()
        return remote(source, one_in(chunk, step), one_send.at[chunk, step], one_recv.at[chunk, step], side)

    def put_second(chunk, step):
        z = far(step)
        if step % 2:
            source, side = mine[chunk].at[z, 1 - here.y, here.x], here.y_side()
        else:
            source, side = mine[chunk].at[z, here.y, 1 - here.x], here.x_side()
        return remote(source, two_in(chunk, step), two_send.at[chunk, step], two_recv.at[chunk, step], side)

    def put_third(chunk, step, act):
        z = far(step)
        source = mine[chunk].at[z, here.y, here.x]
        target = landed[put_table[chunk][0]].at[here.home, :, columns(put_table, chunk, here.core)]
        receive = z_recv.at[chunk, here.home, here.core]
        own = (here.z == z) & (here.core == here.layer)
        if act == "start":

            @pl.when(own)
            def _():
                pltpu.make_async_copy(source, target, receive).start()

        @pl.when(jnp.logical_not(own))
        def _():
            away = remote(source, target, z_send.at[chunk, step], receive, (here.layer, here.chip(z=z)))
            getattr(away, act)()

    def add(target, other):
        target[...] = (target[...].astype(f32) + other[...].astype(f32)).astype(target.dtype)

    def both_sides(array):
        if array:
            left_copy(array - 1).wait_recv()
            right_copy(array - 1).wait_recv()
        else:
            small_copy().wait_recv()

    def place_block(chunk, cut, block):
        rows = features // 16
        for z in range(4):
            for k in range(4):
                at = (z * 4 + k) * rows
                mine[chunk][z, k // 2, k % 2, :, cut] = block[at : at + rows].astype(low)

    def terms(chunk, wait=False):
        array, start, width, shared = put_table[chunk]
        if wait:
            both_sides(array)
        if array == 0:
            place_block(chunk, pl.ds(0, width), (small_terms[here.core] + other_small[...]).T)
        else:
            source, other = right_sides(array - 1)
            own_start = here.core * (widths[array] // 2) + start
            strip = 256 if width % 256 == 0 else width

            def body(i, carry):
                at = i * strip
                block = left_dot(lefts[array - 1][0], source[:, pl.ds(pl.multiple_of(own_start + at, 128), strip)])
                block += left_dot(lefts[array - 1][1], other[:, pl.ds(pl.multiple_of(start + at, 128), strip)])
                place_block(chunk, pl.ds(pl.multiple_of(at, 128), strip), block)
                return carry

            lax.fori_loop(0, width // strip, body, 0)
        if not shared:
            for step in range(4):
                put_first(chunk, step).start()
            return

        @pl.when(here.second_layer)
        def _():
            for step in range(4):
                put_first(chunk, step).start()

        @pl.when(here.first_layer)
        def _():
            if not any(entry[3] for entry in put_table[:chunk]):
                pl.semaphore_wait(ready_mid, 1)
            put_middle(chunk).start()

    def put_middle(chunk):
        source = mine[chunk].at[pl.ds(2 * (1 - here.home), 2)]
        return remote(source, mid_in(chunk), mid_send.at[chunk], mid_recv.at[chunk], here.middle())

    def mid_in(chunk):
        _, start, width, _ = put_table[chunk]
        return weight[4].at[pl.ds(0, 2), :, :, :, pl.ds(start, width)]

    def sum_middle(chunk):
        put_middle(chunk).wait_recv()
        for z in range(2):
            for k in range(4):
                add(mine[chunk].at[2 * here.home + z, k // 2, k % 2], mid_in(chunk).at[z, k // 2, k % 2])
        for step in range(4):
            when(at_home(far(step)), lambda: put_first(chunk, step).start())

    def sum_one(chunk):
        for step in range(4):

            def action():
                z = far(step)
                put_first(chunk, step).wait_recv()
                for k in range(2):
                    if step % 2:
                        add(mine[chunk].at[z, k, here.x], one_in(chunk, step).at[k])
                    else:
                        add(mine[chunk].at[z, here.y, k], one_in(chunk, step).at[k])
                put_second(chunk, step).start()

            when(handled(put_table, chunk, far(step)), action)

    def sum_two(chunk):
        for step in range(4):

            def action():
                put_second(chunk, step).wait_recv()
                add(mine[chunk].at[far(step), here.y, here.x], two_in(chunk, step))
                put_third(chunk, step, "start")

            when(handled(put_table, chunk, far(step)), action)

    last = len(put_table)
    needs = {array: min(k for k, entry in enumerate(put_table) if entry[0] == array) for array in range(5)}
    down = [chunk for chunk in range(last) if put_table[chunk][0] == 4]

    @pl.when(here.first_layer)
    def _():
        for chunk in down:
            terms(chunk, wait=chunk == down[0])

    def expand_back(start):
        again = pl.multiple_of(hidden + start, 128)
        grad_act = left_dot(e_in[...], matrix(4, start, tile))
        gate = expanded[:, pl.ds(start, tile)].astype(f32)
        up = expanded[:, pl.ds(again, tile)].astype(f32)
        sig = sigmoid(gate)
        grad_gate = (grad_act * up * (sig * (1.0 + gate * (1.0 - sig)))).astype(low)
        grad_up = (grad_act * (gate * sig)).astype(low)
        expanded[:, pl.ds(start, tile)] = grad_gate
        expanded[:, pl.ds(again, tile)] = grad_up

    tiles(0, hidden, expand_back)
    total[...] = dot_back(expanded[...], matrix(3, 0, 2 * hidden))
    right_copy(2).start()
    for side in (here.x_side(), here.y_side()):
        pl.semaphore_signal(ready, inc=1, device_id=side, device_id_type=MESH)
    if any(entry[3] for entry in put_table):

        @pl.when(here.first_layer)
        def _():
            pl.semaphore_signal(ready_mid, inc=1, device_id=here.middle(), device_id_type=MESH)


    def norm_grad(rows, grad, normal, scale, gain, at):
        n = normal[rows]
        small_terms[1, at : at + 1] += jnp.sum(grad * n, axis=0, keepdims=True)
        q = grad * gain
        back = q - jnp.mean(q, axis=1, keepdims=True) - n * jnp.mean(q * n, axis=1, keepdims=True)
        return scale[rows][:, :1] * back

    def after_back():
        small_terms[...] = jnp.zeros_like(small_terms)

        def body(rows):
            grad = e_in[rows].astype(f32) + norm_grad(rows, total[rows], norm_two, scale_two, rows8[4:5], 4)
            after[rows] = grad
            after_low[rows] = grad.astype(low)

        in_rows(body)
        right_copy(1).start()

    def gated_back():
        total[...] = dot_back(after_low[...], matrix(2, 0, features))

    def mix_back(m, rows, taken, cut):
        taps = [rows8[j : j + 1, taken] for j in range(3)]
        alive = live_rows(m)
        grad = total[rows, taken]
        projected[rows, taken] = (grad * convolved[rows, taken]).astype(low)
        spec = left_dot(dft[...], parts(grad * queries[rows, taken]))
        g_re, g_im = spec[:slots], spec[slots:]
        pairs = []
        for other in (kernel_spec, value_spec):
            o_re, o_im = other[m, :slots, taken], other[m, slots:, taken]
            both = o_im * g_im
            re = o_re * g_re + jnp.where(first_row, 0.0, both)
            im = jnp.where(first_row, both, o_re * g_im - o_im * g_re)
            pairs.append(jnp.concatenate([re, im], axis=0))
        paired = left_dot(idft[...], parts(jnp.concatenate(pairs, axis=1)))
        at_values = pl.ds(pl.multiple_of(2 * features + cut * 256, 256), 256)
        projected[rows, at_values] = (paired[:, :256] * alive).astype(low)
        grad_kernel = paired[:, 256:]
        small_terms[0, :, taken] += grad_kernel
        k = keys[rows, taken]
        for j in range(3):
            moved = later(k, j) if j else k
            small_terms[1, j : j + 1, taken] += jnp.sum(grad_kernel * moved, axis=0, keepdims=True)
        grad_keys = taps[0] * grad_kernel + taps[1] * sooner(grad_kernel, 1) + taps[2] * sooner(grad_kernel, 2)
        at_keys = pl.ds(pl.multiple_of(features + cut * 256, 256), 256)
        projected[rows, at_keys] = (grad_keys * alive).astype(low)

    def mixed_back(m):
        mixer_blocks(m, mix_back)

    def input_back(m):
        rows = sequence(m)
        total[rows] = dot_back(projected[rows], matrix(1, 0, 3 * features))

        def body(rows):
            grad = after[rows] + norm_grad(rows, total[rows], norm_one, scale_one, rows8[3:4], 3)
            grad_low[rows] = grad.astype(low)

        in_rows(body, m * slots, slots)

    pieces = [after_back, gated_back]
    for m in range(micro):
        pieces += [functools.partial(mixed_back, m), functools.partial(input_back, m)]

    def last_copies():
        right_copy(0).start()
        small_copy().start()

    pieces += [last_copies]

    @pl.when(here.second_layer)
    def _():
        after_back()
        gated_back()
        for m in range(micro):
            mixed_back(m)
            input_back(m)
            if m == micro - 1:
                terms(down[0], wait=True)
            if m:
                give(grad_low, m - 1).wait_send()
            give(grad_low, m).start()
        last_copies()
        turned(2)
        for chunk in down[1:]:
            terms(chunk)
        turned(1)
        turned(0)

    pl.semaphore_wait(ready, 2)

    def one_sum(act):
        @pl.when(here.core == 0)
        def _():
            for chunk, (array, _, width, shared) in enumerate(put_table):
                for half in range(2 if shared else 0):
                    target = landed[array].at[1 - here.home, :, columns(put_table, chunk, half)]
                    copy = pltpu.make_async_copy(nothing.at[:, pl.ds(0, width)], target, nothing_sems.at[chunk, half])
                    getattr(copy, act)()

    nothing[...] = jnp.zeros_like(nothing)
    one_sum("start")

    apart = here.core != here.layer
    over = (1 - here.core, here.partner)

    def swap(source, target, number, act):
        sems = swap_sems.at[number], swap_sems.at[number + 1]

        @pl.when(apart)
        def _():
            getattr(remote(source, target, *sems, over), act)()

        @pl.when(jnp.logical_not(apart))
        def _():
            getattr(pltpu.make_async_copy(source, target, sems[1]), act)()

    due = [max(0, needs[1] - len(pieces) + k) for k in range(len(pieces))]
    shared = [chunk for chunk in range(last) if put_table[chunk][3]]
    met = [4]

    swap(out_low, kept_out, 0, "start")
    for now in range(last + 1):
        for piece, at in zip(pieces, due):
            if at == now:
                pl.when(here.first_layer)(in_background(piece))
        early = shared if now == 1 else []
        for chunk in early + [now + 1]:
            if chunk < last and chunk not in down and (chunk not in shared or chunk in early):
                terms(chunk, wait=put_table[chunk][0] not in met)
                met.append(put_table[chunk][0])
        for chunk in shared:
            if now == chunk - 2:
                pl.when(here.first_layer)(functools.partial(sum_middle, chunk))
        if now < last:
            sum_one(now)
        if 1 <= now:
            sum_two(now - 1)
        if now == needs[0]:
            swap(grad_low, kept_grad, 2, "start")

    one_sum("wait")
    for chunk in range(last):
        for half in (0, 1):
            for slot in (0, 1):
                target = landed[put_table[chunk][0]].at[slot, :, columns(put_table, chunk, half)]
                wanted = (here.core == 1) | (here.home == slot) if put_table[chunk][3] else True
                when(wanted, functools.partial(arrived, target, z_recv.at[chunk, slot, half]))
        for step in range(4):

            def action():
                put_first(chunk, step).wait_send()
                put_second(chunk, step).wait_send()
                put_third(chunk, step, "wait_send")

            when(handled(put_table, chunk, far(step)), action)
        if put_table[chunk][3]:
            pl.when(here.first_layer)(lambda: put_middle(chunk).wait_send())

    @pl.when(own_feed)
    def _():
        remote(hidden_in, feed, feed_sems.at[1], feed_sems.at[0], partner).wait_send()
        remote(live_own, live, feed_sems.at[3], feed_sems.at[2], partner).wait_send()

    for k in range(4):
        left_copy(k).wait_send()
        right_copy(k).wait_send()
    small_copy().wait_send()
    pl.when(here.second_layer)(lambda: give(grad_low, micro - 1).wait_send())
    swap(out_low, kept_out, 0, "wait")
    swap(grad_low, kept_grad, 2, "wait")


def finish_kernel(*refs):
    landed, (out, grad) = refs[:5], refs[5:7]
    s_filters, s_taps, s_one, s_two = refs[7:11]
    sums, (to_out, to_grad) = refs[11:15], refs[15:17]
    to_out[...] = out[...]
    to_grad[...] = grad[...]
    small = landed[0][0].astype(jnp.float32) + landed[0][1].astype(jnp.float32)
    s_filters[...] = small[:, :128]
    own = small.shape[0]
    rows = jnp.pad(small[:, 128:], ((0, 128 - own), (0, 0))).T
    for j in range(3):
        s_taps[j] = rows[j : j + 1, :own]
    s_one[...] = rows[3:4, :own]
    s_two[...] = rows[4:5, :own]
    for number, result in enumerate(sums):
        result[...] = landed[1 + number][0].astype(jnp.float32) + landed[1 + number][1].astype(jnp.float32)


def fast_device(
    hidden_in, out_grad, lengths, gain_mixer, w_input, w_taps, filters, w_output, gain_mlp, w_gate_up, w_down
):
    micro, _, slots, features = hidden_in.shape
    tokens, rows = micro * slots, gain_mixer.shape[1]
    shards = (w_input[0], w_output[0], w_gate_up[0], w_down[0].T)
    widths = [256] + [shard.shape[1] for shard in shards]
    hidden = widths[4]
    get_table, put_table = chunks_of(GET_PIECES), chunks_of(PUT_PIECES)
    dft, idft = (jnp.asarray(table) for table in packed_tables(slots))
    low, f32 = jnp.bfloat16, jnp.float32
    anywhere = pl.BlockSpec(memory_space=pl.ANY)
    inside = pl.BlockSpec(memory_space=pltpu.VMEM)
    dma, vmem = pltpu.SemaphoreType.DMA, pltpu.VMEM
    act, act_low = (tokens, features), vmem((tokens, features), low)
    kinds = [jax.ShapeDtypeStruct((2, rows, width), low) for width in widths]
    kinds += [jax.ShapeDtypeStruct((tokens, features), low)] * 2
    room = [vmem((rows, 256), low), vmem((128, 128), f32)] + [vmem((micro, 8, 128), f32)] * 2
    room += [vmem((rows, max(entry[2] for entry in put_table)), low), dma((len(put_table), 2))]
    room += [vmem((4, 2, 2, rows, width), low) for width in widths]
    room += [act_low] * 6
    room += [vmem((slots, features), f32), vmem((8, features), f32), vmem(act, f32), vmem(act, f32)]
    room += [vmem((tokens, 128), f32)] * 2
    room += [act_low] * 3 + [vmem(act, f32)] * 4 + [vmem((micro, 2 * slots, features), f32)] * 2
    room += [vmem(act, f32)] * 2 + [vmem((tokens, 2 * hidden), low), vmem((tokens, hidden), low)]
    room += [vmem((tokens, 3 * features), low), act_low, vmem((2, slots, features), f32)]
    room += [vmem((2, features, tokens), low)] * 4
    room += [vmem((slots, features), f32)] + [vmem((tokens, width // 2), low) for width in widths[1:]]
    room += [vmem((4, 2, 2, rows, entry[2]), low) for entry in put_table]
    for width in (128, hidden // 2):
        room += [vmem((4, 2, rows, width), low), vmem((4, rows, width), low)]
    got, put = len(get_table), len(put_table)
    room += [dma((got, 2, 2))] + [dma((got, 4))] * 5 + [dma((got, 2))] * 2 + [dma((got,))] * 2 + [dma((4,))]
    room += [dma((4,)), dma((micro,)), dma((micro,)), dma((9,)), dma((9,))]
    room += [dma((put, 4))] * 5 + [dma((put, 2, 2))] + [dma((put,))] * 2 + [pltpu.SemaphoreType.REGULAR] * 2
    results = pl.pallas_call(
        functools.partial(layer_kernel, get_table, put_table, widths),
        out_shape=kinds,
        in_specs=[inside] * 4 + [pl.BlockSpec(memory_space=pltpu.SMEM)] + [inside] * 2 + [anywhere] * 6,
        out_specs=[anywhere] * 7,
        scratch_shapes=room,
        compiler_params=pltpu.CompilerParams(
            collective_id=0, has_side_effects=True, vmem_limit_bytes=62 * 1024 * 1024
        ),
    )(
        filters[0].T,
        w_taps[0],
        gain_mixer,
        gain_mlp,
        lengths.T,
        dft,
        idft,
        *shards,
        hidden_in.reshape(tokens, features),
        out_grad.reshape(tokens, features),
    )
    kinds = [(rows, 128), (3, 1, rows), (1, rows), (1, rows)] + [(rows, width) for width in widths[1:]]
    kinds = [jax.ShapeDtypeStruct(kind, f32) for kind in kinds] + kinds_of(results[5:])
    s_filters, s_taps, s_one, s_two, s_in, s_out, s_gu, s_dt, layer_out, input_grad = pl.pallas_call(
        finish_kernel,
        out_shape=kinds,
        in_specs=[inside] * 7,
        out_specs=[inside] * 10,
        compiler_params=pltpu.CompilerParams(vmem_limit_bytes=62 * 1024 * 1024),
    )(*results)
    shape = (1, micro, 1, slots, features)
    return (
        layer_out.reshape(shape),
        input_grad.reshape(shape),
        s_one,
        s_in[None],
        s_taps.transpose(1, 0, 2),
        s_filters.T[None],
        s_out[None],
        s_two,
        s_gu[None],
        s_dt.T[None],
    )


def kinds_of(arrays):
    return [jax.ShapeDtypeStruct(array.shape, array.dtype) for array in arrays]


def solution(mesh):
    placed = (
        P(None, "dp", None, None),
        P(None, "dp", None, None),
        P(None, "dp"),
        P("section", "dp"),
        P("section", "dp", None),
        P("section", None, "dp"),
        P("section", None, "dp"),
        P("section", "dp", None),
        P("section", "dp"),
        P("section", "dp", None),
        P("section", None, "dp"),
    )
    return jax.shard_map(
        fast_device if mesh.shape["dp"] == 16 and mesh.shape["section"] == 2 else on_device,
        mesh=mesh,
        in_specs=placed,
        out_specs=(
            P("section", None, "dp", None, None),
            P("section", None, "dp", None, None),
            P("section", "dp"),
            P("section", "dp", None),
            P("section", None, "dp"),
            P("section", None, "dp"),
            P("section", "dp", None),
            P("section", "dp"),
            P("section", "dp", None),
            P("section", None, "dp"),
        ),
        check_vma=False,
    )
```

```python
import functools
import math

import jax
import jax.numpy as jnp
import ml_dtypes
import numpy as np
from jax import lax
from jax.experimental import pallas as pl
from jax.experimental.pallas import tpu as pltpu
from jax.sharding import PartitionSpec as P

MESH = pl.DeviceIdType.MESH

epsilon = 1e-05
GET_PIECES = (
    (0, 128, False),
    (1, 384, False),
    (1, 384, False),
    (1, 384, False),
    (2, 384, False),
    (3, 1024, True),
    (3, 1024, False),
    (3, 1024, False),
    (4, 640, False),
    (4, 640, False),
    (4, 256, False),
)
PUT_PIECES = (
    (4, 768, False),
    (4, 768, False),
    (3, 1024, False),
    (3, 1024, False),
    (1, 384, False),
    (1, 384, False),
    (0, 128, False),
    (1, 384, False),
    (2, 384, False),
    (3, 512, True),
    (3, 512, True),
)
GET_LAGS = (4, 7, 1, 2, 3)
SHARED_LAG = 3
STEP_WORK = 4.2
ROWS_UNROLL = 2
MIX_UNROLL = 3
TILE_UNROLL = 2


def passed_along(value, axis, steps):
    count = lax.axis_size(axis)
    first, last = (max(0, -steps), min(count, count - steps))
    return lax.ppermute(value, axis, [(source, source + steps) for source in range(first, last)])


def split_dot(left_side, right_side):
    return jnp.dot(
        left_side, right_side, precision=lax.Precision.HIGH, preferred_element_type=jnp.float32
    )


def split_rows(left_side, right_side):
    return lax.dot_general(
        left_side,
        right_side,
        (((0,), (0,)), ((), ())),
        precision=lax.Precision.HIGH,
        preferred_element_type=jnp.float32,
    )


def dot_rows(left_side, right_side):
    return lax.dot_general(
        left_side, right_side, (((0,), (0,)), ((), ())), preferred_element_type=jnp.float32
    )


def dot_back(left_side, right_side):
    return lax.dot_general(
        left_side, right_side, (((1,), (1,)), ((), ())), preferred_element_type=jnp.float32
    )


def tables(length):
    period = 2 * length
    freq_index = lax.broadcasted_iota(jnp.int32, (length + 1, length), 0)
    time_index = lax.broadcasted_iota(jnp.int32, (length + 1, length), 1)
    angles = (freq_index * time_index % period).astype(jnp.float32) * (2.0 * math.pi / period)
    edge_rows = (freq_index[:, :1] == 0) | (freq_index[:, :1] == length)
    inverse_weight = jnp.where(edge_rows, 1.0, 2.0) / period
    dft_stack = jnp.concatenate([jnp.cos(angles), -jnp.sin(angles)], axis=0)
    return (dft_stack, inverse_weight)


def spectrum(dft_tables, signal):
    dft_stack, inverse_weight = dft_tables
    stacked_out = split_dot(dft_stack, signal)
    middle_row = stacked_out.shape[0] // 2
    return (stacked_out[:middle_row], stacked_out[middle_row:])


def inverse(dft_tables, real_part, imag_part):
    dft_stack, inverse_weight = dft_tables
    return split_rows(
        dft_stack, jnp.concatenate([inverse_weight * real_part, inverse_weight * imag_part], axis=0)
    )


def normalize(input_rows):
    centered = input_rows - jnp.mean(input_rows, axis=1, keepdims=True)
    inv_scale = lax.rsqrt(jnp.mean(centered * centered, axis=1, keepdims=True) + epsilon)
    return (centered * inv_scale, inv_scale)


def norm_back(grad_normed, normed, inv_scale):
    return inv_scale * (
        grad_normed
        - jnp.mean(grad_normed, axis=1, keepdims=True)
        - normed * jnp.mean(grad_normed * normed, axis=1, keepdims=True)
    )


def delayed(input_rows, places):
    return jnp.pad(input_rows, ((places, 0), (0, 0)))[: input_rows.shape[0]]


def advanced(input_rows, places):
    return jnp.pad(input_rows, ((0, places), (0, 0)))[places:]


def layer_forward(input_rows, active_rows, weights, dft_tables):
    gain_one, w_inner, w_tap_rows, filt_static, w_outer, gain_two, w_expand, w_reduce = weights
    hidden_size_model = w_outer.shape[0]
    hidden_width = w_reduce.shape[0]
    tap_weights = w_tap_rows.astype(jnp.float32)
    normed_one, scale_one = normalize(input_rows)
    entered = (normed_one * gain_one.astype(jnp.float32)).astype(jnp.bfloat16)
    projected = jnp.dot(entered, w_inner, preferred_element_type=jnp.float32)
    queries = projected[:, :hidden_size_model]
    keys_part = projected[:, hidden_size_model : 2 * hidden_size_model] * active_rows
    values_part = projected[:, 2 * hidden_size_model :] * active_rows
    dynamic = (
        tap_weights[0] * keys_part
        + tap_weights[1] * delayed(keys_part, 1)
        + tap_weights[2] * delayed(keys_part, 2)
    )
    kernel = filt_static.astype(jnp.float32) + dynamic
    joint_re, joint_im = spectrum(dft_tables, jnp.concatenate([values_part, kernel], axis=1))
    value_re = joint_re[:, :hidden_size_model]
    kernel_re = joint_re[:, hidden_size_model:]
    value_im = joint_im[:, :hidden_size_model]
    kernel_im = joint_im[:, hidden_size_model:]
    convolved = inverse(
        dft_tables,
        kernel_re * value_re - kernel_im * value_im,
        kernel_re * value_im + kernel_im * value_re,
    )
    gated_rows = (queries * convolved).astype(jnp.bfloat16)
    after_mixer = input_rows + jnp.dot(gated_rows, w_outer, preferred_element_type=jnp.float32)
    normed_two, scale_two = normalize(after_mixer)
    entered_two = (normed_two * gain_two.astype(jnp.float32)).astype(jnp.bfloat16)
    expanded = jnp.dot(entered_two, w_expand, preferred_element_type=jnp.float32)
    gate_part = expanded[:, :hidden_width]
    up_part = expanded[:, hidden_width:]
    activated = (jax.nn.silu(gate_part) * up_part).astype(jnp.bfloat16)
    result = after_mixer + jnp.dot(activated, w_reduce, preferred_element_type=jnp.float32)
    stash = (
        normed_one,
        scale_one,
        entered,
        queries,
        keys_part,
        (value_re, value_im, kernel_re, kernel_im),
        convolved,
        gated_rows,
        normed_two,
        scale_two,
        entered_two,
        gate_part,
        up_part,
        activated,
    )
    return (result, stash)


def mlp_backward(received_gradient, weights, stash):
    gain_one, w_inner, w_tap_rows, filt_static, w_outer, gain_two, w_expand, w_reduce = weights
    (
        normed_one,
        scale_one,
        entered,
        queries,
        keys_part,
        spectra,
        convolved,
        gated_rows,
        normed_two,
        scale_two,
        entered_two,
        gate_part,
        up_part,
        activated,
    ) = stash
    grad_low = received_gradient.astype(jnp.bfloat16)
    grad_reduce_w = dot_rows(activated, grad_low)
    grad_act = dot_back(grad_low, w_reduce)
    sigmoid_gate = jax.nn.sigmoid(gate_part)
    grad_gate = grad_act * up_part * (sigmoid_gate * (1.0 + gate_part * (1.0 - sigmoid_gate)))
    grad_up = grad_act * (gate_part * sigmoid_gate)
    grad_expand = jnp.concatenate([grad_gate, grad_up], axis=1).astype(jnp.bfloat16)
    grad_expand_w = dot_rows(entered_two, grad_expand)
    grad_entered_two = dot_back(grad_expand, w_expand)
    grad_gain_two = jnp.sum(grad_entered_two * normed_two, axis=0)
    grad_after = received_gradient + norm_back(
        grad_entered_two * gain_two.astype(jnp.float32), normed_two, scale_two
    )
    return (grad_after, (grad_gain_two, grad_expand_w, grad_reduce_w))


def mixer_backward(grad_after, active_rows, weights, dft_tables, stash):
    gain_one, w_inner, w_tap_rows, filt_static, w_outer, gain_two, w_expand, w_reduce = weights
    (
        normed_one,
        scale_one,
        entered,
        queries,
        keys_part,
        spectra,
        convolved,
        gated_rows,
        normed_two,
        scale_two,
        entered_two,
        gate_part,
        up_part,
        activated,
    ) = stash
    value_re, value_im, kernel_re, kernel_im = spectra
    hidden_size_model = w_outer.shape[0]
    tap_weights = w_tap_rows.astype(jnp.float32)
    grad_mix_low = grad_after.astype(jnp.bfloat16)
    grad_outer_w = dot_rows(gated_rows, grad_mix_low)
    grad_gated = dot_back(grad_mix_low, w_outer)
    grad_queries = grad_gated * convolved
    grad_conv = grad_gated * queries
    grad_re, grad_im = spectrum(dft_tables, grad_conv)
    paired_re = jnp.concatenate(
        [kernel_re * grad_re + kernel_im * grad_im, value_re * grad_re + value_im * grad_im], axis=1
    )
    paired_im = jnp.concatenate(
        [kernel_re * grad_im - kernel_im * grad_re, value_re * grad_im - value_im * grad_re], axis=1
    )
    paired = inverse(dft_tables, paired_re, paired_im)
    grad_values = paired[:, :hidden_size_model] * active_rows
    grad_kernel = paired[:, hidden_size_model:]
    grad_taps = jnp.stack(
        [
            jnp.sum(grad_kernel * keys_part, axis=0),
            jnp.sum(grad_kernel * delayed(keys_part, 1), axis=0),
            jnp.sum(grad_kernel * delayed(keys_part, 2), axis=0),
        ]
    )
    grad_keys = (
        tap_weights[0] * grad_kernel
        + tap_weights[1] * advanced(grad_kernel, 1)
        + tap_weights[2] * advanced(grad_kernel, 2)
    ) * active_rows
    grad_projected = jnp.concatenate([grad_queries, grad_keys, grad_values], axis=1).astype(
        jnp.bfloat16
    )
    inner_weight_gradient = dot_rows(entered, grad_projected)
    grad_entered = dot_back(grad_projected, w_inner)
    grad_gain_one = jnp.sum(grad_entered * normed_one, axis=0)
    grad_inputs = grad_after + norm_back(
        grad_entered * gain_one.astype(jnp.float32), normed_one, scale_one
    )
    return (
        grad_inputs,
        (grad_gain_one, inner_weight_gradient, grad_taps, grad_kernel, grad_outer_w),
    )


def add_terms(received, flipped):
    return tuple(
        (
            jnp.sum(member, axis=0).T if flip else jnp.sum(member, axis=0)
            for member, flip in zip(received, flipped)
        )
    )


def on_device(
    hidden_in,
    out_grad,
    lengths,
    gain_mixer,
    w_input,
    w_taps,
    filters,
    w_output,
    gain_mlp,
    w_gate_up,
    w_down,
):
    first_section = lax.axis_index("section") == 0
    micro_count = hidden_in.shape[0]
    seq_slots = hidden_in.shape[2]
    hidden_size_model = hidden_in.shape[3]
    dft_tables = tables(seq_slots)
    positions = lax.broadcasted_iota(jnp.int32, (seq_slots, 1), 0)
    weights = (
        lax.all_gather(gain_mixer[0], "dp", axis=0, tiled=True),
        lax.all_gather(w_input[0], "dp", axis=0, tiled=True),
        lax.all_gather(w_taps[0], "dp", axis=1, tiled=True),
        lax.all_gather(filters[0], "dp", axis=1, tiled=True),
        lax.all_gather(w_output[0], "dp", axis=0, tiled=True),
        lax.all_gather(gain_mlp[0], "dp", axis=0, tiled=True),
        lax.all_gather(w_gate_up[0], "dp", axis=0, tiled=True),
        lax.all_gather(w_down[0], "dp", axis=1, tiled=True),
    )
    arriving = jnp.zeros((seq_slots, hidden_size_model), jnp.bfloat16)
    outgoing_list = []
    saved_activations = []
    for forward_step in range(micro_count + 1):
        own_index = min(forward_step, micro_count - 1)
        prior_index = max(forward_step - 1, 0)
        input_rows = jnp.where(first_section, hidden_in[own_index, 0], arriving).astype(jnp.float32)
        length_now = jnp.where(first_section, lengths[own_index, 0], lengths[prior_index, 0])
        active_rows = (positions < length_now).astype(jnp.float32)
        result, stash = layer_forward(input_rows, active_rows, weights, dft_tables)
        outgoing = result.astype(jnp.bfloat16)
        outgoing_list.append(outgoing)
        if forward_step < micro_count:
            arriving = passed_along(outgoing, "section", 1)
        saved_activations.append((input_rows, active_rows))
    coming = jnp.zeros((seq_slots, hidden_size_model), jnp.bfloat16)
    mlp_totals = None
    mixer_totals = None
    grads_out = []
    for backward_step in range(micro_count + 1):
        saved_slot_index = micro_count - backward_step
        last_index = max(micro_count - 1 - backward_step, 0)
        live_factor = 1.0 if backward_step < micro_count else 0.0
        received_gradient = jnp.where(
            first_section,
            coming.astype(jnp.float32),
            out_grad[last_index, 0].astype(jnp.float32) * live_factor,
        )
        input_rows, active_rows = saved_activations[saved_slot_index]
        result, stash = layer_forward(input_rows, active_rows, weights, dft_tables)
        grad_after, mlp_grads = mlp_backward(received_gradient, weights, stash)
        mlp_totals = (
            mlp_grads if mlp_totals is None else jax.tree.map(jnp.add, mlp_totals, mlp_grads)
        )
        grad_inputs, mixer_grads = mixer_backward(
            grad_after, active_rows, weights, dft_tables, stash
        )
        mixer_totals = (
            mixer_grads
            if mixer_totals is None
            else jax.tree.map(jnp.add, mixer_totals, mixer_grads)
        )
        outgoing = grad_inputs.astype(jnp.bfloat16)
        grads_out.append(outgoing)
        if backward_step < micro_count:
            coming = passed_along(outgoing, "section", -1)
    first_outputs = jnp.stack(outgoing_list[:micro_count])
    second_outputs = jnp.stack(outgoing_list[1:])
    layer_out = jnp.where(first_section, first_outputs, second_outputs)[None, :, None]
    first_grads = jnp.stack(
        [grads_out[micro_count - batch_index] for batch_index in range(micro_count)]
    )
    second_grads = jnp.stack(
        [grads_out[micro_count - 1 - batch_index] for batch_index in range(micro_count)]
    )
    input_grad = jnp.where(first_section, first_grads, second_grads)[None, :, None]
    all_parts = (
        lax.all_to_all(
            mixer_totals[0][None].astype(jnp.bfloat16),
            "dp",
            split_axis=1,
            concat_axis=0,
            tiled=True,
        ).astype(jnp.float32),
        lax.all_to_all(
            mixer_totals[1][None].astype(jnp.bfloat16),
            "dp",
            split_axis=1,
            concat_axis=0,
            tiled=True,
        ).astype(jnp.float32),
        lax.all_to_all(
            mixer_totals[2].T[None].astype(jnp.bfloat16),
            "dp",
            split_axis=1,
            concat_axis=0,
            tiled=True,
        ).astype(jnp.float32),
        lax.all_to_all(
            mixer_totals[3].T[None].astype(jnp.bfloat16),
            "dp",
            split_axis=1,
            concat_axis=0,
            tiled=True,
        ).astype(jnp.float32),
        lax.all_to_all(
            mixer_totals[4][None].astype(jnp.bfloat16),
            "dp",
            split_axis=1,
            concat_axis=0,
            tiled=True,
        ).astype(jnp.float32),
        lax.all_to_all(
            mlp_totals[0][None].astype(jnp.bfloat16), "dp", split_axis=1, concat_axis=0, tiled=True
        ).astype(jnp.float32),
        lax.all_to_all(
            mlp_totals[1][None].astype(jnp.bfloat16), "dp", split_axis=1, concat_axis=0, tiled=True
        ).astype(jnp.float32),
        lax.all_to_all(
            mlp_totals[2].T[None].astype(jnp.bfloat16),
            "dp",
            split_axis=1,
            concat_axis=0,
            tiled=True,
        ).astype(jnp.float32),
    )
    summed = add_terms(all_parts, (False, False, True, True, False, False, False, True))
    return (
        layer_out,
        input_grad,
        summed[0][None],
        summed[1][None],
        summed[2][None],
        summed[3][None],
        summed[4][None],
        summed[5][None],
        summed[6][None],
        summed[7][None],
    )


class Place:
    def __init__(self):
        self.core = lax.axis_index("section")
        self.index = lax.axis_index("dp")
        self.z = self.index // 4
        self.y = self.index // 2 % 2
        self.x = self.index % 2
        self.layer = 1 - (self.z + 1) // 2 % 2
        self.home = self.z // 2
        self.first_layer = self.layer == 0
        self.second_layer = self.layer == 1
        self.partner = self.chip(z=self.z + 1 - 2 * (self.z % 2))

    def chip(self, z=None, y=None, x=None):
        z, y, x = (a if a is not None else b for a, b in ((z, self.z), (y, self.y), (x, self.x)))
        return z * 4 + y * 2 + x

    def x_side(self):
        return (self.core, self.chip(x=1 - self.x))

    def y_side(self):
        return (self.core, self.chip(y=1 - self.y))

    def sibling(self):
        return (1 - self.core, self.index)

    def middle(self):
        return (self.core, self.chip(z=3 - self.z))

    def greet(self):
        barrier = pltpu.get_barrier_semaphore()
        others = [self.x_side(), self.y_side(), self.sibling()]
        for step in (1, 2, 3):
            chip = self.chip(z=(self.z + step) % 4)
            others += [(0, chip), (1, chip)]
        for other in others:
            pl.semaphore_signal(barrier, inc=1, device_id=other, device_id_type=MESH)
        pl.semaphore_wait(barrier, len(others))


def remote(source, target, send, receive, device):
    return pltpu.make_async_remote_copy(
        src_ref=source,
        dst_ref=target,
        send_sem=send,
        recv_sem=receive,
        device_id=device,
        device_id_type=MESH,
    )


def chunks_of(pieces):
    table, places = [], {}
    for array, width, shared in pieces:
        start = places.get(array, 0)
        table.append((array, start, width, shared))
        places[array] = start + width
    return table


def left_dot(left_side, right_side):
    return lax.dot_general(
        left_side, right_side, (((1,), (0,)), ((), ())), preferred_element_type=jnp.float32
    )


def sigmoid(value):
    return 0.5 * jnp.tanh(0.5 * value) + 0.5


def parts(signal):
    high = signal.astype(jnp.bfloat16)
    rest = (signal - high.astype(jnp.float32)).astype(jnp.bfloat16)
    return jnp.concatenate([high, high, rest], axis=0)


def halves_of(table):
    high = table.astype(ml_dtypes.bfloat16)
    rest = (table - high.astype(np.float64)).astype(ml_dtypes.bfloat16)
    return np.concatenate([high, rest, high], axis=1)


def packed_tables(length):
    period = 2 * length
    freq, time = np.arange(length)[:, None], np.arange(length)[None, :]
    angles = (freq * time % period) * (2.0 * math.pi / period)
    sines = np.where(freq == 0, 1.0 - 2.0 * (time % 2), -np.sin(angles))
    table = np.concatenate([np.cos(angles), sines], axis=0)
    weight = np.where(np.arange(period)[:, None] % length == 0, 1.0, 2.0) / period
    return halves_of(table), halves_of((table * weight).T)


def layer_kernel(get_table, put_table, widths, *refs):
    refs = list(refs)

    def take(number):
        taken = refs[:number]
        del refs[:number]
        return taken

    filters_in, taps_in, gain_one_in, gain_two_in, lengths_in, dft, idft = take(7)
    shards, (hidden_in, grad_in) = [None] + take(4), take(2)
    landed, (kept_out, kept_grad) = take(5), take(2)
    own_small, rows_in, live_own, live, nothing, nothing_sems = take(6)
    weight = take(5)
    feed, arrive, x_in, e_in, out_low, grad_low = take(6)
    filt, rows8, norm_one, norm_two, scale_one, scale_two = take(6)
    entered, gated, again, queries, keys, values, convolved, value_spec, kernel_spec = take(9)
    total, after, expanded, active, projected, after_low, small_terms = take(7)
    lefts = take(4)
    other_small, other_projected, other_after, other_expanded, other_active = take(5)
    mine = take(len(put_table))
    one_small, two_small, one_down, two_down = take(4)
    get_z_send, get_z_recv, get_one_send, get_one_recv, get_two_send, get_two_recv = take(6)
    get_mid_send, get_mid_recv, get_side_send, get_side_recv, feed_sems = take(5)
    swap_sems, give_send, give_recv, send, recv = take(5)
    one_send, one_recv, two_send, two_recv, z_send, z_recv, mid_send, mid_recv, ready, ready_mid = take(10)

    here = Place()
    tokens, features = x_in.shape
    slots = filt.shape[0]
    micro = tokens // slots
    hidden = active.shape[1]
    f32, low = jnp.float32, jnp.bfloat16
    shards[0] = own_small

    here.greet()

    for m in range(micro):
        live_own[m] = jnp.full(live_own.shape[1:], lengths_in[0, m], jnp.int32).astype(f32)

    own_feed = here.core == here.layer
    partner = (here.core, here.partner)
    for layer, kept, given in ((0, hidden_in, grad_in), (1, grad_in, hidden_in)):

        @pl.when(own_feed & (here.layer == layer))
        def _():
            pltpu.make_async_copy(kept, feed, feed_sems.at[0]).start()
            pltpu.make_async_copy(live_own, live, feed_sems.at[2]).start()
            remote(given, feed, feed_sems.at[1], feed_sems.at[0], partner).start()
            remote(live_own, live, feed_sems.at[3], feed_sems.at[2], partner).start()

    def arrived(target, receive):
        pltpu.make_async_copy(target, target, receive).wait()

    def fed():
        arrived(feed, feed_sems.at[0])
        arrived(live, feed_sems.at[2])

    def small_shard():
        rows_in[...] = jnp.zeros_like(rows_in)
        own = taps_in.shape[1]
        rows_in[0:3, 0:own] = taps_in[...].astype(f32)
        rows_in[3:4, 0:own] = gain_one_in[...].astype(f32)
        rows_in[4:5, 0:own] = gain_two_in[...].astype(f32)
        own_small[:, :128] = filters_in[...]
        own_small[:, 128:] = rows_in[...].T[:own].astype(low)

    def columns(table, chunk, half):
        array, start, width, _ = table[chunk]
        return pl.ds(pl.multiple_of(half * (widths[array] // 2) + start, 128), width)

    def at_home(z):
        return z // 2 == here.home

    def when(condition, action):
        if condition is True:
            action()
        else:
            pl.when(condition)(action)

    def z_all(chunk, visit, near):
        array, _, _, shared = get_table[chunk]
        for number, plane in enumerate((1 - here.core, 2 + here.core)):
            wanted = (plane == here.z) if near else (plane != here.z)
            if shared:
                wanted = wanted & ((here.core == 1) | (here.home == number))
            for half in (0, 1):
                cut = columns(get_table, chunk, half)
                source, target = shards[array].at[:, cut], weight[array].at[here.z, here.y, here.x, :, cut]
                sems = get_z_send.at[chunk, number, half], get_z_recv.at[chunk, here.z]
                visit(wanted, here.core == half, source, target, sems, (half, here.chip(z=plane)))

    def z_start(chunk, near):
        def visit(wanted, own, source, target, sems, device):
            if not near:

                @pl.when(wanted)
                def _():
                    remote(source, target, *sems, device).start()

                return

            @pl.when(wanted & own)
            def _():
                pltpu.make_async_copy(source, target, sems[1]).start()

            @pl.when(wanted & jnp.logical_not(own))
            def _():
                remote(source, target, *sems, device).start()

        z_all(chunk, visit, near)

    def z_sent(chunk):
        for near in (False, True):

            def visit(wanted, own, source, target, sems, device):
                @pl.when(wanted & jnp.logical_not(own) if near else wanted)
                def _():
                    remote(source, target, *sems, device).wait_send()

            z_all(chunk, visit, near)

    def far(step):
        return (here.z + step) % 4

    def handled(table, chunk, z):
        return here.second_layer | at_home(z) if table[chunk][3] else True

    def get_first(chunk, step):
        block = weight[get_table[chunk][0]].at[far(step), here.y, here.x, :, columns(get_table, chunk, here.core)]
        side = here.y_side() if (step + chunk) % 2 else here.x_side()
        return remote(block, block, get_one_send.at[chunk, step], get_one_recv.at[chunk, step], side)

    def get_second(chunk, step):
        ref, cut = weight[get_table[chunk][0]], columns(get_table, chunk, here.core)
        if (step + chunk) % 2:
            pair, side = ref.at[far(step), :, here.x, :, cut], here.x_side()
        else:
            pair, side = ref.at[far(step), here.y, :, :, cut], here.y_side()
        return remote(pair, pair, get_two_send.at[chunk, step], get_two_recv.at[chunk, step], side)

    def get_middle(chunk, z):
        block = weight[get_table[chunk][0]].at[z, :, :, :, columns(get_table, chunk, here.core)]
        return remote(block, block, get_mid_send.at[chunk, z % 2], get_mid_recv.at[chunk, z % 2], here.middle())

    def get_across(chunk):
        whole = weight[get_table[chunk][0]].at[:, :, :, :, columns(get_table, chunk, here.core)]
        return remote(whole, whole, get_side_send.at[chunk], get_side_recv.at[chunk], here.sibling())

    def one_step(chunk, step):
        def action():
            z = far(step)
            block = weight[get_table[chunk][0]].at[z, here.y, here.x, :, columns(get_table, chunk, here.core)]
            arrived(block, get_z_recv.at[chunk, z])
            get_first(chunk, step).start()

        when(handled(get_table, chunk, far(step)), action)

    def two_steps(chunk, step):
        def action():
            get_first(chunk, step).wait_recv()
            get_second(chunk, step).start()

        when(handled(get_table, chunk, far(step)), action)

    def three_steps(chunk, step):
        def action():
            get_second(chunk, step).wait_recv()
            if get_table[chunk][3]:

                @pl.when(here.first_layer)
                def _():
                    get_middle(chunk, far(step)).start()

        when(handled(get_table, chunk, far(step)), action)

    def pass_on(chunk):
        if get_table[chunk][3]:

            @pl.when(here.first_layer)
            def _():
                for k in range(2):
                    get_middle(chunk, 2 * (1 - here.home) + k).wait_recv()

        get_across(chunk).start()

    def gather(on_step):
        last = len(get_table)
        ahead, own_ahead, two_lag, three_lag, done_lag = GET_LAGS
        for chunk in range(1, last):
            z_start(chunk, True)
        small_shard()
        z_start(0, True)

        def z_first():
            for chunk in range(min(ahead, last)):
                z_start(chunk, False)

        pl.when(here.core == 0)(z_first)
        for chunk in range(min(own_ahead, last)):
            one_step(chunk, 0)
        for chunk in range(min(own_ahead, last) - 1):
            two_steps(chunk, 0)
        pl.when(here.core == 1)(z_first)
        for now in range(last + done_lag):
            if now + own_ahead < last:
                one_step(now + own_ahead, 0)
            if 0 <= now + own_ahead - 1 < last:
                two_steps(now + own_ahead - 1, 0)
            if now < last:
                for step in (1, 3, 2):
                    one_step(now, step)
            if now + ahead < last:
                z_start(now + ahead, False)
            if 0 <= now - two_lag < last:
                for step in (1, 3, 2):
                    two_steps(now - two_lag, step)
            if 0 <= now - three_lag < last:
                for step in range(4):
                    three_steps(now - three_lag, step)
                if not get_table[now - three_lag][3]:
                    pass_on(now - three_lag)
            if 0 <= now - three_lag - SHARED_LAG < last and get_table[now - three_lag - SHARED_LAG][3]:
                pass_on(now - three_lag - SHARED_LAG)
            for chunk in (now - done_lag - SHARED_LAG, now - done_lag):
                if 0 <= chunk < last and get_table[chunk][3] == (chunk != now - done_lag):
                    get_across(chunk).wait_recv()
            on_step(now, now == last + done_lag - 1)

    def gathered():
        for chunk in range(len(get_table)):
            z_sent(chunk)
            for step in range(4):

                def action():
                    get_first(chunk, step).wait_send()
                    get_second(chunk, step).wait_send()

                when(handled(get_table, chunk, far(step)), action)
            if get_table[chunk][3]:

                @pl.when(here.first_layer)
                def _():
                    for k in range(2):
                        get_middle(chunk, 2 * here.home + k).wait_send()

            get_across(chunk).wait_send()

    def matrix(number, start, width):
        ref = weight[number]
        return ref[:, :, :, :, pl.ds(start, width)].reshape(features, width)

    alone = [True]

    def times(unroll):
        return unroll if alone[0] else 1

    def in_background(body):
        def whole():
            alone[0] = False
            body()
            alone[0] = True

        return whole

    def in_rows(body, start=0, count=tokens):
        block = 64

        def step(i, carry):
            body(pl.ds(pl.multiple_of(start + i * block, block), block))
            return carry

        lax.fori_loop(0, count // block, step, 0, unroll=times(ROWS_UNROLL))

    def sequence(m):
        return pl.ds(pl.multiple_of(m * slots, slots), slots)

    def normed(rows, rows_in, normal, scale, gain, target):
        centered = rows_in - jnp.mean(rows_in, axis=1, keepdims=True)
        inv = lax.rsqrt(jnp.mean(centered * centered, axis=1, keepdims=True) + epsilon)
        n = centered * inv
        normal[rows] = n
        scale[rows] = jnp.broadcast_to(inv, (n.shape[0], 128))
        target[rows] = (n * gain).astype(low)

    row_at = lax.broadcasted_iota(jnp.int32, (slots, 256), 0)
    first_row = row_at == 0

    def later(rows, places):
        return jnp.where(row_at >= places, pltpu.roll(rows, places, 0), 0.0)

    def sooner(rows, places):
        return jnp.where(row_at < slots - places, pltpu.roll(rows, slots - places, 0), 0.0)

    cuts = features // 256

    def mixer_blocks(m, body):
        def step(cut, carry):
            body(m, sequence(m), pl.ds(pl.multiple_of(cut * 256, 256), 256), cut)
            return carry

        lax.fori_loop(0, cuts, step, 0, unroll=times(MIX_UNROLL))

    def live_rows(m):
        return (row_at.astype(f32) < jnp.concatenate([live[m, 0:1, :]] * 2, axis=1)).astype(f32)

    def to_sibling(number, source, target):
        return remote(source, target, send.at[number], recv.at[number], here.sibling())

    def left_copy(k):
        return to_sibling(k, lefts[k].at[0], lefts[k].at[1])

    def right_sides(k):
        return (
            (projected, other_projected),
            (after_low, other_after),
            (expanded, other_expanded),
            (active, other_active),
        )[k]

    def right_copy(k):
        source, target = right_sides(k)
        half = widths[1 + k] // 2
        cut = pl.ds(pl.multiple_of((1 - here.core) * half, 128), half)
        return to_sibling(4 + k, source.at[:, cut], target)

    def small_copy():
        return to_sibling(8, small_terms.at[1 - here.core], other_small)

    def give(source, m):
        rows = pl.ds(m * slots, slots)
        return remote(source.at[rows], arrive.at[rows], give_send.at[m], give_recv.at[m], partner)

    def received(target, m):
        rows = sequence(m)
        arrived(arrive.at[rows], give_recv.at[m])
        target[rows] = arrive[rows]

    def turned(k):
        lefts[k][0] = (entered, gated, again, e_in)[k][...].T
        left_copy(k).start()

    def small_weights():
        filt[...] = matrix(0, 0, 128).astype(f32).T
        rows8[...] = matrix(0, 128, 128).astype(f32).T[:8]

    def enter(m):
        def body(rows):
            normed(rows, x_in[rows].astype(f32), norm_one, scale_one, rows8[3:4], entered)

        in_rows(body, m * slots, slots)

    def mix(m, rows, taken, cut):
        taps = [rows8[j : j + 1, taken] for j in range(3)]
        alive = live_rows(m)
        k = keys[rows, taken] * alive
        keys[rows, taken] = k
        v = values[rows, taken] * alive
        kernel = filt[:, taken] + taps[0] * k + taps[1] * later(k, 1) + taps[2] * later(k, 2)
        spec = left_dot(dft[...], parts(jnp.concatenate([v, kernel], axis=1)))
        value_spec[m, :, taken] = spec[:, :256]
        kernel_spec[m, :, taken] = spec[:, 256:]
        v_re, v_im = spec[:slots, :256], spec[slots:, :256]
        k_re, k_im = spec[:slots, 256:], spec[slots:, 256:]
        both = k_im * v_im
        re = k_re * v_re - jnp.where(first_row, 0.0, both)
        im = jnp.where(first_row, both, k_re * v_im + k_im * v_re)
        out = left_dot(idft[...], parts(jnp.concatenate([re, im], axis=0)))
        convolved[rows, taken] = out
        gated[rows, taken] = (queries[rows, taken] * out).astype(low)

    def project(m):
        rows = sequence(m)
        for k, target in enumerate((queries, keys, values)):
            target[rows] = left_dot(entered[rows], matrix(1, k * features, features))

    def mixer(m):
        mixer_blocks(m, mix)

    def mixer_out(m):
        rows = sequence(m)
        total[rows] = x_in[rows].astype(f32) + left_dot(gated[rows], matrix(2, 0, features))

        def body(rows):
            normed(rows, total[rows], norm_two, scale_two, rows8[4:5], again)

        in_rows(body, m * slots, slots)

    def each_sequence(*bodies):
        def step(m, carry):
            for body in bodies:
                body(m)
            return carry

        lax.fori_loop(0, micro, step, 0)

    tile = 512

    def tiles(start, width, body):
        def step(i, carry):
            body(pl.multiple_of(start + i * tile, 128))
            return carry

        lax.fori_loop(0, width // tile, step, 0, unroll=times(TILE_UNROLL))

    def expand(start):
        gate = left_dot(again[...], matrix(3, start, tile))
        up = left_dot(again[...], matrix(3, pl.multiple_of(hidden + start, 128), tile))
        expanded[:, pl.ds(start, tile)] = gate.astype(low)
        expanded[:, pl.ds(pl.multiple_of(hidden + start, 128), tile)] = up.astype(low)
        active[:, pl.ds(start, tile)] = (gate * sigmoid(gate) * up).astype(low)

    def reduce_on(start, width):
        total[...] += dot_back(active[:, pl.ds(start, width)], matrix(4, start, width))

    def layer_done():
        right_copy(3).start()
        out_low[...] = total[...].astype(low)

    def ready_at(array):
        return max(k for k, entry in enumerate(get_table) if entry[0] == array) + GET_LAGS[-1]

    def begin():
        x_in[...] = feed[...]
        small_weights()
        each_sequence(enter)
        turned(0)

    def mixed():
        mixer(micro - 1)
        turned(1)

    def mixed_out():
        each_sequence(mixer_out)
        turned(2)

    def reduce_both(start, width):
        for half in (0, 1):
            reduce_on(half * (hidden // 2) + start, width)

    plan = [(ready_at(0), 1.3, begin), (ready_at(1), 1.4, lambda: each_sequence(project))]
    plan += [(0, 2.2, functools.partial(mixer, m)) for m in range(micro - 1)] + [(0, 2.4, mixed)]
    plan += [(ready_at(2), 1.9, mixed_out)]
    ups = [
        (chunk + GET_LAGS[-1] + (SHARED_LAG if shared else 0), 1.7 * width / 1024, functools.partial(tiles, start, width, expand))
        for chunk, (array, start, width, shared) in enumerate(get_table)
        if array == 3
    ]
    plan += sorted(ups, key=lambda piece: piece[0])
    plan += [
        (chunk + GET_LAGS[-1], 1.0 * width / 1024, functools.partial(reduce_both, start, width))
        for chunk, (array, start, width, _) in enumerate(get_table)
        if array == 4
    ]

    def on_step(now, final):
        if now == ready_at(0):
            fed()
        chosen, spent = [], 0.0
        while plan and plan[0][0] <= now and (final or not chosen or spent + plan[0][1] <= STEP_WORK):
            chosen.append(plan[0][2])
            spent += plan.pop(0)[1]

        @pl.when(here.first_layer)
        @in_background
        def _():
            for piece in chosen:
                piece()

    gather(on_step)

    @pl.when(here.first_layer)
    def _():
        layer_done()
        for m in range(micro):
            give(out_low, m).start()
            give(out_low, m).wait_send()
        gathered()
        for m in range(micro):
            received(e_in, m)
        turned(3)

    @pl.when(here.second_layer)
    def _():
        small_weights()
        e_in[...] = feed[...]
        turned(3)
        gathered()
        each_sequence(functools.partial(received, x_in), enter, project, mixer, mixer_out)

        tiles(0, hidden, expand)
        reduce_on(0, hidden)
        layer_done()

    offsets, place = [], 0
    for array, _, width, _ in put_table:
        offsets.append(place)
        place += width if array in (1, 2, 3) else 0

    def one_in(chunk, z):
        array, start, width, _ = put_table[chunk]
        if array == 0:
            return one_small.at[z]
        if array == 4:
            return one_down.at[z, :, :, pl.ds(start, width)]
        return weight[3].at[z, 0, :, :, pl.ds(offsets[chunk], width)]

    def two_in(chunk, z):
        array, start, width, _ = put_table[chunk]
        if array == 0:
            return two_small.at[z]
        if array == 4:
            return two_down.at[z, :, pl.ds(start, width)]
        return weight[3].at[z, 1, 0, :, pl.ds(offsets[chunk], width)]

    def put_first(chunk, step):
        z = far(step)
        if step % 2:
            source, side = mine[chunk].at[z, :, 1 - here.x], here.x_side()
        else:
            source, side = mine[chunk].at[z, 1 - here.y], here.y_side()
        return remote(source, one_in(chunk, step), one_send.at[chunk, step], one_recv.at[chunk, step], side)

    def put_second(chunk, step):
        z = far(step)
        if step % 2:
            source, side = mine[chunk].at[z, 1 - here.y, here.x], here.y_side()
        else:
            source, side = mine[chunk].at[z, here.y, 1 - here.x], here.x_side()
        return remote(source, two_in(chunk, step), two_send.at[chunk, step], two_recv.at[chunk, step], side)

    def put_third(chunk, step, act):
        z = far(step)
        source = mine[chunk].at[z, here.y, here.x]
        target = landed[put_table[chunk][0]].at[here.home, :, columns(put_table, chunk, here.core)]
        receive = z_recv.at[chunk, here.home, here.core]
        own = (here.z == z) & (here.core == here.layer)
        if act == "start":

            @pl.when(own)
            def _():
                pltpu.make_async_copy(source, target, receive).start()

        @pl.when(jnp.logical_not(own))
        def _():
            away = remote(source, target, z_send.at[chunk, step], receive, (here.layer, here.chip(z=z)))
            getattr(away, act)()

    def add(target, other):
        target[...] = (target[...].astype(f32) + other[...].astype(f32)).astype(target.dtype)

    def both_sides(array):
        if array:
            left_copy(array - 1).wait_recv()
            right_copy(array - 1).wait_recv()
        else:
            small_copy().wait_recv()

    def place_block(chunk, cut, block):
        rows = features // 16
        for z in range(4):
            for k in range(4):
                at = (z * 4 + k) * rows
                mine[chunk][z, k // 2, k % 2, :, cut] = block[at : at + rows].astype(low)

    def terms(chunk, wait=False):
        array, start, width, shared = put_table[chunk]
        if wait:
            both_sides(array)
        if array == 0:
            place_block(chunk, pl.ds(0, width), (small_terms[here.core] + other_small[...]).T)
        else:
            source, other = right_sides(array - 1)
            own_start = here.core * (widths[array] // 2) + start
            strip = 256 if width % 256 == 0 else width

            def body(i, carry):
                at = i * strip
                block = left_dot(lefts[array - 1][0], source[:, pl.ds(pl.multiple_of(own_start + at, 128), strip)])
                block += left_dot(lefts[array - 1][1], other[:, pl.ds(pl.multiple_of(start + at, 128), strip)])
                place_block(chunk, pl.ds(pl.multiple_of(at, 128), strip), block)
                return carry

            lax.fori_loop(0, width // strip, body, 0)
        if not shared:
            for step in range(4):
                put_first(chunk, step).start()
            return

        @pl.when(here.second_layer)
        def _():
            for step in range(4):
                put_first(chunk, step).start()

        @pl.when(here.first_layer)
        def _():
            if not any(entry[3] for entry in put_table[:chunk]):
                pl.semaphore_wait(ready_mid, 1)
            put_middle(chunk).start()

    def put_middle(chunk):
        source = mine[chunk].at[pl.ds(2 * (1 - here.home), 2)]
        return remote(source, mid_in(chunk), mid_send.at[chunk], mid_recv.at[chunk], here.middle())

    def mid_in(chunk):
        _, start, width, _ = put_table[chunk]
        return weight[4].at[pl.ds(0, 2), :, :, :, pl.ds(start, width)]

    def sum_middle(chunk):
        put_middle(chunk).wait_recv()
        for z in range(2):
            for k in range(4):
                add(mine[chunk].at[2 * here.home + z, k // 2, k % 2], mid_in(chunk).at[z, k // 2, k % 2])
        for step in range(4):
            when(at_home(far(step)), lambda: put_first(chunk, step).start())

    def sum_one(chunk):
        for step in range(4):

            def action():
                z = far(step)
                put_first(chunk, step).wait_recv()
                for k in range(2):
                    if step % 2:
                        add(mine[chunk].at[z, k, here.x], one_in(chunk, step).at[k])
                    else:
                        add(mine[chunk].at[z, here.y, k], one_in(chunk, step).at[k])
                put_second(chunk, step).start()

            when(handled(put_table, chunk, far(step)), action)

    def sum_two(chunk):
        for step in range(4):

            def action():
                put_second(chunk, step).wait_recv()
                add(mine[chunk].at[far(step), here.y, here.x], two_in(chunk, step))
                put_third(chunk, step, "start")

            when(handled(put_table, chunk, far(step)), action)

    last = len(put_table)
    needs = {array: min(k for k, entry in enumerate(put_table) if entry[0] == array) for array in range(5)}
    down = [chunk for chunk in range(last) if put_table[chunk][0] == 4]

    @pl.when(here.first_layer)
    def _():
        for chunk in down:
            terms(chunk, wait=chunk == down[0])

    def expand_back(start):
        again = pl.multiple_of(hidden + start, 128)
        grad_act = left_dot(e_in[...], matrix(4, start, tile))
        gate = expanded[:, pl.ds(start, tile)].astype(f32)
        up = expanded[:, pl.ds(again, tile)].astype(f32)
        sig = sigmoid(gate)
        grad_gate = (grad_act * up * (sig * (1.0 + gate * (1.0 - sig)))).astype(low)
        grad_up = (grad_act * (gate * sig)).astype(low)
        expanded[:, pl.ds(start, tile)] = grad_gate
        expanded[:, pl.ds(again, tile)] = grad_up

    tiles(0, hidden, expand_back)
    total[...] = dot_back(expanded[...], matrix(3, 0, 2 * hidden))
    right_copy(2).start()
    for side in (here.x_side(), here.y_side()):
        pl.semaphore_signal(ready, inc=1, device_id=side, device_id_type=MESH)
    if any(entry[3] for entry in put_table):

        @pl.when(here.first_layer)
        def _():
            pl.semaphore_signal(ready_mid, inc=1, device_id=here.middle(), device_id_type=MESH)


    def norm_grad(rows, grad, normal, scale, gain, at):
        n = normal[rows]
        small_terms[1, at : at + 1] += jnp.sum(grad * n, axis=0, keepdims=True)
        q = grad * gain
        back = q - jnp.mean(q, axis=1, keepdims=True) - n * jnp.mean(q * n, axis=1, keepdims=True)
        return scale[rows][:, :1] * back

    def after_back():
        small_terms[...] = jnp.zeros_like(small_terms)

        def body(rows):
            grad = e_in[rows].astype(f32) + norm_grad(rows, total[rows], norm_two, scale_two, rows8[4:5], 4)
            after[rows] = grad
            after_low[rows] = grad.astype(low)

        in_rows(body)
        right_copy(1).start()

    def gated_back():
        total[...] = dot_back(after_low[...], matrix(2, 0, features))

    def mix_back(m, rows, taken, cut):
        taps = [rows8[j : j + 1, taken] for j in range(3)]
        alive = live_rows(m)
        grad = total[rows, taken]
        projected[rows, taken] = (grad * convolved[rows, taken]).astype(low)
        spec = left_dot(dft[...], parts(grad * queries[rows, taken]))
        g_re, g_im = spec[:slots], spec[slots:]
        pairs = []
        for other in (kernel_spec, value_spec):
            o_re, o_im = other[m, :slots, taken], other[m, slots:, taken]
            both = o_im * g_im
            re = o_re * g_re + jnp.where(first_row, 0.0, both)
            im = jnp.where(first_row, both, o_re * g_im - o_im * g_re)
            pairs.append(jnp.concatenate([re, im], axis=0))
        paired = left_dot(idft[...], parts(jnp.concatenate(pairs, axis=1)))
        at_values = pl.ds(pl.multiple_of(2 * features + cut * 256, 256), 256)
        projected[rows, at_values] = (paired[:, :256] * alive).astype(low)
        grad_kernel = paired[:, 256:]
        small_terms[0, :, taken] += grad_kernel
        k = keys[rows, taken]
        for j in range(3):
            moved = later(k, j) if j else k
            small_terms[1, j : j + 1, taken] += jnp.sum(grad_kernel * moved, axis=0, keepdims=True)
        grad_keys = taps[0] * grad_kernel + taps[1] * sooner(grad_kernel, 1) + taps[2] * sooner(grad_kernel, 2)
        at_keys = pl.ds(pl.multiple_of(features + cut * 256, 256), 256)
        projected[rows, at_keys] = (grad_keys * alive).astype(low)

    def mixed_back(m):
        mixer_blocks(m, mix_back)

    def input_back(m):
        rows = sequence(m)
        total[rows] = dot_back(projected[rows], matrix(1, 0, 3 * features))

        def body(rows):
            grad = after[rows] + norm_grad(rows, total[rows], norm_one, scale_one, rows8[3:4], 3)
            grad_low[rows] = grad.astype(low)

        in_rows(body, m * slots, slots)

    pieces = [after_back, gated_back]
    mixing = [functools.partial(mixed_back, m) for m in range(micro)]
    for m in range(micro):
        pieces += [mixing[m], functools.partial(input_back, m)]

    def last_copies():
        right_copy(0).start()
        small_copy().start()

    pieces += [last_copies]

    @pl.when(here.second_layer)
    def _():
        after_back()
        gated_back()
        for m in range(micro):
            mixed_back(m)
            input_back(m)
            if m == micro - 1:
                terms(down[0], wait=True)
            if m:
                give(grad_low, m - 1).wait_send()
            give(grad_low, m).start()
        last_copies()
        turned(2)
        for chunk in down[1:]:
            terms(chunk)
        turned(1)
        turned(0)

    pl.semaphore_wait(ready, 2)

    def one_sum(act):
        @pl.when(here.core == 0)
        def _():
            for chunk, (array, _, width, shared) in enumerate(put_table):
                for half in range(2 if shared else 0):
                    target = landed[array].at[1 - here.home, :, columns(put_table, chunk, half)]
                    copy = pltpu.make_async_copy(nothing.at[:, pl.ds(0, width)], target, nothing_sems.at[chunk, half])
                    getattr(copy, act)()

    nothing[...] = jnp.zeros_like(nothing)
    one_sum("start")

    apart = here.core != here.layer
    over = (1 - here.core, here.partner)

    def swap(source, target, number, act):
        sems = swap_sems.at[number], swap_sems.at[number + 1]

        @pl.when(apart)
        def _():
            getattr(remote(source, target, *sems, over), act)()

        @pl.when(jnp.logical_not(apart))
        def _():
            getattr(pltpu.make_async_copy(source, target, sems[1]), act)()

    due = [max(0, needs[1] - len(pieces) + k) for k in range(len(pieces))]
    shared = [chunk for chunk in range(last) if put_table[chunk][3]]
    met = [4]

    swap(out_low, kept_out, 0, "start")
    for now in range(last + 1):
        for piece, at in zip(pieces, due):
            if at == now:
                pl.when(here.first_layer)(piece if piece in mixing else in_background(piece))
        early = shared if now == 1 else []
        for chunk in early + [now + 1]:
            if chunk < last and chunk not in down and (chunk not in shared or chunk in early):
                terms(chunk, wait=put_table[chunk][0] not in met)
                met.append(put_table[chunk][0])
        for chunk in shared:
            if now == chunk - 2:
                pl.when(here.first_layer)(functools.partial(sum_middle, chunk))
        if now < last:
            sum_one(now)
        if 1 <= now:
            sum_two(now - 1)
        if now == needs[0]:
            swap(grad_low, kept_grad, 2, "start")

    one_sum("wait")
    for chunk in range(last):
        for half in (0, 1):
            for slot in (0, 1):
                target = landed[put_table[chunk][0]].at[slot, :, columns(put_table, chunk, half)]
                wanted = (here.core == 1) | (here.home == slot) if put_table[chunk][3] else True
                when(wanted, functools.partial(arrived, target, z_recv.at[chunk, slot, half]))
        for step in range(4):

            def action():
                put_first(chunk, step).wait_send()
                put_second(chunk, step).wait_send()
                put_third(chunk, step, "wait_send")

            when(handled(put_table, chunk, far(step)), action)
        if put_table[chunk][3]:
            pl.when(here.first_layer)(lambda: put_middle(chunk).wait_send())

    @pl.when(own_feed)
    def _():
        remote(hidden_in, feed, feed_sems.at[1], feed_sems.at[0], partner).wait_send()
        remote(live_own, live, feed_sems.at[3], feed_sems.at[2], partner).wait_send()

    for k in range(4):
        left_copy(k).wait_send()
        right_copy(k).wait_send()
    small_copy().wait_send()
    pl.when(here.second_layer)(lambda: give(grad_low, micro - 1).wait_send())
    swap(out_low, kept_out, 0, "wait")
    swap(grad_low, kept_grad, 2, "wait")


def finish_kernel(*refs):
    landed, (out, grad) = refs[:5], refs[5:7]
    s_filters, s_taps, s_one, s_two = refs[7:11]
    sums, (to_out, to_grad) = refs[11:15], refs[15:17]
    to_out[...] = out[...]
    to_grad[...] = grad[...]
    small = landed[0][0].astype(jnp.float32) + landed[0][1].astype(jnp.float32)
    s_filters[...] = small[:, :128]
    own = small.shape[0]
    rows = jnp.pad(small[:, 128:], ((0, 128 - own), (0, 0))).T
    for j in range(3):
        s_taps[j] = rows[j : j + 1, :own]
    s_one[...] = rows[3:4, :own]
    s_two[...] = rows[4:5, :own]
    for number, result in enumerate(sums):
        result[...] = landed[1 + number][0].astype(jnp.float32) + landed[1 + number][1].astype(jnp.float32)


def fast_device(
    hidden_in, out_grad, lengths, gain_mixer, w_input, w_taps, filters, w_output, gain_mlp, w_gate_up, w_down
):
    micro, _, slots, features = hidden_in.shape
    tokens, rows = micro * slots, gain_mixer.shape[1]
    shards = (w_input[0], w_output[0], w_gate_up[0], w_down[0].T)
    widths = [256] + [shard.shape[1] for shard in shards]
    hidden = widths[4]
    get_table, put_table = chunks_of(GET_PIECES), chunks_of(PUT_PIECES)
    dft, idft = (jnp.asarray(table) for table in packed_tables(slots))
    low, f32 = jnp.bfloat16, jnp.float32
    anywhere = pl.BlockSpec(memory_space=pl.ANY)
    inside = pl.BlockSpec(memory_space=pltpu.VMEM)
    dma, vmem = pltpu.SemaphoreType.DMA, pltpu.VMEM
    act, act_low = (tokens, features), vmem((tokens, features), low)
    kinds = [jax.ShapeDtypeStruct((2, rows, width), low) for width in widths]
    kinds += [jax.ShapeDtypeStruct((tokens, features), low)] * 2
    room = [vmem((rows, 256), low), vmem((128, 128), f32)] + [vmem((micro, 8, 128), f32)] * 2
    room += [vmem((rows, max(entry[2] for entry in put_table)), low), dma((len(put_table), 2))]
    room += [vmem((4, 2, 2, rows, width), low) for width in widths]
    room += [act_low] * 6
    room += [vmem((slots, features), f32), vmem((8, features), f32), vmem(act, f32), vmem(act, f32)]
    room += [vmem((tokens, 128), f32)] * 2
    room += [act_low] * 3 + [vmem(act, f32)] * 4 + [vmem((micro, 2 * slots, features), f32)] * 2
    room += [vmem(act, f32)] * 2 + [vmem((tokens, 2 * hidden), low), vmem((tokens, hidden), low)]
    room += [vmem((tokens, 3 * features), low), act_low, vmem((2, slots, features), f32)]
    room += [vmem((2, features, tokens), low)] * 4
    room += [vmem((slots, features), f32)] + [vmem((tokens, width // 2), low) for width in widths[1:]]
    room += [vmem((4, 2, 2, rows, entry[2]), low) for entry in put_table]
    for width in (128, hidden // 2):
        room += [vmem((4, 2, rows, width), low), vmem((4, rows, width), low)]
    got, put = len(get_table), len(put_table)
    room += [dma((got, 2, 2))] + [dma((got, 4))] * 5 + [dma((got, 2))] * 2 + [dma((got,))] * 2 + [dma((4,))]
    room += [dma((4,)), dma((micro,)), dma((micro,)), dma((9,)), dma((9,))]
    room += [dma((put, 4))] * 5 + [dma((put, 2, 2))] + [dma((put,))] * 2 + [pltpu.SemaphoreType.REGULAR] * 2
    results = pl.pallas_call(
        functools.partial(layer_kernel, get_table, put_table, widths),
        out_shape=kinds,
        in_specs=[inside] * 4 + [pl.BlockSpec(memory_space=pltpu.SMEM)] + [inside] * 2 + [anywhere] * 6,
        out_specs=[anywhere] * 7,
        scratch_shapes=room,
        compiler_params=pltpu.CompilerParams(
            collective_id=0, has_side_effects=True, vmem_limit_bytes=62 * 1024 * 1024
        ),
    )(
        filters[0].T,
        w_taps[0],
        gain_mixer,
        gain_mlp,
        lengths.T,
        dft,
        idft,
        *shards,
        hidden_in.reshape(tokens, features),
        out_grad.reshape(tokens, features),
    )
    kinds = [(rows, 128), (3, 1, rows), (1, rows), (1, rows)] + [(rows, width) for width in widths[1:]]
    kinds = [jax.ShapeDtypeStruct(kind, f32) for kind in kinds] + kinds_of(results[5:])
    s_filters, s_taps, s_one, s_two, s_in, s_out, s_gu, s_dt, layer_out, input_grad = pl.pallas_call(
        finish_kernel,
        out_shape=kinds,
        in_specs=[inside] * 7,
        out_specs=[inside] * 10,
        compiler_params=pltpu.CompilerParams(vmem_limit_bytes=62 * 1024 * 1024),
    )(*results)
    shape = (1, micro, 1, slots, features)
    return (
        layer_out.reshape(shape),
        input_grad.reshape(shape),
        s_one,
        s_in[None],
        s_taps.transpose(1, 0, 2),
        s_filters.T[None],
        s_out[None],
        s_two,
        s_gu[None],
        s_dt.T[None],
    )


def kinds_of(arrays):
    return [jax.ShapeDtypeStruct(array.shape, array.dtype) for array in arrays]


def solution(mesh):
    placed = (
        P(None, "dp", None, None),
        P(None, "dp", None, None),
        P(None, "dp"),
        P("section", "dp"),
        P("section", "dp", None),
        P("section", None, "dp"),
        P("section", None, "dp"),
        P("section", "dp", None),
        P("section", "dp"),
        P("section", "dp", None),
        P("section", None, "dp"),
    )
    return jax.shard_map(
        fast_device if mesh.shape["dp"] == 16 and mesh.shape["section"] == 2 else on_device,
        mesh=mesh,
        in_specs=placed,
        out_specs=(
            P("section", None, "dp", None, None),
            P("section", None, "dp", None, None),
            P("section", "dp"),
            P("section", "dp", None),
            P("section", None, "dp"),
            P("section", None, "dp"),
            P("section", "dp", None),
            P("section", "dp"),
            P("section", "dp", None),
            P("section", None, "dp"),
        ),
        check_vma=False,
    )
```
